32 devices in a mesh: lon: 8 (over z, x), lat: 4 (over y, core).
Axes of the slice: x: 2, y: 2, z: 4, core: 2. Of those that a mesh axis runs over, the one named last changes fastest.
Arguments:
- state: float32 [25, 512, 1024], P(None, 'lat', 'lon'), may hold values from -6 to 6
- adjoint_in: float32 [25, 512, 1024], P(None, 'lat', 'lon'), may hold values from -6 to 6
- land_mask: int32 [512, 1024], P('lat', 'lon'), may hold values 0 or 1
- east_coef: float32 [512, 1024], P('lat', 'lon'), may hold values from 0.03 to 0.25
- north_coef: float32 [512, 1024], P('lat', 'lon'), may hold values from 0.03 to 0.25
- zonal_flow: float32 [512, 1024], P('lat', 'lon'), may hold values from -0.2 to 0.2
- vertical_coef: float32 [512, 1024], P('lat', 'lon'), may hold values from 0.05 to 0.3
- slot_cell: int32 [32, 2048], P(('lon', 'lat')), may hold values from -1 to 16383, as said below
- slot_weight: float32 [32, 2048], P(('lon', 'lat')), may hold values from 0.1 to 1
- arrive_obs: int32 [32, 2048], P(('lon', 'lat')), may hold values from -1 to 511, as said below
- obs_value: float32 [25, 16384], P(None, ('lon', 'lat')), may hold values from -6 to 6
- obs_invvar: float32 [25, 16384], P(None, ('lon', 'lat')), may hold values from 0.5 to 4
Outputs:
- adjoint_state: float32 [25, 512, 1024], P(None, 'lat', 'lon')
- misfit: float32 [25, 16384], P(None, ('lon', 'lat'))
The draws below stay inside these ranges and needn't reach their ends.
Inputs may be any that keep to these rules, and one draw needn't show every extreme that they name: slot_cell[s, t * 64 + p] is the index, row-major over the 128 x 128 block of device s, of the cell that slot p from device s to device t reads, or -1 where that slot is empty; from each device to each device the live slots are those with p below a count of 1 to 64, and some device receives 64 live slots from every device. arrive_obs[t, s * 64 + p] is the observation of device t fed by slot p from device s, and is -1 exactly where slot_cell[s, t * 64 + p] is -1.
All inputs are finite; a program needn't handle non-finite values. No bound on the sum of `land_mask` on one device may be relied on, other than what follows from the above.
Results may differ from the reference program's by a relative error of at most 0.00002.
Values sent between devices are 32-bit elements; how exact they have to be, the bound alone decides.
No kernel may reach another device: no remote copies, remote signals or barrier semaphores. Data moves between devices by JAX's collectives and lax.ppermute only.
A program may use at most 64 MiB of HBM per device.

```python
import math
import jax
import jax.numpy as jnp

LEVELS = 25
STEPS = 2
CLAT = 128
CLON = 128
CAP = 64
OBS_DEV = 512
NLAT = 512
NLON = 1024
CELLS = 16384
SLOTS = 2048
NOBS = 16384
N_LON = 8
N_LAT = 4
DEVICES = 32


def slot_plan(key):
    base_key = jax.random.fold_in(key, 11)
    keys = jax.random.split(base_key, 4)
    counts = jax.random.randint(keys[0], (DEVICES, DEVICES), 1, CAP + 1)
    full_owner = jax.random.randint(keys[1], (), 0, DEVICES)
    counts = jnp.where(jnp.arange(DEVICES)[None, :] == full_owner, CAP, counts)
    live_slot = jnp.arange(CAP)[None, None, :] < counts[:, :, None]
    cell_draw = jax.random.randint(keys[2], (DEVICES, DEVICES, CAP), 0, CLAT * CLON)
    target_draw = jax.random.randint(keys[3], (DEVICES, DEVICES, CAP), 0, OBS_DEV)
    return (live_slot, cell_draw, target_draw)


def draw_slot_cell(key, part):
    live_slot, cell_draw, target_draw = slot_plan(key)
    return jnp.where(live_slot, cell_draw, -1).reshape(DEVICES, DEVICES * CAP).astype(jnp.int32)


def draw_arrive_obs(key, part):
    live_slot, cell_draw, target_draw = slot_plan(key)
    marked = jnp.where(live_slot, target_draw, -1)
    return marked.transpose(1, 0, 2).reshape(DEVICES, DEVICES * CAP).astype(jnp.int32)


def plant(entries, own_key, low, largest):
    extent = entries.shape
    index_at = [jax.random.randint(jax.random.fold_in(own_key, axis), (), 0, extent[axis]) for axis in range(len(extent))]
    entries = entries.at[tuple(index_at)].set(low)
    longest = extent.index(max(extent))
    index_at[longest] = (index_at[longest] + 1) % extent[longest]
    return entries.at[tuple(index_at)].set(largest)


def level_of(own_key, shape, pieces, low, largest):
    def one(position, parts):
        draws = jax.random.uniform(jax.random.fold_in(jax.random.fold_in(own_key, 6), position), (parts,), jnp.float32, low / len(pieces), largest / len(pieces))
        return jnp.repeat(jnp.exp(draws), shape[position] // parts).reshape((-1,) + (1,) * (len(shape) - position - 1))

    gain = one(*pieces[0])
    for cut in pieces[1:]:
        gain = gain * one(*cut)
    return gain


def gaussian(stream_key, dims, scale, bound, shards=(), dtype=jnp.bfloat16):
    values = scale * jax.random.normal(stream_key, dims, jnp.float32)
    if shards:
        values = values * level_of(stream_key, dims, shards, -0.22, 0.18)
    return jnp.clip(values, -bound, bound).astype(dtype)


def setup_inputs(seed: int = 0) -> dict:
    splits = jax.random.split(jax.random.key(seed), 13)
    return {
        "state": gaussian(splits[0], (LEVELS, NLAT, NLON), 1.0, 6.0, ((1, 4), (2, 8)), jnp.float32),
        "adjoint_in": gaussian(splits[1], (LEVELS, NLAT, NLON), 1.0, 6.0, ((1, 4), (2, 8)), jnp.float32),
        "land_mask": plant((jax.random.randint(splits[2], (NLAT, NLON), 0, 4) < 3).astype(jnp.int32), jax.random.fold_in(splits[2], 1), 0, 1),
        "east_coef": jnp.clip(jnp.exp(math.log(0.25) - 2.1202636 * jax.random.uniform(splits[3], (NLAT, NLON), jnp.float32) ** level_of(splits[3], (NLAT, NLON), ((0, 4), (1, 8)), -0.2, 0.2)), 0.03, 0.25),
        "north_coef": jnp.clip(jnp.exp(math.log(0.25) - 2.1202636 * jax.random.uniform(splits[4], (NLAT, NLON), jnp.float32) ** level_of(splits[4], (NLAT, NLON), ((0, 4), (1, 8)), -0.2, 0.2)), 0.03, 0.25),
        "zonal_flow": jnp.clip(jax.random.uniform(splits[5], (NLAT, NLON), jnp.float32, -0.2, 0.2) * level_of(splits[5], (NLAT, NLON), ((0, 4), (1, 8)), -0.4, 0.0), -0.2, 0.2),
        "vertical_coef": jnp.clip(jnp.exp(math.log(0.3) - 1.7917595 * jax.random.uniform(splits[6], (NLAT, NLON), jnp.float32) ** level_of(splits[6], (NLAT, NLON), ((0, 4), (1, 8)), -0.2, 0.2)), 0.05, 0.3),
        "slot_cell": draw_slot_cell(jax.random.fold_in(splits[12], 71), 0),
        "slot_weight": jnp.clip(0.1 + 0.9 * jax.random.uniform(splits[8], (DEVICES, SLOTS), jnp.float32) ** level_of(splits[8], (DEVICES, SLOTS), ((0, 32),), -0.2, 0.2), 0.1, 1.0),
        "arrive_obs": draw_arrive_obs(jax.random.fold_in(splits[12], 71), 0),
        "obs_value": gaussian(splits[10], (LEVELS, NOBS), 1.0, 6.0, ((1, 32),), jnp.float32),
        "obs_invvar": jnp.clip(jnp.exp(math.log(4.0) - 2.0794415 * jax.random.uniform(splits[11], (LEVELS, NOBS), jnp.float32) ** level_of(splits[11], (LEVELS, NOBS), ((1, 32),), -0.2, 0.2)), 0.5, 4.0),
    }


def to_blocks(field):
    return field.reshape(LEVELS, N_LAT, CLAT, N_LON, CLON).transpose(0, 3, 1, 2, 4).reshape(LEVELS, DEVICES, CELLS)

def from_blocks(blocked):
    return blocked.reshape(LEVELS, N_LON, N_LAT, CLAT, CLON).transpose(0, 2, 3, 1, 4).reshape(LEVELS, NLAT, NLON)

def model_step(field, ocean, east_coef, north_coef, zonal_flow, vertical_coef):
    east_field = jnp.roll(field, -1, axis=2)
    north_field = jnp.concatenate([field[:, 1:, :], field[:, -1:, ::-1]], axis=1)
    east_flux = east_coef * (east_field - field) - 0.5 * zonal_flow * (field + east_field)
    north_flux = north_coef * (north_field - field)
    zero_row = jnp.zeros_like(north_flux[:, :1, :])
    divergence = east_flux - jnp.roll(east_flux, 1, axis=2)
    divergence = divergence + north_flux - jnp.concatenate([zero_row, north_flux[:, :-1, :]], axis=1)
    vertical_flux = vertical_coef * (field[1:] - field[:-1])
    zero_level = jnp.zeros_like(field[:1])
    divergence = divergence + jnp.concatenate([vertical_flux, zero_level], axis=0)
    divergence = divergence - jnp.concatenate([zero_level, vertical_flux], axis=0)
    return field + ocean * divergence

def reference(state, adjoint_in, land_mask, east_coef, north_coef, zonal_flow, vertical_coef, slot_cell, slot_weight, arrive_obs, obs_value, obs_invvar):
    blocked = to_blocks(state)
    live_slot = slot_cell >= 0
    cell_index = jnp.where(live_slot, slot_cell, 0).astype(jnp.int32)
    weights = jnp.where(live_slot, slot_weight, jnp.zeros_like(slot_weight))
    picked = jnp.take_along_axis(blocked, cell_index[None], axis=2)
    partial_vals = picked * weights[None]
    at_owner = partial_vals.reshape(LEVELS, DEVICES, DEVICES, CAP).transpose(0, 2, 1, 3).reshape(LEVELS, DEVICES, SLOTS)
    live_target = arrive_obs >= 0
    owner_base = (jnp.arange(DEVICES).astype(jnp.int32) * OBS_DEV)[:, None]
    global_id = jnp.where(live_target, owner_base + arrive_obs, NOBS).astype(jnp.int32)
    interp = jnp.zeros((LEVELS, NOBS + 1), jnp.float32).at[:, global_id.reshape(-1)].add(at_owner.reshape(LEVELS, -1))[:, :NOBS]
    misfit = obs_invvar * (interp - obs_value)
    clipped = jnp.minimum(global_id, NOBS - 1).astype(jnp.int32)
    returned = jnp.where(live_target[None], misfit[:, clipped], jnp.zeros((), jnp.float32))
    returned = returned.reshape(LEVELS, DEVICES, DEVICES, CAP).transpose(0, 2, 1, 3).reshape(LEVELS, DEVICES, SLOTS)
    weighted = returned * weights[None]
    cell_base = (jnp.arange(DEVICES).astype(jnp.int32) * CELLS)[:, None]
    cell_id = jnp.where(live_slot, cell_base + slot_cell, DEVICES * CELLS).astype(jnp.int32)
    forcing = jnp.zeros((LEVELS, DEVICES * CELLS + 1), jnp.float32).at[:, cell_id.reshape(-1)].add(weighted.reshape(LEVELS, -1))
    forcing = forcing[:, :DEVICES * CELLS].reshape(LEVELS, DEVICES, CELLS)
    adjoint_seed = adjoint_in + from_blocks(forcing)
    ocean = land_mask.astype(jnp.float32)

    def advance(field):
        return model_step(field, ocean, east_coef, north_coef, zonal_flow, vertical_coef)
    unused, pull_back = jax.vjp(advance, state)
    adjoint_state = adjoint_seed
    for repeat in range(STEPS):
        adjoint_state = pull_back(adjoint_state)[0]
    return (adjoint_state, misfit)
```

```python
import functools

import jax
import jax.numpy as jnp
from jax import lax
from jax.experimental import pallas as pl
from jax.experimental.pallas import tpu as pltpu
from jax.sharding import PartitionSpec as P

STEPS = 2
LANES = 128
GROUP = 32
VMEM_BYTES = 48 * 1024 * 1024
BOTH = ("lon", "lat")


def pieces(value):
    high = value.astype(jnp.bfloat16)
    rest = value - high.astype(jnp.float32)
    middle = rest.astype(jnp.bfloat16)
    low = (rest - middle.astype(jnp.float32)).astype(jnp.bfloat16)
    return high, middle, low


def log2(size):
    assert size & (size - 1) == 0
    return size.bit_length() - 1


def cell_parts(cell, rows_n, cols_n):
    cell = jnp.maximum(cell, 0)
    row = jnp.right_shift(cell, log2(cols_n))
    group = jnp.right_shift(row, log2(GROUP))
    place = jnp.bitwise_and(cell, cols_n - 1) + group * cols_n
    return place, jnp.bitwise_and(row, GROUP - 1)


def one_hot(index, size):
    rows = lax.broadcasted_iota(jnp.int32, (size, index.shape[1]), 0)
    return jnp.where(rows == index, 1.0, 0.0).astype(jnp.bfloat16)


def packed_pair(values):
    half = values.shape[0] // 2
    first = lax.broadcasted_iota(jnp.int32, (half, LANES), 1) < LANES // 2
    top, bottom = values[:half], values[half:]
    left = jnp.where(first, top, pltpu.roll(bottom, LANES // 2, 1))
    right = jnp.where(first, pltpu.roll(top, LANES // 2, 1), bottom)
    return left, right


def unpacked_pair(left, right):
    half = left.shape[0]
    first = lax.broadcasted_iota(jnp.int32, (half, LANES), 1) < LANES // 2
    top = jnp.where(first, left, pltpu.roll(right, LANES // 2, 1))
    bottom = jnp.where(first, pltpu.roll(left, LANES // 2, 1), right)
    return jnp.concatenate([top, bottom], axis=0)


def padded_levels(values, levels):
    return jnp.concatenate(
        [values, jnp.zeros((levels - values.shape[0], values.shape[1]), values.dtype)], axis=0
    )


def gather_kernel(cell_ref, weight_ref, state_ref, out_ref, field_ref):
    levels_n, rows_n, cols_n = state_ref.shape
    groups = rows_n // GROUP
    width = groups * cols_n
    for group in range(groups):
        block = state_ref[:, group * GROUP : (group + 1) * GROUP, :]
        for part, piece in enumerate(pieces(block.reshape(levels_n * GROUP, cols_n))):
            at = part * width + group * cols_n
            field_ref[:, at : at + cols_n] = piece
    tile = 2 * LANES

    def body(step, carry):
        at = pl.ds(pl.multiple_of(step * tile, tile), tile)
        cell = cell_ref[:, at]
        weight = jnp.where(cell >= 0, weight_ref[:, at], 0.0)
        place, row = cell_parts(cell, rows_n, cols_n)
        hot = one_hot(place, width)
        found = jnp.dot(
            field_ref[...],
            jnp.concatenate([hot, hot, hot], axis=0),
            preferred_element_type=jnp.float32,
        ).reshape(levels_n, GROUP, tile)
        mine = lax.broadcasted_iota(jnp.int32, (GROUP, tile), 0) == row
        values = jnp.sum(jnp.where(mine[None], found, 0.0), axis=1) * weight
        values = padded_levels(values, 2 * out_ref.shape[1])
        for pair in range(tile // LANES):
            left, right = packed_pair(values[:, pair * LANES : (pair + 1) * LANES])
            out_ref[step * (2 * tile // LANES) + 2 * pair] = left
            out_ref[step * (2 * tile // LANES) + 2 * pair + 1] = right
        return carry

    lax.fori_loop(0, cell_ref.shape[1] // tile, body, 0)


def observe_kernel(arrived_ref, target_ref, value_ref, invvar_ref, misfit_ref, out_ref, hot_ref, in_ref):
    devices, half, _ = arrived_ref.shape
    levels_n, obs_n = value_ref.shape
    levels = 2 * half

    def load(pair, carry):
        at = pl.ds(pl.multiple_of(pair * LANES, LANES), LANES)
        values = unpacked_pair(arrived_ref[2 * pair], arrived_ref[2 * pair + 1])
        for part, piece in enumerate(pieces(values)):
            in_ref[part * levels : (part + 1) * levels, at] = piece
        hot_ref[:, at] = one_hot(target_ref[:, at], obs_n)
        return carry

    lax.fori_loop(0, devices // 2, load, 0)
    sums = lax.dot_general(
        in_ref[...], hot_ref[...], (((1,), (1,)), ((), ())), preferred_element_type=jnp.float32
    )
    interp = sums[:levels] + sums[levels : 2 * levels] + sums[2 * levels :]
    misfit = invvar_ref[...] * (interp[:levels_n] - value_ref[...])
    misfit_ref[...] = misfit
    back = jnp.concatenate(pieces(padded_levels(misfit, levels)), axis=0)
    tile = 4 * LANES

    def store(step, carry):
        at = pl.ds(pl.multiple_of(step * tile, tile), tile)
        found = jnp.dot(back, hot_ref[:, at], preferred_element_type=jnp.float32)
        values = found[:levels] + found[levels : 2 * levels] + found[2 * levels :]
        for pair in range(tile // LANES):
            left, right = packed_pair(values[:, pair * LANES : (pair + 1) * LANES])
            out_ref[step * (2 * tile // LANES) + 2 * pair] = left
            out_ref[step * (2 * tile // LANES) + 2 * pair + 1] = right
        return carry

    lax.fori_loop(0, target_ref.shape[1] // tile, store, 0)


def scatter_kernel(returned_ref, cell_ref, weight_ref, adjoint_ref, out_ref, rows_ref, hot_ref, sum_ref):
    levels_n, rows_n, cols_n = out_ref.shape
    groups = rows_n // GROUP
    width = groups * cols_n
    tile = hot_ref.shape[1] // 3

    sum_ref[...] = jnp.zeros_like(sum_ref)

    def body(step, carry):
        at = pl.ds(pl.multiple_of(step * tile, tile), tile)
        cell = cell_ref[:, at]
        weight = jnp.where(cell >= 0, weight_ref[:, at], 0.0)
        place, row = cell_parts(cell, rows_n, cols_n)
        base = step * (2 * tile // LANES)
        values = jnp.concatenate(
            [
                unpacked_pair(returned_ref[base + 2 * pair], returned_ref[base + 2 * pair + 1])
                for pair in range(tile // LANES)
            ],
            axis=1,
        )
        values = pieces(values * weight)
        hot = one_hot(place, width)
        mine = one_hot(row, GROUP)
        for part in range(3):
            hot_ref[:, part * tile : (part + 1) * tile] = hot
            for level in range(levels_n):
                rows_ref[level * GROUP : (level + 1) * GROUP, part * tile : (part + 1) * tile] = (
                    mine * values[part][level : level + 1, :]
                )
        sum_ref[...] += lax.dot_general(
            rows_ref[...], hot_ref[...], (((1,), (1,)), ((), ())), preferred_element_type=jnp.float32
        )
        return carry

    lax.fori_loop(0, cell_ref.shape[1] // tile, body, 0)
    for group in range(groups):
        at = slice(group * GROUP, (group + 1) * GROUP)
        forcing = sum_ref[:, group * cols_n : (group + 1) * cols_n]
        out_ref[:, at, :] = adjoint_ref[:, at, :] + forcing.reshape(levels_n, GROUP, cols_n)


def kernel_call(body, out_shape, scratch):
    return pl.pallas_call(
        body,
        out_shape=out_shape,
        scratch_shapes=scratch,
        compiler_params=pltpu.CompilerParams(vmem_limit_bytes=VMEM_BYTES),
    )


def f32(*shape):
    return jax.ShapeDtypeStruct(shape, jnp.float32)


def from_behind(value, axis, steps):
    count = lax.axis_size(axis)
    pairs = [(source, (source + steps) % count) for source in range(count)]
    return lax.ppermute(value, axis, pairs)


def from_behind_2(block, axis, distance):
    devices = range(lax.axis_size(axis))
    route = [(i - distance, i) for i in devices if i - distance in devices]
    return lax.ppermute(block, axis, route)


def padded(cells, sides, width, closed):
    for axis, dim in sides:
        count = lax.axis_size(axis)
        ends = count if closed else count - 1
        head = lax.slice_in_dim(cells, 0, width, axis=dim)
        tail = lax.slice_in_dim(cells, cells.shape[dim] - width, cells.shape[dim], axis=dim)
        cells = jnp.concatenate(
            [
                lax.ppermute(tail, axis, [(i, (i + 1) % count) for i in range(ends)]),
                cells,
                lax.ppermute(head, axis, [((i + 1) % count, i) for i in range(ends)]),
            ],
            axis=dim,
        )
    return cells


def from_partner(value, axis, bit):
    return lax.ppermute(value, axis, [(i, i ^ 1 << bit) for i in range(lax.axis_size(axis))])


def on_device(
    state,
    adjoint_in,
    land_mask,
    east_coef,
    north_coef,
    zonal_flow,
    vertical_coef,
    slot_cell,
    slot_weight,
    arrive_obs,
    obs_value,
    obs_invvar,
):
    levels_n, rows_n, cols_n = state.shape
    devices = lax.axis_size(BOTH)
    slots = slot_cell.shape[1]
    obs_n = obs_value.shape[1]
    assert 2 * (slots // devices) == LANES
    half = (levels_n + 15) // 16 * 8
    width = rows_n // GROUP * cols_n
    bf16 = jnp.bfloat16

    partial_vals = kernel_call(
        gather_kernel, f32(devices, half, LANES), [pltpu.VMEM((levels_n * GROUP, 3 * width), bf16)]
    )(slot_cell, slot_weight, state)
    arrived = lax.all_to_all(partial_vals, BOTH, split_axis=0, concat_axis=0, tiled=True)
    misfit, outgoing = kernel_call(
        observe_kernel,
        (f32(levels_n, obs_n), f32(devices, half, LANES)),
        [pltpu.VMEM((obs_n, slots), bf16), pltpu.VMEM((6 * half, slots), bf16)],
    )(arrived, arrive_obs, obs_value, obs_invvar)
    returned = lax.all_to_all(outgoing, BOTH, split_axis=0, concat_axis=0, tiled=True)
    tile = 4 * LANES
    adjoint_state = kernel_call(
        scatter_kernel,
        f32(levels_n, rows_n, cols_n),
        [
            pltpu.VMEM((levels_n * GROUP, 3 * tile), bf16),
            pltpu.VMEM((width, 3 * tile), bf16),
            pltpu.VMEM((levels_n * GROUP, width), jnp.float32),
        ],
    )(returned, slot_cell, slot_weight, adjoint_in)
    ocean = land_mask.astype(jnp.float32)
    east_weight = east_coef - 0.5 * zonal_flow
    own_east = east_coef + 0.5 * zonal_flow
    west_column = from_behind(east_weight[:, -1:], "lon", 1)
    west_weight = jnp.concatenate([west_column, east_weight[:, :-1]], axis=1)
    south_row = from_behind_2(north_coef[-1:, :], "lat", 1)
    south_weight = jnp.concatenate([south_row, north_coef[:-1, :]], axis=0)
    lat_last = lax.axis_index("lat") == lax.axis_size("lat") - 1
    zero_level = jnp.zeros((1, rows_n, cols_n), jnp.float32)
    for repeat in range(STEPS):
        masked = ocean * adjoint_state
        zonal_pad = padded(masked, (("lon", 2),), 1, True)
        merid_pad = padded(masked, (("lat", 1),), 1, False)
        east_vals = zonal_pad[:, :, 2:]
        west_vals = zonal_pad[:, :, :-2]
        north_vals = merid_pad[:, 2:, :]
        south_vals = merid_pad[:, :-2, :]
        east_diff = masked - east_vals
        north_diff = masked - north_vals
        updated = adjoint_state - own_east * east_diff + west_weight * (west_vals - masked)
        updated = updated - north_coef * north_diff + south_weight * (south_vals - masked)
        fold_top = north_coef[-1][None, :] * masked[:, -1, :]
        for bit_index in range(lax.axis_size("lon").bit_length() - 1):
            fold_top = from_partner(fold_top, "lon", bit_index)
        mirrored = fold_top[:, ::-1]
        updated = updated.at[:, -1, :].add(jnp.where(lat_last, mirrored, 0.0))
        vertical_term = vertical_coef[None] * (masked[:-1] - masked[1:])
        updated = updated - jnp.concatenate([vertical_term, zero_level], axis=0)
        updated = updated + jnp.concatenate([zero_level, vertical_term], axis=0)
        adjoint_state = updated
    return (adjoint_state, misfit)


def solution(mesh):
    in_specs = (
        P(None, "lat", "lon"),
        P(None, "lat", "lon"),
        P("lat", "lon"),
        P("lat", "lon"),
        P("lat", "lon"),
        P("lat", "lon"),
        P("lat", "lon"),
        P(("lon", "lat"), None),
        P(("lon", "lat"), None),
        P(("lon", "lat"), None),
        P(None, ("lon", "lat")),
        P(None, ("lon", "lat")),
    )
    out_specs = (P(None, "lat", "lon"), P(None, ("lon", "lat")))
    return jax.shard_map(
        on_device, mesh=mesh, in_specs=in_specs, out_specs=out_specs, check_vma=False
    )
```

```python
import functools

import jax
import jax.numpy as jnp
from jax import lax
from jax.experimental import pallas as pl
from jax.experimental.pallas import tpu as pltpu
from jax.sharding import PartitionSpec as P

STEPS = 2
LANES = 128
GROUP = 32
SUB = 8
VMEM_BYTES = 48 * 1024 * 1024
BOTH = ("lon", "lat")


def pieces(value):
    high = value.astype(jnp.bfloat16)
    rest = value - high.astype(jnp.float32)
    middle = rest.astype(jnp.bfloat16)
    low = (rest - middle.astype(jnp.float32)).astype(jnp.bfloat16)
    return high, middle, low


def log2(size):
    assert size & (size - 1) == 0
    return size.bit_length() - 1


def cell_parts(cell, rows_n, cols_n):
    cell = jnp.maximum(cell, 0)
    row = jnp.right_shift(cell, log2(cols_n))
    group = jnp.right_shift(row, log2(GROUP))
    place = jnp.bitwise_and(cell, cols_n - 1) + group * cols_n
    return place, jnp.bitwise_and(row, GROUP - 1)


def one_hot(index, size):
    rows = lax.broadcasted_iota(jnp.int32, (size, index.shape[1]), 0)
    return jnp.where(rows == index, 1.0, 0.0).astype(jnp.bfloat16)


def packed_pair(values):
    half = values.shape[0] // 2
    first = lax.broadcasted_iota(jnp.int32, (half, LANES), 1) < LANES // 2
    top, bottom = values[:half], values[half:]
    left = jnp.where(first, top, pltpu.roll(bottom, LANES // 2, 1))
    right = jnp.where(first, pltpu.roll(top, LANES // 2, 1), bottom)
    return left, right


def unpacked_pair(left, right):
    half = left.shape[0]
    first = lax.broadcasted_iota(jnp.int32, (half, LANES), 1) < LANES // 2
    top = jnp.where(first, left, pltpu.roll(right, LANES // 2, 1))
    bottom = jnp.where(first, pltpu.roll(left, LANES // 2, 1), right)
    return jnp.concatenate([top, bottom], axis=0)


def padded_levels(values, levels):
    return jnp.concatenate(
        [values, jnp.zeros((levels - values.shape[0], values.shape[1]), values.dtype)], axis=0
    )


def gather_kernel(cell_ref, weight_ref, state_ref, out_ref, field_ref):
    levels_n, rows_n, cols_n = state_ref.shape
    groups = rows_n // GROUP
    width = groups * cols_n
    for group in range(groups):
        block = state_ref[:, group * GROUP : (group + 1) * GROUP, :]
        for part, piece in enumerate(pieces(block.reshape(levels_n * GROUP, cols_n))):
            at = part * width + group * cols_n
            field_ref[:, at : at + cols_n] = piece
    tile = 2 * LANES

    def body(step, carry):
        at = pl.ds(pl.multiple_of(step * tile, tile), tile)
        cell = cell_ref[:, at]
        weight = jnp.where(cell >= 0, weight_ref[:, at], 0.0)
        place, row = cell_parts(cell, rows_n, cols_n)
        hot = one_hot(place, width)
        found = jnp.dot(
            field_ref[...],
            jnp.concatenate([hot, hot, hot], axis=0),
            preferred_element_type=jnp.float32,
        ).reshape(levels_n, GROUP, tile)
        mine = lax.broadcasted_iota(jnp.int32, (GROUP, tile), 0) == row
        values = jnp.sum(jnp.where(mine[None], found, 0.0), axis=1) * weight
        values = padded_levels(values, 2 * out_ref.shape[1])
        for pair in range(tile // LANES):
            left, right = packed_pair(values[:, pair * LANES : (pair + 1) * LANES])
            out_ref[step * (2 * tile // LANES) + 2 * pair] = left
            out_ref[step * (2 * tile // LANES) + 2 * pair + 1] = right
        return carry

    lax.fori_loop(0, cell_ref.shape[1] // tile, body, 0)


def observe_kernel(arrived_ref, target_ref, value_ref, invvar_ref, misfit_ref, out_ref, hot_ref, in_ref):
    devices, half, _ = arrived_ref.shape
    levels_n, obs_n = value_ref.shape
    levels = 2 * half

    def load(pair, carry):
        at = pl.ds(pl.multiple_of(pair * LANES, LANES), LANES)
        values = unpacked_pair(arrived_ref[2 * pair], arrived_ref[2 * pair + 1])
        for part, piece in enumerate(pieces(values)):
            in_ref[part * levels : (part + 1) * levels, at] = piece
        hot_ref[:, at] = one_hot(target_ref[:, at], obs_n)
        return carry

    lax.fori_loop(0, devices // 2, load, 0)
    sums = lax.dot_general(
        in_ref[...], hot_ref[...], (((1,), (1,)), ((), ())), preferred_element_type=jnp.float32
    )
    interp = sums[:levels] + sums[levels : 2 * levels] + sums[2 * levels :]
    misfit = invvar_ref[...] * (interp[:levels_n] - value_ref[...])
    misfit_ref[...] = misfit
    back = jnp.concatenate(pieces(padded_levels(misfit, levels)), axis=0)
    tile = 4 * LANES

    def store(step, carry):
        at = pl.ds(pl.multiple_of(step * tile, tile), tile)
        found = jnp.dot(back, hot_ref[:, at], preferred_element_type=jnp.float32)
        values = found[:levels] + found[levels : 2 * levels] + found[2 * levels :]
        for pair in range(tile // LANES):
            left, right = packed_pair(values[:, pair * LANES : (pair + 1) * LANES])
            out_ref[step * (2 * tile // LANES) + 2 * pair] = left
            out_ref[step * (2 * tile // LANES) + 2 * pair + 1] = right
        return carry

    lax.fori_loop(0, target_ref.shape[1] // tile, store, 0)


def scatter_kernel(
    returned_ref, cell_ref, weight_ref, adjoint_ref, mask_ref,
    out_ref, columns_ref, edges_ref,
    rows_ref, hot_ref, sum_ref,
):
    levels_n, rows_n, cols_n = out_ref.shape
    groups = rows_n // GROUP
    width = groups * cols_n
    tile = hot_ref.shape[1] // 3

    sum_ref[...] = jnp.zeros_like(sum_ref)

    def body(step, carry):
        at = pl.ds(pl.multiple_of(step * tile, tile), tile)
        cell = cell_ref[:, at]
        weight = jnp.where(cell >= 0, weight_ref[:, at], 0.0)
        place, row = cell_parts(cell, rows_n, cols_n)
        base = step * (2 * tile // LANES)
        values = jnp.concatenate(
            [
                unpacked_pair(returned_ref[base + 2 * pair], returned_ref[base + 2 * pair + 1])
                for pair in range(tile // LANES)
            ],
            axis=1,
        )
        values = pieces(values * weight)
        hot = one_hot(place, width)
        mine = one_hot(row, GROUP)
        for part in range(3):
            hot_ref[:, part * tile : (part + 1) * tile] = hot
            for level in range(levels_n):
                rows_ref[level * GROUP : (level + 1) * GROUP, part * tile : (part + 1) * tile] = (
                    mine * values[part][level : level + 1, :]
                )
        sum_ref[...] += lax.dot_general(
            rows_ref[...], hot_ref[...], (((1,), (1,)), ((), ())), preferred_element_type=jnp.float32
        )
        return carry

    lax.fori_loop(0, cell_ref.shape[1] // tile, body, 0)
    for group in range(groups):
        at = slice(group * GROUP, (group + 1) * GROUP)
        forcing = sum_ref[:, group * cols_n : (group + 1) * cols_n]
        out_ref[:, at, :] = adjoint_ref[:, at, :] + forcing.reshape(levels_n, GROUP, cols_n)

    level_at = jnp.right_shift(lax.broadcasted_iota(jnp.int32, (SUB, cols_n), 1), 2)
    for top in range(0, rows_n, SUB):
        ocean = mask_ref[top : top + SUB, :].astype(jnp.float32)
        found = jnp.zeros((SUB, cols_n), jnp.float32)
        for level in range(levels_n):
            block = pltpu.roll(out_ref[level, top : top + SUB, :], 4 * level + 2, 1)
            found = jnp.where(level_at == level, block, found)
        sides = pltpu.roll(ocean, 2, 1)
        spread = jnp.where(level_at == 0, sides, 0.0)
        shift = 4
        while shift < cols_n:
            spread = spread + pltpu.roll(spread, shift, 1)
            shift *= 2
        columns_ref[top : top + SUB, :] = found * spread
    for place, row in enumerate((0, 1, rows_n - 2, rows_n - 1)):
        ocean = mask_ref[row : row + 1, :].astype(jnp.float32)
        for level in range(levels_n):
            edges_ref[place, level : level + 1, :] = out_ref[level, row : row + 1, :] * ocean


def lane(shape):
    return lax.broadcasted_iota(jnp.int32, shape, 1)


def sublane(shape):
    return lax.broadcasted_iota(jnp.int32, shape, 0)


def shifted(block, steps, axis, edge):
    size = block.shape[axis]
    at = lax.broadcasted_iota(jnp.int32, block.shape, axis)
    moved = pltpu.roll(block, steps % size, axis)
    return jnp.where(at == (0 if steps > 0 else size - 1), edge, moved)


def reversed_lanes(block):
    at = block.shape[1] - 1 - lane(block.shape)
    return jnp.take_along_axis(block, at, axis=1, mode="promise_in_bounds")


def lon_neighbours(flag_ref, first, second):
    even = flag_ref[0] == 1
    return jnp.where(even, first, second), jnp.where(even, second, first)


def lat_neighbours(flag_ref, first, second):
    even = flag_ref[1] == 1
    return jnp.where(even, first, second), jnp.where(even, second, first)


def coefficient_columns_kernel(mask_ref, east_ref, north_ref, flow_ref, vertical_ref, out_ref):
    rows_n, cols_n = mask_ref.shape
    ocean = mask_ref[...].astype(jnp.float32)
    here = east_ref[...] + 0.5 * flow_ref[...]
    behind = east_ref[...] - 0.5 * flow_ref[...]
    north, vertical = north_ref[...], vertical_ref[...]
    last = cols_n - 1
    wanted = (
        (ocean, 0), (here, 0), (north, 0), (vertical, 0),
        (ocean, last), (here, last), (behind, last), (behind, last - 1), (north, last), (vertical, last),
    )
    found = jnp.zeros((rows_n, cols_n), jnp.float32)
    for place, (field, column) in enumerate(wanted):
        found = jnp.where(
            lane(found.shape) == place, pltpu.roll(field, (place - column) % cols_n, 1), found
        )
    out_ref[...] = found


def coefficient_rows_kernel(
    flag_ref, mask_ref, east_ref, north_ref, flow_ref, vertical_ref, first_ref, second_ref, out_ref
):
    rows_n, cols_n = mask_ref.shape
    east, west = lon_neighbours(flag_ref, first_ref[...], second_ref[...])
    top, last = slice(0, 1), slice(rows_n - 1, rows_n)
    found = []
    for at in (top, last):
        behind = east_ref[at, :] - 0.5 * flow_ref[at, :]
        found.append(mask_ref[at, :].astype(jnp.float32))
        found.append(east_ref[at, :] + 0.5 * flow_ref[at, :])
        found.append(shifted(behind, 1, 1, west[at, 6:7]))
        found.append(north_ref[at, :])
        if at is last:
            found.append(north_ref[rows_n - 2 : rows_n - 1, :])
        found.append(vertical_ref[at, :])
    found += [east[top], east[last], west[top], west[last]]
    for place, row in enumerate(found):
        out_ref[place : place + 1, :] = row
    out_ref[len(found) :, :] = jnp.zeros((out_ref.shape[0] - len(found), cols_n), jnp.float32)


def coefficients_kernel(
    flag_ref, mask_ref, east_ref, north_ref, flow_ref, vertical_ref,
    lon_first_ref, lon_second_ref, lat_first_ref, lat_second_ref,
    field_ref, side_ref, edge_ref,
):
    rows_n, cols_n = mask_ref.shape
    fold = flag_ref[2] == 1
    east, west = lon_neighbours(flag_ref, lon_first_ref[...], lon_second_ref[...])
    up, down = lat_neighbours(flag_ref, lat_first_ref[...], lat_second_ref[...])
    mirrored = reversed_lanes(up)
    ocean = mask_ref[...].astype(jnp.float32)
    here = east_ref[...] + 0.5 * flow_ref[...]
    behind = east_ref[...] - 0.5 * flow_ref[...]
    north = north_ref[...]
    back = shifted(behind, 1, 1, west[:, 6:7])
    south = shifted(north, 1, 0, down[8:9])
    top = sublane((rows_n, cols_n)) == rows_n - 1
    onto = jnp.where(jnp.logical_and(top, fold), mirrored[8:9], north)
    parts = (ocean, here + back + north + south, here, back, onto, south, vertical_ref[...])
    for place, part in enumerate(parts):
        field_ref[place] = part

    def side(ocean, here, back, north, vertical, below, fold_top):
        south = shifted(north, 1, 0, below)
        top = sublane(north.shape) == rows_n - 1
        onto = jnp.where(jnp.logical_and(top, fold), fold_top, north)
        return ocean, here + back + north + south, here, back, onto, south, vertical

    def spread(columns, place):
        return jnp.broadcast_to(columns[:, place : place + 1], (columns.shape[0], cols_n))

    eastern = side(
        spread(east, 0), spread(east, 1), spread(behind, cols_n - 1), spread(east, 2), spread(east, 3),
        spread(down[12:13], 2), spread(up[14:15], 8),
    )
    western = side(
        spread(west, 4), spread(west, 5), spread(west, 7), spread(west, 8), spread(west, 9),
        spread(down[14:15], 8), spread(up[12:13], 2),
    )
    found = jnp.zeros((rows_n, cols_n), jnp.float32)
    for place, part in enumerate(eastern + western):
        found = jnp.where(lane(found.shape) == place, part, found)
    side_ref[...] = found

    into = north[rows_n - 1 :, :]
    plain = (up[0:1], up[1:2] + up[2:3] + up[3:4] + into, up[1:2], up[2:3], into, up[3:4], up[4:5])
    turned = mirrored
    folded = (
        turned[5:6], turned[6:7] + turned[7:8] + turned[8:9] + turned[9:10],
        turned[7:8], turned[6:7], into, turned[9:10], turned[10:11],
    )
    low = (
        down[5:6], down[6:7] + down[7:8] + down[8:9] + down[9:10],
        down[6:7], down[7:8], down[8:9], down[9:10], down[10:11],
    )
    for place in range(len(plain)):
        edge_ref[place : place + 1, :] = jnp.where(fold, folded[place], plain[place])
        edge_ref[SUB + place : SUB + place + 1, :] = low[place]
    for place in (len(plain), SUB + len(plain)):
        edge_ref[place : place + 1, :] = jnp.zeros((1, cols_n), jnp.float32)


def edge_message_kernel(flag_ref, edges_ref, first_ref, second_ref, out_ref):
    places, levels, cols_n = edges_ref.shape
    last = first_ref.shape[0] - 1
    for place in range(places):
        out_ref[place * levels : (place + 1) * levels, :] = edges_ref[place]
    ends = []
    for row in (0, last):
        ends.append(lon_neighbours(flag_ref, first_ref[row : row + 1, :], second_ref[row : row + 1, :]))
    found = (ends[0][0], ends[1][0], ends[0][1], ends[1][1])
    for place, row in enumerate(found):
        out_ref[places * levels + place : places * levels + place + 1, :] = row


def steps_kernel(
    flag_ref, seed_ref, field_ref, side_ref, edge_ref,
    columns_ref, edges_ref, lon_first_ref, lon_second_ref, lat_first_ref, lat_second_ref,
    out_ref,
    masked_ref, next_ref, half_ref, turn_ref,
):
    levels_n, rows_n, cols_n = seed_ref.shape
    levels = edges_ref.shape[1]
    fold = flag_ref[2] == 1
    east, west = lon_neighbours(flag_ref, lon_first_ref[...], lon_second_ref[...])
    up, down = lat_neighbours(flag_ref, lat_first_ref[...], lat_second_ref[...])
    own = columns_ref[...]

    ends = edges_ref.shape[0] * levels
    east_up = jnp.where(fold, pltpu.roll(up[ends + 3 : ends + 4], 1, 1), up[ends : ends + 1])
    west_up = jnp.where(fold, pltpu.roll(up[ends + 1 : ends + 2], cols_n - 1, 1), up[ends + 2 : ends + 3])
    east_down, west_down = down[ends + 1 : ends + 2], down[ends + 3 : ends + 4]

    level_at = jnp.right_shift(lane((rows_n, cols_n)), 2)

    def side_step(block, eastern, western, above, below, base):
        def coefficient(place):
            return side_ref[:, base + place : base + place + 1]

        higher = jnp.where(level_at > 0, pltpu.roll(block, 4, 1) - block, 0.0)
        lower = jnp.where(level_at < levels_n - 1, pltpu.roll(block, cols_n - 4, 1) - block, 0.0)
        change = (
            coefficient(2) * eastern
            + coefficient(3) * western
            + coefficient(4) * shifted(block, -1, 0, above)
            + coefficient(5) * shifted(block, 1, 0, below)
            - coefficient(1) * block
            + coefficient(6) * (higher + lower)
        )
        return block + coefficient(0) * change

    east_next = side_step(
        east, pltpu.roll(east, cols_n - 1, 1), pltpu.roll(own, 1, 1), east_up, east_down, 0
    )
    west_next = side_step(
        west, pltpu.roll(own, cols_n - 1, 1), pltpu.roll(west, 1, 1), west_up, west_down, 7
    )
    slot = jnp.bitwise_and(lane((rows_n, cols_n)), 3)
    for step, (eastern, western) in enumerate(((east, west), (east_next, west_next))):
        turn_ref[step] = jnp.where(
            slot == 1, pltpu.roll(eastern, cols_n - 1, 1), pltpu.roll(western, 1, 1)
        )

    plane = (levels, cols_n)
    corner_at = 4 * sublane(plane)

    def corner(row, place):
        found = jnp.where(lane(plane) == corner_at + place, jnp.broadcast_to(row, plane), 0.0)
        return jnp.sum(found, axis=1, keepdims=True)

    def edge(block, place):
        return block[place * levels : (place + 1) * levels]

    def edge_step(block, outer, inner, eastern, western, base):
        def coefficient(place):
            return edge_ref[base + place : base + place + 1, :]

        level = sublane(plane)
        higher = jnp.where(level > 0, pltpu.roll(block, 1, 0) - block, 0.0)
        lower = jnp.where(level < levels_n - 1, pltpu.roll(block, levels - 1, 0) - block, 0.0)
        change = (
            coefficient(2) * shifted(block, -1, 1, eastern)
            + coefficient(3) * shifted(block, 1, 1, western)
            + coefficient(4) * inner
            + coefficient(5) * outer
            - coefficient(1) * block
            + coefficient(6) * (higher + lower)
        )
        return block + coefficient(0) * change

    above = jnp.where(fold, reversed_lanes(edge(up, 3)), edge(up, 0))
    above_outer = jnp.where(fold, reversed_lanes(edge(up, 2)), edge(up, 1))
    below, below_outer = edge(down, 3), edge(down, 2)
    above_next = edge_step(
        above, above_outer, edges_ref[3], corner(east_up, 2), corner(west_up, 1), 0
    )
    below_next = edge_step(
        below, below_outer, edges_ref[0], corner(east_down, 2), corner(west_down, 1), SUB
    )
    for level in range(levels_n):
        for ref, high, low in ((masked_ref, above, below), (next_ref, above_next, below_next)):
            ref[level, SUB + rows_n : SUB + rows_n + 1, :] = high[level : level + 1, :]
            ref[level, SUB - 1 : SUB, :] = low[level : level + 1, :]

    def mask(level, carry):
        masked_ref[level, SUB : SUB + rows_n, :] = field_ref[0] * seed_ref[level]
        return carry

    lax.fori_loop(0, levels_n, mask, 0)
    first = lane((SUB, cols_n)) == 0
    last = lane((SUB, cols_n)) == cols_n - 1

    def advance(step, level, source_ref, from_ref, store):
        higher, lower = jnp.maximum(level - 1, 0), jnp.minimum(level + 1, levels_n - 1)
        turn = lax.rem(2 * cols_n - 2 - 4 * level, cols_n)
        for top in range(0, rows_n, SUB):
            at = slice(top, top + SUB)
            inner = slice(SUB + top, 2 * SUB + top)
            block = from_ref[level, inner, :]
            sides = pltpu.roll(turn_ref[step, at, :], turn, 1)
            eastern = jnp.where(last, sides, pltpu.roll(block, cols_n - 1, 1))
            western = jnp.where(first, sides, pltpu.roll(block, 1, 1))
            north = from_ref[level, SUB + top + 1 : 2 * SUB + top + 1, :]
            south = from_ref[level, SUB + top - 1 : 2 * SUB + top - 1, :]
            vertical = (from_ref[higher, inner, :] - block) + (from_ref[lower, inner, :] - block)
            found = (
                source_ref[level, at, :]
                - field_ref[1, at, :] * block
                + field_ref[2, at, :] * eastern
                + field_ref[3, at, :] * western
                + field_ref[4, at, :] * north
                + field_ref[5, at, :] * south
                + field_ref[6, at, :] * vertical
            )
            store(level, top, found)

    def keep(level, top, found):
        half_ref[level, top : top + SUB, :] = found
        next_ref[level, SUB + top : 2 * SUB + top, :] = field_ref[0, top : top + SUB, :] * found

    def finish(level, top, found):
        out_ref[level, top : top + SUB, :] = found

    def first_step(level, carry):
        advance(0, level, seed_ref, masked_ref, keep)
        return carry

    def second_step(level, carry):
        advance(1, level, half_ref, next_ref, finish)
        return carry

    lax.fori_loop(0, levels_n, first_step, 0)
    lax.fori_loop(0, levels_n, second_step, 0)


def kernel_call(body, out_shape, scratch=(), flagged=False, inputs=0):
    memory = {}
    if flagged:
        memory["in_specs"] = [pl.BlockSpec(memory_space=pltpu.SMEM)] + [
            pl.BlockSpec(memory_space=pltpu.VMEM)
        ] * (inputs - 1)
    return pl.pallas_call(
        body,
        out_shape=out_shape,
        scratch_shapes=list(scratch),
        compiler_params=pltpu.CompilerParams(vmem_limit_bytes=VMEM_BYTES),
        **memory,
    )


def f32(*shape):
    return jax.ShapeDtypeStruct(shape, jnp.float32)


def lon_swaps(value):
    count = lax.axis_size("lon")
    assert count % 2 == 0
    first = [(i, i ^ 1) for i in range(count)]
    second = [(i, (i + 1 if i % 2 else i - 1) % count) for i in range(count)]
    return lax.ppermute(value, "lon", first), lax.ppermute(value, "lon", second)


def lat_swaps(value):
    lons, lats = lax.axis_size("lon"), lax.axis_size("lat")
    found = []
    for parity in (0, 1):
        pairs = []
        for i in range(lons):
            for j in range(lats):
                other = j + 1 if j % 2 == parity else j - 1
                if other == lats:
                    pairs.append((i * lats + j, (lons - 1 - i) * lats + j))
                elif other >= 0:
                    pairs.append((i * lats + j, i * lats + other))
        found.append(lax.ppermute(value, BOTH, pairs))
    return tuple(found)


def on_device(
    state,
    adjoint_in,
    land_mask,
    east_coef,
    north_coef,
    zonal_flow,
    vertical_coef,
    slot_cell,
    slot_weight,
    arrive_obs,
    obs_value,
    obs_invvar,
):
    levels_n, rows_n, cols_n = state.shape
    devices = lax.axis_size(BOTH)
    slots = slot_cell.shape[1]
    obs_n = obs_value.shape[1]
    assert 2 * (slots // devices) == LANES and cols_n == LANES and 4 * levels_n <= LANES
    half = (levels_n + 15) // 16 * 8
    width = rows_n // GROUP * cols_n
    bf16 = jnp.bfloat16
    raw = (land_mask, east_coef, north_coef, zonal_flow, vertical_coef)
    lon, lat = lax.axis_index("lon"), lax.axis_index("lat")
    flags = jnp.stack([1 - lon % 2, 1 - lat % 2, lat == lax.axis_size("lat") - 1]).astype(jnp.int32)

    partial_vals = kernel_call(
        gather_kernel, f32(devices, half, LANES), [pltpu.VMEM((levels_n * GROUP, 3 * width), bf16)]
    )(slot_cell, slot_weight, state)
    arrived = lax.all_to_all(partial_vals, BOTH, split_axis=0, concat_axis=0, tiled=True)

    side_coefs = lon_swaps(kernel_call(coefficient_columns_kernel, f32(rows_n, cols_n))(*raw))
    row_coefs = kernel_call(coefficient_rows_kernel, f32(2 * SUB, cols_n), (), True, 8)(
        flags, *raw, *side_coefs
    )
    edge_coefs = lat_swaps(row_coefs)
    fields, sides, edges = kernel_call(
        coefficients_kernel,
        (f32(7, rows_n, cols_n), f32(rows_n, cols_n), f32(2 * SUB, cols_n)),
        (), True, 10,
    )(flags, *raw, *side_coefs, *edge_coefs)

    misfit, outgoing = kernel_call(
        observe_kernel,
        (f32(levels_n, obs_n), f32(devices, half, LANES)),
        [pltpu.VMEM((obs_n, slots), bf16), pltpu.VMEM((6 * half, slots), bf16)],
    )(arrived, arrive_obs, obs_value, obs_invvar)
    returned = lax.all_to_all(outgoing, BOTH, split_axis=0, concat_axis=0, tiled=True)
    tile = 4 * LANES
    seed, own_columns, own_edges = kernel_call(
        scatter_kernel,
        (f32(levels_n, rows_n, cols_n), f32(rows_n, cols_n), f32(4, 2 * half, cols_n)),
        [
            pltpu.VMEM((levels_n * GROUP, 3 * tile), bf16),
            pltpu.VMEM((width, 3 * tile), bf16),
            pltpu.VMEM((levels_n * GROUP, width), jnp.float32),
        ],
    )(returned, slot_cell, slot_weight, adjoint_in, land_mask)
    side_columns = lon_swaps(own_columns)
    message = kernel_call(edge_message_kernel, f32(8 * half + SUB, cols_n), (), True, 4)(
        flags, own_edges, *side_columns
    )
    side_edges = lat_swaps(message)
    extended = (levels_n, rows_n + 2 * SUB, cols_n)
    adjoint_state = kernel_call(
        steps_kernel,
        f32(levels_n, rows_n, cols_n),
        [
            pltpu.VMEM(extended, jnp.float32),
            pltpu.VMEM(extended, jnp.float32),
            pltpu.VMEM((levels_n, rows_n, cols_n), jnp.float32),
            pltpu.VMEM((STEPS, rows_n, cols_n), jnp.float32),
        ],
        True, 11,
    )(flags, seed, fields, sides, edges, own_columns, own_edges, *side_columns, *side_edges)
    return (adjoint_state, misfit)


def solution(mesh):
    in_specs = (
        P(None, "lat", "lon"),
        P(None, "lat", "lon"),
        P("lat", "lon"),
        P("lat", "lon"),
        P("lat", "lon"),
        P("lat", "lon"),
        P("lat", "lon"),
        P(("lon", "lat"), None),
        P(("lon", "lat"), None),
        P(("lon", "lat"), None),
        P(None, ("lon", "lat")),
        P(None, ("lon", "lat")),
    )
    out_specs = (P(None, "lat", "lon"), P(None, ("lon", "lat")))
    return jax.shard_map(
        on_device, mesh=mesh, in_specs=in_specs, out_specs=out_specs, check_vma=False
    )
```

```python
import functools

import jax
import jax.numpy as jnp
from jax import lax
from jax.experimental import pallas as pl
from jax.experimental.pallas import tpu as pltpu
from jax.sharding import PartitionSpec as P

STEPS = 2
LANES = 128
GROUP = 32
SUB = 8
VMEM_BYTES = 48 * 1024 * 1024
BOTH = ("lon", "lat")


def pieces(value):
    high = value.astype(jnp.bfloat16)
    rest = value - high.astype(jnp.float32)
    middle = rest.astype(jnp.bfloat16)
    low = (rest - middle.astype(jnp.float32)).astype(jnp.bfloat16)
    return high, middle, low


def log2(size):
    assert size & (size - 1) == 0
    return size.bit_length() - 1


def cell_parts(cell, rows_n, cols_n):
    cell = jnp.maximum(cell, 0)
    row = jnp.right_shift(cell, log2(cols_n))
    group = jnp.right_shift(row, log2(GROUP))
    place = jnp.bitwise_and(cell, cols_n - 1) + group * cols_n
    return place, jnp.bitwise_and(row, GROUP - 1)


def one_hot(index, size):
    rows = lax.broadcasted_iota(jnp.int32, (size, index.shape[1]), 0)
    return jnp.where(rows == index, 1.0, 0.0).astype(jnp.bfloat16)


def packed_pair(values):
    half = values.shape[0] // 2
    first = lax.broadcasted_iota(jnp.int32, (half, LANES), 1) < LANES // 2
    top, bottom = values[:half], values[half:]
    left = jnp.where(first, top, pltpu.roll(bottom, LANES // 2, 1))
    right = jnp.where(first, pltpu.roll(top, LANES // 2, 1), bottom)
    return left, right


def unpacked_pair(left, right):
    half = left.shape[0]
    first = lax.broadcasted_iota(jnp.int32, (half, LANES), 1) < LANES // 2
    top = jnp.where(first, left, pltpu.roll(right, LANES // 2, 1))
    bottom = jnp.where(first, pltpu.roll(left, LANES // 2, 1), right)
    return jnp.concatenate([top, bottom], axis=0)


def padded_levels(values, levels):
    return jnp.concatenate(
        [values, jnp.zeros((levels - values.shape[0], values.shape[1]), values.dtype)], axis=0
    )


def gather_kernel(cell_ref, weight_ref, state_ref, out_ref, field_ref):
    levels_n, rows_n, cols_n = state_ref.shape
    groups = rows_n // GROUP
    width = groups * cols_n
    for group in range(groups):
        block = state_ref[:, group * GROUP : (group + 1) * GROUP, :]
        for part, piece in enumerate(pieces(block.reshape(levels_n * GROUP, cols_n))):
            at = part * width + group * cols_n
            field_ref[:, at : at + cols_n] = piece
    tile = 2 * LANES

    def body(step, carry):
        at = pl.ds(pl.multiple_of(step * tile, tile), tile)
        cell = cell_ref[:, at]
        weight = jnp.where(cell >= 0, weight_ref[:, at], 0.0)
        place, row = cell_parts(cell, rows_n, cols_n)
        hot = one_hot(place, width)
        found = jnp.dot(
            field_ref[...],
            jnp.concatenate([hot, hot, hot], axis=0),
            preferred_element_type=jnp.float32,
        ).reshape(levels_n, GROUP, tile)
        mine = lax.broadcasted_iota(jnp.int32, (GROUP, tile), 0) == row
        values = jnp.sum(jnp.where(mine[None], found, 0.0), axis=1) * weight
        values = padded_levels(values, 2 * out_ref.shape[1])
        for pair in range(tile // LANES):
            left, right = packed_pair(values[:, pair * LANES : (pair + 1) * LANES])
            out_ref[step * (2 * tile // LANES) + 2 * pair] = left
            out_ref[step * (2 * tile // LANES) + 2 * pair + 1] = right
        return carry

    lax.fori_loop(0, cell_ref.shape[1] // tile, body, 0)


def observe_kernel(arrived_ref, target_ref, value_ref, invvar_ref, misfit_ref, out_ref, hot_ref, in_ref):
    devices, half, _ = arrived_ref.shape
    levels_n, obs_n = value_ref.shape
    levels = 2 * half

    def load(pair, carry):
        at = pl.ds(pl.multiple_of(pair * LANES, LANES), LANES)
        values = unpacked_pair(arrived_ref[2 * pair], arrived_ref[2 * pair + 1])
        for part, piece in enumerate(pieces(values)):
            in_ref[part * levels : (part + 1) * levels, at] = piece
        hot_ref[:, at] = one_hot(target_ref[:, at], obs_n)
        return carry

    lax.fori_loop(0, devices // 2, load, 0)
    sums = lax.dot_general(
        in_ref[...], hot_ref[...], (((1,), (1,)), ((), ())), preferred_element_type=jnp.float32
    )
    interp = sums[:levels] + sums[levels : 2 * levels] + sums[2 * levels :]
    misfit = invvar_ref[...] * (interp[:levels_n] - value_ref[...])
    misfit_ref[...] = misfit
    back = jnp.concatenate(pieces(padded_levels(misfit, levels)), axis=0)
    tile = 4 * LANES

    def store(step, carry):
        at = pl.ds(pl.multiple_of(step * tile, tile), tile)
        found = jnp.dot(back, hot_ref[:, at], preferred_element_type=jnp.float32)
        values = found[:levels] + found[levels : 2 * levels] + found[2 * levels :]
        for pair in range(tile // LANES):
            left, right = packed_pair(values[:, pair * LANES : (pair + 1) * LANES])
            out_ref[step * (2 * tile // LANES) + 2 * pair] = left
            out_ref[step * (2 * tile // LANES) + 2 * pair + 1] = right
        return carry

    lax.fori_loop(0, target_ref.shape[1] // tile, store, 0)


def returned_values(returned_ref, cell_ref, weight_ref, start, tile):
    at = pl.ds(pl.multiple_of(start, tile), tile)
    weight = jnp.where(cell_ref[:, at] >= 0, weight_ref[:, at], 0.0)
    base = start // (LANES // 2)
    values = jnp.concatenate(
        [
            unpacked_pair(returned_ref[base + 2 * pair], returned_ref[base + 2 * pair + 1])
            for pair in range(tile // LANES)
        ],
        axis=1,
    )
    return pieces(values * weight)


def across(left, right):
    return lax.dot_general(
        left, right, (((1,), (1,)), ((), ())), preferred_element_type=jnp.float32
    )


def seed_strips_kernel(adjoint_ref, mask_ref, columns_ref, ocean_ref, edges_ref):
    levels_n, rows_n, cols_n = adjoint_ref.shape
    level_at = jnp.right_shift(lane((SUB, cols_n)), 2)
    for top in range(0, rows_n, SUB):
        at = slice(top, top + SUB)
        found = jnp.zeros((SUB, cols_n), jnp.float32)
        for level in range(levels_n):
            block = pltpu.roll(adjoint_ref[level, at, :], (4 * level + 2) % cols_n, 1)
            found = jnp.where(level_at == level, block, found)
        columns_ref[at, :] = found
        spread = jnp.where(level_at == 0, pltpu.roll(mask_ref[at, :].astype(jnp.float32), 2, 1), 0.0)
        shift = 4
        while shift < cols_n:
            spread = spread + pltpu.roll(spread, shift, 1)
            shift *= 2
        ocean_ref[at, :] = spread
    places, levels, _ = edges_ref.shape
    for place, row in enumerate((0, 1, rows_n - 2, rows_n - 1)):
        for level in range(levels_n):
            edges_ref[place, level : level + 1, :] = adjoint_ref[level, row : row + 1, :]
        edges_ref[place, levels_n:, :] = jnp.zeros((levels - levels_n, cols_n), jnp.float32)


def strips_kernel(
    returned_ref, cell_ref, weight_ref, mask_ref, seed_columns_ref, ocean_ref, seed_edges_ref,
    columns_ref, edges_ref,
    left_ref, right_ref,
):
    rows_n, cols_n = mask_ref.shape
    places, levels, _ = edges_ref.shape
    slots = cell_ref.shape[1]
    tile = left_ref.shape[1] // 3
    column_sum = jnp.zeros((rows_n, LANES), jnp.float32)
    edge_sum = jnp.zeros((places * levels, cols_n), jnp.float32)
    for start in range(0, slots, tile):
        cell = jnp.maximum(cell_ref[:, start : start + tile], 0)
        row, column = jnp.right_shift(cell, log2(cols_n)), jnp.bitwise_and(cell, cols_n - 1)
        values = returned_values(returned_ref, cell_ref, weight_ref, start, tile)

        def chosen(index, wanted):
            for place, number in enumerate(wanted):
                here = jnp.where(index == number, 1.0, 0.0).astype(jnp.bfloat16)
                for part in range(3):
                    right_ref[place * levels : (place + 1) * levels, part * tile : (part + 1) * tile] = (
                        values[part] * here
                    )

        def repeated(hot):
            for part in range(3):
                left_ref[:, part * tile : (part + 1) * tile] = hot

        repeated(one_hot(row, rows_n))
        chosen(column, (cols_n - 2, cols_n - 1, 0, 1))
        column_sum += across(left_ref[...], right_ref[...])
        repeated(one_hot(column, cols_n))
        chosen(row, (0, 1, rows_n - 2, rows_n - 1))
        edge_sum += across(right_ref[...], left_ref[...])
    source, target = sublane((LANES, LANES)), lane((LANES, LANES))
    turn = jnp.bitwise_and(target, 3) * levels + jnp.right_shift(target, 2)
    turn = jnp.where(source == turn, 1.0, 0.0).astype(jnp.bfloat16)
    column_sum = sum(
        jnp.dot(piece, turn, preferred_element_type=jnp.float32) for piece in pieces(column_sum)
    )
    columns_ref[...] = (seed_columns_ref[...] + column_sum) * ocean_ref[...]
    for place, row in enumerate((0, 1, rows_n - 2, rows_n - 1)):
        ocean = mask_ref[row : row + 1, :].astype(jnp.float32)
        forcing = edge_sum[place * levels : (place + 1) * levels]
        edges_ref[place] = (seed_edges_ref[place] + forcing) * ocean


def scatter_kernel(
    returned_ref, cell_ref, weight_ref, adjoint_ref, field_ref,
    out_ref,
    rows_ref, hot_ref, seed_ref, masked_ref,
):
    levels_n, rows_n, cols_n = out_ref.shape
    groups = rows_n // GROUP
    width = groups * cols_n
    tile = hot_ref.shape[1] // 3
    total = None
    for start in range(0, cell_ref.shape[1], tile):
        place, row = cell_parts(cell_ref[:, start : start + tile], rows_n, cols_n)
        values = returned_values(returned_ref, cell_ref, weight_ref, start, tile)
        hot = one_hot(place, width)
        mine = one_hot(row, GROUP)
        for part in range(3):
            hot_ref[:, part * tile : (part + 1) * tile] = hot
            for level in range(levels_n):
                rows_ref[level * GROUP : (level + 1) * GROUP, part * tile : (part + 1) * tile] = (
                    mine * values[part][level : level + 1, :]
                )
        found = across(rows_ref[...], hot_ref[...])
        total = found if total is None else total + found
    zero = jnp.zeros((1, cols_n), jnp.float32)
    for level in range(levels_n):
        masked_ref[level, SUB - 1 : SUB, :] = zero
        masked_ref[level, SUB + rows_n : SUB + rows_n + 1, :] = zero
    for group in range(groups):
        at = slice(group * GROUP, (group + 1) * GROUP)
        forcing = total[:, group * cols_n : (group + 1) * cols_n].reshape(levels_n, GROUP, cols_n)
        seed = adjoint_ref[:, at, :] + forcing
        seed_ref[:, at, :] = seed
        masked_ref[:, SUB + group * GROUP : SUB + (group + 1) * GROUP, :] = seed * field_ref[0, at, :]

    def store(level, top, ocean, found):
        out_ref[level, top : top + SUB, :] = found

    advance(seed_ref, masked_ref, field_ref, None, store)


def advance(source_ref, from_ref, field_ref, turn_ref, store):
    levels_n, rows_n, cols_n = source_ref.shape
    first = lane((SUB, cols_n)) == 0
    last = lane((SUB, cols_n)) == cols_n - 1
    for top in range(0, rows_n, SUB):
        at, inner = slice(top, top + SUB), slice(top + SUB, top + 2 * SUB)
        ocean, own, here, back, onto, south_at, mixing = (
            field_ref[place, at, :] for place in range(7)
        )
        if turn_ref is None:
            here_in, back_in = jnp.where(last, 0.0, here), jnp.where(first, 0.0, back)
        else:
            turned = turn_ref[at, :]
        higher = block = from_ref[0, inner, :]
        for level in range(levels_n):
            lower = from_ref[level + 1, inner, :] if level + 1 < levels_n else block
            eastern, western = pltpu.roll(block, cols_n - 1, 1), pltpu.roll(block, 1, 1)
            if turn_ref is None:
                sides = here_in * eastern + back_in * western
            else:
                beyond = pltpu.roll(turned, (2 * cols_n - 2 - 4 * level) % cols_n, 1)
                sides = here * jnp.where(last, beyond, eastern) + back * jnp.where(first, beyond, western)
            north = from_ref[level, top + SUB + 1 : top + 2 * SUB + 1, :]
            south = from_ref[level, top + SUB - 1 : top + 2 * SUB - 1, :]
            vertical = (higher - block) + (lower - block)
            found = (
                (source_ref[level, at, :] - own * block)
                + sides
                + (onto * north + south_at * south)
                + mixing * vertical
            )
            store(level, top, ocean, found)
            higher, block = block, lower


def lane(shape):
    return lax.broadcasted_iota(jnp.int32, shape, 1)


def sublane(shape):
    return lax.broadcasted_iota(jnp.int32, shape, 0)


def shifted(block, steps, axis, edge):
    size = block.shape[axis]
    at = lax.broadcasted_iota(jnp.int32, block.shape, axis)
    moved = pltpu.roll(block, steps % size, axis)
    return jnp.where(at == (0 if steps > 0 else size - 1), edge, moved)


def reversed_lanes(block):
    at = block.shape[1] - 1 - lane(block.shape)
    return jnp.take_along_axis(block, at, axis=1, mode="promise_in_bounds")


def lon_neighbours(flag_ref, first, second):
    even = flag_ref[0] == 1
    return jnp.where(even, first, second), jnp.where(even, second, first)


def lat_neighbours(flag_ref, first, second):
    even = flag_ref[1] == 1
    return jnp.where(even, first, second), jnp.where(even, second, first)


def coefficient_columns_kernel(mask_ref, east_ref, north_ref, flow_ref, vertical_ref, out_ref):
    rows_n, cols_n = mask_ref.shape
    ocean = mask_ref[...].astype(jnp.float32)
    here = east_ref[...] + 0.5 * flow_ref[...]
    behind = east_ref[...] - 0.5 * flow_ref[...]
    north, vertical = north_ref[...], vertical_ref[...]
    last = cols_n - 1
    wanted = (
        (ocean, 0), (here, 0), (north, 0), (vertical, 0),
        (ocean, last), (here, last), (behind, last), (behind, last - 1), (north, last), (vertical, last),
    )
    found = jnp.zeros((rows_n, cols_n), jnp.float32)
    for place, (field, column) in enumerate(wanted):
        found = jnp.where(
            lane(found.shape) == place, pltpu.roll(field, (place - column) % cols_n, 1), found
        )
    out_ref[...] = found


def coefficient_rows_kernel(
    flag_ref, mask_ref, east_ref, north_ref, flow_ref, vertical_ref, first_ref, second_ref, out_ref
):
    rows_n, cols_n = mask_ref.shape
    east, west = lon_neighbours(flag_ref, first_ref[...], second_ref[...])
    top, last = slice(0, 1), slice(rows_n - 1, rows_n)
    found = []
    for at in (top, last):
        behind = east_ref[at, :] - 0.5 * flow_ref[at, :]
        found.append(mask_ref[at, :].astype(jnp.float32))
        found.append(east_ref[at, :] + 0.5 * flow_ref[at, :])
        found.append(shifted(behind, 1, 1, west[at, 6:7]))
        found.append(north_ref[at, :])
        if at is last:
            found.append(north_ref[rows_n - 2 : rows_n - 1, :])
        found.append(vertical_ref[at, :])
    found += [east[top], east[last], west[top], west[last]]
    for place, row in enumerate(found):
        out_ref[place : place + 1, :] = row
    out_ref[len(found) :, :] = jnp.zeros((out_ref.shape[0] - len(found), cols_n), jnp.float32)


def coefficients_kernel(
    flag_ref, mask_ref, east_ref, north_ref, flow_ref, vertical_ref,
    lon_first_ref, lon_second_ref, lat_first_ref, lat_second_ref,
    field_ref, side_ref, edge_ref,
):
    rows_n, cols_n = mask_ref.shape
    fold = flag_ref[2] == 1
    east, west = lon_neighbours(flag_ref, lon_first_ref[...], lon_second_ref[...])
    up, down = lat_neighbours(flag_ref, lat_first_ref[...], lat_second_ref[...])
    mirrored = reversed_lanes(up)
    ocean = mask_ref[...].astype(jnp.float32)
    here = east_ref[...] + 0.5 * flow_ref[...]
    behind = east_ref[...] - 0.5 * flow_ref[...]
    north = north_ref[...]
    back = shifted(behind, 1, 1, west[:, 6:7])
    south = shifted(north, 1, 0, down[8:9])
    top = sublane((rows_n, cols_n)) == rows_n - 1
    onto = jnp.where(jnp.logical_and(top, fold), mirrored[8:9], north)
    parts = (ocean, here + back + north + south, here, back, onto, south, vertical_ref[...])
    for place, part in enumerate(parts):
        field_ref[place] = part

    def side(ocean, here, back, north, vertical, below, fold_top):
        south = shifted(north, 1, 0, below)
        top = sublane(north.shape) == rows_n - 1
        onto = jnp.where(jnp.logical_and(top, fold), fold_top, north)
        return ocean, here + back + north + south, here, back, onto, south, vertical

    def spread(columns, place):
        return jnp.broadcast_to(columns[:, place : place + 1], (columns.shape[0], cols_n))

    eastern = side(
        spread(east, 0), spread(east, 1), spread(behind, cols_n - 1), spread(east, 2), spread(east, 3),
        spread(down[12:13], 2), spread(up[14:15], 8),
    )
    western = side(
        spread(west, 4), spread(west, 5), spread(west, 7), spread(west, 8), spread(west, 9),
        spread(down[14:15], 8), spread(up[12:13], 2),
    )
    found = jnp.zeros((rows_n, cols_n), jnp.float32)
    for place, part in enumerate(eastern + western):
        found = jnp.where(lane(found.shape) == place, part, found)
    side_ref[...] = found

    into = north[rows_n - 1 :, :]
    plain = (up[0:1], up[1:2] + up[2:3] + up[3:4] + into, up[1:2], up[2:3], into, up[3:4], up[4:5])
    turned = mirrored
    folded = (
        turned[5:6], turned[6:7] + turned[7:8] + turned[8:9] + turned[9:10],
        turned[7:8], turned[6:7], into, turned[9:10], turned[10:11],
    )
    low = (
        down[5:6], down[6:7] + down[7:8] + down[8:9] + down[9:10],
        down[6:7], down[7:8], down[8:9], down[9:10], down[10:11],
    )
    for place in range(len(plain)):
        edge_ref[place : place + 1, :] = jnp.where(fold, folded[place], plain[place])
        edge_ref[SUB + place : SUB + place + 1, :] = low[place]
    for place in (len(plain), SUB + len(plain)):
        edge_ref[place : place + 1, :] = jnp.zeros((1, cols_n), jnp.float32)


def edge_message_kernel(flag_ref, edges_ref, first_ref, second_ref, out_ref):
    places, levels, cols_n = edges_ref.shape
    last = first_ref.shape[0] - 1
    for place in range(places):
        out_ref[place * levels : (place + 1) * levels, :] = edges_ref[place]
    ends = []
    for row in (0, last):
        ends.append(lon_neighbours(flag_ref, first_ref[row : row + 1, :], second_ref[row : row + 1, :]))
    found = (ends[0][0], ends[1][0], ends[0][1], ends[1][1])
    for place, row in enumerate(found):
        out_ref[places * levels + place : places * levels + place + 1, :] = row


def steps_kernel(
    flag_ref, inner_ref, field_ref, side_ref, edge_ref,
    columns_ref, edges_ref, lon_first_ref, lon_second_ref, lat_first_ref, lat_second_ref,
    out_ref,
    masked_ref, half_ref, turn_ref,
):
    levels_n, rows_n, cols_n = inner_ref.shape
    levels = edges_ref.shape[1]
    fold = flag_ref[2] == 1
    east, west = lon_neighbours(flag_ref, lon_first_ref[...], lon_second_ref[...])
    up, down = lat_neighbours(flag_ref, lat_first_ref[...], lat_second_ref[...])
    own = columns_ref[...]

    ends = edges_ref.shape[0] * levels
    east_up = jnp.where(fold, pltpu.roll(up[ends + 3 : ends + 4], 1, 1), up[ends : ends + 1])
    west_up = jnp.where(fold, pltpu.roll(up[ends + 1 : ends + 2], cols_n - 1, 1), up[ends + 2 : ends + 3])
    east_down, west_down = down[ends + 1 : ends + 2], down[ends + 3 : ends + 4]

    level_at = jnp.right_shift(lane((rows_n, cols_n)), 2)

    def side_step(block, eastern, western, above, below, base):
        def coefficient(place):
            return side_ref[:, base + place : base + place + 1]

        higher = jnp.where(level_at > 0, pltpu.roll(block, 4, 1) - block, 0.0)
        lower = jnp.where(level_at < levels_n - 1, pltpu.roll(block, cols_n - 4, 1) - block, 0.0)
        change = (
            coefficient(2) * eastern
            + coefficient(3) * western
            + coefficient(4) * shifted(block, -1, 0, above)
            + coefficient(5) * shifted(block, 1, 0, below)
            - coefficient(1) * block
            + coefficient(6) * (higher + lower)
        )
        return block + coefficient(0) * change

    east_next = side_step(
        east, pltpu.roll(east, cols_n - 1, 1), pltpu.roll(own, 1, 1), east_up, east_down, 0
    )
    west_next = side_step(
        west, pltpu.roll(own, cols_n - 1, 1), pltpu.roll(west, 1, 1), west_up, west_down, 7
    )
    slot = jnp.bitwise_and(lane((rows_n, cols_n)), 3)
    for step, (eastern, western) in enumerate(((east, west), (east_next, west_next))):
        turn_ref[step] = jnp.where(
            slot == 1, pltpu.roll(eastern, cols_n - 1, 1), pltpu.roll(western, 1, 1)
        )

    plane = (levels, cols_n)
    corner_at = 4 * sublane(plane)

    def corner(row, place):
        found = jnp.where(lane(plane) == corner_at + place, jnp.broadcast_to(row, plane), 0.0)
        return jnp.sum(found, axis=1, keepdims=True)

    def edge(block, place):
        return block[place * levels : (place + 1) * levels]

    def edge_step(block, outer, inner, eastern, western, base):
        def coefficient(place):
            return edge_ref[base + place : base + place + 1, :]

        level = sublane(plane)
        higher = jnp.where(level > 0, pltpu.roll(block, 1, 0) - block, 0.0)
        lower = jnp.where(level < levels_n - 1, pltpu.roll(block, levels - 1, 0) - block, 0.0)
        change = (
            coefficient(2) * shifted(block, -1, 1, eastern)
            + coefficient(3) * shifted(block, 1, 1, western)
            + coefficient(4) * inner
            + coefficient(5) * outer
            - coefficient(1) * block
            + coefficient(6) * (higher + lower)
        )
        return block + coefficient(0) * change

    above = jnp.where(fold, reversed_lanes(edge(up, 3)), edge(up, 0))
    above_outer = jnp.where(fold, reversed_lanes(edge(up, 2)), edge(up, 1))
    below, below_outer = edge(down, 3), edge(down, 2)
    above_next = edge_step(
        above, above_outer, edges_ref[3], corner(east_up, 2), corner(west_up, 1), 0
    )
    below_next = edge_step(
        below, below_outer, edges_ref[0], corner(east_down, 2), corner(west_down, 1), SUB
    )
    for level in range(levels_n):
        masked_ref[level, SUB + rows_n : SUB + rows_n + 1, :] = above_next[level : level + 1, :]
        masked_ref[level, SUB - 1 : SUB, :] = below_next[level : level + 1, :]
    first = lane((SUB, cols_n)) == 0
    last = lane((SUB, cols_n)) == cols_n - 1
    for top in range(0, rows_n, SUB):
        at, inner = slice(top, top + SUB), slice(top + SUB, top + 2 * SUB)
        ocean = field_ref[0, at, :]
        side = jnp.where(last, field_ref[2, at, :], jnp.where(first, field_ref[3, at, :], 0.0))
        turned = turn_ref[0, at, :]
        place = sublane((SUB, cols_n))
        for level in range(levels_n):
            beyond = pltpu.roll(turned, (2 * cols_n - 2 - 4 * level) % cols_n, 1)
            found = inner_ref[level, at, :] + side * beyond
            if top == 0:
                below_row = field_ref[5, 0:1, :] * below[level : level + 1, :]
                found = found + jnp.where(place == 0, below_row, 0.0)
            if top == rows_n - SUB:
                above_row = field_ref[4, rows_n - 1 : rows_n, :] * above[level : level + 1, :]
                found = found + jnp.where(place == SUB - 1, above_row, 0.0)
            half_ref[level, at, :] = found
            masked_ref[level, inner, :] = ocean * found

    def store(level, top, ocean, found):
        out_ref[level, top : top + SUB, :] = found

    advance(half_ref, masked_ref, field_ref, turn_ref.at[1], store)


def kernel_call(body, out_shape, scratch=(), flagged=False, inputs=0):
    memory = {}
    if flagged:
        memory["in_specs"] = [pl.BlockSpec(memory_space=pltpu.SMEM)] + [
            pl.BlockSpec(memory_space=pltpu.VMEM)
        ] * (inputs - 1)
    return pl.pallas_call(
        body,
        out_shape=out_shape,
        scratch_shapes=list(scratch),
        compiler_params=pltpu.CompilerParams(vmem_limit_bytes=VMEM_BYTES),
        **memory,
    )


def f32(*shape):
    return jax.ShapeDtypeStruct(shape, jnp.float32)


def lon_swaps(value):
    count = lax.axis_size("lon")
    assert count % 2 == 0
    first = [(i, i ^ 1) for i in range(count)]
    second = [(i, (i + 1 if i % 2 else i - 1) % count) for i in range(count)]
    return lax.ppermute(value, "lon", first), lax.ppermute(value, "lon", second)


def lat_swaps(value):
    lons, lats = lax.axis_size("lon"), lax.axis_size("lat")
    found = []
    for parity in (0, 1):
        pairs = []
        for i in range(lons):
            for j in range(lats):
                other = j + 1 if j % 2 == parity else j - 1
                if other == lats:
                    pairs.append((i * lats + j, (lons - 1 - i) * lats + j))
                elif other >= 0:
                    pairs.append((i * lats + j, i * lats + other))
        found.append(lax.ppermute(value, BOTH, pairs))
    return tuple(found)


def on_device(
    state,
    adjoint_in,
    land_mask,
    east_coef,
    north_coef,
    zonal_flow,
    vertical_coef,
    slot_cell,
    slot_weight,
    arrive_obs,
    obs_value,
    obs_invvar,
):
    levels_n, rows_n, cols_n = state.shape
    devices = lax.axis_size(BOTH)
    slots = slot_cell.shape[1]
    obs_n = obs_value.shape[1]
    assert 2 * (slots // devices) == LANES and cols_n == LANES and 4 * levels_n <= LANES
    half = (levels_n + 15) // 16 * 8
    width = rows_n // GROUP * cols_n
    bf16 = jnp.bfloat16
    raw = (land_mask, east_coef, north_coef, zonal_flow, vertical_coef)
    lon, lat = lax.axis_index("lon"), lax.axis_index("lat")
    flags = jnp.stack([1 - lon % 2, 1 - lat % 2, lat == lax.axis_size("lat") - 1]).astype(jnp.int32)

    partial_vals = kernel_call(
        gather_kernel, f32(devices, half, LANES), [pltpu.VMEM((levels_n * GROUP, 3 * width), bf16)]
    )(slot_cell, slot_weight, state)
    columns = kernel_call(coefficient_columns_kernel, f32(rows_n, cols_n))(*raw)
    partial_vals, columns = lax.optimization_barrier((partial_vals, columns))
    arrived = lax.all_to_all(partial_vals, BOTH, split_axis=0, concat_axis=0, tiled=True)
    arrived, side_coefs = lax.optimization_barrier((arrived, lon_swaps(columns)))
    row_coefs = kernel_call(coefficient_rows_kernel, f32(2 * SUB, cols_n), (), True, 8)(
        flags, *raw, *side_coefs
    )
    misfit, outgoing = kernel_call(
        observe_kernel,
        (f32(levels_n, obs_n), f32(devices, half, LANES)),
        [pltpu.VMEM((obs_n, slots), bf16), pltpu.VMEM((6 * half, slots), bf16)],
    )(arrived, arrive_obs, obs_value, obs_invvar)
    outgoing, row_coefs, adjoint_in, land_mask = lax.optimization_barrier(
        (outgoing, row_coefs, adjoint_in, land_mask)
    )
    returned = lax.all_to_all(outgoing, BOTH, split_axis=0, concat_axis=0, tiled=True)
    levels = 2 * half
    fields, sides, edges = kernel_call(
        coefficients_kernel,
        (f32(7, rows_n, cols_n), f32(rows_n, cols_n), f32(2 * SUB, cols_n)),
        (), True, 10,
    )(flags, *raw, *side_coefs, *lat_swaps(row_coefs))
    strips = kernel_call(
        seed_strips_kernel,
        (f32(rows_n, cols_n), f32(rows_n, cols_n), f32(4, levels, cols_n)),
    )(adjoint_in, land_mask)
    returned, fields, sides, edges, strips = lax.optimization_barrier(
        (returned, fields, sides, edges, strips)
    )
    tile = min(slots, 16 * LANES)
    own_columns, own_edges = kernel_call(
        strips_kernel,
        (f32(rows_n, cols_n), f32(4, levels, cols_n)),
        [pltpu.VMEM((rows_n, 3 * tile), bf16), pltpu.VMEM((4 * levels, 3 * tile), bf16)],
    )(returned, slot_cell, slot_weight, land_mask, *strips)
    side_columns = lon_swaps(own_columns)
    extended = (levels_n, rows_n + 2 * SUB, cols_n)
    inner = kernel_call(
        scatter_kernel,
        f32(levels_n, rows_n, cols_n),
        [
            pltpu.VMEM((levels_n * GROUP, 3 * tile), bf16),
            pltpu.VMEM((width, 3 * tile), bf16),
            pltpu.VMEM((levels_n, rows_n, cols_n), jnp.float32),
            pltpu.VMEM(extended, jnp.float32),
        ],
    )(returned, slot_cell, slot_weight, adjoint_in, fields)
    inner, side_columns = lax.optimization_barrier((inner, side_columns))
    message = kernel_call(edge_message_kernel, f32(8 * half + SUB, cols_n), (), True, 4)(
        flags, own_edges, *side_columns
    )
    side_edges = lat_swaps(message)
    adjoint_state = kernel_call(
        steps_kernel,
        f32(levels_n, rows_n, cols_n),
        [
            pltpu.VMEM(extended, jnp.float32),
            pltpu.VMEM((levels_n, rows_n, cols_n), jnp.float32),
            pltpu.VMEM((STEPS, rows_n, cols_n), jnp.float32),
        ],
        True, 11,
    )(flags, inner, fields, sides, edges, own_columns, own_edges, *side_columns, *side_edges)
    return (adjoint_state, misfit)


def solution(mesh):
    in_specs = (
        P(None, "lat", "lon"),
        P(None, "lat", "lon"),
        P("lat", "lon"),
        P("lat", "lon"),
        P("lat", "lon"),
        P("lat", "lon"),
        P("lat", "lon"),
        P(("lon", "lat"), None),
        P(("lon", "lat"), None),
        P(("lon", "lat"), None),
        P(None, ("lon", "lat")),
        P(None, ("lon", "lat")),
    )
    out_specs = (P(None, "lat", "lon"), P(None, ("lon", "lat")))
    return jax.shard_map(
        on_device, mesh=mesh, in_specs=in_specs, out_specs=out_specs, check_vma=False
    )
```

```python
import functools

import jax
import jax.numpy as jnp
from jax import lax
from jax.experimental import pallas as pl
from jax.experimental.pallas import tpu as pltpu
from jax.sharding import PartitionSpec as P

STEPS = 2
LANES = 128
GROUP = 32
SUB = 8
SLOT_TILE = 16 * LANES
MIB = 1024 * 1024
BOTH = ("lon", "lat")


def pieces(value):
    high = value.astype(jnp.bfloat16)
    rest = value - high.astype(jnp.float32)
    middle = rest.astype(jnp.bfloat16)
    low = (rest - middle.astype(jnp.float32)).astype(jnp.bfloat16)
    return high, middle, low


def log2(size):
    assert size & (size - 1) == 0
    return size.bit_length() - 1


def cell_parts(cell, rows_n, cols_n):
    cell = jnp.maximum(cell, 0)
    row = jnp.right_shift(cell, log2(cols_n))
    group = jnp.right_shift(row, log2(GROUP))
    place = jnp.bitwise_and(cell, cols_n - 1) + group * cols_n
    return place, jnp.bitwise_and(row, GROUP - 1)


def one_hot(index, size):
    rows = lax.broadcasted_iota(jnp.int32, (size, index.shape[1]), 0)
    return jnp.where(rows == index, 1.0, 0.0).astype(jnp.bfloat16)


def first_half(rows):
    return lane((rows, LANES)) < LANES // 2


def pack(values, out_ref, first_pair):
    half = values.shape[0] // 2
    for pair in range(values.shape[1] // LANES):
        block = values[:, pair * LANES : (pair + 1) * LANES]
        top, bottom = block[:half], block[half:]
        at = 2 * (first_pair + pair) * half
        out_ref[at : at + half, :] = jnp.where(
            first_half(half), top, pltpu.roll(bottom, LANES // 2, 1)
        )
        out_ref[at + half : at + 2 * half, :] = jnp.where(
            first_half(half), pltpu.roll(top, LANES // 2, 1), bottom
        )


def unpack(in_ref, half, first_pair, pairs, levels):
    found = []
    for pair in range(first_pair, first_pair + pairs):
        at = 2 * pair * half
        left, right = in_ref[at : at + half, :], in_ref[at + half : at + 2 * half, :]
        top = jnp.where(first_half(half), left, pltpu.roll(right, LANES // 2, 1))
        bottom = jnp.where(first_half(half), pltpu.roll(left, LANES // 2, 1), right)
        filler = jnp.zeros((levels - 2 * half, LANES), jnp.float32)
        found.append(jnp.concatenate([top, bottom, filler], axis=0))
    return jnp.concatenate(found, axis=1)


def gather_kernel(
    cell_in, weight_in, state_in, out_ref, cell_ref, weight_ref, state_ref, field_ref, sems
):
    levels_n, rows_n, cols_n = state_ref.shape
    groups = rows_n // GROUP
    width = groups * cols_n
    slots = cell_ref.shape[1]
    tile = min(slots, SLOT_TILE)
    chunk = max(n for n in range(1, 9) if levels_n % n == 0)
    copies = [
        pltpu.make_async_copy(cell_in, cell_ref, sems.at[0]),
        pltpu.make_async_copy(weight_in, weight_ref, sems.at[1]),
    ]
    for place, level in enumerate(range(0, levels_n, chunk)):
        at = slice(level, level + chunk)
        copies.append(pltpu.make_async_copy(state_in.at[at], state_ref.at[at], sems.at[2 + place]))
    for copy in copies:
        copy.start()
    copies[0].wait()
    for start in range(0, slots, tile):
        cell = cell_ref[:, start : start + tile]
        place, row = cell_parts(cell, rows_n, cols_n)
        hot = one_hot(place, width)
        hot = jnp.concatenate([hot, hot, hot], axis=0)
        mine = sublane((GROUP, tile)) == row
        values = []
        for index, level in enumerate(range(0, levels_n, chunk)):
            at = slice(level * GROUP, (level + chunk) * GROUP)
            if start == 0:
                copies[2 + index].wait()
                for group in range(groups):
                    block = state_ref[
                        level : level + chunk, group * GROUP : (group + 1) * GROUP, :
                    ].reshape(chunk * GROUP, cols_n)
                    for part, piece in enumerate(pieces(block)):
                        begin = part * width + group * cols_n
                        field_ref[at, begin : begin + cols_n] = piece
            found = jnp.dot(field_ref[at, :], hot, preferred_element_type=jnp.float32)
            found = found.reshape(chunk, GROUP, tile)
            values.append(jnp.sum(jnp.where(mine[None], found, 0.0), axis=1))
        if start == 0:
            copies[1].wait()
        weight = jnp.where(cell >= 0, weight_ref[:, start : start + tile], 0.0)
        if levels_n % 2:
            values.append(jnp.zeros((1, tile), jnp.float32))
        pack(jnp.concatenate(values, axis=0) * weight, out_ref, start // LANES)


def observe_kernel(arrived_ref, target_ref, value_ref, invvar_ref, misfit_ref, out_ref, hot_ref):
    levels_n, obs_n = value_ref.shape
    half = (levels_n + 1) // 2
    levels = padded_levels(levels_n)
    slots = target_ref.shape[1]
    tile = min(slots, SLOT_TILE)
    sums = None
    for start in range(0, slots, tile):
        hot = one_hot(target_ref[:, start : start + tile], obs_n)
        hot_ref[:, start : start + tile] = hot
        values = unpack(arrived_ref, half, start // LANES, tile // LANES, levels)
        found = across(jnp.concatenate(pieces(values), axis=0), hot)
        sums = found if sums is None else sums + found
    interp = sums[:levels] + sums[levels : 2 * levels] + sums[2 * levels :]
    misfit = invvar_ref[...] * (interp[:levels_n] - value_ref[...])
    misfit_ref[...] = misfit
    filler = jnp.zeros((levels - levels_n, obs_n), jnp.float32)
    back = jnp.concatenate(pieces(jnp.concatenate([misfit, filler], axis=0)), axis=0)
    for start in range(0, slots, tile):
        found = jnp.dot(
            back, hot_ref[:, start : start + tile], preferred_element_type=jnp.float32
        )
        values = found[:levels] + found[levels : 2 * levels] + found[2 * levels :]
        pack(values[: 2 * half], out_ref, start // LANES)


def padded_levels(levels_n):
    return (levels_n + 15) // 16 * 16


def returned_values(returned_ref, cell_ref, weight_ref, levels_n, start, tile):
    at = slice(start, start + tile)
    weight = jnp.where(cell_ref[:, at] >= 0, weight_ref[:, at], 0.0)
    values = unpack(
        returned_ref, (levels_n + 1) // 2, start // LANES, tile // LANES, padded_levels(levels_n)
    )
    return pieces(values * weight)


def across(left, right):
    return lax.dot_general(
        left, right, (((1,), (1,)), ((), ())), preferred_element_type=jnp.float32
    )


def seed_strips_kernel(adjoint_ref, mask_ref, columns_ref, ocean_ref, edges_ref):
    levels_n, rows_n, cols_n = adjoint_ref.shape
    level_at = jnp.right_shift(lane((SUB, cols_n)), 2)
    for top in range(0, rows_n, SUB):
        at = slice(top, top + SUB)
        found = jnp.zeros((SUB, cols_n), jnp.float32)
        for level in range(levels_n):
            block = pltpu.roll(adjoint_ref[level, at, :], (4 * level + 2) % cols_n, 1)
            found = jnp.where(level_at == level, block, found)
        columns_ref[at, :] = found
        spread = jnp.where(level_at == 0, pltpu.roll(mask_ref[at, :].astype(jnp.float32), 2, 1), 0.0)
        shift = 4
        while shift < cols_n:
            spread = spread + pltpu.roll(spread, shift, 1)
            shift *= 2
        ocean_ref[at, :] = spread
    places, levels, _ = edges_ref.shape
    for place, row in enumerate((0, 1, rows_n - 2, rows_n - 1)):
        for level in range(levels_n):
            edges_ref[place, level : level + 1, :] = adjoint_ref[level, row : row + 1, :]
        edges_ref[place, levels_n:, :] = jnp.zeros((levels - levels_n, cols_n), jnp.float32)


def strips_kernel(
    levels_n, returned_ref, cell_ref, weight_ref, mask_ref, seed_columns_ref, ocean_ref, seed_edges_ref,
    columns_ref, edges_ref,
    left_ref, right_ref,
):
    rows_n, cols_n = mask_ref.shape
    places, levels, _ = edges_ref.shape
    slots = cell_ref.shape[1]
    tile = left_ref.shape[1] // 3
    column_sum = jnp.zeros((rows_n, LANES), jnp.float32)
    edge_sum = jnp.zeros((places * levels, cols_n), jnp.float32)
    for start in range(0, slots, tile):
        cell = jnp.maximum(cell_ref[:, start : start + tile], 0)
        row, column = jnp.right_shift(cell, log2(cols_n)), jnp.bitwise_and(cell, cols_n - 1)
        values = returned_values(returned_ref, cell_ref, weight_ref, levels_n, start, tile)

        def chosen(index, wanted):
            for place, number in enumerate(wanted):
                here = jnp.where(index == number, 1.0, 0.0).astype(jnp.bfloat16)
                for part in range(3):
                    right_ref[place * levels : (place + 1) * levels, part * tile : (part + 1) * tile] = (
                        values[part] * here
                    )

        def repeated(hot):
            for part in range(3):
                left_ref[:, part * tile : (part + 1) * tile] = hot

        repeated(one_hot(row, rows_n))
        chosen(column, (cols_n - 2, cols_n - 1, 0, 1))
        column_sum += across(left_ref[...], right_ref[...])
        repeated(one_hot(column, cols_n))
        chosen(row, (0, 1, rows_n - 2, rows_n - 1))
        edge_sum += across(right_ref[...], left_ref[...])
    source, target = sublane((LANES, LANES)), lane((LANES, LANES))
    turn = jnp.bitwise_and(target, 3) * levels + jnp.right_shift(target, 2)
    turn = jnp.where(source == turn, 1.0, 0.0).astype(jnp.bfloat16)
    column_sum = sum(
        jnp.dot(piece, turn, preferred_element_type=jnp.float32) for piece in pieces(column_sum)
    )
    columns_ref[...] = (seed_columns_ref[...] + column_sum) * ocean_ref[...]
    for place, row in enumerate((0, 1, rows_n - 2, rows_n - 1)):
        ocean = mask_ref[row : row + 1, :].astype(jnp.float32)
        forcing = edge_sum[place * levels : (place + 1) * levels]
        edges_ref[place] = (seed_edges_ref[place] + forcing) * ocean


def scatter_kernel(
    returned_ref, cell_ref, weight_ref, adjoint_ref, field_ref,
    out_ref,
    rows_ref, hot_ref, seed_ref, masked_ref,
):
    levels_n, rows_n, cols_n = out_ref.shape
    groups = rows_n // GROUP
    width = groups * cols_n
    tile = hot_ref.shape[1] // 3
    total = None
    for start in range(0, cell_ref.shape[1], tile):
        place, row = cell_parts(cell_ref[:, start : start + tile], rows_n, cols_n)
        values = returned_values(returned_ref, cell_ref, weight_ref, levels_n, start, tile)
        hot = one_hot(place, width)
        mine = one_hot(row, GROUP)
        for part in range(3):
            hot_ref[:, part * tile : (part + 1) * tile] = hot
            for level in range(levels_n):
                rows_ref[level * GROUP : (level + 1) * GROUP, part * tile : (part + 1) * tile] = (
                    mine * values[part][level : level + 1, :]
                )
        found = across(rows_ref[...], hot_ref[...])
        total = found if total is None else total + found
    zero = jnp.zeros((1, cols_n), jnp.float32)
    for level in range(levels_n):
        masked_ref[level, SUB - 1 : SUB, :] = zero
        masked_ref[level, SUB + rows_n : SUB + rows_n + 1, :] = zero
    for group in range(groups):
        at = slice(group * GROUP, (group + 1) * GROUP)
        forcing = total[:, group * cols_n : (group + 1) * cols_n].reshape(levels_n, GROUP, cols_n)
        seed = adjoint_ref[:, at, :] + forcing
        seed_ref[:, at, :] = seed
        masked_ref[:, SUB + group * GROUP : SUB + (group + 1) * GROUP, :] = seed * field_ref[0, at, :]

    def store(level, top, ocean, found):
        out_ref[level, top : top + SUB, :] = found

    advance(seed_ref, masked_ref, field_ref, None, store)


def advance(source_ref, from_ref, field_ref, turn_ref, store):
    levels_n, rows_n, cols_n = source_ref.shape
    first = lane((SUB, cols_n)) == 0
    last = lane((SUB, cols_n)) == cols_n - 1
    for top in range(0, rows_n, SUB):
        at, inner = slice(top, top + SUB), slice(top + SUB, top + 2 * SUB)
        ocean, own, here, back, onto, south_at, mixing = (
            field_ref[place, at, :] for place in range(7)
        )
        if turn_ref is None:
            here_in, back_in = jnp.where(last, 0.0, here), jnp.where(first, 0.0, back)
        else:
            turned = turn_ref[at, :]
        higher = block = from_ref[0, inner, :]
        for level in range(levels_n):
            lower = from_ref[level + 1, inner, :] if level + 1 < levels_n else block
            eastern, western = pltpu.roll(block, cols_n - 1, 1), pltpu.roll(block, 1, 1)
            if turn_ref is None:
                sides = here_in * eastern + back_in * western
            else:
                beyond = pltpu.roll(turned, (2 * cols_n - 2 - 4 * level) % cols_n, 1)
                sides = here * jnp.where(last, beyond, eastern) + back * jnp.where(first, beyond, western)
            north = from_ref[level, top + SUB + 1 : top + 2 * SUB + 1, :]
            south = from_ref[level, top + SUB - 1 : top + 2 * SUB - 1, :]
            vertical = (higher - block) + (lower - block)
            found = (
                (source_ref[level, at, :] - own * block)
                + sides
                + (onto * north + south_at * south)
                + mixing * vertical
            )
            store(level, top, ocean, found)
            higher, block = block, lower


def lane(shape):
    return lax.broadcasted_iota(jnp.int32, shape, 1)


def sublane(shape):
    return lax.broadcasted_iota(jnp.int32, shape, 0)


def shifted(block, steps, axis, edge):
    size = block.shape[axis]
    at = lax.broadcasted_iota(jnp.int32, block.shape, axis)
    moved = pltpu.roll(block, steps % size, axis)
    return jnp.where(at == (0 if steps > 0 else size - 1), edge, moved)


def reversed_lanes(block):
    at = block.shape[1] - 1 - lane(block.shape)
    return jnp.take_along_axis(block, at, axis=1, mode="promise_in_bounds")


def lon_neighbours(flag_ref, first, second):
    even = flag_ref[0] == 1
    return jnp.where(even, first, second), jnp.where(even, second, first)


def lat_neighbours(flag_ref, first, second):
    even = flag_ref[1] == 1
    return jnp.where(even, first, second), jnp.where(even, second, first)


def coefficient_columns_kernel(mask_ref, east_ref, north_ref, flow_ref, vertical_ref, out_ref):
    rows_n, cols_n = mask_ref.shape
    ocean = mask_ref[...].astype(jnp.float32)
    here = east_ref[...] + 0.5 * flow_ref[...]
    behind = east_ref[...] - 0.5 * flow_ref[...]
    north, vertical = north_ref[...], vertical_ref[...]
    last = cols_n - 1
    wanted = (
        (ocean, 0), (here, 0), (north, 0), (vertical, 0),
        (ocean, last), (here, last), (behind, last), (behind, last - 1), (north, last), (vertical, last),
    )
    found = jnp.zeros((rows_n, cols_n), jnp.float32)
    for place, (field, column) in enumerate(wanted):
        found = jnp.where(
            lane(found.shape) == place, pltpu.roll(field, (place - column) % cols_n, 1), found
        )
    out_ref[...] = found


def coefficient_rows_kernel(
    flag_ref, mask_ref, east_ref, north_ref, flow_ref, vertical_ref, first_ref, second_ref, out_ref
):
    rows_n, cols_n = mask_ref.shape
    east, west = lon_neighbours(flag_ref, first_ref[...], second_ref[...])
    top, last = slice(0, 1), slice(rows_n - 1, rows_n)
    found = []
    for at in (top, last):
        behind = east_ref[at, :] - 0.5 * flow_ref[at, :]
        found.append(mask_ref[at, :].astype(jnp.float32))
        found.append(east_ref[at, :] + 0.5 * flow_ref[at, :])
        found.append(shifted(behind, 1, 1, west[at, 6:7]))
        found.append(north_ref[at, :])
        if at is last:
            found.append(north_ref[rows_n - 2 : rows_n - 1, :])
        found.append(vertical_ref[at, :])
    found += [east[top], east[last], west[top], west[last]]
    for place, row in enumerate(found):
        out_ref[place : place + 1, :] = row
    out_ref[len(found) :, :] = jnp.zeros((out_ref.shape[0] - len(found), cols_n), jnp.float32)


def coefficients_kernel(
    flag_ref, mask_ref, east_ref, north_ref, flow_ref, vertical_ref,
    lon_first_ref, lon_second_ref, lat_first_ref, lat_second_ref,
    field_ref, side_ref, edge_ref,
):
    rows_n, cols_n = mask_ref.shape
    fold = flag_ref[2] == 1
    east, west = lon_neighbours(flag_ref, lon_first_ref[...], lon_second_ref[...])
    up, down = lat_neighbours(flag_ref, lat_first_ref[...], lat_second_ref[...])
    mirrored = reversed_lanes(up)
    ocean = mask_ref[...].astype(jnp.float32)
    here = east_ref[...] + 0.5 * flow_ref[...]
    behind = east_ref[...] - 0.5 * flow_ref[...]
    north = north_ref[...]
    back = shifted(behind, 1, 1, west[:, 6:7])
    south = shifted(north, 1, 0, down[8:9])
    top = sublane((rows_n, cols_n)) == rows_n - 1
    onto = jnp.where(jnp.logical_and(top, fold), mirrored[8:9], north)
    parts = (ocean, here + back + north + south, here, back, onto, south, vertical_ref[...])
    for place, part in enumerate(parts):
        field_ref[place] = part

    def side(ocean, here, back, north, vertical, below, fold_top):
        south = shifted(north, 1, 0, below)
        top = sublane(north.shape) == rows_n - 1
        onto = jnp.where(jnp.logical_and(top, fold), fold_top, north)
        return ocean, here + back + north + south, here, back, onto, south, vertical

    def spread(columns, place):
        return jnp.broadcast_to(columns[:, place : place + 1], (columns.shape[0], cols_n))

    eastern = side(
        spread(east, 0), spread(east, 1), spread(behind, cols_n - 1), spread(east, 2), spread(east, 3),
        spread(down[12:13], 2), spread(up[14:15], 8),
    )
    western = side(
        spread(west, 4), spread(west, 5), spread(west, 7), spread(west, 8), spread(west, 9),
        spread(down[14:15], 8), spread(up[12:13], 2),
    )
    found = jnp.zeros((rows_n, cols_n), jnp.float32)
    for place, part in enumerate(eastern + western):
        found = jnp.where(lane(found.shape) == place, part, found)
    side_ref[...] = found

    into = north[rows_n - 1 :, :]
    plain = (up[0:1], up[1:2] + up[2:3] + up[3:4] + into, up[1:2], up[2:3], into, up[3:4], up[4:5])
    turned = mirrored
    folded = (
        turned[5:6], turned[6:7] + turned[7:8] + turned[8:9] + turned[9:10],
        turned[7:8], turned[6:7], into, turned[9:10], turned[10:11],
    )
    low = (
        down[5:6], down[6:7] + down[7:8] + down[8:9] + down[9:10],
        down[6:7], down[7:8], down[8:9], down[9:10], down[10:11],
    )
    for place in range(len(plain)):
        edge_ref[place : place + 1, :] = jnp.where(fold, folded[place], plain[place])
        edge_ref[SUB + place : SUB + place + 1, :] = low[place]
    for place in (len(plain), SUB + len(plain)):
        edge_ref[place : place + 1, :] = jnp.zeros((1, cols_n), jnp.float32)


def edge_message_kernel(flag_ref, edges_ref, first_ref, second_ref, out_ref):
    places, levels, cols_n = edges_ref.shape
    last = first_ref.shape[0] - 1
    for place in range(places):
        out_ref[place * levels : (place + 1) * levels, :] = edges_ref[place]
    ends = []
    for row in (0, last):
        ends.append(lon_neighbours(flag_ref, first_ref[row : row + 1, :], second_ref[row : row + 1, :]))
    found = (ends[0][0], ends[1][0], ends[0][1], ends[1][1])
    for place, row in enumerate(found):
        out_ref[places * levels + place : places * levels + place + 1, :] = row


def steps_kernel(
    flag_ref, inner_ref, field_ref, side_ref, edge_ref,
    columns_ref, edges_ref, lon_first_ref, lon_second_ref, lat_first_ref, lat_second_ref,
    out_ref,
    masked_ref, half_ref, turn_ref, sems,
):
    levels_n, rows_n, cols_n = inner_ref.shape
    levels = edges_ref.shape[1]
    fold = flag_ref[2] == 1
    east, west = lon_neighbours(flag_ref, lon_first_ref[...], lon_second_ref[...])
    up, down = lat_neighbours(flag_ref, lat_first_ref[...], lat_second_ref[...])
    own = columns_ref[...]

    ends = edges_ref.shape[0] * levels
    east_up = jnp.where(fold, pltpu.roll(up[ends + 3 : ends + 4], 1, 1), up[ends : ends + 1])
    west_up = jnp.where(fold, pltpu.roll(up[ends + 1 : ends + 2], cols_n - 1, 1), up[ends + 2 : ends + 3])
    east_down, west_down = down[ends + 1 : ends + 2], down[ends + 3 : ends + 4]

    level_at = jnp.right_shift(lane((rows_n, cols_n)), 2)

    def side_step(block, eastern, western, above, below, base):
        def coefficient(place):
            return side_ref[:, base + place : base + place + 1]

        higher = jnp.where(level_at > 0, pltpu.roll(block, 4, 1) - block, 0.0)
        lower = jnp.where(level_at < levels_n - 1, pltpu.roll(block, cols_n - 4, 1) - block, 0.0)
        change = (
            coefficient(2) * eastern
            + coefficient(3) * western
            + coefficient(4) * shifted(block, -1, 0, above)
            + coefficient(5) * shifted(block, 1, 0, below)
            - coefficient(1) * block
            + coefficient(6) * (higher + lower)
        )
        return block + coefficient(0) * change

    east_next = side_step(
        east, pltpu.roll(east, cols_n - 1, 1), pltpu.roll(own, 1, 1), east_up, east_down, 0
    )
    west_next = side_step(
        west, pltpu.roll(own, cols_n - 1, 1), pltpu.roll(west, 1, 1), west_up, west_down, 7
    )
    slot = jnp.bitwise_and(lane((rows_n, cols_n)), 3)
    for step, (eastern, western) in enumerate(((east, west), (east_next, west_next))):
        turn_ref[step] = jnp.where(
            slot == 1, pltpu.roll(eastern, cols_n - 1, 1), pltpu.roll(western, 1, 1)
        )

    plane = (levels, cols_n)
    corner_at = 4 * sublane(plane)

    def corner(row, place):
        found = jnp.where(lane(plane) == corner_at + place, jnp.broadcast_to(row, plane), 0.0)
        return jnp.sum(found, axis=1, keepdims=True)

    def edge(block, place):
        return block[place * levels : (place + 1) * levels]

    def edge_step(block, outer, inner, eastern, western, base):
        def coefficient(place):
            return edge_ref[base + place : base + place + 1, :]

        level = sublane(plane)
        higher = jnp.where(level > 0, pltpu.roll(block, 1, 0) - block, 0.0)
        lower = jnp.where(level < levels_n - 1, pltpu.roll(block, levels - 1, 0) - block, 0.0)
        change = (
            coefficient(2) * shifted(block, -1, 1, eastern)
            + coefficient(3) * shifted(block, 1, 1, western)
            + coefficient(4) * inner
            + coefficient(5) * outer
            - coefficient(1) * block
            + coefficient(6) * (higher + lower)
        )
        return block + coefficient(0) * change

    above = jnp.where(fold, reversed_lanes(edge(up, 3)), edge(up, 0))
    above_outer = jnp.where(fold, reversed_lanes(edge(up, 2)), edge(up, 1))
    below, below_outer = edge(down, 3), edge(down, 2)
    above_next = edge_step(
        above, above_outer, edges_ref[3], corner(east_up, 2), corner(west_up, 1), 0
    )
    below_next = edge_step(
        below, below_outer, edges_ref[0], corner(east_down, 2), corner(west_down, 1), SUB
    )
    for level in range(levels_n):
        masked_ref[level, SUB + rows_n : SUB + rows_n + 1, :] = above_next[level : level + 1, :]
        masked_ref[level, SUB - 1 : SUB, :] = below_next[level : level + 1, :]
    first = lane((SUB, cols_n)) == 0
    last = lane((SUB, cols_n)) == cols_n - 1
    for top in range(0, rows_n, SUB):
        at, inner = slice(top, top + SUB), slice(top + SUB, top + 2 * SUB)
        ocean = field_ref[0, at, :]
        side = jnp.where(last, field_ref[2, at, :], jnp.where(first, field_ref[3, at, :], 0.0))
        turned = turn_ref[0, at, :]
        place = sublane((SUB, cols_n))
        for level in range(levels_n):
            beyond = pltpu.roll(turned, (2 * cols_n - 2 - 4 * level) % cols_n, 1)
            found = inner_ref[level, at, :] + side * beyond
            if top == 0:
                below_row = field_ref[5, 0:1, :] * below[level : level + 1, :]
                found = found + jnp.where(place == 0, below_row, 0.0)
            if top == rows_n - SUB:
                above_row = field_ref[4, rows_n - 1 : rows_n, :] * above[level : level + 1, :]
                found = found + jnp.where(place == SUB - 1, above_row, 0.0)
            half_ref[level, at, :] = found
            masked_ref[level, inner, :] = ocean * found

    copies = []

    def store(level, top, ocean, found):
        half_ref[level, top : top + SUB, :] = found
        if level == levels_n - 1 and (top + SUB) % (rows_n // sems.shape[0]) == 0:
            rows = slice(top + SUB - rows_n // sems.shape[0], top + SUB)
            copy = pltpu.make_async_copy(
                half_ref.at[:, rows, :], out_ref.at[:, rows, :], sems.at[len(copies)]
            )
            copy.start()
            copies.append(copy)

    advance(half_ref, masked_ref, field_ref, turn_ref.at[1], store)
    for copy in copies:
        copy.wait()


def kernel_call(mebibytes, body, out_shape, scratch=(), ins=None, outs=None):
    memory = {}
    if ins is not None:
        memory["in_specs"] = [pl.BlockSpec(memory_space=space) for space in ins]
    if outs is not None:
        memory["out_specs"] = pl.BlockSpec(memory_space=outs)
    return pl.pallas_call(
        body,
        out_shape=out_shape,
        scratch_shapes=list(scratch),
        compiler_params=pltpu.CompilerParams(vmem_limit_bytes=mebibytes * MIB),
        **memory,
    )


def flagged(inputs):
    return [pltpu.SMEM] + [pltpu.VMEM] * (inputs - 1)


def exchanged(value, devices):
    rows = value.reshape(devices, 1, value.size // devices)
    return lax.all_to_all(rows, BOTH, split_axis=0, concat_axis=0, tiled=True).reshape(value.shape)


def f32(*shape):
    return jax.ShapeDtypeStruct(shape, jnp.float32)


def lon_swaps(value):
    count = lax.axis_size("lon")
    assert count % 2 == 0
    first = [(i, i ^ 1) for i in range(count)]
    second = [(i, (i + 1 if i % 2 else i - 1) % count) for i in range(count)]
    return lax.ppermute(value, "lon", first), lax.ppermute(value, "lon", second)


def lat_swaps(value):
    lons, lats = lax.axis_size("lon"), lax.axis_size("lat")
    found = []
    for parity in (0, 1):
        pairs = []
        for i in range(lons):
            for j in range(lats):
                other = j + 1 if j % 2 == parity else j - 1
                if other == lats:
                    pairs.append((i * lats + j, (lons - 1 - i) * lats + j))
                elif other >= 0:
                    pairs.append((i * lats + j, i * lats + other))
        found.append(lax.ppermute(value, BOTH, pairs))
    return tuple(found)


def on_device(
    state,
    adjoint_in,
    land_mask,
    east_coef,
    north_coef,
    zonal_flow,
    vertical_coef,
    slot_cell,
    slot_weight,
    arrive_obs,
    obs_value,
    obs_invvar,
):
    levels_n, rows_n, cols_n = state.shape
    devices = lax.axis_size(BOTH)
    slots = slot_cell.shape[1]
    obs_n = obs_value.shape[1]
    assert 2 * (slots // devices) == LANES and cols_n == LANES and 4 * levels_n <= LANES
    half = (levels_n + 1) // 2
    width = rows_n // GROUP * cols_n
    bf16 = jnp.bfloat16
    raw = (land_mask, east_coef, north_coef, zonal_flow, vertical_coef)
    lon, lat = lax.axis_index("lon"), lax.axis_index("lat")
    flags = jnp.stack([1 - lon % 2, 1 - lat % 2, lat == lax.axis_size("lat") - 1]).astype(jnp.int32)

    partial_vals = kernel_call(
        60,
        gather_kernel,
        f32(devices * half, LANES),
        [
            pltpu.VMEM((1, slots), jnp.int32),
            pltpu.VMEM((1, slots), jnp.float32),
            pltpu.VMEM((levels_n, rows_n, cols_n), jnp.float32),
            pltpu.VMEM((levels_n * GROUP, 3 * width), bf16),
            pltpu.SemaphoreType.DMA((2 + levels_n,)),
        ],
        [pltpu.HBM] * 3,
    )(slot_cell, slot_weight, state)
    columns = kernel_call(8, coefficient_columns_kernel, f32(rows_n, cols_n))(*raw)
    partial_vals, columns = lax.optimization_barrier((partial_vals, columns))
    arrived = exchanged(partial_vals, devices)
    arrived, side_coefs = lax.optimization_barrier((arrived, lon_swaps(columns)))
    row_coefs = kernel_call(8, coefficient_rows_kernel, f32(2 * SUB, cols_n), (), flagged(8))(
        flags, *raw, *side_coefs
    )
    misfit, outgoing = kernel_call(
        32,
        observe_kernel,
        (f32(levels_n, obs_n), f32(devices * half, LANES)),
        [pltpu.VMEM((obs_n, slots), bf16)],
    )(arrived, arrive_obs, obs_value, obs_invvar)
    outgoing, row_coefs, adjoint_in, land_mask = lax.optimization_barrier(
        (outgoing, row_coefs, adjoint_in, land_mask)
    )
    returned = exchanged(outgoing, devices)
    levels = padded_levels(levels_n)
    fields, sides, edges = kernel_call(
        8,
        coefficients_kernel,
        (f32(7, rows_n, cols_n), f32(rows_n, cols_n), f32(2 * SUB, cols_n)),
        (), flagged(10),
    )(flags, *raw, *side_coefs, *lat_swaps(row_coefs))
    strips = kernel_call(
        8,
        seed_strips_kernel,
        (f32(rows_n, cols_n), f32(rows_n, cols_n), f32(4, levels, cols_n)),
    )(adjoint_in, land_mask)
    returned, fields, sides, edges, strips = lax.optimization_barrier(
        (returned, fields, sides, edges, strips)
    )
    tile = min(slots, SLOT_TILE)
    own_columns, own_edges = kernel_call(
        32,
        functools.partial(strips_kernel, levels_n),
        (f32(rows_n, cols_n), f32(4, levels, cols_n)),
        [pltpu.VMEM((rows_n, 3 * tile), bf16), pltpu.VMEM((4 * levels, 3 * tile), bf16)],
    )(returned, slot_cell, slot_weight, land_mask, *strips)
    side_columns = lon_swaps(own_columns)
    extended = (levels_n, rows_n + 2 * SUB, cols_n)
    inner = kernel_call(
        40,
        scatter_kernel,
        f32(levels_n, rows_n, cols_n),
        [
            pltpu.VMEM((levels_n * GROUP, 3 * tile), bf16),
            pltpu.VMEM((width, 3 * tile), bf16),
            pltpu.VMEM((levels_n, rows_n, cols_n), jnp.float32),
            pltpu.VMEM(extended, jnp.float32),
        ],
    )(returned, slot_cell, slot_weight, adjoint_in, fields)
    inner, side_columns = lax.optimization_barrier((inner, side_columns))
    message = kernel_call(8, edge_message_kernel, f32(4 * levels + SUB, cols_n), (), flagged(4))(
        flags, own_edges, *side_columns
    )
    side_edges = lat_swaps(message)
    adjoint_state = kernel_call(
        16,
        steps_kernel,
        f32(levels_n, rows_n, cols_n),
        [
            pltpu.VMEM(extended, jnp.float32),
            pltpu.VMEM((levels_n, rows_n, cols_n), jnp.float32),
            pltpu.VMEM((STEPS, rows_n, cols_n), jnp.float32),
            pltpu.SemaphoreType.DMA((4,)),
        ],
        flagged(11), pltpu.HBM,
    )(flags, inner, fields, sides, edges, own_columns, own_edges, *side_columns, *side_edges)
    return (adjoint_state, misfit)


def solution(mesh):
    in_specs = (
        P(None, "lat", "lon"),
        P(None, "lat", "lon"),
        P("lat", "lon"),
        P("lat", "lon"),
        P("lat", "lon"),
        P("lat", "lon"),
        P("lat", "lon"),
        P(("lon", "lat"), None),
        P(("lon", "lat"), None),
        P(("lon", "lat"), None),
        P(None, ("lon", "lat")),
        P(None, ("lon", "lat")),
    )
    out_specs = (P(None, "lat", "lon"), P(None, ("lon", "lat")))
    return jax.shard_map(
        on_device, mesh=mesh, in_specs=in_specs, out_specs=out_specs, check_vma=False
    )
```

```python
import functools

import jax
import jax.numpy as jnp
from jax import lax
from jax.experimental import pallas as pl
from jax.experimental.pallas import tpu as pltpu
from jax.sharding import PartitionSpec as P

STEPS = 2
LANES = 128
GROUP = 32
SUB = 8
SLOT_TILE = 16 * LANES
MIB = 1024 * 1024
BOTH = ("lon", "lat")


def pieces(value):
    high = value.astype(jnp.bfloat16)
    rest = value - high.astype(jnp.float32)
    middle = rest.astype(jnp.bfloat16)
    low = (rest - middle.astype(jnp.float32)).astype(jnp.bfloat16)
    return high, middle, low


def log2(size):
    assert size & (size - 1) == 0
    return size.bit_length() - 1


def cell_parts(cell, rows_n, cols_n):
    cell = jnp.maximum(cell, 0)
    row = jnp.right_shift(cell, log2(cols_n))
    group = jnp.right_shift(row, log2(GROUP))
    place = jnp.bitwise_and(cell, cols_n - 1) + group * cols_n
    return place, jnp.bitwise_and(row, GROUP - 1)


def one_hot(index, size):
    rows = lax.broadcasted_iota(jnp.int32, (size, index.shape[1]), 0)
    return jnp.where(rows == index, 1.0, 0.0).astype(jnp.bfloat16)


def first_half(rows):
    return lane((rows, LANES)) < LANES // 2


def pack(values, out_ref, first_pair):
    half = values.shape[0] // 2
    for pair in range(values.shape[1] // LANES):
        block = values[:, pair * LANES : (pair + 1) * LANES]
        top, bottom = block[:half], block[half:]
        at = 2 * (first_pair + pair) * half
        out_ref[at : at + half, :] = jnp.where(
            first_half(half), top, pltpu.roll(bottom, LANES // 2, 1)
        )
        out_ref[at + half : at + 2 * half, :] = jnp.where(
            first_half(half), pltpu.roll(top, LANES // 2, 1), bottom
        )


def unpack(in_ref, half, first_pair, pairs, levels):
    found = []
    for pair in range(first_pair, first_pair + pairs):
        at = 2 * pair * half
        left, right = in_ref[at : at + half, :], in_ref[at + half : at + 2 * half, :]
        top = jnp.where(first_half(half), left, pltpu.roll(right, LANES // 2, 1))
        bottom = jnp.where(first_half(half), pltpu.roll(left, LANES // 2, 1), right)
        filler = jnp.zeros((levels - 2 * half, LANES), jnp.float32)
        found.append(jnp.concatenate([top, bottom, filler], axis=0))
    return jnp.concatenate(found, axis=1)


def gather_kernel(
    cell_in, weight_in, state_in, out_ref, cell_ref, weight_ref, state_ref, field_ref, sems
):
    levels_n, rows_n, cols_n = state_ref.shape
    groups = rows_n // GROUP
    width = groups * cols_n
    slots = cell_ref.shape[1]
    tile = min(slots, SLOT_TILE)
    chunk = max(n for n in range(1, 9) if levels_n % n == 0)
    copies = [
        pltpu.make_async_copy(cell_in, cell_ref, sems.at[0]),
        pltpu.make_async_copy(weight_in, weight_ref, sems.at[1]),
    ]
    for place, level in enumerate(range(0, levels_n, chunk)):
        at = slice(level, level + chunk)
        copies.append(pltpu.make_async_copy(state_in.at[at], state_ref.at[at], sems.at[2 + place]))
    for copy in copies:
        copy.start()
    copies[0].wait()
    for start in range(0, slots, tile):
        cell = cell_ref[:, start : start + tile]
        place, row = cell_parts(cell, rows_n, cols_n)
        hot = one_hot(place, width)
        hot = jnp.concatenate([hot, hot, hot], axis=0)
        mine = sublane((GROUP, tile)) == row
        values = []
        for index, level in enumerate(range(0, levels_n, chunk)):
            at = slice(level * GROUP, (level + chunk) * GROUP)
            if start == 0:
                copies[2 + index].wait()
                for group in range(groups):
                    block = state_ref[
                        level : level + chunk, group * GROUP : (group + 1) * GROUP, :
                    ].reshape(chunk * GROUP, cols_n)
                    for part, piece in enumerate(pieces(block)):
                        begin = part * width + group * cols_n
                        field_ref[at, begin : begin + cols_n] = piece
            found = jnp.dot(field_ref[at, :], hot, preferred_element_type=jnp.float32)
            found = found.reshape(chunk, GROUP, tile)
            values.append(jnp.sum(jnp.where(mine[None], found, 0.0), axis=1))
        if start == 0:
            copies[1].wait()
        weight = jnp.where(cell >= 0, weight_ref[:, start : start + tile], 0.0)
        if levels_n % 2:
            values.append(jnp.zeros((1, tile), jnp.float32))
        pack(jnp.concatenate(values, axis=0) * weight, out_ref, start // LANES)


def observe_kernel(arrived_ref, target_ref, value_ref, invvar_ref, misfit_ref, out_ref, hot_ref):
    levels_n, obs_n = value_ref.shape
    half = (levels_n + 1) // 2
    levels = padded_levels(levels_n)
    slots = target_ref.shape[1]
    tile = min(slots, SLOT_TILE)
    sums = None
    for start in range(0, slots, tile):
        hot = one_hot(target_ref[:, start : start + tile], obs_n)
        hot_ref[:, start : start + tile] = hot
        values = unpack(arrived_ref, half, start // LANES, tile // LANES, levels)
        found = across(jnp.concatenate(pieces(values), axis=0), hot)
        sums = found if sums is None else sums + found
    interp = sums[:levels] + sums[levels : 2 * levels] + sums[2 * levels :]
    misfit = invvar_ref[...] * (interp[:levels_n] - value_ref[...])
    misfit_ref[...] = misfit
    filler = jnp.zeros((levels - levels_n, obs_n), jnp.float32)
    back = jnp.concatenate(pieces(jnp.concatenate([misfit, filler], axis=0)), axis=0)
    for start in range(0, slots, tile):
        found = jnp.dot(
            back, hot_ref[:, start : start + tile], preferred_element_type=jnp.float32
        )
        values = found[:levels] + found[levels : 2 * levels] + found[2 * levels :]
        pack(values[: 2 * half], out_ref, start // LANES)


def padded_levels(levels_n):
    return (levels_n + 15) // 16 * 16


def returned_values(returned_ref, cell_ref, weight_ref, levels_n, start, tile):
    at = slice(start, start + tile)
    weight = jnp.where(cell_ref[:, at] >= 0, weight_ref[:, at], 0.0)
    values = unpack(
        returned_ref, (levels_n + 1) // 2, start // LANES, tile // LANES, padded_levels(levels_n)
    )
    return pieces(values * weight)


def across(left, right):
    return lax.dot_general(
        left, right, (((1,), (1,)), ((), ())), preferred_element_type=jnp.float32
    )


def seed_strips_kernel(adjoint_ref, mask_ref, columns_ref, ocean_ref, edges_ref):
    levels_n, rows_n, cols_n = adjoint_ref.shape
    level_at = jnp.right_shift(lane((SUB, cols_n)), 2)
    for top in range(0, rows_n, SUB):
        at = slice(top, top + SUB)
        found = jnp.zeros((SUB, cols_n), jnp.float32)
        for level in range(levels_n):
            block = pltpu.roll(adjoint_ref[level, at, :], (4 * level + 2) % cols_n, 1)
            found = jnp.where(level_at == level, block, found)
        columns_ref[at, :] = found
        spread = jnp.where(level_at == 0, pltpu.roll(mask_ref[at, :].astype(jnp.float32), 2, 1), 0.0)
        shift = 4
        while shift < cols_n:
            spread = spread + pltpu.roll(spread, shift, 1)
            shift *= 2
        ocean_ref[at, :] = spread
    places, levels, _ = edges_ref.shape
    for place, row in enumerate((0, 1, rows_n - 2, rows_n - 1)):
        for level in range(levels_n):
            edges_ref[place, level : level + 1, :] = adjoint_ref[level, row : row + 1, :]
        edges_ref[place, levels_n:, :] = jnp.zeros((levels - levels_n, cols_n), jnp.float32)


def strips_kernel(
    levels_n, returned_ref, cell_ref, weight_ref, mask_ref, seed_columns_ref, ocean_ref, seed_edges_ref,
    columns_ref, edges_ref,
    left_ref, right_ref,
):
    rows_n, cols_n = mask_ref.shape
    places, levels, _ = edges_ref.shape
    slots = cell_ref.shape[1]
    tile = left_ref.shape[1] // 3
    column_sum = jnp.zeros((rows_n, LANES), jnp.float32)
    edge_sum = jnp.zeros((places * levels, cols_n), jnp.float32)
    for start in range(0, slots, tile):
        cell = jnp.maximum(cell_ref[:, start : start + tile], 0)
        row, column = jnp.right_shift(cell, log2(cols_n)), jnp.bitwise_and(cell, cols_n - 1)
        values = returned_values(returned_ref, cell_ref, weight_ref, levels_n, start, tile)

        def chosen(index, wanted):
            for place, number in enumerate(wanted):
                here = jnp.where(index == number, 1.0, 0.0).astype(jnp.bfloat16)
                for part in range(3):
                    right_ref[place * levels : (place + 1) * levels, part * tile : (part + 1) * tile] = (
                        values[part] * here
                    )

        def repeated(hot):
            for part in range(3):
                left_ref[:, part * tile : (part + 1) * tile] = hot

        repeated(one_hot(row, rows_n))
        chosen(column, (cols_n - 2, cols_n - 1, 0, 1))
        column_sum += across(left_ref[...], right_ref[...])
        repeated(one_hot(column, cols_n))
        chosen(row, (0, 1, rows_n - 2, rows_n - 1))
        edge_sum += across(right_ref[...], left_ref[...])
    source, target = sublane((LANES, LANES)), lane((LANES, LANES))
    turn = jnp.bitwise_and(target, 3) * levels + jnp.right_shift(target, 2)
    turn = jnp.where(source == turn, 1.0, 0.0).astype(jnp.bfloat16)
    column_sum = sum(
        jnp.dot(piece, turn, preferred_element_type=jnp.float32) for piece in pieces(column_sum)
    )
    columns_ref[...] = (seed_columns_ref[...] + column_sum) * ocean_ref[...]
    for place, row in enumerate((0, 1, rows_n - 2, rows_n - 1)):
        ocean = mask_ref[row : row + 1, :].astype(jnp.float32)
        forcing = edge_sum[place * levels : (place + 1) * levels]
        edges_ref[place] = (seed_edges_ref[place] + forcing) * ocean


def scatter_kernel(returned_ref, cell_ref, weight_ref, adjoint_ref, out_ref, rows_ref, hot_ref):
    levels_n, rows_n, cols_n = out_ref.shape
    groups = rows_n // GROUP
    width = groups * cols_n
    tile = hot_ref.shape[1] // 3
    total = None
    for start in range(0, cell_ref.shape[1], tile):
        place, row = cell_parts(cell_ref[:, start : start + tile], rows_n, cols_n)
        values = returned_values(returned_ref, cell_ref, weight_ref, levels_n, start, tile)
        hot = one_hot(place, width)
        mine = one_hot(row, GROUP)
        for part in range(3):
            hot_ref[:, part * tile : (part + 1) * tile] = hot
            for level in range(levels_n):
                rows_ref[level * GROUP : (level + 1) * GROUP, part * tile : (part + 1) * tile] = (
                    mine * values[part][level : level + 1, :]
                )
        found = across(rows_ref[...], hot_ref[...])
        total = found if total is None else total + found
    for group in range(groups):
        at = slice(group * GROUP, (group + 1) * GROUP)
        forcing = total[:, group * cols_n : (group + 1) * cols_n].reshape(levels_n, GROUP, cols_n)
        out_ref[:, at, :] = adjoint_ref[:, at, :] + forcing


def inner_step_kernel(seed_ref, field_ref, out_ref, masked_ref):
    levels_n, rows_n, cols_n = out_ref.shape
    zero = jnp.zeros((1, cols_n), jnp.float32)
    for level in range(levels_n):
        masked_ref[level, SUB - 1 : SUB, :] = zero
        masked_ref[level, SUB + rows_n : SUB + rows_n + 1, :] = zero
    for top in range(0, rows_n, SUB):
        ocean = field_ref[0, top : top + SUB, :]
        for level in range(levels_n):
            masked_ref[level, SUB + top : 2 * SUB + top, :] = ocean * seed_ref[level, top : top + SUB, :]

    def store(level, top, ocean, found):
        out_ref[level, top : top + SUB, :] = found

    advance(seed_ref, masked_ref, field_ref, None, store)


def advance(source_ref, from_ref, field_ref, turn_ref, store):
    levels_n, rows_n, cols_n = source_ref.shape
    first = lane((SUB, cols_n)) == 0
    last = lane((SUB, cols_n)) == cols_n - 1
    for top in range(0, rows_n, SUB):
        at, inner = slice(top, top + SUB), slice(top + SUB, top + 2 * SUB)
        ocean, own, here, back, onto, south_at, mixing = (
            field_ref[place, at, :] for place in range(7)
        )
        if turn_ref is None:
            here_in, back_in = jnp.where(last, 0.0, here), jnp.where(first, 0.0, back)
        else:
            turned = turn_ref[at, :]
        higher = block = from_ref[0, inner, :]
        for level in range(levels_n):
            lower = from_ref[level + 1, inner, :] if level + 1 < levels_n else block
            eastern, western = pltpu.roll(block, cols_n - 1, 1), pltpu.roll(block, 1, 1)
            if turn_ref is None:
                sides = here_in * eastern + back_in * western
            else:
                beyond = pltpu.roll(turned, (2 * cols_n - 2 - 4 * level) % cols_n, 1)
                sides = here * jnp.where(last, beyond, eastern) + back * jnp.where(first, beyond, western)
            north = from_ref[level, top + SUB + 1 : top + 2 * SUB + 1, :]
            south = from_ref[level, top + SUB - 1 : top + 2 * SUB - 1, :]
            vertical = (higher - block) + (lower - block)
            found = (
                (source_ref[level, at, :] - own * block)
                + sides
                + (onto * north + south_at * south)
                + mixing * vertical
            )
            store(level, top, ocean, found)
            higher, block = block, lower


def lane(shape):
    return lax.broadcasted_iota(jnp.int32, shape, 1)


def sublane(shape):
    return lax.broadcasted_iota(jnp.int32, shape, 0)


def shifted(block, steps, axis, edge):
    size = block.shape[axis]
    at = lax.broadcasted_iota(jnp.int32, block.shape, axis)
    moved = pltpu.roll(block, steps % size, axis)
    return jnp.where(at == (0 if steps > 0 else size - 1), edge, moved)


def reversed_lanes(block):
    at = block.shape[1] - 1 - lane(block.shape)
    return jnp.take_along_axis(block, at, axis=1, mode="promise_in_bounds")


def lon_neighbours(flag_ref, first, second):
    even = flag_ref[0] == 1
    return jnp.where(even, first, second), jnp.where(even, second, first)


def lat_neighbours(flag_ref, first, second):
    even = flag_ref[1] == 1
    return jnp.where(even, first, second), jnp.where(even, second, first)


def side_columns(flag_ref, first_ref, second_ref):
    filler = jnp.zeros((first_ref.shape[1] - first_ref.shape[0], first_ref.shape[1]), jnp.float32)
    east, west = lon_neighbours(flag_ref, first_ref[...], second_ref[...])
    return tuple(jnp.concatenate([block, filler], axis=0).T for block in (east, west))


def coefficient_columns_kernel(mask_ref, east_ref, north_ref, flow_ref, vertical_ref, out_ref):
    rows_n, cols_n = mask_ref.shape
    ocean = mask_ref[...].astype(jnp.float32)
    here = east_ref[...] + 0.5 * flow_ref[...]
    behind = east_ref[...] - 0.5 * flow_ref[...]
    north, vertical = north_ref[...], vertical_ref[...]
    last = cols_n - 1
    wanted = (
        (ocean, 0), (here, 0), (north, 0), (vertical, 0),
        (ocean, last), (here, last), (behind, last), (behind, last - 1), (north, last), (vertical, last),
    )
    found = jnp.zeros((rows_n, cols_n), jnp.float32)
    for place, (field, column) in enumerate(wanted):
        found = jnp.where(
            lane(found.shape) == place, pltpu.roll(field, (place - column) % cols_n, 1), found
        )
    out_ref[...] = found.T[: out_ref.shape[0]]


def coefficient_rows_kernel(
    flag_ref, mask_ref, east_ref, north_ref, flow_ref, vertical_ref, first_ref, second_ref, out_ref
):
    rows_n, cols_n = mask_ref.shape
    east, west = side_columns(flag_ref, first_ref, second_ref)
    top, last = slice(0, 1), slice(rows_n - 1, rows_n)
    found = []
    for at in (top, last):
        behind = east_ref[at, :] - 0.5 * flow_ref[at, :]
        found.append(mask_ref[at, :].astype(jnp.float32))
        found.append(east_ref[at, :] + 0.5 * flow_ref[at, :])
        found.append(shifted(behind, 1, 1, west[at, 6:7]))
        found.append(north_ref[at, :])
        if at is last:
            found.append(north_ref[rows_n - 2 : rows_n - 1, :])
        found.append(vertical_ref[at, :])
    found += [east[top], east[last], west[top], west[last]]
    for place, row in enumerate(found):
        out_ref[place : place + 1, :] = row
    out_ref[len(found) :, :] = jnp.zeros((out_ref.shape[0] - len(found), cols_n), jnp.float32)


def coefficients_kernel(
    flag_ref, mask_ref, east_ref, north_ref, flow_ref, vertical_ref,
    lon_first_ref, lon_second_ref, lat_first_ref, lat_second_ref,
    field_ref, side_ref, edge_ref,
):
    rows_n, cols_n = mask_ref.shape
    fold = flag_ref[2] == 1
    east, west = side_columns(flag_ref, lon_first_ref, lon_second_ref)
    up, down = lat_neighbours(flag_ref, lat_first_ref[...], lat_second_ref[...])
    mirrored = reversed_lanes(up)
    ocean = mask_ref[...].astype(jnp.float32)
    here = east_ref[...] + 0.5 * flow_ref[...]
    behind = east_ref[...] - 0.5 * flow_ref[...]
    north = north_ref[...]
    back = shifted(behind, 1, 1, west[:, 6:7])
    south = shifted(north, 1, 0, down[8:9])
    top = sublane((rows_n, cols_n)) == rows_n - 1
    onto = jnp.where(jnp.logical_and(top, fold), mirrored[8:9], north)
    parts = (ocean, here + back + north + south, here, back, onto, south, vertical_ref[...])
    for place, part in enumerate(parts):
        field_ref[place] = part

    def side(ocean, here, back, north, vertical, below, fold_top):
        south = shifted(north, 1, 0, below)
        top = sublane(north.shape) == rows_n - 1
        onto = jnp.where(jnp.logical_and(top, fold), fold_top, north)
        return ocean, here + back + north + south, here, back, onto, south, vertical

    def spread(columns, place):
        return jnp.broadcast_to(columns[:, place : place + 1], (columns.shape[0], cols_n))

    eastern = side(
        spread(east, 0), spread(east, 1), spread(behind, cols_n - 1), spread(east, 2), spread(east, 3),
        spread(down[12:13], 2), spread(up[14:15], 8),
    )
    western = side(
        spread(west, 4), spread(west, 5), spread(west, 7), spread(west, 8), spread(west, 9),
        spread(down[14:15], 8), spread(up[12:13], 2),
    )
    found = jnp.zeros((rows_n, cols_n), jnp.float32)
    for place, part in enumerate(eastern + western):
        found = jnp.where(lane(found.shape) == place, part, found)
    side_ref[...] = found

    into = north[rows_n - 1 :, :]
    plain = (up[0:1], up[1:2] + up[2:3] + up[3:4] + into, up[1:2], up[2:3], into, up[3:4], up[4:5])
    turned = mirrored
    folded = (
        turned[5:6], turned[6:7] + turned[7:8] + turned[8:9] + turned[9:10],
        turned[7:8], turned[6:7], into, turned[9:10], turned[10:11],
    )
    low = (
        down[5:6], down[6:7] + down[7:8] + down[8:9] + down[9:10],
        down[6:7], down[7:8], down[8:9], down[9:10], down[10:11],
    )
    for place in range(len(plain)):
        edge_ref[place : place + 1, :] = jnp.where(fold, folded[place], plain[place])
        edge_ref[SUB + place : SUB + place + 1, :] = low[place]
    for place in (len(plain), SUB + len(plain)):
        edge_ref[place : place + 1, :] = jnp.zeros((1, cols_n), jnp.float32)


def edge_message_kernel(flag_ref, edges_ref, lon_first_ref, lon_second_ref, first_ref, second_ref):
    places, levels, cols_n = edges_ref.shape
    last = lon_first_ref.shape[0] - 1
    even = flag_ref[1] == 1
    first_ref[2 * levels :, :] = jnp.zeros((SUB, cols_n), jnp.float32)
    second_ref[2 * levels :, :] = jnp.zeros((SUB, cols_n), jnp.float32)
    for place, (north, south) in enumerate(((places - 1, 0), (places - 2, 1))):
        at = slice(place * levels, (place + 1) * levels)
        northern, southern = edges_ref[north], edges_ref[south]
        first_ref[at, :] = jnp.where(even, northern, southern)
        second_ref[at, :] = jnp.where(even, southern, northern)
    northern = lon_neighbours(flag_ref, lon_first_ref[last:, :], lon_second_ref[last:, :])
    southern = lon_neighbours(flag_ref, lon_first_ref[0:1, :], lon_second_ref[0:1, :])
    for place in range(2):
        at = slice(2 * levels + place, 2 * levels + place + 1)
        first_ref[at, :] = jnp.where(even, northern[place], southern[place])
        second_ref[at, :] = jnp.where(even, southern[place], northern[place])


def steps_kernel(
    flag_ref, inner_ref, field_ref, side_ref, edge_ref,
    columns_ref, edges_ref, lon_first_ref, lon_second_ref, lat_first_ref, lat_second_ref,
    out_ref,
    masked_ref, half_ref, turn_ref, sems,
):
    levels_n, rows_n, cols_n = inner_ref.shape
    levels = edges_ref.shape[1]
    fold = flag_ref[2] == 1
    east, west = lon_neighbours(flag_ref, lon_first_ref[...], lon_second_ref[...])
    up, down = lat_neighbours(flag_ref, lat_first_ref[...], lat_second_ref[...])
    own = columns_ref[...]

    ends = 2 * levels
    east_up = jnp.where(fold, pltpu.roll(up[ends + 1 : ends + 2], 1, 1), up[ends : ends + 1])
    west_up = jnp.where(fold, pltpu.roll(up[ends : ends + 1], cols_n - 1, 1), up[ends + 1 : ends + 2])
    east_down, west_down = down[ends : ends + 1], down[ends + 1 : ends + 2]

    level_at = jnp.right_shift(lane((rows_n, cols_n)), 2)

    def side_step(block, eastern, western, above, below, base):
        def coefficient(place):
            return side_ref[:, base + place : base + place + 1]

        higher = jnp.where(level_at > 0, pltpu.roll(block, 4, 1) - block, 0.0)
        lower = jnp.where(level_at < levels_n - 1, pltpu.roll(block, cols_n - 4, 1) - block, 0.0)
        change = (
            coefficient(2) * eastern
            + coefficient(3) * western
            + coefficient(4) * shifted(block, -1, 0, above)
            + coefficient(5) * shifted(block, 1, 0, below)
            - coefficient(1) * block
            + coefficient(6) * (higher + lower)
        )
        return block + coefficient(0) * change

    east_next = side_step(
        east, pltpu.roll(east, cols_n - 1, 1), pltpu.roll(own, 1, 1), east_up, east_down, 0
    )
    west_next = side_step(
        west, pltpu.roll(own, cols_n - 1, 1), pltpu.roll(west, 1, 1), west_up, west_down, 7
    )
    slot = jnp.bitwise_and(lane((rows_n, cols_n)), 3)
    for step, (eastern, western) in enumerate(((east, west), (east_next, west_next))):
        turn_ref[step] = jnp.where(
            slot == 1, pltpu.roll(eastern, cols_n - 1, 1), pltpu.roll(western, 1, 1)
        )

    plane = (levels, cols_n)
    corner_at = 4 * sublane(plane)

    def corner(row, place):
        found = jnp.where(lane(plane) == corner_at + place, jnp.broadcast_to(row, plane), 0.0)
        return jnp.sum(found, axis=1, keepdims=True)

    def edge(block, place):
        return block[place * levels : (place + 1) * levels]

    def edge_step(block, outer, inner, eastern, western, base):
        def coefficient(place):
            return edge_ref[base + place : base + place + 1, :]

        level = sublane(plane)
        higher = jnp.where(level > 0, pltpu.roll(block, 1, 0) - block, 0.0)
        lower = jnp.where(level < levels_n - 1, pltpu.roll(block, levels - 1, 0) - block, 0.0)
        change = (
            coefficient(2) * shifted(block, -1, 1, eastern)
            + coefficient(3) * shifted(block, 1, 1, western)
            + coefficient(4) * inner
            + coefficient(5) * outer
            - coefficient(1) * block
            + coefficient(6) * (higher + lower)
        )
        return block + coefficient(0) * change

    above = jnp.where(fold, reversed_lanes(edge(up, 0)), edge(up, 0))
    above_outer = jnp.where(fold, reversed_lanes(edge(up, 1)), edge(up, 1))
    below, below_outer = edge(down, 0), edge(down, 1)
    above_next = edge_step(
        above, above_outer, edges_ref[3], corner(east_up, 2), corner(west_up, 1), 0
    )
    below_next = edge_step(
        below, below_outer, edges_ref[0], corner(east_down, 2), corner(west_down, 1), SUB
    )
    for level in range(levels_n):
        masked_ref[level, SUB + rows_n : SUB + rows_n + 1, :] = above_next[level : level + 1, :]
        masked_ref[level, SUB - 1 : SUB, :] = below_next[level : level + 1, :]
    first = lane((SUB, cols_n)) == 0
    last = lane((SUB, cols_n)) == cols_n - 1
    for top in range(0, rows_n, SUB):
        at, inner = slice(top, top + SUB), slice(top + SUB, top + 2 * SUB)
        ocean = field_ref[0, at, :]
        side = jnp.where(last, field_ref[2, at, :], jnp.where(first, field_ref[3, at, :], 0.0))
        turned = turn_ref[0, at, :]
        place = sublane((SUB, cols_n))
        for level in range(levels_n):
            beyond = pltpu.roll(turned, (2 * cols_n - 2 - 4 * level) % cols_n, 1)
            found = inner_ref[level, at, :] + side * beyond
            if top == 0:
                below_row = field_ref[5, 0:1, :] * below[level : level + 1, :]
                found = found + jnp.where(place == 0, below_row, 0.0)
            if top == rows_n - SUB:
                above_row = field_ref[4, rows_n - 1 : rows_n, :] * above[level : level + 1, :]
                found = found + jnp.where(place == SUB - 1, above_row, 0.0)
            half_ref[level, at, :] = found
            masked_ref[level, inner, :] = ocean * found

    copies = []

    def store(level, top, ocean, found):
        half_ref[level, top : top + SUB, :] = found
        if level == levels_n - 1 and (top + SUB) % (rows_n // sems.shape[0]) == 0:
            rows = slice(top + SUB - rows_n // sems.shape[0], top + SUB)
            copy = pltpu.make_async_copy(
                half_ref.at[:, rows, :], out_ref.at[:, rows, :], sems.at[len(copies)]
            )
            copy.start()
            copies.append(copy)

    advance(half_ref, masked_ref, field_ref, turn_ref.at[1], store)
    for copy in copies:
        copy.wait()


def kernel_call(mebibytes, body, out_shape, scratch=(), ins=None, outs=None):
    memory = {}
    if ins is not None:
        memory["in_specs"] = [pl.BlockSpec(memory_space=space) for space in ins]
    if outs is not None:
        memory["out_specs"] = pl.BlockSpec(memory_space=outs)
    return pl.pallas_call(
        body,
        out_shape=out_shape,
        scratch_shapes=list(scratch),
        compiler_params=pltpu.CompilerParams(vmem_limit_bytes=mebibytes * MIB),
        **memory,
    )


def flagged(inputs):
    return [pltpu.SMEM] + [pltpu.VMEM] * (inputs - 1)


def exchanged(value, devices):
    rows = value.reshape(devices, 1, value.size // devices)
    return lax.all_to_all(rows, BOTH, split_axis=0, concat_axis=0, tiled=True).reshape(value.shape)


def f32(*shape):
    return jax.ShapeDtypeStruct(shape, jnp.float32)


def lon_swaps(value):
    count = lax.axis_size("lon")
    assert count % 2 == 0
    first = [(i, i ^ 1) for i in range(count)]
    second = [(i, (i + 1 if i % 2 else i - 1) % count) for i in range(count)]
    return lax.ppermute(value, "lon", first), lax.ppermute(value, "lon", second)


def lat_swaps(*values):
    lons, lats = lax.axis_size("lon"), lax.axis_size("lat")
    found = []
    for parity in (0, 1):
        pairs = []
        for i in range(lons):
            for j in range(lats):
                other = j + 1 if j % 2 == parity else j - 1
                if other == lats:
                    pairs.append((i * lats + j, (lons - 1 - i) * lats + j))
                elif other >= 0:
                    pairs.append((i * lats + j, i * lats + other))
        found.append(lax.ppermute(values[parity], BOTH, pairs))
    return tuple(found)


def on_device(
    state,
    adjoint_in,
    land_mask,
    east_coef,
    north_coef,
    zonal_flow,
    vertical_coef,
    slot_cell,
    slot_weight,
    arrive_obs,
    obs_value,
    obs_invvar,
):
    levels_n, rows_n, cols_n = state.shape
    devices = lax.axis_size(BOTH)
    slots = slot_cell.shape[1]
    obs_n = obs_value.shape[1]
    assert 2 * (slots // devices) == LANES and cols_n == LANES and 4 * levels_n <= LANES
    half = (levels_n + 1) // 2
    width = rows_n // GROUP * cols_n
    bf16 = jnp.bfloat16
    raw = (land_mask, east_coef, north_coef, zonal_flow, vertical_coef)
    lon, lat = lax.axis_index("lon"), lax.axis_index("lat")
    flags = jnp.stack([1 - lon % 2, 1 - lat % 2, lat == lax.axis_size("lat") - 1]).astype(jnp.int32)

    partial_vals = kernel_call(
        60,
        gather_kernel,
        f32(devices * half, LANES),
        [
            pltpu.VMEM((1, slots), jnp.int32),
            pltpu.VMEM((1, slots), jnp.float32),
            pltpu.VMEM((levels_n, rows_n, cols_n), jnp.float32),
            pltpu.VMEM((levels_n * GROUP, 3 * width), bf16),
            pltpu.SemaphoreType.DMA((2 + levels_n,)),
        ],
        [pltpu.HBM] * 3,
    )(slot_cell, slot_weight, state)
    columns = kernel_call(8, coefficient_columns_kernel, f32(2 * SUB, rows_n))(*raw)
    partial_vals, columns = lax.optimization_barrier((partial_vals, columns))
    arrived = exchanged(partial_vals, devices)
    arrived, side_coefs = lax.optimization_barrier((arrived, lon_swaps(columns)))
    row_coefs = kernel_call(8, coefficient_rows_kernel, f32(2 * SUB, cols_n), (), flagged(8))(
        flags, *raw, *side_coefs
    )
    misfit, outgoing = kernel_call(
        32,
        observe_kernel,
        (f32(levels_n, obs_n), f32(devices * half, LANES)),
        [pltpu.VMEM((obs_n, slots), bf16)],
    )(arrived, arrive_obs, obs_value, obs_invvar)
    outgoing, row_coefs, adjoint_in, land_mask = lax.optimization_barrier(
        (outgoing, row_coefs, adjoint_in, land_mask)
    )
    returned = exchanged(outgoing, devices)
    levels = padded_levels(levels_n)
    fields, sides, edges = kernel_call(
        8,
        coefficients_kernel,
        (f32(7, rows_n, cols_n), f32(rows_n, cols_n), f32(2 * SUB, cols_n)),
        (), flagged(10),
    )(flags, *raw, *side_coefs, *lat_swaps(row_coefs, row_coefs))
    strips = kernel_call(
        8,
        seed_strips_kernel,
        (f32(rows_n, cols_n), f32(rows_n, cols_n), f32(4, levels, cols_n)),
    )(adjoint_in, land_mask)
    returned, fields, sides, edges, strips = lax.optimization_barrier(
        (returned, fields, sides, edges, strips)
    )
    tile = min(slots, SLOT_TILE)
    own_columns, own_edges = kernel_call(
        32,
        functools.partial(strips_kernel, levels_n),
        (f32(rows_n, cols_n), f32(4, levels, cols_n)),
        [pltpu.VMEM((rows_n, 3 * tile), bf16), pltpu.VMEM((4 * levels, 3 * tile), bf16)],
    )(returned, slot_cell, slot_weight, land_mask, *strips)
    columns_beside = lon_swaps(own_columns)
    extended = (levels_n, rows_n + 2 * SUB, cols_n)
    seed = kernel_call(
        40,
        scatter_kernel,
        f32(levels_n, rows_n, cols_n),
        [pltpu.VMEM((levels_n * GROUP, 3 * tile), bf16), pltpu.VMEM((width, 3 * tile), bf16)],
    )(returned, slot_cell, slot_weight, adjoint_in)
    seed, columns_beside = lax.optimization_barrier((seed, columns_beside))
    message = f32(2 * levels + SUB, cols_n)
    messages = kernel_call(8, edge_message_kernel, (message, message), (), flagged(4))(
        flags, own_edges, *columns_beside
    )
    rows_beside = lat_swaps(*messages)
    seed, messages = lax.optimization_barrier((seed, messages))
    inner = kernel_call(
        16,
        inner_step_kernel,
        f32(levels_n, rows_n, cols_n),
        [pltpu.VMEM(extended, jnp.float32)],
    )(seed, fields)
    inner, rows_beside = lax.optimization_barrier((inner, rows_beside))
    adjoint_state = kernel_call(
        16,
        steps_kernel,
        f32(levels_n, rows_n, cols_n),
        [
            pltpu.VMEM(extended, jnp.float32),
            pltpu.VMEM((levels_n, rows_n, cols_n), jnp.float32),
            pltpu.VMEM((STEPS, rows_n, cols_n), jnp.float32),
            pltpu.SemaphoreType.DMA((4,)),
        ],
        flagged(11), pltpu.HBM,
    )(flags, inner, fields, sides, edges, own_columns, own_edges, *columns_beside, *rows_beside)
    return (adjoint_state, misfit)


def solution(mesh):
    in_specs = (
        P(None, "lat", "lon"),
        P(None, "lat", "lon"),
        P("lat", "lon"),
        P("lat", "lon"),
        P("lat", "lon"),
        P("lat", "lon"),
        P("lat", "lon"),
        P(("lon", "lat"), None),
        P(("lon", "lat"), None),
        P(("lon", "lat"), None),
        P(None, ("lon", "lat")),
        P(None, ("lon", "lat")),
    )
    out_specs = (P(None, "lat", "lon"), P(None, ("lon", "lat")))
    return jax.shard_map(
        on_device, mesh=mesh, in_specs=in_specs, out_specs=out_specs, check_vma=False
    )
```

```python
import functools

import jax
import jax.numpy as jnp
from jax import lax
from jax.experimental import pallas as pl
from jax.experimental.pallas import tpu as pltpu
from jax.sharding import PartitionSpec as P

STEPS = 2
LANES = 128
GROUP = 32
SUB = 8
SLOT_TILE = 16 * LANES
MIB = 1024 * 1024
BOTH = ("lon", "lat")


def pieces(value):
    high = value.astype(jnp.bfloat16)
    rest = value - high.astype(jnp.float32)
    middle = rest.astype(jnp.bfloat16)
    low = (rest - middle.astype(jnp.float32)).astype(jnp.bfloat16)
    return high, middle, low


def log2(size):
    assert size & (size - 1) == 0
    return size.bit_length() - 1


def cell_parts(cell, rows_n, cols_n):
    cell = jnp.maximum(cell, 0)
    row = jnp.right_shift(cell, log2(cols_n))
    group = jnp.right_shift(row, log2(GROUP))
    place = jnp.bitwise_and(cell, cols_n - 1) + group * cols_n
    return place, jnp.bitwise_and(row, GROUP - 1)


def one_hot(index, size):
    rows = lax.broadcasted_iota(jnp.int32, (size, index.shape[1]), 0)
    return jnp.where(rows == index, 1.0, 0.0).astype(jnp.bfloat16)


def first_half(rows):
    return lane((rows, LANES)) < LANES // 2


def pack(values, out_ref, first_pair):
    half = values.shape[0] // 2
    for pair in range(values.shape[1] // LANES):
        block = values[:, pair * LANES : (pair + 1) * LANES]
        top, bottom = block[:half], block[half:]
        at = 2 * (first_pair + pair) * half
        out_ref[at : at + half, :] = jnp.where(
            first_half(half), top, pltpu.roll(bottom, LANES // 2, 1)
        )
        out_ref[at + half : at + 2 * half, :] = jnp.where(
            first_half(half), pltpu.roll(top, LANES // 2, 1), bottom
        )


def unpack(in_ref, half, first_pair, pairs, levels):
    found = []
    for pair in range(first_pair, first_pair + pairs):
        at = 2 * pair * half
        left, right = in_ref[at : at + half, :], in_ref[at + half : at + 2 * half, :]
        top = jnp.where(first_half(half), left, pltpu.roll(right, LANES // 2, 1))
        bottom = jnp.where(first_half(half), pltpu.roll(left, LANES // 2, 1), right)
        filler = jnp.zeros((levels - 2 * half, LANES), jnp.float32)
        found.append(jnp.concatenate([top, bottom, filler], axis=0))
    return jnp.concatenate(found, axis=1)


def gather_kernel(
    cell_in, weight_in, state_in, out_ref, cell_ref, weight_ref, state_ref, field_ref, sems
):
    levels_n, rows_n, cols_n = state_ref.shape
    groups = rows_n // GROUP
    width = groups * cols_n
    slots = cell_ref.shape[1]
    tile = min(slots, SLOT_TILE)
    chunk = max(n for n in range(1, 9) if levels_n % n == 0)
    copies = [
        pltpu.make_async_copy(cell_in, cell_ref, sems.at[0]),
        pltpu.make_async_copy(weight_in, weight_ref, sems.at[1]),
    ]
    for place, level in enumerate(range(0, levels_n, chunk)):
        at = slice(level, level + chunk)
        copies.append(pltpu.make_async_copy(state_in.at[at], state_ref.at[at], sems.at[2 + place]))
    for copy in copies:
        copy.start()
    copies[0].wait()
    for start in range(0, slots, tile):
        cell = cell_ref[:, start : start + tile]
        place, row = cell_parts(cell, rows_n, cols_n)
        hot = one_hot(place, width)
        hot = jnp.concatenate([hot, hot, hot], axis=0)
        mine = sublane((GROUP, tile)) == row
        values = []
        for index, level in enumerate(range(0, levels_n, chunk)):
            at = slice(level * GROUP, (level + chunk) * GROUP)
            if start == 0:
                copies[2 + index].wait()
                for group in range(groups):
                    block = state_ref[
                        level : level + chunk, group * GROUP : (group + 1) * GROUP, :
                    ].reshape(chunk * GROUP, cols_n)
                    for part, piece in enumerate(pieces(block)):
                        begin = part * width + group * cols_n
                        field_ref[at, begin : begin + cols_n] = piece
            found = jnp.dot(field_ref[at, :], hot, preferred_element_type=jnp.float32)
            found = found.reshape(chunk, GROUP, tile)
            values.append(jnp.sum(jnp.where(mine[None], found, 0.0), axis=1))
        if start == 0:
            copies[1].wait()
        weight = jnp.where(cell >= 0, weight_ref[:, start : start + tile], 0.0)
        if levels_n % 2:
            values.append(jnp.zeros((1, tile), jnp.float32))
        pack(jnp.concatenate(values, axis=0) * weight, out_ref, start // LANES)


def observe_kernel(arrived_ref, target_ref, value_ref, invvar_ref, misfit_ref, out_ref, hot_ref):
    levels_n, obs_n = value_ref.shape
    half = (levels_n + 1) // 2
    levels = padded_levels(levels_n)
    slots = target_ref.shape[1]
    tile = min(slots, SLOT_TILE)
    sums = None
    for start in range(0, slots, tile):
        hot = one_hot(target_ref[:, start : start + tile], obs_n)
        hot_ref[:, start : start + tile] = hot
        values = unpack(arrived_ref, half, start // LANES, tile // LANES, levels)
        found = across(jnp.concatenate(pieces(values), axis=0), hot)
        sums = found if sums is None else sums + found
    interp = sums[:levels] + sums[levels : 2 * levels] + sums[2 * levels :]
    misfit = invvar_ref[...] * (interp[:levels_n] - value_ref[...])
    misfit_ref[...] = misfit
    filler = jnp.zeros((levels - levels_n, obs_n), jnp.float32)
    back = jnp.concatenate(pieces(jnp.concatenate([misfit, filler], axis=0)), axis=0)
    for start in range(0, slots, tile):
        found = jnp.dot(
            back, hot_ref[:, start : start + tile], preferred_element_type=jnp.float32
        )
        values = found[:levels] + found[levels : 2 * levels] + found[2 * levels :]
        pack(values[: 2 * half], out_ref, start // LANES)


def padded_levels(levels_n):
    return (levels_n + 15) // 16 * 16


def returned_values(returned_ref, cell_ref, weight_ref, levels_n, start, tile):
    at = slice(start, start + tile)
    weight = jnp.where(cell_ref[:, at] >= 0, weight_ref[:, at], 0.0)
    values = unpack(
        returned_ref, (levels_n + 1) // 2, start // LANES, tile // LANES, padded_levels(levels_n)
    )
    return pieces(values * weight)


def across(left, right):
    return lax.dot_general(
        left, right, (((1,), (1,)), ((), ())), preferred_element_type=jnp.float32
    )


def seed_strips_kernel(adjoint_ref, mask_ref, columns_ref, ocean_ref, edges_ref):
    levels_n, rows_n, cols_n = adjoint_ref.shape
    level_at = jnp.right_shift(lane((SUB, cols_n)), 2)
    for top in range(0, rows_n, SUB):
        at = slice(top, top + SUB)
        found = jnp.zeros((SUB, cols_n), jnp.float32)
        for level in range(levels_n):
            block = pltpu.roll(adjoint_ref[level, at, :], (4 * level + 2) % cols_n, 1)
            found = jnp.where(level_at == level, block, found)
        columns_ref[at, :] = found
        spread = jnp.where(level_at == 0, pltpu.roll(mask_ref[at, :].astype(jnp.float32), 2, 1), 0.0)
        shift = 4
        while shift < cols_n:
            spread = spread + pltpu.roll(spread, shift, 1)
            shift *= 2
        ocean_ref[at, :] = spread
    places, levels, _ = edges_ref.shape
    for place, row in enumerate((0, 1, rows_n - 2, rows_n - 1)):
        for level in range(levels_n):
            edges_ref[place, level : level + 1, :] = adjoint_ref[level, row : row + 1, :]
        edges_ref[place, levels_n:, :] = jnp.zeros((levels - levels_n, cols_n), jnp.float32)


def strips_kernel(
    levels_n, returned_ref, cell_ref, weight_ref, mask_ref, seed_columns_ref, ocean_ref, seed_edges_ref,
    columns_ref, edges_ref,
    left_ref, right_ref,
):
    rows_n, cols_n = mask_ref.shape
    places, levels, _ = edges_ref.shape
    slots = cell_ref.shape[1]
    tile = left_ref.shape[1] // 3
    column_sum = jnp.zeros((rows_n, LANES), jnp.float32)
    edge_sum = jnp.zeros((places * levels, cols_n), jnp.float32)
    for start in range(0, slots, tile):
        cell = jnp.maximum(cell_ref[:, start : start + tile], 0)
        row, column = jnp.right_shift(cell, log2(cols_n)), jnp.bitwise_and(cell, cols_n - 1)
        values = returned_values(returned_ref, cell_ref, weight_ref, levels_n, start, tile)

        def chosen(index, wanted):
            for place, number in enumerate(wanted):
                here = jnp.where(index == number, 1.0, 0.0).astype(jnp.bfloat16)
                for part in range(3):
                    right_ref[place * levels : (place + 1) * levels, part * tile : (part + 1) * tile] = (
                        values[part] * here
                    )

        def repeated(hot):
            for part in range(3):
                left_ref[:, part * tile : (part + 1) * tile] = hot

        repeated(one_hot(row, rows_n))
        chosen(column, (cols_n - 2, cols_n - 1, 0, 1))
        column_sum += across(left_ref[...], right_ref[...])
        repeated(one_hot(column, cols_n))
        chosen(row, (0, 1, rows_n - 2, rows_n - 1))
        edge_sum += across(right_ref[...], left_ref[...])
    source, target = sublane((LANES, LANES)), lane((LANES, LANES))
    turn = jnp.bitwise_and(target, 3) * levels + jnp.right_shift(target, 2)
    turn = jnp.where(source == turn, 1.0, 0.0).astype(jnp.bfloat16)
    column_sum = sum(
        jnp.dot(piece, turn, preferred_element_type=jnp.float32) for piece in pieces(column_sum)
    )
    columns_ref[...] = (seed_columns_ref[...] + column_sum) * ocean_ref[...]
    for place, row in enumerate((0, 1, rows_n - 2, rows_n - 1)):
        ocean = mask_ref[row : row + 1, :].astype(jnp.float32)
        forcing = edge_sum[place * levels : (place + 1) * levels]
        edges_ref[place] = (seed_edges_ref[place] + forcing) * ocean


def scatter_kernel(returned_ref, cell_ref, weight_ref, adjoint_ref, out_ref, rows_ref, hot_ref):
    levels_n, rows_n, cols_n = out_ref.shape
    groups = rows_n // GROUP
    width = groups * cols_n
    tile = hot_ref.shape[1] // 3
    total = None
    for start in range(0, cell_ref.shape[1], tile):
        place, row = cell_parts(cell_ref[:, start : start + tile], rows_n, cols_n)
        values = returned_values(returned_ref, cell_ref, weight_ref, levels_n, start, tile)
        hot = one_hot(place, width)
        mine = one_hot(row, GROUP)
        for part in range(3):
            hot_ref[:, part * tile : (part + 1) * tile] = hot
            for level in range(levels_n):
                rows_ref[level * GROUP : (level + 1) * GROUP, part * tile : (part + 1) * tile] = (
                    mine * values[part][level : level + 1, :]
                )
        found = across(rows_ref[...], hot_ref[...])
        total = found if total is None else total + found
    for group in range(groups):
        at = slice(group * GROUP, (group + 1) * GROUP)
        forcing = total[:, group * cols_n : (group + 1) * cols_n].reshape(levels_n, GROUP, cols_n)
        out_ref[:, at, :] = adjoint_ref[:, at, :] + forcing


def inner_step_kernel(seed_ref, field_ref, out_ref, masked_ref):
    levels_n, rows_n, cols_n = out_ref.shape
    zero = jnp.zeros((1, cols_n), jnp.float32)
    for level in range(levels_n):
        masked_ref[level, SUB - 1 : SUB, :] = zero
        masked_ref[level, SUB + rows_n : SUB + rows_n + 1, :] = zero
    for top in range(0, rows_n, SUB):
        ocean = field_ref[0, top : top + SUB, :]
        for level in range(levels_n):
            masked_ref[level, SUB + top : 2 * SUB + top, :] = ocean * seed_ref[level, top : top + SUB, :]

    def store(level, top, ocean, found):
        out_ref[level, top : top + SUB, :] = found

    advance(seed_ref, masked_ref, field_ref, None, store)


def advance(source_ref, from_ref, field_ref, turn_ref, store, south_row=None, north_row=None):
    levels_n, rows_n, cols_n = source_ref.shape
    first = lane((SUB, cols_n)) == 0
    last = lane((SUB, cols_n)) == cols_n - 1
    for top in range(0, rows_n, SUB):
        at, inner = slice(top, top + SUB), slice(top + SUB, top + 2 * SUB)
        ocean, own, here, back, onto, south_at, mixing = (
            field_ref[place, at, :] for place in range(7)
        )
        if south_row is not None and top == 0:
            south_at = jnp.where(sublane(own.shape) == 0, south_row, south_at)
            own = jnp.where(sublane(own.shape) == 0, own + south_row, own)
        if north_row is not None and top == rows_n - SUB:
            onto = jnp.where(sublane(own.shape) == SUB - 1, north_row, onto)
        if turn_ref is None:
            here_in, back_in = jnp.where(last, 0.0, here), jnp.where(first, 0.0, back)
        else:
            turned = turn_ref[at, :]
        higher = block = from_ref[0, inner, :]
        for level in range(levels_n):
            lower = from_ref[level + 1, inner, :] if level + 1 < levels_n else block
            eastern, western = pltpu.roll(block, cols_n - 1, 1), pltpu.roll(block, 1, 1)
            if turn_ref is None:
                sides = here_in * eastern + back_in * western
            else:
                beyond = pltpu.roll(turned, (2 * cols_n - 2 - 4 * level) % cols_n, 1)
                sides = here * jnp.where(last, beyond, eastern) + back * jnp.where(first, beyond, western)
            north = from_ref[level, top + SUB + 1 : top + 2 * SUB + 1, :]
            south = from_ref[level, top + SUB - 1 : top + 2 * SUB - 1, :]
            vertical = (higher - block) + (lower - block)
            found = (
                (source_ref[level, at, :] - own * block)
                + sides
                + (onto * north + south_at * south)
                + mixing * vertical
            )
            store(level, top, ocean, found)
            higher, block = block, lower


def lane(shape):
    return lax.broadcasted_iota(jnp.int32, shape, 1)


def sublane(shape):
    return lax.broadcasted_iota(jnp.int32, shape, 0)


def shifted(block, steps, axis, edge):
    size = block.shape[axis]
    at = lax.broadcasted_iota(jnp.int32, block.shape, axis)
    moved = pltpu.roll(block, steps % size, axis)
    return jnp.where(at == (0 if steps > 0 else size - 1), edge, moved)


def reversed_lanes(block):
    at = block.shape[1] - 1 - lane(block.shape)
    return jnp.take_along_axis(block, at, axis=1, mode="promise_in_bounds")


def lon_neighbours(flag_ref, first, second):
    even = flag_ref[0] == 1
    return jnp.where(even, first, second), jnp.where(even, second, first)


def lat_neighbours(flag_ref, first, second):
    even = flag_ref[1] == 1
    return jnp.where(even, first, second), jnp.where(even, second, first)


def side_columns(flag_ref, first_ref, second_ref):
    filler = jnp.zeros((first_ref.shape[1] - first_ref.shape[0], first_ref.shape[1]), jnp.float32)
    east, west = lon_neighbours(flag_ref, first_ref[...], second_ref[...])
    return tuple(jnp.concatenate([block, filler], axis=0).T for block in (east, west))


def coefficient_columns_kernel(mask_ref, east_ref, north_ref, flow_ref, vertical_ref, out_ref):
    rows_n, cols_n = mask_ref.shape
    ocean = mask_ref[...].astype(jnp.float32)
    here = east_ref[...] + 0.5 * flow_ref[...]
    behind = east_ref[...] - 0.5 * flow_ref[...]
    north, vertical = north_ref[...], vertical_ref[...]
    last = cols_n - 1
    wanted = (
        (ocean, 0), (here, 0), (north, 0), (vertical, 0),
        (ocean, last), (here, last), (behind, last), (behind, last - 1), (north, last), (vertical, last),
    )
    found = jnp.zeros((rows_n, cols_n), jnp.float32)
    for place, (field, column) in enumerate(wanted):
        found = jnp.where(
            lane(found.shape) == place, pltpu.roll(field, (place - column) % cols_n, 1), found
        )
    out_ref[...] = found.T[: out_ref.shape[0]]


def coefficients_kernel(
    flag_ref, mask_ref, east_ref, north_ref, flow_ref, vertical_ref, lon_first_ref, lon_second_ref,
    field_ref, side_ref, row_ref,
):
    rows_n, cols_n = mask_ref.shape
    east, west = side_columns(flag_ref, lon_first_ref, lon_second_ref)
    ocean = mask_ref[...].astype(jnp.float32)
    here = east_ref[...] + 0.5 * flow_ref[...]
    behind = east_ref[...] - 0.5 * flow_ref[...]
    north, vertical = north_ref[...], vertical_ref[...]
    back = shifted(behind, 1, 1, west[:, 6:7])
    south = shifted(north, 1, 0, 0.0)
    parts = (ocean, here + back + north + south, here, back, north, south, vertical)
    for place, part in enumerate(parts):
        field_ref[place] = part

    def side(ocean, here, back, north, vertical):
        south = shifted(north, 1, 0, 0.0)
        return ocean, here + back + north + south, here, back, north, south, vertical

    def spread(columns, place):
        return jnp.broadcast_to(columns[:, place : place + 1], (columns.shape[0], cols_n))

    eastern = side(
        spread(east, 0), spread(east, 1), spread(behind, cols_n - 1), spread(east, 2), spread(east, 3)
    )
    western = side(
        spread(west, 4), spread(west, 5), spread(west, 7), spread(west, 8), spread(west, 9)
    )
    found = jnp.zeros((rows_n, cols_n), jnp.float32)
    for place, part in enumerate(eastern + western):
        found = jnp.where(lane(found.shape) == place, part, found)
    side_ref[...] = found

    top, last = slice(0, 1), slice(rows_n - 1, rows_n)
    rows = []
    for at in (top, last):
        rows += [ocean[at], here[at], back[at], north[at]]
        if at is last:
            rows.append(north[rows_n - 2 : rows_n - 1])
        rows.append(vertical[at])
    rows += [east[top], east[last], west[top], west[last]]
    for place, row in enumerate(rows):
        row_ref[place : place + 1, :] = row
    row_ref[len(rows) :, :] = jnp.zeros((row_ref.shape[0] - len(rows), cols_n), jnp.float32)


def edge_message_kernel(
    flag_ref, edges_ref, lon_first_ref, lon_second_ref, row_ref, first_ref, second_ref
):
    places, levels, cols_n = edges_ref.shape
    last = lon_first_ref.shape[0] - 1
    even = flag_ref[1] == 1
    for ref in (first_ref, second_ref):
        ref[2 * levels : 2 * levels + SUB, :] = jnp.zeros((SUB, cols_n), jnp.float32)
        ref[2 * levels + SUB :, :] = row_ref[...]
    for place, (north, south) in enumerate(((places - 1, 0), (places - 2, 1))):
        at = slice(place * levels, (place + 1) * levels)
        northern, southern = edges_ref[north], edges_ref[south]
        first_ref[at, :] = jnp.where(even, northern, southern)
        second_ref[at, :] = jnp.where(even, southern, northern)
    northern = lon_neighbours(flag_ref, lon_first_ref[last:, :], lon_second_ref[last:, :])
    southern = lon_neighbours(flag_ref, lon_first_ref[0:1, :], lon_second_ref[0:1, :])
    for place in range(2):
        at = slice(2 * levels + place, 2 * levels + place + 1)
        first_ref[at, :] = jnp.where(even, northern[place], southern[place])
        second_ref[at, :] = jnp.where(even, southern[place], northern[place])


def steps_kernel(
    flag_ref, inner_ref, field_ref, side_in_ref,
    columns_ref, edges_ref, lon_first_ref, lon_second_ref, lat_first_ref, lat_second_ref,
    out_ref,
    masked_ref, half_ref, turn_ref, side_ref, edge_ref, sems,
):
    levels_n, rows_n, cols_n = inner_ref.shape
    levels = edges_ref.shape[1]
    fold = flag_ref[2] == 1
    east, west = lon_neighbours(flag_ref, lon_first_ref[...], lon_second_ref[...])
    up, down = lat_neighbours(flag_ref, lat_first_ref[...], lat_second_ref[...])
    own = columns_ref[...]

    ends = 2 * levels
    east_up = jnp.where(fold, pltpu.roll(up[ends + 1 : ends + 2], 1, 1), up[ends : ends + 1])
    west_up = jnp.where(fold, pltpu.roll(up[ends : ends + 1], cols_n - 1, 1), up[ends + 1 : ends + 2])
    east_down, west_down = down[ends : ends + 1], down[ends + 1 : ends + 2]

    up_rows, down_rows = up[ends + SUB :], down[ends + SUB :]
    turned = reversed_lanes(up_rows)
    into = field_ref[4, rows_n - 1 : rows_n, :]
    south_row = down_rows[8:9]
    north_row = jnp.where(fold, turned[8:9], into)
    plain = (
        up_rows[0:1], up_rows[1:2] + up_rows[2:3] + up_rows[3:4] + into,
        up_rows[1:2], up_rows[2:3], into, up_rows[3:4], up_rows[4:5],
    )
    folded = (
        turned[5:6], turned[6:7] + turned[7:8] + turned[8:9] + turned[9:10],
        turned[7:8], turned[6:7], into, turned[9:10], turned[10:11],
    )
    low = (
        down_rows[5:6], down_rows[6:7] + down_rows[7:8] + down_rows[8:9] + down_rows[9:10],
        down_rows[6:7], down_rows[7:8], down_rows[8:9], down_rows[9:10], down_rows[10:11],
    )
    for place in range(len(plain)):
        edge_ref[place : place + 1, :] = jnp.where(fold, folded[place], plain[place])
        edge_ref[SUB + place : SUB + place + 1, :] = low[place]
    lanes = lane((1, cols_n))

    def moved(row, source, target):
        return jnp.where(lanes == target, pltpu.roll(row, (target - source) % cols_n, 1), 0.0)

    added = (
        moved(down_rows[12:13], 2, 1) + moved(down_rows[12:13], 2, 5)
        + moved(down_rows[14:15], 8, 8) + moved(down_rows[14:15], 8, 12)
    )
    side_ref[...] = side_in_ref[...]
    side_ref[0:1, :] = side_in_ref[0:1, :] + added
    folding = jnp.logical_and(fold, jnp.logical_or(lanes == 4, lanes == 11))
    side_ref[rows_n - 1 : rows_n, :] = jnp.where(
        folding,
        moved(up_rows[14:15], 8, 4) + moved(up_rows[12:13], 2, 11),
        side_in_ref[rows_n - 1 : rows_n, :],
    )

    level_at = jnp.right_shift(lane((rows_n, cols_n)), 2)

    def side_step(block, eastern, western, above, below, base):
        def coefficient(place):
            return side_ref[:, base + place : base + place + 1]

        higher = jnp.where(level_at > 0, pltpu.roll(block, 4, 1) - block, 0.0)
        lower = jnp.where(level_at < levels_n - 1, pltpu.roll(block, cols_n - 4, 1) - block, 0.0)
        change = (
            coefficient(2) * eastern
            + coefficient(3) * western
            + coefficient(4) * shifted(block, -1, 0, above)
            + coefficient(5) * shifted(block, 1, 0, below)
            - coefficient(1) * block
            + coefficient(6) * (higher + lower)
        )
        return block + coefficient(0) * change

    east_next = side_step(
        east, pltpu.roll(east, cols_n - 1, 1), pltpu.roll(own, 1, 1), east_up, east_down, 0
    )
    west_next = side_step(
        west, pltpu.roll(own, cols_n - 1, 1), pltpu.roll(west, 1, 1), west_up, west_down, 7
    )
    slot = jnp.bitwise_and(lane((rows_n, cols_n)), 3)
    for step, (eastern, western) in enumerate(((east, west), (east_next, west_next))):
        turn_ref[step] = jnp.where(
            slot == 1, pltpu.roll(eastern, cols_n - 1, 1), pltpu.roll(western, 1, 1)
        )

    plane = (levels, cols_n)
    corner_at = 4 * sublane(plane)

    def corner(row, place):
        found = jnp.where(lane(plane) == corner_at + place, jnp.broadcast_to(row, plane), 0.0)
        return jnp.sum(found, axis=1, keepdims=True)

    def edge(block, place):
        return block[place * levels : (place + 1) * levels]

    def edge_step(block, outer, inner, eastern, western, base):
        def coefficient(place):
            return edge_ref[base + place : base + place + 1, :]

        level = sublane(plane)
        higher = jnp.where(level > 0, pltpu.roll(block, 1, 0) - block, 0.0)
        lower = jnp.where(level < levels_n - 1, pltpu.roll(block, levels - 1, 0) - block, 0.0)
        change = (
            coefficient(2) * shifted(block, -1, 1, eastern)
            + coefficient(3) * shifted(block, 1, 1, western)
            + coefficient(4) * inner
            + coefficient(5) * outer
            - coefficient(1) * block
            + coefficient(6) * (higher + lower)
        )
        return block + coefficient(0) * change

    above = jnp.where(fold, reversed_lanes(edge(up, 0)), edge(up, 0))
    above_outer = jnp.where(fold, reversed_lanes(edge(up, 1)), edge(up, 1))
    below, below_outer = edge(down, 0), edge(down, 1)
    above_next = edge_step(
        above, above_outer, edges_ref[3], corner(east_up, 2), corner(west_up, 1), 0
    )
    below_next = edge_step(
        below, below_outer, edges_ref[0], corner(east_down, 2), corner(west_down, 1), SUB
    )
    for level in range(levels_n):
        masked_ref[level, SUB + rows_n : SUB + rows_n + 1, :] = above_next[level : level + 1, :]
        masked_ref[level, SUB - 1 : SUB, :] = below_next[level : level + 1, :]
    first = lane((SUB, cols_n)) == 0
    last = lane((SUB, cols_n)) == cols_n - 1
    for top in range(0, rows_n, SUB):
        at, inner = slice(top, top + SUB), slice(top + SUB, top + 2 * SUB)
        ocean = field_ref[0, at, :]
        side = jnp.where(last, field_ref[2, at, :], jnp.where(first, field_ref[3, at, :], 0.0))
        turned = turn_ref[0, at, :]
        place = sublane((SUB, cols_n))
        for level in range(levels_n):
            beyond = pltpu.roll(turned, (2 * cols_n - 2 - 4 * level) % cols_n, 1)
            found = inner_ref[level, at, :] + side * beyond
            if top == 0:
                below_row = south_row * (below - edges_ref[0])[level : level + 1, :]
                found = found + jnp.where(place == 0, below_row, 0.0)
            if top == rows_n - SUB:
                above_row = north_row * above[level : level + 1, :]
                found = found + jnp.where(place == SUB - 1, above_row, 0.0)
            half_ref[level, at, :] = found
            masked_ref[level, inner, :] = ocean * found

    copies = []

    def store(level, top, ocean, found):
        half_ref[level, top : top + SUB, :] = found
        if level == levels_n - 1 and (top + SUB) % (rows_n // sems.shape[0]) == 0:
            rows = slice(top + SUB - rows_n // sems.shape[0], top + SUB)
            copy = pltpu.make_async_copy(
                half_ref.at[:, rows, :], out_ref.at[:, rows, :], sems.at[len(copies)]
            )
            copy.start()
            copies.append(copy)

    advance(half_ref, masked_ref, field_ref, turn_ref.at[1], store, south_row, north_row)
    for copy in copies:
        copy.wait()


def kernel_call(mebibytes, body, out_shape, scratch=(), ins=None, outs=None):
    memory = {}
    if ins is not None:
        memory["in_specs"] = [pl.BlockSpec(memory_space=space) for space in ins]
    if outs is not None:
        memory["out_specs"] = pl.BlockSpec(memory_space=outs)
    return pl.pallas_call(
        body,
        out_shape=out_shape,
        scratch_shapes=list(scratch),
        compiler_params=pltpu.CompilerParams(vmem_limit_bytes=mebibytes * MIB),
        **memory,
    )


def flagged(inputs):
    return [pltpu.SMEM] + [pltpu.VMEM] * (inputs - 1)


def exchanged(value, devices):
    rows = value.reshape(devices, 1, value.size // devices)
    return lax.all_to_all(rows, BOTH, split_axis=0, concat_axis=0, tiled=True).reshape(value.shape)


def f32(*shape):
    return jax.ShapeDtypeStruct(shape, jnp.float32)


def lon_swaps(value):
    count = lax.axis_size("lon")
    assert count % 2 == 0
    first = [(i, i ^ 1) for i in range(count)]
    second = [(i, (i + 1 if i % 2 else i - 1) % count) for i in range(count)]
    return lax.ppermute(value, "lon", first), lax.ppermute(value, "lon", second)


def lat_swaps(*values):
    lons, lats = lax.axis_size("lon"), lax.axis_size("lat")
    found = []
    for parity in (0, 1):
        pairs = []
        for i in range(lons):
            for j in range(lats):
                other = j + 1 if j % 2 == parity else j - 1
                if other == lats:
                    pairs.append((i * lats + j, (lons - 1 - i) * lats + j))
                elif other >= 0:
                    pairs.append((i * lats + j, i * lats + other))
        found.append(lax.ppermute(values[parity], BOTH, pairs))
    return tuple(found)


def on_device(
    state,
    adjoint_in,
    land_mask,
    east_coef,
    north_coef,
    zonal_flow,
    vertical_coef,
    slot_cell,
    slot_weight,
    arrive_obs,
    obs_value,
    obs_invvar,
):
    levels_n, rows_n, cols_n = state.shape
    devices = lax.axis_size(BOTH)
    slots = slot_cell.shape[1]
    obs_n = obs_value.shape[1]
    assert 2 * (slots // devices) == LANES and cols_n == LANES and 4 * levels_n <= LANES
    half = (levels_n + 1) // 2
    width = rows_n // GROUP * cols_n
    bf16 = jnp.bfloat16
    raw = (land_mask, east_coef, north_coef, zonal_flow, vertical_coef)
    lon, lat = lax.axis_index("lon"), lax.axis_index("lat")
    flags = jnp.stack([1 - lon % 2, 1 - lat % 2, lat == lax.axis_size("lat") - 1]).astype(jnp.int32)

    partial_vals = kernel_call(
        60,
        gather_kernel,
        f32(devices * half, LANES),
        [
            pltpu.VMEM((1, slots), jnp.int32),
            pltpu.VMEM((1, slots), jnp.float32),
            pltpu.VMEM((levels_n, rows_n, cols_n), jnp.float32),
            pltpu.VMEM((levels_n * GROUP, 3 * width), bf16),
            pltpu.SemaphoreType.DMA((2 + levels_n,)),
        ],
        [pltpu.HBM] * 3,
    )(slot_cell, slot_weight, state)
    levels = padded_levels(levels_n)
    partial_vals, raw = lax.optimization_barrier((partial_vals, raw))
    arrived = exchanged(partial_vals, devices)
    columns = kernel_call(8, coefficient_columns_kernel, f32(2 * SUB, rows_n))(*raw)
    arrived, side_coefs = lax.optimization_barrier((arrived, lon_swaps(columns)))

    misfit, outgoing = kernel_call(
        32,
        observe_kernel,
        (f32(levels_n, obs_n), f32(devices * half, LANES)),
        [pltpu.VMEM((obs_n, slots), bf16)],
    )(arrived, arrive_obs, obs_value, obs_invvar)
    outgoing, raw, side_coefs, adjoint_early = lax.optimization_barrier(
        (outgoing, raw, side_coefs, adjoint_in)
    )
    returned = exchanged(outgoing, devices)
    strips = kernel_call(
        8,
        seed_strips_kernel,
        (f32(rows_n, cols_n), f32(rows_n, cols_n), f32(4, levels, cols_n)),
    )(adjoint_early, raw[0])
    fields, sides, row_coefs = kernel_call(
        8,
        coefficients_kernel,
        (f32(7, rows_n, cols_n), f32(rows_n, cols_n), f32(2 * SUB, cols_n)),
        (), flagged(8),
    )(flags, *raw, *side_coefs)
    returned, strips, fields, sides, row_coefs = lax.optimization_barrier(
        (returned, strips, fields, sides, row_coefs)
    )
    tile = min(slots, SLOT_TILE)
    own_columns, own_edges = kernel_call(
        32,
        functools.partial(strips_kernel, levels_n),
        (f32(rows_n, cols_n), f32(4, levels, cols_n)),
        [pltpu.VMEM((rows_n, 3 * tile), bf16), pltpu.VMEM((4 * levels, 3 * tile), bf16)],
    )(returned, slot_cell, slot_weight, land_mask, *strips)
    columns_beside = lon_swaps(own_columns)
    extended = (levels_n, rows_n + 2 * SUB, cols_n)
    seed = kernel_call(
        40,
        scatter_kernel,
        f32(levels_n, rows_n, cols_n),
        [pltpu.VMEM((levels_n * GROUP, 3 * tile), bf16), pltpu.VMEM((width, 3 * tile), bf16)],
    )(returned, slot_cell, slot_weight, adjoint_in)
    seed, columns_beside = lax.optimization_barrier((seed, columns_beside))
    message = f32(2 * levels + 3 * SUB, cols_n)
    messages = kernel_call(8, edge_message_kernel, (message, message), (), flagged(5))(
        flags, own_edges, *columns_beside, row_coefs
    )
    rows_beside = lat_swaps(*messages)
    seed, messages = lax.optimization_barrier((seed, messages))
    inner = kernel_call(
        16,
        inner_step_kernel,
        f32(levels_n, rows_n, cols_n),
        [pltpu.VMEM(extended, jnp.float32)],
    )(seed, fields)
    inner, rows_beside = lax.optimization_barrier((inner, rows_beside))
    adjoint_state = kernel_call(
        16,
        steps_kernel,
        f32(levels_n, rows_n, cols_n),
        [
            pltpu.VMEM(extended, jnp.float32),
            pltpu.VMEM((levels_n, rows_n, cols_n), jnp.float32),
            pltpu.VMEM((STEPS, rows_n, cols_n), jnp.float32),
            pltpu.VMEM((rows_n, cols_n), jnp.float32),
            pltpu.VMEM((2 * SUB, cols_n), jnp.float32),
            pltpu.SemaphoreType.DMA((4,)),
        ],
        flagged(10), pltpu.HBM,
    )(flags, inner, fields, sides, own_columns, own_edges, *columns_beside, *rows_beside)
    return (adjoint_state, misfit)


def solution(mesh):
    in_specs = (
        P(None, "lat", "lon"),
        P(None, "lat", "lon"),
        P("lat", "lon"),
        P("lat", "lon"),
        P("lat", "lon"),
        P("lat", "lon"),
        P("lat", "lon"),
        P(("lon", "lat"), None),
        P(("lon", "lat"), None),
        P(("lon", "lat"), None),
        P(None, ("lon", "lat")),
        P(None, ("lon", "lat")),
    )
    out_specs = (P(None, "lat", "lon"), P(None, ("lon", "lat")))
    return jax.shard_map(
        on_device, mesh=mesh, in_specs=in_specs, out_specs=out_specs, check_vma=False
    )
```

```python
import functools

import jax
import jax.numpy as jnp
from jax import lax
from jax.experimental import pallas as pl
from jax.experimental.pallas import tpu as pltpu
from jax.sharding import PartitionSpec as P

LANES = 128
GROUP = 32
SUB = 8
SLOT_TILE = 16 * LANES
MIB = 1024 * 1024
BOTH = ("lon", "lat")


def pieces(value):
    high = value.astype(jnp.bfloat16)
    rest = value - high.astype(jnp.float32)
    middle = rest.astype(jnp.bfloat16)
    low = (rest - middle.astype(jnp.float32)).astype(jnp.bfloat16)
    return high, middle, low


def log2(size):
    assert size & (size - 1) == 0
    return size.bit_length() - 1


def cell_parts(cell, rows_n, cols_n):
    cell = jnp.maximum(cell, 0)
    row = jnp.right_shift(cell, log2(cols_n))
    group = jnp.right_shift(row, log2(GROUP))
    place = jnp.bitwise_and(cell, cols_n - 1) + group * cols_n
    return place, jnp.bitwise_and(row, GROUP - 1)


def one_hot(index, size):
    rows = lax.broadcasted_iota(jnp.int32, (size, index.shape[1]), 0)
    return jnp.where(rows == index, 1.0, 0.0).astype(jnp.bfloat16)


def first_half(rows):
    return lane((rows, LANES)) < LANES // 2


def pack(values, out_ref, first_pair):
    half = values.shape[0] // 2
    for pair in range(values.shape[1] // LANES):
        block = values[:, pair * LANES : (pair + 1) * LANES]
        top, bottom = block[:half], block[half:]
        at = 2 * (first_pair + pair) * half
        out_ref[at : at + half, :] = jnp.where(
            first_half(half), top, pltpu.roll(bottom, LANES // 2, 1)
        )
        out_ref[at + half : at + 2 * half, :] = jnp.where(
            first_half(half), pltpu.roll(top, LANES // 2, 1), bottom
        )


def unpack(in_ref, half, first_pair, pairs, levels):
    found = []
    for pair in range(first_pair, first_pair + pairs):
        at = 2 * pair * half
        left, right = in_ref[at : at + half, :], in_ref[at + half : at + 2 * half, :]
        top = jnp.where(first_half(half), left, pltpu.roll(right, LANES // 2, 1))
        bottom = jnp.where(first_half(half), pltpu.roll(left, LANES // 2, 1), right)
        filler = jnp.zeros((levels - 2 * half, LANES), jnp.float32)
        found.append(jnp.concatenate([top, bottom, filler], axis=0))
    return jnp.concatenate(found, axis=1)


def gather_kernel(
    cell_in, weight_in, state_in, out_ref, cell_ref, weight_ref, state_ref, field_ref, sems
):
    levels_n, rows_n, cols_n = state_ref.shape
    groups = rows_n // GROUP
    width = groups * cols_n
    slots = cell_ref.shape[1]
    tile = min(slots, SLOT_TILE)
    chunk = max(n for n in range(1, 9) if levels_n % n == 0)
    copies = [
        pltpu.make_async_copy(cell_in, cell_ref, sems.at[0]),
        pltpu.make_async_copy(weight_in, weight_ref, sems.at[1]),
    ]
    for place, level in enumerate(range(0, levels_n, chunk)):
        at = slice(level, level + chunk)
        copies.append(pltpu.make_async_copy(state_in.at[at], state_ref.at[at], sems.at[2 + place]))
    for copy in copies:
        copy.start()
    copies[0].wait()
    for start in range(0, slots, tile):
        cell = cell_ref[:, start : start + tile]
        place, row = cell_parts(cell, rows_n, cols_n)
        hot = one_hot(place, width)
        hot = jnp.concatenate([hot, hot, hot], axis=0)
        mine = sublane((GROUP, tile)) == row
        values = []
        for index, level in enumerate(range(0, levels_n, chunk)):
            at = slice(level * GROUP, (level + chunk) * GROUP)
            if start == 0:
                copies[2 + index].wait()
                for group in range(groups):
                    block = state_ref[
                        level : level + chunk, group * GROUP : (group + 1) * GROUP, :
                    ].reshape(chunk * GROUP, cols_n)
                    for part, piece in enumerate(pieces(block)):
                        begin = part * width + group * cols_n
                        field_ref[at, begin : begin + cols_n] = piece
            found = jnp.dot(field_ref[at, :], hot, preferred_element_type=jnp.float32)
            found = found.reshape(chunk, GROUP, tile)
            values.append(jnp.sum(jnp.where(mine[None], found, 0.0), axis=1))
        if start == 0:
            copies[1].wait()
        weight = jnp.where(cell >= 0, weight_ref[:, start : start + tile], 0.0)
        if levels_n % 2:
            values.append(jnp.zeros((1, tile), jnp.float32))
        pack(jnp.concatenate(values, axis=0) * weight, out_ref, start // LANES)


def observe_kernel(arrived_ref, target_ref, value_ref, invvar_ref, misfit_ref, out_ref, hot_ref):
    levels_n, obs_n = value_ref.shape
    half = (levels_n + 1) // 2
    levels = padded_levels(levels_n)
    slots = hot_ref.shape[1]
    tile = min(slots, SLOT_TILE)
    sums = None
    for start in range(0, slots, tile):
        hot = one_hot(target_ref[:, start : start + tile], obs_n)
        hot_ref[:, start : start + tile] = hot
        values = unpack(arrived_ref, half, start // LANES, tile // LANES, levels)
        found = across(jnp.concatenate(pieces(values), axis=0), hot)
        sums = found if sums is None else sums + found
    interp = sums[:levels] + sums[levels : 2 * levels] + sums[2 * levels :]
    misfit = invvar_ref[...] * (interp[:levels_n] - value_ref[...])
    misfit_ref[...] = misfit
    filler = jnp.zeros((levels - levels_n, obs_n), jnp.float32)
    back = jnp.concatenate(pieces(jnp.concatenate([misfit, filler], axis=0)), axis=0)
    for start in range(0, slots, tile):
        found = jnp.dot(
            back, hot_ref[:, start : start + tile], preferred_element_type=jnp.float32
        )
        values = found[:levels] + found[levels : 2 * levels] + found[2 * levels :]
        pack(values[: 2 * half], out_ref, start // LANES)


def padded_levels(levels_n):
    return (levels_n + 15) // 16 * 16


def returned_values(returned_ref, cell_ref, weight_ref, levels_n, start, tile):
    at = slice(start, start + tile)
    weight = jnp.where(cell_ref[:, at] >= 0, weight_ref[:, at], 0.0)
    values = unpack(
        returned_ref, (levels_n + 1) // 2, start // LANES, tile // LANES, padded_levels(levels_n)
    )
    return pieces(values * weight)[:2]


def across(left, right):
    return lax.dot_general(
        left, right, (((1,), (1,)), ((), ())), preferred_element_type=jnp.float32
    )


def seed_strips_kernel(adjoint_ref, mask_ref, columns_ref, ocean_ref, edges_ref):
    levels_n, rows_n, cols_n = adjoint_ref.shape
    level_at = jnp.right_shift(lane((SUB, cols_n)), 2)
    for top in range(0, rows_n, SUB):
        at = slice(top, top + SUB)
        found = jnp.zeros((SUB, cols_n), jnp.float32)
        for level in range(levels_n):
            block = pltpu.roll(adjoint_ref[level, at, :], (4 * level + 2) % cols_n, 1)
            found = jnp.where(level_at == level, block, found)
        columns_ref[at, :] = found
        spread = jnp.where(level_at == 0, pltpu.roll(mask_ref[at, :].astype(jnp.float32), 2, 1), 0.0)
        shift = 4
        while shift < cols_n:
            spread = spread + pltpu.roll(spread, shift, 1)
            shift *= 2
        ocean_ref[at, :] = spread
    places, levels, _ = edges_ref.shape
    for place, row in enumerate((0, 1, rows_n - 2, rows_n - 1)):
        for level in range(levels_n):
            edges_ref[place, level : level + 1, :] = adjoint_ref[level, row : row + 1, :]
        edges_ref[place, levels_n:, :] = jnp.zeros((levels - levels_n, cols_n), jnp.float32)


def strips_kernel(
    levels_n, flag_ref, returned_ref, cell_ref, weight_ref, mask_ref, seed_columns_ref, ocean_ref, seed_edges_ref,
    columns_ref, first_ref, second_ref, edges_ref,
):
    rows_n, cols_n = mask_ref.shape
    places, levels, _ = edges_ref.shape
    slots = cell_ref.shape[1]
    tile = min(slots, SLOT_TILE)
    column_sum = jnp.zeros((rows_n, LANES), jnp.float32)
    edge_sum = jnp.zeros((places * levels, cols_n), jnp.float32)
    for start in range(0, slots, tile):
        at = slice(start, start + tile)
        cell = jnp.maximum(cell_ref[:, at], 0)
        row, column = jnp.right_shift(cell, log2(cols_n)), jnp.bitwise_and(cell, cols_n - 1)
        values = returned_values(returned_ref, cell_ref, weight_ref, levels_n, start, tile)

        def chosen(piece, index, wanted):
            found = [
                piece * jnp.where(index == number, 1.0, 0.0).astype(jnp.bfloat16)
                for number in wanted
            ]
            return jnp.concatenate(found, axis=0)

        row_hot, column_hot = one_hot(row, rows_n), one_hot(column, cols_n)
        for piece in values:
            beside = chosen(piece, column, (cols_n - 2, cols_n - 1, 0, 1))
            column_sum += across(row_hot, beside)
            beyond = chosen(piece, row, (0, 1, rows_n - 2, rows_n - 1))
            edge_sum += across(beyond, column_hot)
    source, target = sublane((LANES, LANES)), lane((LANES, LANES))
    turn = jnp.bitwise_and(target, 3) * levels + jnp.right_shift(target, 2)
    turn = jnp.where(source == turn, 1.0, 0.0).astype(jnp.bfloat16)
    column_sum = sum(
        jnp.dot(piece, turn, preferred_element_type=jnp.float32) for piece in pieces(column_sum)
    )
    columns = (seed_columns_ref[...] + column_sum) * ocean_ref[...]
    columns_ref[...] = columns
    first_ref[...], second_ref[...] = lon_messages(flag_ref, columns)
    for place, row in enumerate((0, 1, rows_n - 2, rows_n - 1)):
        ocean = mask_ref[row : row + 1, :].astype(jnp.float32)
        forcing = edge_sum[place * levels : (place + 1) * levels]
        edges_ref[place] = (seed_edges_ref[place] + forcing) * ocean


def scatter_kernel(
    returned_ref, cell_ref, weight_ref, adjoint_ref, out_ref, rows_ref
):
    levels_n, rows_n, cols_n = out_ref.shape
    groups = rows_n // GROUP
    tile = rows_ref.shape[1]
    total = jnp.zeros((levels_n * GROUP, groups * cols_n), jnp.float32)
    for start in range(0, cell_ref.shape[1], tile):
        at = slice(start, start + tile)
        values = returned_values(returned_ref, cell_ref, weight_ref, levels_n, start, tile)
        place, member = cell_parts(cell_ref[:, at], rows_n, cols_n)
        hot, member = one_hot(place, groups * cols_n), one_hot(member, GROUP)
        for part, piece in enumerate(values):
            for level in range(levels_n):
                begin = (part * levels_n + level) * GROUP
                rows_ref[begin : begin + GROUP, :] = member * piece[level : level + 1, :]
        for part in range(len(values)):
            begin = part * levels_n * GROUP
            total += across(rows_ref[begin : begin + levels_n * GROUP, :], hot)
    for group in range(groups):
        at = slice(group * GROUP, (group + 1) * GROUP)
        forcing = total[:, group * cols_n : (group + 1) * cols_n].reshape(levels_n, GROUP, cols_n)
        out_ref[:, at, :] = adjoint_ref[:, at, :] + forcing


def beside_kernel(
    flag_ref, seed_ref, field_ref, side_ref, columns_ref, first_ref, second_ref,
    half_ref, masked_ref, turn_ref,
    from_ref,
):
    levels_n, rows_n, cols_n = seed_ref.shape
    east, west = lon_columns(flag_ref, first_ref[...], second_ref[...])
    own = columns_ref[...]
    level_at = jnp.right_shift(lane((rows_n, cols_n)), 2)

    def side_step(block, eastern, western, base):
        def coefficient(place):
            return side_ref[:, base + place : base + place + 1]

        higher = jnp.where(level_at > 0, pltpu.roll(block, 4, 1) - block, 0.0)
        lower = jnp.where(level_at < levels_n - 1, pltpu.roll(block, cols_n - 4, 1) - block, 0.0)
        change = (
            coefficient(2) * eastern
            + coefficient(3) * western
            + coefficient(4) * shifted(block, -1, 0, 0.0)
            + coefficient(5) * shifted(block, 1, 0, 0.0)
            - coefficient(1) * block
            + coefficient(6) * (higher + lower)
        )
        return block + coefficient(0) * change

    east_next = side_step(east, pltpu.roll(east, cols_n - 1, 1), pltpu.roll(own, 1, 1), 0)
    west_next = side_step(west, pltpu.roll(own, cols_n - 1, 1), pltpu.roll(west, 1, 1), 7)
    turn_ref[...] = turned_columns(east_next, west_next)
    for top in range(0, rows_n, SUB):
        at = slice(top, top + SUB)
        for level in range(levels_n):
            from_ref[level, at, :] = field_ref[0, at, :] * seed_ref[level, at, :]
    none = [jnp.zeros((1, cols_n), jnp.float32)] * levels_n

    def store(level, top, found):
        at = slice(top, top + SUB)
        half_ref[level, at, :] = found
        masked_ref[level, at, :] = field_ref[0, at, :] * found

    advance(seed_ref, from_ref, field_ref, turned_columns(east, west), none, none, store)


def turned_columns(eastern, western):
    slot = jnp.bitwise_and(lane(eastern.shape), 3)
    cols_n = eastern.shape[1]
    return jnp.where(slot == 1, pltpu.roll(eastern, cols_n - 1, 1), pltpu.roll(western, 1, 1))


def advance(source_ref, from_ref, field_ref, turn, below, above, store, patch=None):
    levels_n, rows_n, cols_n = source_ref.shape
    place = sublane((SUB, cols_n))
    first = lane((SUB, cols_n)) == 0
    last = lane((SUB, cols_n)) == cols_n - 1
    for top in range(0, rows_n, SUB):
        at = slice(top, top + SUB)
        bottom, ceiling = top == 0, top == rows_n - SUB
        ocean, own, here, back, onto, south_at, mixing = (
            field_ref[part, at, :] for part in range(7)
        )
        extra = None
        if patch is not None and (bottom or ceiling):
            south_row, north_row, added_below, added_above = patch
            if bottom:
                south_at = jnp.where(place == 0, south_row, south_at)
                own = jnp.where(place == 0, own + south_row, own)
                extra = [jnp.where(place == 0, row, 0.0) for row in added_below]
            else:
                onto = jnp.where(place == SUB - 1, north_row, onto)
                extra = [jnp.where(place == SUB - 1, row, 0.0) for row in added_above]

        def block_of(level):
            block = from_ref[level, at, :]
            return block if extra is None else block + ocean * extra[level]

        higher = block = block_of(0)
        for level in range(levels_n):
            lower = block_of(level + 1) if level + 1 < levels_n else block
            eastern, western = pltpu.roll(block, cols_n - 1, 1), pltpu.roll(block, 1, 1)
            beyond = pltpu.roll(turn[at], (2 * cols_n - 2 - 4 * level) % cols_n, 1)
            sides = here * jnp.where(last, beyond, eastern) + back * jnp.where(first, beyond, western)
            if ceiling:
                north = shifted(block, -1, 0, above[level])
            else:
                north = from_ref[level, top + 1 : top + SUB + 1, :]
            if bottom:
                south = shifted(block, 1, 0, below[level])
            else:
                south = from_ref[level, top - 1 : top + SUB - 1, :]
            source = source_ref[level, at, :]
            if extra is not None:
                source = source + extra[level]
            vertical = (higher - block) + (lower - block)
            found = (
                (source - own * block)
                + sides
                + (onto * north + south_at * south)
                + mixing * vertical
            )
            store(level, top, found)
            higher, block = block, lower


def lane(shape):
    return lax.broadcasted_iota(jnp.int32, shape, 1)


def sublane(shape):
    return lax.broadcasted_iota(jnp.int32, shape, 0)


def shifted(block, steps, axis, edge):
    size = block.shape[axis]
    at = lax.broadcasted_iota(jnp.int32, block.shape, axis)
    moved = pltpu.roll(block, steps % size, axis)
    return jnp.where(at == (0 if steps > 0 else size - 1), edge, moved)


def reversed_lanes(block):
    at = block.shape[1] - 1 - lane(block.shape)
    return jnp.take_along_axis(block, at, axis=1, mode="promise_in_bounds")


def by_flag(flag_ref, place, chosen, other):
    flag = jnp.broadcast_to(flag_ref[place : place + 1, : chosen.shape[1]], chosen.shape)
    return jnp.where(flag == 1, chosen, other)


def lon_neighbours(flag_ref, first, second):
    return by_flag(flag_ref, 0, first, second), by_flag(flag_ref, 0, second, first)


def lon_columns(flag_ref, first, second):
    east, west = lon_neighbours(flag_ref, first, second)
    east = jnp.concatenate([pltpu.roll(east, 2, 1), east], axis=0)
    west = jnp.concatenate([west, pltpu.roll(west, LANES - 2, 1)], axis=0)
    return east, west


def lon_messages(flag_ref, columns):
    low, high = columns[: columns.shape[0] // 2], columns[columns.shape[0] // 2 :]
    left = jnp.bitwise_and(lane(low.shape), 3) < 2
    eastward = jnp.where(left, low, pltpu.roll(high, 2, 1))
    westward = jnp.where(left, pltpu.roll(low, LANES - 2, 1), high)
    return lon_neighbours(flag_ref, eastward, westward)


def lat_neighbours(flag_ref, first, second):
    return by_flag(flag_ref, 1, first, second), by_flag(flag_ref, 1, second, first)


def side_columns(flag_ref, first_ref, second_ref):
    filler = jnp.zeros((first_ref.shape[1] - first_ref.shape[0], first_ref.shape[1]), jnp.float32)
    east, west = lon_neighbours(flag_ref, first_ref[...], second_ref[...])
    return tuple(jnp.concatenate([block, filler], axis=0).T for block in (east, west))


def coefficient_columns_kernel(mask_ref, east_ref, north_ref, flow_ref, vertical_ref, out_ref):
    rows_n, cols_n = mask_ref.shape
    ocean = mask_ref[...].astype(jnp.float32)
    here = east_ref[...] + 0.5 * flow_ref[...]
    behind = east_ref[...] - 0.5 * flow_ref[...]
    north, vertical = north_ref[...], vertical_ref[...]
    last = cols_n - 1
    wanted = (
        (ocean, 0), (here, 0), (north, 0), (vertical, 0),
        (ocean, last), (here, last), (behind, last), (behind, last - 1), (north, last), (vertical, last),
    )
    found = jnp.zeros((rows_n, cols_n), jnp.float32)
    for place, (field, column) in enumerate(wanted):
        found = jnp.where(
            lane(found.shape) == place, pltpu.roll(field, (place - column) % cols_n, 1), found
        )
    out_ref[...] = found.T[: out_ref.shape[0]]


def coefficients_kernel(
    flag_ref, mask_ref, east_ref, north_ref, flow_ref, vertical_ref, lon_first_ref, lon_second_ref,
    field_ref, side_ref, row_ref,
):
    rows_n, cols_n = mask_ref.shape
    east, west = side_columns(flag_ref, lon_first_ref, lon_second_ref)
    ocean = mask_ref[...].astype(jnp.float32)
    here = east_ref[...] + 0.5 * flow_ref[...]
    behind = east_ref[...] - 0.5 * flow_ref[...]
    north, vertical = north_ref[...], vertical_ref[...]
    back = shifted(behind, 1, 1, west[:, 6:7])
    south = shifted(north, 1, 0, 0.0)
    parts = (ocean, here + back + north + south, here, back, north, south, vertical)
    for place, part in enumerate(parts):
        field_ref[place] = part

    def side(ocean, here, back, north, vertical):
        south = shifted(north, 1, 0, 0.0)
        return ocean, here + back + north + south, here, back, north, south, vertical

    def spread(columns, place):
        return jnp.broadcast_to(columns[:, place : place + 1], (columns.shape[0], cols_n))

    eastern = side(
        spread(east, 0), spread(east, 1), spread(behind, cols_n - 1), spread(east, 2), spread(east, 3)
    )
    western = side(
        spread(west, 4), spread(west, 5), spread(west, 7), spread(west, 8), spread(west, 9)
    )
    found = jnp.zeros((rows_n, cols_n), jnp.float32)
    for place, part in enumerate(eastern + western):
        found = jnp.where(lane(found.shape) == place, part, found)
    side_ref[...] = found

    top, last = slice(0, 1), slice(rows_n - 1, rows_n)
    rows = []
    for at in (top, last):
        rows += [ocean[at], here[at], back[at], north[at]]
        if at is last:
            rows.append(north[rows_n - 2 : rows_n - 1])
        rows.append(vertical[at])
    rows += [east[top], east[last], west[top], west[last]]
    for place, row in enumerate(rows):
        row_ref[place : place + 1, :] = row
    row_ref[len(rows) :, :] = jnp.zeros((row_ref.shape[0] - len(rows), cols_n), jnp.float32)


def edge_message_kernel(
    flag_ref, edges_ref, lon_first_ref, lon_second_ref, row_ref, first_ref, second_ref
):
    places, levels, cols_n = edges_ref.shape
    for ref in (first_ref, second_ref):
        ref[2 * levels : 2 * levels + SUB, :] = jnp.zeros((SUB, cols_n), jnp.float32)
        ref[2 * levels + SUB :, :] = row_ref[...]
    for place, (north, south) in enumerate(((places - 1, 0), (places - 2, 1))):
        at = slice(place * levels, (place + 1) * levels)
        northern, southern = edges_ref[north], edges_ref[south]
        first_ref[at, :] = by_flag(flag_ref, 1, northern, southern)
        second_ref[at, :] = by_flag(flag_ref, 1, southern, northern)
    east, west = lon_columns(flag_ref, lon_first_ref[...], lon_second_ref[...])
    northern = east[-1:], west[-1:]
    southern = east[:1], west[:1]
    for place in range(2):
        at = slice(2 * levels + place, 2 * levels + place + 1)
        first_ref[at, :] = by_flag(flag_ref, 1, northern[place], southern[place])
        second_ref[at, :] = by_flag(flag_ref, 1, southern[place], northern[place])


def steps_kernel(
    flag_ref, half_ref, masked_ref, turn_in_ref, field_ref, side_ref,
    edges_ref, lon_first_ref, lon_second_ref, lat_first_ref, lat_second_ref,
    out_ref,
    done_ref, turn_ref, edge_ref, sems,
):
    levels_n, rows_n, cols_n = half_ref.shape
    levels = edges_ref.shape[1]
    up, down = lat_neighbours(flag_ref, lat_first_ref[...], lat_second_ref[...])

    ends = 2 * levels
    east_up = by_flag(flag_ref, 2, pltpu.roll(up[ends + 1 : ends + 2], 1, 1), up[ends : ends + 1])
    west_up = by_flag(flag_ref, 2, pltpu.roll(up[ends : ends + 1], cols_n - 1, 1), up[ends + 1 : ends + 2])
    east_down, west_down = down[ends : ends + 1], down[ends + 1 : ends + 2]

    up_rows, down_rows = up[ends + SUB :], down[ends + SUB :]
    turned = reversed_lanes(up_rows)
    into = field_ref[4, rows_n - 1 : rows_n, :]
    south_row = down_rows[8:9]
    north_row = by_flag(flag_ref, 2, turned[8:9], into)
    plain = (
        up_rows[0:1], up_rows[1:2] + up_rows[2:3] + up_rows[3:4] + into,
        up_rows[1:2], up_rows[2:3], into, up_rows[3:4], up_rows[4:5],
    )
    folded = (
        turned[5:6], turned[6:7] + turned[7:8] + turned[8:9] + turned[9:10],
        turned[7:8], turned[6:7], into, turned[9:10], turned[10:11],
    )
    low = (
        down_rows[5:6], down_rows[6:7] + down_rows[7:8] + down_rows[8:9] + down_rows[9:10],
        down_rows[6:7], down_rows[7:8], down_rows[8:9], down_rows[9:10], down_rows[10:11],
    )
    for place in range(len(plain)):
        edge_ref[place : place + 1, :] = by_flag(flag_ref, 2, folded[place], plain[place])
        edge_ref[SUB + place : SUB + place + 1, :] = low[place]

    east, west = lon_columns(flag_ref, lon_first_ref[0:1, :], lon_second_ref[0:1, :])
    east, west = east[:1], west[:1]
    east_low = side_ref[0:1, 0:1] * down_rows[12:13, 2:3] * (east_down - east)
    west_low = side_ref[0:1, 7:8] * down_rows[14:15, 8:9] * (west_down - west)
    at = slice(rows_n - 1, rows_n)
    east_onto = by_flag(flag_ref, 2, up_rows[14:15, 8:9], side_ref[at, 4:5])
    west_onto = by_flag(flag_ref, 2, up_rows[12:13, 2:3], side_ref[at, 11:12])
    east_high = side_ref[at, 0:1] * east_onto * east_up
    west_high = side_ref[at, 7:8] * west_onto * west_up
    turn_ref[...] = turn_in_ref[...]
    turn_ref[0:1, :] = turn_in_ref[0:1, :] + turned_columns(east_low, west_low)
    turn_ref[at, :] = turn_in_ref[at, :] + turned_columns(east_high, west_high)

    plane = (levels, cols_n)
    corner_at = 4 * sublane(plane)

    def corner(row, place):
        found = jnp.where(lane(plane) == corner_at + place, jnp.broadcast_to(row, plane), 0.0)
        return jnp.sum(found, axis=1, keepdims=True)

    def edge(block, place):
        return block[place * levels : (place + 1) * levels]

    def edge_step(block, outer, inner, eastern, western, base):
        def coefficient(place):
            return edge_ref[base + place : base + place + 1, :]

        level = sublane(plane)
        higher = jnp.where(level > 0, pltpu.roll(block, 1, 0) - block, 0.0)
        lower = jnp.where(level < levels_n - 1, pltpu.roll(block, levels - 1, 0) - block, 0.0)
        change = (
            coefficient(2) * shifted(block, -1, 1, eastern)
            + coefficient(3) * shifted(block, 1, 1, western)
            + coefficient(4) * inner
            + coefficient(5) * outer
            - coefficient(1) * block
            + coefficient(6) * (higher + lower)
        )
        return block + coefficient(0) * change

    above = by_flag(flag_ref, 2, reversed_lanes(edge(up, 0)), edge(up, 0))
    above_outer = by_flag(flag_ref, 2, reversed_lanes(edge(up, 1)), edge(up, 1))
    below, below_outer = edge(down, 0), edge(down, 1)
    above_next = edge_step(
        above, above_outer, edges_ref[3], corner(east_up, 2), corner(west_up, 1), 0
    )
    below_next = edge_step(
        below, below_outer, edges_ref[0], corner(east_down, 2), corner(west_down, 1), SUB
    )
    def rows_of(block):
        return [block[level : level + 1] for level in range(levels_n)]

    patch = (
        south_row, north_row, rows_of(south_row * (below - edges_ref[0])), rows_of(north_row * above)
    )
    copies = []

    def store(level, top, found):
        done_ref[level, top : top + SUB, :] = found
        if level == levels_n - 1 and (top + SUB) % (rows_n // sems.shape[0]) == 0:
            rows = slice(top + SUB - rows_n // sems.shape[0], top + SUB)
            copy = pltpu.make_async_copy(
                done_ref.at[:, rows, :], out_ref.at[:, rows, :], sems.at[len(copies)]
            )
            copy.start()
            copies.append(copy)

    advance(
        half_ref, masked_ref, field_ref, turn_ref, rows_of(below_next), rows_of(above_next), store, patch
    )
    for copy in copies:
        copy.wait()


def kernel_call(mebibytes, body, out_shape, scratch=(), ins=None, outs=None):
    memory = {}
    if ins is not None:
        memory["in_specs"] = [pl.BlockSpec(memory_space=space) for space in ins]
    if outs is not None:
        memory["out_specs"] = pl.BlockSpec(memory_space=outs)
    return pl.pallas_call(
        body,
        out_shape=out_shape,
        scratch_shapes=list(scratch),
        compiler_params=pltpu.CompilerParams(vmem_limit_bytes=mebibytes * MIB),
        **memory,
    )


def exchanged(value, devices):
    rows = value.reshape(devices, 1, value.size // devices)
    return lax.all_to_all(rows, BOTH, split_axis=0, concat_axis=0, tiled=True).reshape(value.shape)


def f32(*shape):
    return jax.ShapeDtypeStruct(shape, jnp.float32)


def lon_swaps(first_value, second_value):
    count = lax.axis_size("lon")
    assert count % 2 == 0
    first = [(i, i ^ 1) for i in range(count)]
    second = [(i, (i + 1 if i % 2 else i - 1) % count) for i in range(count)]
    return lax.ppermute(first_value, "lon", first), lax.ppermute(second_value, "lon", second)


def lat_swaps(*values):
    lons, lats = lax.axis_size("lon"), lax.axis_size("lat")
    found = []
    for parity in (0, 1):
        pairs = []
        for i in range(lons):
            for j in range(lats):
                other = j + 1 if j % 2 == parity else j - 1
                if other == lats:
                    pairs.append((i * lats + j, (lons - 1 - i) * lats + j))
                elif other >= 0:
                    pairs.append((i * lats + j, i * lats + other))
        found.append(lax.ppermute(values[parity], BOTH, pairs))
    return tuple(found)


def on_device(
    state,
    adjoint_in,
    land_mask,
    east_coef,
    north_coef,
    zonal_flow,
    vertical_coef,
    slot_cell,
    slot_weight,
    arrive_obs,
    obs_value,
    obs_invvar,
):
    levels_n, rows_n, cols_n = state.shape
    devices = lax.axis_size(BOTH)
    slots = slot_cell.shape[1]
    obs_n = obs_value.shape[1]
    assert 2 * (slots // devices) == LANES and cols_n == LANES and 4 * levels_n <= LANES
    half = (levels_n + 1) // 2
    width = rows_n // GROUP * cols_n
    tile = min(slots, SLOT_TILE)
    tiles = slots // tile
    bf16 = jnp.bfloat16
    raw = (land_mask, east_coef, north_coef, zonal_flow, vertical_coef)
    lon, lat = lax.axis_index("lon"), lax.axis_index("lat")
    flags = jnp.stack([1 - lon % 2, 1 - lat % 2, lat == lax.axis_size("lat") - 1]).astype(jnp.int32)
    flags = jnp.broadcast_to(flags[:, None], (3, LANES))

    partial_vals = kernel_call(
        60,
        gather_kernel,
        f32(devices * half, LANES),
        [
            pltpu.VMEM((1, slots), jnp.int32),
            pltpu.VMEM((1, slots), jnp.float32),
            pltpu.VMEM((levels_n, rows_n, cols_n), jnp.float32),
            pltpu.VMEM((levels_n * GROUP, 3 * width), bf16),
            pltpu.SemaphoreType.DMA((2 + levels_n,)),
        ],
        [pltpu.HBM] * 3,
    )(slot_cell, slot_weight, state)
    levels = padded_levels(levels_n)
    partial_vals, raw = lax.optimization_barrier((partial_vals, raw))
    arrived = exchanged(partial_vals, devices)
    columns = kernel_call(4, coefficient_columns_kernel, f32(2 * SUB, rows_n))(*raw)
    arrived, side_coefs = lax.optimization_barrier((arrived, lon_swaps(columns, columns)))

    misfit, outgoing = kernel_call(
        8 + 4 * tiles,
        observe_kernel,
        (f32(levels_n, obs_n), f32(devices * half, LANES)),
        [pltpu.VMEM((obs_n, slots), bf16)],
    )(arrived, arrive_obs, obs_value, obs_invvar)
    outgoing, raw, side_coefs, adjoint_early = lax.optimization_barrier(
        (outgoing, raw, side_coefs, adjoint_in)
    )
    returned = exchanged(outgoing, devices)
    strips = kernel_call(
        5,
        seed_strips_kernel,
        (f32(rows_n, cols_n), f32(rows_n, cols_n), f32(4, levels, cols_n)),
    )(adjoint_early, raw[0])
    fields, sides, row_coefs = kernel_call(
        5,
        coefficients_kernel,
        (f32(7, rows_n, cols_n), f32(rows_n, cols_n), f32(2 * SUB, cols_n)),
        (),
    )(flags, *raw, *side_coefs)
    returned, strips, fields, sides, row_coefs = lax.optimization_barrier(
        (returned, strips, fields, sides, row_coefs)
    )
    own_columns, for_first, for_second, own_edges = kernel_call(
        7 + 3 * tiles,
        functools.partial(strips_kernel, levels_n),
        (
            f32(rows_n, cols_n),
            f32(rows_n // 2, cols_n),
            f32(rows_n // 2, cols_n),
            f32(4, levels, cols_n),
        ),
        (),
    )(flags, returned, slot_cell, slot_weight, land_mask, *strips)
    columns_beside = lon_swaps(for_first, for_second)
    whole = (levels_n, rows_n, cols_n)
    seed = kernel_call(
        22 + 3 * tiles,
        scatter_kernel,
        f32(levels_n, rows_n, cols_n),
        [pltpu.VMEM((2 * levels_n * GROUP, tile), bf16)],
    )(returned, slot_cell, slot_weight, adjoint_in)
    seed, columns_beside = lax.optimization_barrier((seed, columns_beside))
    message = f32(2 * levels + 3 * SUB, cols_n)
    messages = kernel_call(2, edge_message_kernel, (message, message), ())(
        flags, own_edges, *columns_beside, row_coefs
    )
    rows_beside = lat_swaps(*messages)
    seed, messages = lax.optimization_barrier((seed, messages))
    beside = kernel_call(
        8,
        beside_kernel,
        (f32(*whole), f32(*whole), f32(rows_n, cols_n)),
        [pltpu.VMEM(whole, jnp.float32)],
    )(flags, seed, fields, sides, own_columns, *columns_beside)
    beside, rows_beside = lax.optimization_barrier((beside, rows_beside))
    adjoint_state = kernel_call(
        10,
        steps_kernel,
        f32(*whole),
        [
            pltpu.VMEM(whole, jnp.float32),
            pltpu.VMEM((rows_n, cols_n), jnp.float32),
            pltpu.VMEM((2 * SUB, cols_n), jnp.float32),
            pltpu.SemaphoreType.DMA((4,)),
        ],
        [pltpu.VMEM] * 11, pltpu.HBM,
    )(flags, *beside, fields, sides, own_edges, *columns_beside, *rows_beside)
    return (adjoint_state, misfit)


def solution(mesh):
    in_specs = (
        P(None, "lat", "lon"),
        P(None, "lat", "lon"),
        P("lat", "lon"),
        P("lat", "lon"),
        P("lat", "lon"),
        P("lat", "lon"),
        P("lat", "lon"),
        P(("lon", "lat"), None),
        P(("lon", "lat"), None),
        P(("lon", "lat"), None),
        P(None, ("lon", "lat")),
        P(None, ("lon", "lat")),
    )
    out_specs = (P(None, "lat", "lon"), P(None, ("lon", "lat")))
    return jax.shard_map(
        on_device, mesh=mesh, in_specs=in_specs, out_specs=out_specs, check_vma=False
    )
```

```python
import functools

import jax
import jax.numpy as jnp
from jax import lax
from jax.experimental import pallas as pl
from jax.experimental.pallas import tpu as pltpu
from jax.sharding import PartitionSpec as P

LANES = 128
GROUP = 32
SUB = 8
SLOT_TILE = 16 * LANES
MIB = 1024 * 1024
BOTH = ("lon", "lat")


def pieces(value):
    high = value.astype(jnp.bfloat16)
    rest = value - high.astype(jnp.float32)
    middle = rest.astype(jnp.bfloat16)
    low = (rest - middle.astype(jnp.float32)).astype(jnp.bfloat16)
    return high, middle, low


def log2(size):
    assert size & (size - 1) == 0
    return size.bit_length() - 1


def cell_parts(cell, rows_n, cols_n):
    cell = jnp.maximum(cell, 0)
    row = jnp.right_shift(cell, log2(cols_n))
    group = jnp.right_shift(row, log2(GROUP))
    place = jnp.bitwise_and(cell, cols_n - 1) + group * cols_n
    return place, jnp.bitwise_and(row, GROUP - 1)


def one_hot(index, size):
    rows = lax.broadcasted_iota(jnp.int32, (size, index.shape[1]), 0)
    return jnp.where(rows == index, 1.0, 0.0).astype(jnp.bfloat16)


def first_half(rows):
    return lane((rows, LANES)) < LANES // 2


def pack(values, out_ref, first_pair):
    half = values.shape[0] // 2
    for pair in range(values.shape[1] // LANES):
        block = values[:, pair * LANES : (pair + 1) * LANES]
        top, bottom = block[:half], block[half:]
        at = 2 * (first_pair + pair) * half
        out_ref[at : at + half, :] = jnp.where(
            first_half(half), top, pltpu.roll(bottom, LANES // 2, 1)
        )
        out_ref[at + half : at + 2 * half, :] = jnp.where(
            first_half(half), pltpu.roll(top, LANES // 2, 1), bottom
        )


def unpack(in_ref, half, first_pair, pairs, levels):
    found = []
    for pair in range(first_pair, first_pair + pairs):
        at = 2 * pair * half
        left, right = in_ref[at : at + half, :], in_ref[at + half : at + 2 * half, :]
        top = jnp.where(first_half(half), left, pltpu.roll(right, LANES // 2, 1))
        bottom = jnp.where(first_half(half), pltpu.roll(left, LANES // 2, 1), right)
        filler = jnp.zeros((levels - 2 * half, LANES), jnp.float32)
        found.append(jnp.concatenate([top, bottom, filler], axis=0))
    return jnp.concatenate(found, axis=1)


def gather_kernel(
    cell_in, weight_in, state_in, out_ref, cell_ref, weight_ref, state_ref, field_ref, sems
):
    levels_n, rows_n, cols_n = state_ref.shape
    groups = rows_n // GROUP
    width = groups * cols_n
    slots = cell_ref.shape[1]
    tile = min(slots, SLOT_TILE)
    chunk = levels_n
    copies = [
        pltpu.make_async_copy(cell_in, cell_ref, sems.at[0]),
        pltpu.make_async_copy(weight_in, weight_ref, sems.at[1]),
    ]
    for place, level in enumerate(range(0, levels_n, chunk)):
        at = slice(level, level + chunk)
        copies.append(pltpu.make_async_copy(state_in.at[at], state_ref.at[at], sems.at[2 + place]))
    for copy in copies:
        copy.start()
    copies[0].wait()
    for start in range(0, slots, tile):
        cell = cell_ref[:, start : start + tile]
        place, row = cell_parts(cell, rows_n, cols_n)
        hot = one_hot(place, width)
        hot = jnp.concatenate([hot, hot, hot], axis=0)
        mine = sublane((GROUP, tile)) == row
        values = []
        for index, level in enumerate(range(0, levels_n, chunk)):
            at = slice(level * GROUP, (level + chunk) * GROUP)
            if start == 0:
                copies[2 + index].wait()
                for group in range(groups):
                    block = state_ref[
                        level : level + chunk, group * GROUP : (group + 1) * GROUP, :
                    ].reshape(chunk * GROUP, cols_n)
                    for part, piece in enumerate(pieces(block)):
                        begin = part * width + group * cols_n
                        field_ref[at, begin : begin + cols_n] = piece
            found = jnp.dot(field_ref[at, :], hot, preferred_element_type=jnp.float32)
            found = found.reshape(chunk, GROUP, tile)
            values.append(jnp.sum(jnp.where(mine[None], found, 0.0), axis=1))
        if start == 0:
            copies[1].wait()
        weight = jnp.where(cell >= 0, weight_ref[:, start : start + tile], 0.0)
        if levels_n % 2:
            values.append(jnp.zeros((1, tile), jnp.float32))
        pack(jnp.concatenate(values, axis=0) * weight, out_ref, start // LANES)


def observe_kernel(arrived_ref, target_ref, value_ref, invvar_ref, misfit_ref, out_ref, hot_ref):
    levels_n, obs_n = value_ref.shape
    half = (levels_n + 1) // 2
    levels = padded_levels(levels_n)
    slots = hot_ref.shape[1]
    tile = min(slots, SLOT_TILE)
    sums = None
    for start in range(0, slots, tile):
        hot = one_hot(target_ref[:, start : start + tile], obs_n)
        hot_ref[:, start : start + tile] = hot
        values = unpack(arrived_ref, half, start // LANES, tile // LANES, levels)
        found = across(jnp.concatenate(pieces(values), axis=0), hot)
        sums = found if sums is None else sums + found
    interp = sums[:levels] + sums[levels : 2 * levels] + sums[2 * levels :]
    misfit = invvar_ref[...] * (interp[:levels_n] - value_ref[...])
    misfit_ref[...] = misfit
    filler = jnp.zeros((levels - levels_n, obs_n), jnp.float32)
    back = jnp.concatenate(pieces(jnp.concatenate([misfit, filler], axis=0)), axis=0)
    for start in range(0, slots, tile):
        found = jnp.dot(
            back, hot_ref[:, start : start + tile], preferred_element_type=jnp.float32
        )
        values = found[:levels] + found[levels : 2 * levels] + found[2 * levels :]
        pack(values[: 2 * half], out_ref, start // LANES)


def padded_levels(levels_n):
    return (levels_n + 15) // 16 * 16


def returned_values(returned_ref, cell_ref, weight_ref, levels_n, start, tile):
    at = slice(start, start + tile)
    weight = jnp.where(cell_ref[:, at] >= 0, weight_ref[:, at], 0.0)
    values = unpack(
        returned_ref, (levels_n + 1) // 2, start // LANES, tile // LANES, padded_levels(levels_n)
    )
    return pieces(values * weight)[:2]


def across(left, right):
    return lax.dot_general(
        left, right, (((1,), (1,)), ((), ())), preferred_element_type=jnp.float32
    )


def seed_strips_kernel(adjoint_ref, mask_ref, columns_ref, ocean_ref, edges_ref):
    levels_n, rows_n, cols_n = adjoint_ref.shape
    level_at = jnp.right_shift(lane((SUB, cols_n)), 2)
    for top in range(0, rows_n, SUB):
        at = slice(top, top + SUB)
        found = jnp.zeros((SUB, cols_n), jnp.float32)
        for level in range(levels_n):
            block = pltpu.roll(adjoint_ref[level, at, :], (4 * level + 2) % cols_n, 1)
            found = jnp.where(level_at == level, block, found)
        columns_ref[at, :] = found
        spread = jnp.where(level_at == 0, pltpu.roll(mask_ref[at, :].astype(jnp.float32), 2, 1), 0.0)
        shift = 4
        while shift < cols_n:
            spread = spread + pltpu.roll(spread, shift, 1)
            shift *= 2
        ocean_ref[at, :] = spread
    places, levels, _ = edges_ref.shape
    for place, row in enumerate((0, 1, rows_n - 2, rows_n - 1)):
        for level in range(levels_n):
            edges_ref[place, level : level + 1, :] = adjoint_ref[level, row : row + 1, :]
        edges_ref[place, levels_n:, :] = jnp.zeros((levels - levels_n, cols_n), jnp.float32)


def strips_kernel(
    levels_n, flag_ref, returned_ref, cell_ref, weight_ref, mask_ref, seed_columns_ref, ocean_ref, seed_edges_ref,
    columns_ref, second_ref, first_ref, edges_ref,
):
    rows_n, cols_n = mask_ref.shape
    places, levels, _ = edges_ref.shape
    slots = cell_ref.shape[1]
    tile = min(slots, SLOT_TILE)
    column_sum = jnp.zeros((rows_n, LANES), jnp.float32)
    edge_sum = jnp.zeros((places * levels, cols_n), jnp.float32)
    for start in range(0, slots, tile):
        at = slice(start, start + tile)
        cell = jnp.maximum(cell_ref[:, at], 0)
        row, column = jnp.right_shift(cell, log2(cols_n)), jnp.bitwise_and(cell, cols_n - 1)
        values = returned_values(returned_ref, cell_ref, weight_ref, levels_n, start, tile)

        def chosen(piece, index, wanted):
            found = [
                piece * jnp.where(index == number, 1.0, 0.0).astype(jnp.bfloat16)
                for number in wanted
            ]
            return jnp.concatenate(found, axis=0)

        row_hot, column_hot = one_hot(row, rows_n), one_hot(column, cols_n)
        for piece in values:
            beside = chosen(piece, column, (cols_n - 2, cols_n - 1, 0, 1))
            column_sum += across(row_hot, beside)
            beyond = chosen(piece, row, (0, 1, rows_n - 2, rows_n - 1))
            edge_sum += across(beyond, column_hot)
    source, target = sublane((LANES, LANES)), lane((LANES, LANES))
    turn = jnp.bitwise_and(target, 3) * levels + jnp.right_shift(target, 2)
    turn = jnp.where(source == turn, 1.0, 0.0).astype(jnp.bfloat16)
    column_sum = sum(
        jnp.dot(piece, turn, preferred_element_type=jnp.float32) for piece in pieces(column_sum)
    )
    columns = (seed_columns_ref[...] + column_sum) * ocean_ref[...]
    columns_ref[...] = columns
    first_ref[...], second_ref[...] = lon_messages(flag_ref, columns)
    for place, row in enumerate((0, 1, rows_n - 2, rows_n - 1)):
        ocean = mask_ref[row : row + 1, :].astype(jnp.float32)
        forcing = edge_sum[place * levels : (place + 1) * levels]
        edges_ref[place] = (seed_edges_ref[place] + forcing) * ocean


def scatter_kernel(
    returned_ref, cell_ref, weight_ref, adjoint_ref, out_ref, rows_ref
):
    levels_n, rows_n, cols_n = out_ref.shape
    groups = rows_n // GROUP
    tile = rows_ref.shape[1]
    total = jnp.zeros((levels_n * GROUP, groups * cols_n), jnp.float32)
    for start in range(0, cell_ref.shape[1], tile):
        at = slice(start, start + tile)
        values = returned_values(returned_ref, cell_ref, weight_ref, levels_n, start, tile)
        place, member = cell_parts(cell_ref[:, at], rows_n, cols_n)
        hot, member = one_hot(place, groups * cols_n), one_hot(member, GROUP)
        for part, piece in enumerate(values):
            for level in range(levels_n):
                begin = (part * levels_n + level) * GROUP
                rows_ref[begin : begin + GROUP, :] = member * piece[level : level + 1, :]
        for part in range(len(values)):
            begin = part * levels_n * GROUP
            total += across(rows_ref[begin : begin + levels_n * GROUP, :], hot)
    for group in range(groups):
        at = slice(group * GROUP, (group + 1) * GROUP)
        forcing = total[:, group * cols_n : (group + 1) * cols_n].reshape(levels_n, GROUP, cols_n)
        out_ref[:, at, :] = adjoint_ref[:, at, :] + forcing


def beside_kernel(
    flag_ref, seed_ref, field_ref, side_ref, columns_ref, first_ref, second_ref,
    half_ref, masked_ref, turn_ref,
    from_ref,
):
    levels_n, rows_n, cols_n = seed_ref.shape
    east, west = lon_columns(flag_ref, first_ref[...], second_ref[...])
    own = columns_ref[...]
    level_at = jnp.right_shift(lane((rows_n, cols_n)), 2)

    def side_step(block, eastern, western, base):
        def coefficient(place):
            return side_ref[:, base + place : base + place + 1]

        higher = jnp.where(level_at > 0, pltpu.roll(block, 4, 1) - block, 0.0)
        lower = jnp.where(level_at < levels_n - 1, pltpu.roll(block, cols_n - 4, 1) - block, 0.0)
        change = (
            coefficient(2) * eastern
            + coefficient(3) * western
            + coefficient(4) * shifted(block, -1, 0, 0.0)
            + coefficient(5) * shifted(block, 1, 0, 0.0)
            - coefficient(1) * block
            + coefficient(6) * (higher + lower)
        )
        return block + coefficient(0) * change

    east_next = side_step(east, pltpu.roll(east, cols_n - 1, 1), pltpu.roll(own, 1, 1), 0)
    west_next = side_step(west, pltpu.roll(own, cols_n - 1, 1), pltpu.roll(west, 1, 1), 7)
    turn_ref[...] = turned_columns(east_next, west_next)
    for top in range(0, rows_n, SUB):
        at = slice(top, top + SUB)
        for level in range(levels_n):
            from_ref[level, at, :] = field_ref[0, at, :] * seed_ref[level, at, :]
    none = [jnp.zeros((1, cols_n), jnp.float32)] * levels_n

    def store(level, top, found):
        at = slice(top, top + SUB)
        half_ref[level, at, :] = found
        masked_ref[level, at, :] = field_ref[0, at, :] * found

    advance(seed_ref, from_ref, field_ref, turned_columns(east, west), none, none, store)


def turned_columns(eastern, western):
    slot = jnp.bitwise_and(lane(eastern.shape), 3)
    cols_n = eastern.shape[1]
    return jnp.where(slot == 1, pltpu.roll(eastern, cols_n - 1, 1), pltpu.roll(western, 1, 1))


def advance(source_ref, from_ref, field_ref, turn, below, above, store, patch=None):
    levels_n, rows_n, cols_n = source_ref.shape
    place = sublane((SUB, cols_n))
    first = lane((SUB, cols_n)) == 0
    last = lane((SUB, cols_n)) == cols_n - 1
    for top in range(0, rows_n, SUB):
        at = slice(top, top + SUB)
        bottom, ceiling = top == 0, top == rows_n - SUB
        ocean, own, here, back, onto, south_at, mixing = (
            field_ref[part, at, :] for part in range(7)
        )
        extra = None
        if patch is not None and (bottom or ceiling):
            south_row, north_row, added_below, added_above = patch
            if bottom:
                south_at = jnp.where(place == 0, south_row, south_at)
                own = jnp.where(place == 0, own + south_row, own)
                extra = [jnp.where(place == 0, row, 0.0) for row in added_below]
            else:
                onto = jnp.where(place == SUB - 1, north_row, onto)
                extra = [jnp.where(place == SUB - 1, row, 0.0) for row in added_above]

        def block_of(level):
            block = from_ref[level, at, :]
            return block if extra is None else block + ocean * extra[level]

        higher = block = block_of(0)
        for level in range(levels_n):
            lower = block_of(level + 1) if level + 1 < levels_n else block
            eastern, western = pltpu.roll(block, cols_n - 1, 1), pltpu.roll(block, 1, 1)
            beyond = pltpu.roll(turn[at], (2 * cols_n - 2 - 4 * level) % cols_n, 1)
            sides = here * jnp.where(last, beyond, eastern) + back * jnp.where(first, beyond, western)
            if ceiling:
                north = shifted(block, -1, 0, above[level])
            else:
                north = from_ref[level, top + 1 : top + SUB + 1, :]
            if bottom:
                south = shifted(block, 1, 0, below[level])
            else:
                south = from_ref[level, top - 1 : top + SUB - 1, :]
            source = source_ref[level, at, :]
            if extra is not None:
                source = source + extra[level]
            vertical = (higher - block) + (lower - block)
            found = (
                (source - own * block)
                + sides
                + (onto * north + south_at * south)
                + mixing * vertical
            )
            store(level, top, found)
            higher, block = block, lower


def lane(shape):
    return lax.broadcasted_iota(jnp.int32, shape, 1)


def sublane(shape):
    return lax.broadcasted_iota(jnp.int32, shape, 0)


def shifted(block, steps, axis, edge):
    size = block.shape[axis]
    at = lax.broadcasted_iota(jnp.int32, block.shape, axis)
    moved = pltpu.roll(block, steps % size, axis)
    return jnp.where(at == (0 if steps > 0 else size - 1), edge, moved)


def reversed_lanes(block):
    at = block.shape[1] - 1 - lane(block.shape)
    return jnp.take_along_axis(block, at, axis=1, mode="promise_in_bounds")


def by_flag(flag_ref, place, chosen, other):
    flag = jnp.broadcast_to(flag_ref[place : place + 1, : chosen.shape[1]], chosen.shape)
    return jnp.where(flag == 1, chosen, other)


def lon_neighbours(flag_ref, first, second):
    return by_flag(flag_ref, 0, first, second), by_flag(flag_ref, 0, second, first)


def lon_columns(flag_ref, first, second):
    east, west = lon_neighbours(flag_ref, first, second)
    east = jnp.concatenate([pltpu.roll(east, 2, 1), east], axis=0)
    west = jnp.concatenate([west, pltpu.roll(west, LANES - 2, 1)], axis=0)
    return east, west


def lon_messages(flag_ref, columns):
    low, high = columns[: columns.shape[0] // 2], columns[columns.shape[0] // 2 :]
    left = jnp.bitwise_and(lane(low.shape), 3) < 2
    eastward = jnp.where(left, low, pltpu.roll(high, 2, 1))
    westward = jnp.where(left, pltpu.roll(low, LANES - 2, 1), high)
    return lon_neighbours(flag_ref, eastward, westward)


def lat_neighbours(flag_ref, first, second):
    return by_flag(flag_ref, 1, first, second), by_flag(flag_ref, 1, second, first)


def side_columns(flag_ref, first_ref, second_ref):
    filler = jnp.zeros((first_ref.shape[1] - first_ref.shape[0], first_ref.shape[1]), jnp.float32)
    east, west = lon_neighbours(flag_ref, first_ref[...], second_ref[...])
    return tuple(jnp.concatenate([block, filler], axis=0).T for block in (east, west))


def coefficient_columns_kernel(mask_ref, east_ref, north_ref, flow_ref, vertical_ref, out_ref):
    rows_n, cols_n = mask_ref.shape
    ocean = mask_ref[...].astype(jnp.float32)
    here = east_ref[...] + 0.5 * flow_ref[...]
    behind = east_ref[...] - 0.5 * flow_ref[...]
    north, vertical = north_ref[...], vertical_ref[...]
    last = cols_n - 1
    wanted = (
        (ocean, 0), (here, 0), (north, 0), (vertical, 0),
        (ocean, last), (here, last), (behind, last), (behind, last - 1), (north, last), (vertical, last),
    )
    found = jnp.zeros((rows_n, cols_n), jnp.float32)
    for place, (field, column) in enumerate(wanted):
        found = jnp.where(
            lane(found.shape) == place, pltpu.roll(field, (place - column) % cols_n, 1), found
        )
    out_ref[...] = found.T[: out_ref.shape[0]]


def coefficients_kernel(
    flag_ref, mask_ref, east_ref, north_ref, flow_ref, vertical_ref, lon_first_ref, lon_second_ref,
    field_ref, side_ref, row_ref,
):
    rows_n, cols_n = mask_ref.shape
    east, west = side_columns(flag_ref, lon_first_ref, lon_second_ref)
    ocean = mask_ref[...].astype(jnp.float32)
    here = east_ref[...] + 0.5 * flow_ref[...]
    behind = east_ref[...] - 0.5 * flow_ref[...]
    north, vertical = north_ref[...], vertical_ref[...]
    back = shifted(behind, 1, 1, west[:, 6:7])
    south = shifted(north, 1, 0, 0.0)
    parts = (ocean, here + back + north + south, here, back, north, south, vertical)
    for place, part in enumerate(parts):
        field_ref[place] = part

    def side(ocean, here, back, north, vertical):
        south = shifted(north, 1, 0, 0.0)
        return ocean, here + back + north + south, here, back, north, south, vertical

    def spread(columns, place):
        return jnp.broadcast_to(columns[:, place : place + 1], (columns.shape[0], cols_n))

    eastern = side(
        spread(east, 0), spread(east, 1), spread(behind, cols_n - 1), spread(east, 2), spread(east, 3)
    )
    western = side(
        spread(west, 4), spread(west, 5), spread(west, 7), spread(west, 8), spread(west, 9)
    )
    found = jnp.zeros((rows_n, cols_n), jnp.float32)
    for place, part in enumerate(eastern + western):
        found = jnp.where(lane(found.shape) == place, part, found)
    side_ref[...] = found

    top, last = slice(0, 1), slice(rows_n - 1, rows_n)
    rows = []
    for at in (top, last):
        rows += [ocean[at], here[at], back[at], north[at]]
        if at is last:
            rows.append(north[rows_n - 2 : rows_n - 1])
        rows.append(vertical[at])
    rows += [east[top], east[last], west[top], west[last]]
    for place, row in enumerate(rows):
        row_ref[place : place + 1, :] = row
    row_ref[len(rows) :, :] = jnp.zeros((row_ref.shape[0] - len(rows), cols_n), jnp.float32)


def edge_message_kernel(
    flag_ref, edges_ref, lon_first_ref, lon_second_ref, row_ref, second_ref, first_ref
):
    places, levels, cols_n = edges_ref.shape
    for ref in (first_ref, second_ref):
        ref[2 * levels : 2 * levels + SUB, :] = jnp.zeros((SUB, cols_n), jnp.float32)
        ref[2 * levels + SUB :, :] = row_ref[...]
    for place, (north, south) in enumerate(((places - 1, 0), (places - 2, 1))):
        at = slice(place * levels, (place + 1) * levels)
        northern, southern = edges_ref[north], edges_ref[south]
        first_ref[at, :] = by_flag(flag_ref, 1, northern, southern)
        second_ref[at, :] = by_flag(flag_ref, 1, southern, northern)
    east, west = lon_columns(flag_ref, lon_first_ref[...], lon_second_ref[...])
    northern = east[-1:], west[-1:]
    southern = east[:1], west[:1]
    for place in range(2):
        at = slice(2 * levels + place, 2 * levels + place + 1)
        first_ref[at, :] = by_flag(flag_ref, 1, northern[place], southern[place])
        second_ref[at, :] = by_flag(flag_ref, 1, southern[place], northern[place])


def steps_kernel(
    flag_ref, half_ref, masked_ref, turn_in_ref, field_ref, side_ref,
    edges_ref, lon_first_ref, lon_second_ref, lat_first_ref, lat_second_ref,
    out_ref,
    done_ref, turn_ref, edge_ref, sems,
):
    levels_n, rows_n, cols_n = half_ref.shape
    levels = edges_ref.shape[1]
    up, down = lat_neighbours(flag_ref, lat_first_ref[...], lat_second_ref[...])

    ends = 2 * levels
    east_up = by_flag(flag_ref, 2, pltpu.roll(up[ends + 1 : ends + 2], 1, 1), up[ends : ends + 1])
    west_up = by_flag(flag_ref, 2, pltpu.roll(up[ends : ends + 1], cols_n - 1, 1), up[ends + 1 : ends + 2])
    east_down, west_down = down[ends : ends + 1], down[ends + 1 : ends + 2]

    up_rows, down_rows = up[ends + SUB :], down[ends + SUB :]
    turned = reversed_lanes(up_rows)
    into = field_ref[4, rows_n - 1 : rows_n, :]
    south_row = down_rows[8:9]
    north_row = by_flag(flag_ref, 2, turned[8:9], into)
    plain = (
        up_rows[0:1], up_rows[1:2] + up_rows[2:3] + up_rows[3:4] + into,
        up_rows[1:2], up_rows[2:3], into, up_rows[3:4], up_rows[4:5],
    )
    folded = (
        turned[5:6], turned[6:7] + turned[7:8] + turned[8:9] + turned[9:10],
        turned[7:8], turned[6:7], into, turned[9:10], turned[10:11],
    )
    low = (
        down_rows[5:6], down_rows[6:7] + down_rows[7:8] + down_rows[8:9] + down_rows[9:10],
        down_rows[6:7], down_rows[7:8], down_rows[8:9], down_rows[9:10], down_rows[10:11],
    )
    for place in range(len(plain)):
        edge_ref[place : place + 1, :] = by_flag(flag_ref, 2, folded[place], plain[place])
        edge_ref[SUB + place : SUB + place + 1, :] = low[place]

    east, west = lon_columns(flag_ref, lon_first_ref[0:1, :], lon_second_ref[0:1, :])
    east, west = east[:1], west[:1]
    east_low = side_ref[0:1, 0:1] * down_rows[12:13, 2:3] * (east_down - east)
    west_low = side_ref[0:1, 7:8] * down_rows[14:15, 8:9] * (west_down - west)
    at = slice(rows_n - 1, rows_n)
    east_onto = by_flag(flag_ref, 2, up_rows[14:15, 8:9], side_ref[at, 4:5])
    west_onto = by_flag(flag_ref, 2, up_rows[12:13, 2:3], side_ref[at, 11:12])
    east_high = side_ref[at, 0:1] * east_onto * east_up
    west_high = side_ref[at, 7:8] * west_onto * west_up
    turn_ref[...] = turn_in_ref[...]
    turn_ref[0:1, :] = turn_in_ref[0:1, :] + turned_columns(east_low, west_low)
    turn_ref[at, :] = turn_in_ref[at, :] + turned_columns(east_high, west_high)

    plane = (levels, cols_n)
    corner_at = 4 * sublane(plane)

    def corner(row, place):
        found = jnp.where(lane(plane) == corner_at + place, jnp.broadcast_to(row, plane), 0.0)
        return jnp.sum(found, axis=1, keepdims=True)

    def edge(block, place):
        return block[place * levels : (place + 1) * levels]

    def edge_step(block, outer, inner, eastern, western, base):
        def coefficient(place):
            return edge_ref[base + place : base + place + 1, :]

        level = sublane(plane)
        higher = jnp.where(level > 0, pltpu.roll(block, 1, 0) - block, 0.0)
        lower = jnp.where(level < levels_n - 1, pltpu.roll(block, levels - 1, 0) - block, 0.0)
        change = (
            coefficient(2) * shifted(block, -1, 1, eastern)
            + coefficient(3) * shifted(block, 1, 1, western)
            + coefficient(4) * inner
            + coefficient(5) * outer
            - coefficient(1) * block
            + coefficient(6) * (higher + lower)
        )
        return block + coefficient(0) * change

    above = by_flag(flag_ref, 2, reversed_lanes(edge(up, 0)), edge(up, 0))
    above_outer = by_flag(flag_ref, 2, reversed_lanes(edge(up, 1)), edge(up, 1))
    below, below_outer = edge(down, 0), edge(down, 1)
    above_next = edge_step(
        above, above_outer, edges_ref[3], corner(east_up, 2), corner(west_up, 1), 0
    )
    below_next = edge_step(
        below, below_outer, edges_ref[0], corner(east_down, 2), corner(west_down, 1), SUB
    )
    def rows_of(block):
        return [block[level : level + 1] for level in range(levels_n)]

    patch = (
        south_row, north_row, rows_of(south_row * (below - edges_ref[0])), rows_of(north_row * above)
    )
    copies = []

    def store(level, top, found):
        done_ref[level, top : top + SUB, :] = found
        if level == levels_n - 1 and (top + SUB) % (rows_n // sems.shape[0]) == 0:
            rows = slice(top + SUB - rows_n // sems.shape[0], top + SUB)
            copy = pltpu.make_async_copy(
                done_ref.at[:, rows, :], out_ref.at[:, rows, :], sems.at[len(copies)]
            )
            copy.start()
            copies.append(copy)

    advance(
        half_ref, masked_ref, field_ref, turn_ref, rows_of(below_next), rows_of(above_next), store, patch
    )
    for copy in copies:
        copy.wait()


def kernel_call(mebibytes, body, out_shape, scratch=(), ins=None, outs=None):
    memory = {}
    if ins is not None:
        memory["in_specs"] = [pl.BlockSpec(memory_space=space) for space in ins]
    if outs is not None:
        memory["out_specs"] = pl.BlockSpec(memory_space=outs)
    return pl.pallas_call(
        body,
        out_shape=out_shape,
        scratch_shapes=list(scratch),
        compiler_params=pltpu.CompilerParams(vmem_limit_bytes=mebibytes * MIB),
        **memory,
    )


def exchanged(value, devices):
    rows = value.reshape(devices, 1, value.size // devices)
    return lax.all_to_all(rows, BOTH, split_axis=0, concat_axis=0, tiled=True).reshape(value.shape)


def f32(*shape):
    return jax.ShapeDtypeStruct(shape, jnp.float32)


def lon_swaps(first_value, second_value):
    count = lax.axis_size("lon")
    assert count % 2 == 0
    first = [(i, i ^ 1) for i in range(count)]
    second = [(i, (i + 1 if i % 2 else i - 1) % count) for i in range(count)]
    return lax.ppermute(first_value, "lon", first), lax.ppermute(second_value, "lon", second)


def lat_swaps(*values):
    lons, lats = lax.axis_size("lon"), lax.axis_size("lat")
    found = []
    for parity in (0, 1):
        pairs = []
        for i in range(lons):
            for j in range(lats):
                other = j + 1 if j % 2 == parity else j - 1
                if other == lats:
                    pairs.append((i * lats + j, (lons - 1 - i) * lats + j))
                elif other >= 0:
                    pairs.append((i * lats + j, i * lats + other))
        found.append(lax.ppermute(values[parity], BOTH, pairs))
    return tuple(found)


def on_device(
    state,
    adjoint_in,
    land_mask,
    east_coef,
    north_coef,
    zonal_flow,
    vertical_coef,
    slot_cell,
    slot_weight,
    arrive_obs,
    obs_value,
    obs_invvar,
):
    levels_n, rows_n, cols_n = state.shape
    devices = lax.axis_size(BOTH)
    slots = slot_cell.shape[1]
    obs_n = obs_value.shape[1]
    assert 2 * (slots // devices) == LANES and cols_n == LANES and 4 * levels_n <= LANES
    half = (levels_n + 1) // 2
    width = rows_n // GROUP * cols_n
    tile = min(slots, SLOT_TILE)
    tiles = slots // tile
    bf16 = jnp.bfloat16
    raw = (land_mask, east_coef, north_coef, zonal_flow, vertical_coef)
    lon, lat = lax.axis_index("lon"), lax.axis_index("lat")
    flags = jnp.stack([1 - lon % 2, 1 - lat % 2, lat == lax.axis_size("lat") - 1]).astype(jnp.int32)
    flags = jnp.broadcast_to(flags[:, None], (3, LANES))

    partial_vals = kernel_call(
        60,
        gather_kernel,
        f32(devices * half, LANES),
        [
            pltpu.VMEM((1, slots), jnp.int32),
            pltpu.VMEM((1, slots), jnp.float32),
            pltpu.VMEM((levels_n, rows_n, cols_n), jnp.float32),
            pltpu.VMEM((levels_n * GROUP, 3 * width), bf16),
            pltpu.SemaphoreType.DMA((2 + levels_n,)),
        ],
        [pltpu.HBM] * 3,
    )(slot_cell, slot_weight, state)
    levels = padded_levels(levels_n)
    partial_vals, raw = lax.optimization_barrier((partial_vals, raw))
    arrived = exchanged(partial_vals, devices)
    columns = kernel_call(4, coefficient_columns_kernel, f32(2 * SUB, rows_n))(*raw)
    arrived, side_coefs = lax.optimization_barrier((arrived, lon_swaps(columns, columns)))

    misfit, outgoing = kernel_call(
        8 + 4 * tiles,
        observe_kernel,
        (f32(levels_n, obs_n), f32(devices * half, LANES)),
        [pltpu.VMEM((obs_n, slots), bf16)],
    )(arrived, arrive_obs, obs_value, obs_invvar)
    outgoing, raw, side_coefs, adjoint_early = lax.optimization_barrier(
        (outgoing, raw, side_coefs, adjoint_in)
    )
    returned = exchanged(outgoing, devices)
    strips = kernel_call(
        5,
        seed_strips_kernel,
        (f32(rows_n, cols_n), f32(rows_n, cols_n), f32(4, levels, cols_n)),
    )(adjoint_early, raw[0])
    fields, sides, row_coefs = kernel_call(
        5,
        coefficients_kernel,
        (f32(7, rows_n, cols_n), f32(rows_n, cols_n), f32(2 * SUB, cols_n)),
        (),
    )(flags, *raw, *side_coefs)
    returned, strips, fields, sides, row_coefs = lax.optimization_barrier(
        (returned, strips, fields, sides, row_coefs)
    )
    own_columns, for_second, for_first, own_edges = kernel_call(
        7 + 3 * tiles,
        functools.partial(strips_kernel, levels_n),
        (
            f32(rows_n, cols_n),
            f32(rows_n // 2, cols_n),
            f32(rows_n // 2, cols_n),
            f32(4, levels, cols_n),
        ),
        (),
    )(flags, returned, slot_cell, slot_weight, land_mask, *strips)
    columns_beside = lon_swaps(for_first, for_second)
    whole = (levels_n, rows_n, cols_n)
    seed = kernel_call(
        22 + 3 * tiles,
        scatter_kernel,
        f32(levels_n, rows_n, cols_n),
        [pltpu.VMEM((2 * levels_n * GROUP, tile), bf16)],
    )(returned, slot_cell, slot_weight, adjoint_in)
    seed, columns_beside = lax.optimization_barrier((seed, columns_beside))
    message = f32(2 * levels + 3 * SUB, cols_n)
    messages = kernel_call(2, edge_message_kernel, (message, message), ())(
        flags, own_edges, *columns_beside, row_coefs
    )
    rows_beside = lat_swaps(messages[1], messages[0])
    seed, messages = lax.optimization_barrier((seed, messages))
    beside = kernel_call(
        8,
        beside_kernel,
        (f32(*whole), f32(*whole), f32(rows_n, cols_n)),
        [pltpu.VMEM(whole, jnp.float32)],
    )(flags, seed, fields, sides, own_columns, *columns_beside)
    beside, rows_beside = lax.optimization_barrier((beside, rows_beside))
    adjoint_state = kernel_call(
        10,
        steps_kernel,
        f32(*whole),
        [
            pltpu.VMEM(whole, jnp.float32),
            pltpu.VMEM((rows_n, cols_n), jnp.float32),
            pltpu.VMEM((2 * SUB, cols_n), jnp.float32),
            pltpu.SemaphoreType.DMA((4,)),
        ],
        [pltpu.VMEM] * 11, pltpu.HBM,
    )(flags, *beside, fields, sides, own_edges, *columns_beside, *rows_beside)
    return (adjoint_state, misfit)


def solution(mesh):
    in_specs = (
        P(None, "lat", "lon"),
        P(None, "lat", "lon"),
        P("lat", "lon"),
        P("lat", "lon"),
        P("lat", "lon"),
        P("lat", "lon"),
        P("lat", "lon"),
        P(("lon", "lat"), None),
        P(("lon", "lat"), None),
        P(("lon", "lat"), None),
        P(None, ("lon", "lat")),
        P(None, ("lon", "lat")),
    )
    out_specs = (P(None, "lat", "lon"), P(None, ("lon", "lat")))
    return jax.shard_map(
        on_device, mesh=mesh, in_specs=in_specs, out_specs=out_specs, check_vma=False
    )
```

```python
import functools

import jax
import jax.numpy as jnp
from jax import lax
from jax.experimental import pallas as pl
from jax.experimental.pallas import tpu as pltpu
from jax.sharding import PartitionSpec as P

LANES = 128
GROUP = 32
SUB = 8
SLOT_TILE = 16 * LANES
MIB = 1024 * 1024
BOTH = ("lon", "lat")


def pieces(value):
    high = value.astype(jnp.bfloat16)
    rest = value - high.astype(jnp.float32)
    middle = rest.astype(jnp.bfloat16)
    low = (rest - middle.astype(jnp.float32)).astype(jnp.bfloat16)
    return high, middle, low


def log2(size):
    assert size & (size - 1) == 0
    return size.bit_length() - 1


def cell_parts(cell, rows_n, cols_n):
    cell = jnp.maximum(cell, 0)
    row = jnp.right_shift(cell, log2(cols_n))
    group = jnp.right_shift(row, log2(GROUP))
    place = jnp.bitwise_and(cell, cols_n - 1) + group * cols_n
    return place, jnp.bitwise_and(row, GROUP - 1)


def one_hot(index, size):
    rows = lax.broadcasted_iota(jnp.int32, (size, index.shape[1]), 0)
    return jnp.where(rows == index, 1.0, 0.0).astype(jnp.bfloat16)


def first_half(rows):
    return lane((rows, LANES)) < LANES // 2


def pack(values, out_ref, first_pair):
    half = values.shape[0] // 2
    for pair in range(values.shape[1] // LANES):
        block = values[:, pair * LANES : (pair + 1) * LANES]
        top, bottom = block[:half], block[half:]
        at = 2 * (first_pair + pair) * half
        out_ref[at : at + half, :] = jnp.where(
            first_half(half), top, pltpu.roll(bottom, LANES // 2, 1)
        )
        out_ref[at + half : at + 2 * half, :] = jnp.where(
            first_half(half), pltpu.roll(top, LANES // 2, 1), bottom
        )


def unpack(in_ref, half, first_pair, pairs, levels):
    found = []
    for pair in range(first_pair, first_pair + pairs):
        at = 2 * pair * half
        left, right = in_ref[at : at + half, :], in_ref[at + half : at + 2 * half, :]
        top = jnp.where(first_half(half), left, pltpu.roll(right, LANES // 2, 1))
        bottom = jnp.where(first_half(half), pltpu.roll(left, LANES // 2, 1), right)
        filler = jnp.zeros((levels - 2 * half, LANES), jnp.float32)
        found.append(jnp.concatenate([top, bottom, filler], axis=0))
    return jnp.concatenate(found, axis=1)


def gather_kernel(
    cell_in, weight_in, state_in, out_ref, cell_ref, weight_ref, state_ref, field_ref, sems
):
    levels_n, rows_n, cols_n = state_ref.shape
    groups = rows_n // GROUP
    width = groups * cols_n
    slots = cell_ref.shape[1]
    tile = min(slots, SLOT_TILE)
    chunk = levels_n
    copies = [
        pltpu.make_async_copy(cell_in, cell_ref, sems.at[0]),
        pltpu.make_async_copy(weight_in, weight_ref, sems.at[1]),
    ]
    for place, level in enumerate(range(0, levels_n, chunk)):
        at = slice(level, level + chunk)
        copies.append(pltpu.make_async_copy(state_in.at[at], state_ref.at[at], sems.at[2 + place]))
    for copy in copies:
        copy.start()
    copies[0].wait()
    for start in range(0, slots, tile):
        cell = cell_ref[:, start : start + tile]
        place, row = cell_parts(cell, rows_n, cols_n)
        hot = one_hot(place, width)
        hot = jnp.concatenate([hot, hot, hot], axis=0)
        mine = sublane((GROUP, tile)) == row
        values = []
        for index, level in enumerate(range(0, levels_n, chunk)):
            at = slice(level * GROUP, (level + chunk) * GROUP)
            if start == 0:
                copies[2 + index].wait()
                for group in range(groups):
                    block = state_ref[
                        level : level + chunk, group * GROUP : (group + 1) * GROUP, :
                    ].reshape(chunk * GROUP, cols_n)
                    for part, piece in enumerate(pieces(block)):
                        begin = part * width + group * cols_n
                        field_ref[at, begin : begin + cols_n] = piece
            found = jnp.dot(field_ref[at, :], hot, preferred_element_type=jnp.float32)
            found = found.reshape(chunk, GROUP, tile)
            values.append(jnp.sum(jnp.where(mine[None], found, 0.0), axis=1))
        if start == 0:
            copies[1].wait()
        weight = jnp.where(cell >= 0, weight_ref[:, start : start + tile], 0.0)
        if levels_n % 2:
            values.append(jnp.zeros((1, tile), jnp.float32))
        pack(jnp.concatenate(values, axis=0) * weight, out_ref, start // LANES)


def observe_kernel(
    arrived_ref, target_ref, value_ref, invvar_ref, misfit_out, out_ref, hot_ref, misfit_ref, part_ref, sems
):
    levels_n, obs_n = value_ref.shape
    half = (levels_n + 1) // 2
    levels = padded_levels(levels_n)
    slots = hot_ref.shape[1]
    tile = min(slots, SLOT_TILE)
    sums = None
    for start in range(0, slots, tile):
        hot = one_hot(target_ref[:, start : start + tile], obs_n)
        hot_ref[:, start : start + tile] = hot
        values = unpack(arrived_ref, half, start // LANES, tile // LANES, levels)
        found = across(jnp.concatenate(pieces(values), axis=0), hot)
        sums = found if sums is None else sums + found
    interp = sums[:levels] + sums[levels : 2 * levels] + sums[2 * levels :]
    misfit = invvar_ref[...] * (interp[:levels_n] - value_ref[...])
    misfit_ref[...] = misfit
    copies = [pltpu.make_async_copy(misfit_ref, misfit_out, sems.at[0])]
    copies[0].start()
    filler = jnp.zeros((levels - levels_n, obs_n), jnp.float32)
    back = jnp.concatenate(pieces(jnp.concatenate([misfit, filler], axis=0)), axis=0)
    part = slots // (sems.shape[0] - 1)
    rows_n = part_ref.shape[0] * part // slots
    for index in range(slots // part):
        start = index * part
        found = jnp.dot(
            back, hot_ref[:, start : start + part], preferred_element_type=jnp.float32
        )
        values = found[:levels] + found[levels : 2 * levels] + found[2 * levels :]
        pack(values[: 2 * half], part_ref, start // LANES)
        rows = slice(index * rows_n, (index + 1) * rows_n)
        copies.append(pltpu.make_async_copy(part_ref.at[rows], out_ref.at[rows], sems.at[index + 1]))
        copies[-1].start()
    for copy in copies:
        copy.wait()


def padded_levels(levels_n):
    return (levels_n + 15) // 16 * 16


def returned_values(returned_ref, cell_ref, weight_ref, levels_n, start, tile):
    at = slice(start, start + tile)
    weight = jnp.where(cell_ref[:, at] >= 0, weight_ref[:, at], 0.0)
    values = unpack(
        returned_ref, (levels_n + 1) // 2, start // LANES, tile // LANES, padded_levels(levels_n)
    )
    return pieces(values * weight)[:2]


def across(left, right):
    return lax.dot_general(
        left, right, (((1,), (1,)), ((), ())), preferred_element_type=jnp.float32
    )


def seed_strips_kernel(adjoint_ref, mask_ref, columns_ref, ocean_ref, edges_ref):
    levels_n, rows_n, cols_n = adjoint_ref.shape
    level_at = jnp.right_shift(lane((SUB, cols_n)), 2)
    for top in range(0, rows_n, SUB):
        at = slice(top, top + SUB)
        found = jnp.zeros((SUB, cols_n), jnp.float32)
        for level in range(levels_n):
            block = pltpu.roll(adjoint_ref[level, at, :], (4 * level + 2) % cols_n, 1)
            found = jnp.where(level_at == level, block, found)
        columns_ref[at, :] = found
        spread = jnp.where(level_at == 0, pltpu.roll(mask_ref[at, :].astype(jnp.float32), 2, 1), 0.0)
        shift = 4
        while shift < cols_n:
            spread = spread + pltpu.roll(spread, shift, 1)
            shift *= 2
        ocean_ref[at, :] = spread
    places, levels, _ = edges_ref.shape
    for place, row in enumerate((0, 1, rows_n - 2, rows_n - 1)):
        for level in range(levels_n):
            edges_ref[place, level : level + 1, :] = adjoint_ref[level, row : row + 1, :]
        edges_ref[place, levels_n:, :] = jnp.zeros((levels - levels_n, cols_n), jnp.float32)


def strips_kernel(
    levels_n, flag_ref, returned_ref, cell_ref, weight_ref, mask_ref, seed_columns_ref, ocean_ref, seed_edges_ref,
    second_ref, first_ref, columns_ref, edges_ref,
):
    rows_n, cols_n = mask_ref.shape
    places, levels, _ = edges_ref.shape
    slots = cell_ref.shape[1]
    tile = min(slots, SLOT_TILE)
    column_sum = jnp.zeros((rows_n, LANES), jnp.float32)
    edge_sum = jnp.zeros((places * levels, cols_n), jnp.float32)
    for start in range(0, slots, tile):
        at = slice(start, start + tile)
        cell = jnp.maximum(cell_ref[:, at], 0)
        row, column = jnp.right_shift(cell, log2(cols_n)), jnp.bitwise_and(cell, cols_n - 1)
        values = returned_values(returned_ref, cell_ref, weight_ref, levels_n, start, tile)

        def chosen(piece, index, wanted):
            found = [
                piece * jnp.where(index == number, 1.0, 0.0).astype(jnp.bfloat16)
                for number in wanted
            ]
            return jnp.concatenate(found, axis=0)

        row_hot, column_hot = one_hot(row, rows_n), one_hot(column, cols_n)
        for piece in values:
            beside = chosen(piece, column, (cols_n - 2, cols_n - 1, 0, 1))
            column_sum += across(row_hot, beside)
            beyond = chosen(piece, row, (0, 1, rows_n - 2, rows_n - 1))
            edge_sum += across(beyond, column_hot)
    source, target = sublane((LANES, LANES)), lane((LANES, LANES))
    turn = jnp.bitwise_and(target, 3) * levels + jnp.right_shift(target, 2)
    turn = jnp.where(source == turn, 1.0, 0.0).astype(jnp.bfloat16)
    column_sum = sum(
        jnp.dot(piece, turn, preferred_element_type=jnp.float32) for piece in pieces(column_sum)
    )
    columns = (seed_columns_ref[...] + column_sum) * ocean_ref[...]
    columns_ref[...] = columns
    first_ref[...], second_ref[...] = lon_messages(flag_ref, columns)
    for place, row in enumerate((0, 1, rows_n - 2, rows_n - 1)):
        ocean = mask_ref[row : row + 1, :].astype(jnp.float32)
        forcing = edge_sum[place * levels : (place + 1) * levels]
        edges_ref[place] = (seed_edges_ref[place] + forcing) * ocean


def scatter_kernel(
    returned_ref, cell_ref, weight_ref, adjoint_ref, out_ref, rows_ref
):
    levels_n, rows_n, cols_n = out_ref.shape
    groups = rows_n // GROUP
    tile = rows_ref.shape[1]
    total = jnp.zeros((levels_n * GROUP, groups * cols_n), jnp.float32)
    for start in range(0, cell_ref.shape[1], tile):
        at = slice(start, start + tile)
        values = returned_values(returned_ref, cell_ref, weight_ref, levels_n, start, tile)
        place, member = cell_parts(cell_ref[:, at], rows_n, cols_n)
        hot, member = one_hot(place, groups * cols_n), one_hot(member, GROUP)
        for part, piece in enumerate(values):
            for level in range(levels_n):
                begin = (part * levels_n + level) * GROUP
                rows_ref[begin : begin + GROUP, :] = member * piece[level : level + 1, :]
        for part in range(len(values)):
            begin = part * levels_n * GROUP
            total += across(rows_ref[begin : begin + levels_n * GROUP, :], hot)
    for group in range(groups):
        at = slice(group * GROUP, (group + 1) * GROUP)
        forcing = total[:, group * cols_n : (group + 1) * cols_n].reshape(levels_n, GROUP, cols_n)
        out_ref[:, at, :] = adjoint_ref[:, at, :] + forcing


def beside_kernel(
    flag_ref, seed_ref, field_ref, side_ref, columns_ref, second_ref, first_ref,
    half_ref, masked_ref, turn_ref,
    from_ref,
):
    levels_n, rows_n, cols_n = seed_ref.shape
    east, west = lon_columns(flag_ref, first_ref[...], second_ref[...])
    own = columns_ref[...]
    level_at = jnp.right_shift(lane((rows_n, cols_n)), 2)

    def side_step(block, eastern, western, base):
        def coefficient(place):
            return side_ref[:, base + place : base + place + 1]

        higher = jnp.where(level_at > 0, pltpu.roll(block, 4, 1) - block, 0.0)
        lower = jnp.where(level_at < levels_n - 1, pltpu.roll(block, cols_n - 4, 1) - block, 0.0)
        change = (
            coefficient(2) * eastern
            + coefficient(3) * western
            + coefficient(4) * shifted(block, -1, 0, 0.0)
            + coefficient(5) * shifted(block, 1, 0, 0.0)
            - coefficient(1) * block
            + coefficient(6) * (higher + lower)
        )
        return block + coefficient(0) * change

    east_next = side_step(east, pltpu.roll(east, cols_n - 1, 1), pltpu.roll(own, 1, 1), 0)
    west_next = side_step(west, pltpu.roll(own, cols_n - 1, 1), pltpu.roll(west, 1, 1), 7)
    turn_ref[...] = turned_columns(east_next, west_next)
    for top in range(0, rows_n, SUB):
        at = slice(top, top + SUB)
        for level in range(levels_n):
            from_ref[level, at, :] = field_ref[0, at, :] * seed_ref[level, at, :]
    none = [jnp.zeros((1, cols_n), jnp.float32)] * levels_n

    def store(level, top, found):
        at = slice(top, top + SUB)
        half_ref[level, at, :] = found
        masked_ref[level, at, :] = field_ref[0, at, :] * found

    advance(seed_ref, from_ref, field_ref, turned_columns(east, west), none, none, store)


def turned_columns(eastern, western):
    slot = jnp.bitwise_and(lane(eastern.shape), 3)
    cols_n = eastern.shape[1]
    return jnp.where(slot == 1, pltpu.roll(eastern, cols_n - 1, 1), pltpu.roll(western, 1, 1))


def advance(source_ref, from_ref, field_ref, turn, below, above, store, patch=None):
    levels_n, rows_n, cols_n = source_ref.shape
    place = sublane((SUB, cols_n))
    first = lane((SUB, cols_n)) == 0
    last = lane((SUB, cols_n)) == cols_n - 1
    for top in range(0, rows_n, SUB):
        at = slice(top, top + SUB)
        bottom, ceiling = top == 0, top == rows_n - SUB
        ocean, own, here, back, onto, south_at, mixing = (
            field_ref[part, at, :] for part in range(7)
        )
        extra = None
        if patch is not None and (bottom or ceiling):
            south_row, north_row, added_below, added_above = patch
            if bottom:
                south_at = jnp.where(place == 0, south_row, south_at)
                own = jnp.where(place == 0, own + south_row, own)
                extra = [jnp.where(place == 0, row, 0.0) for row in added_below]
            else:
                onto = jnp.where(place == SUB - 1, north_row, onto)
                extra = [jnp.where(place == SUB - 1, row, 0.0) for row in added_above]

        def block_of(level):
            block = from_ref[level, at, :]
            return block if extra is None else block + ocean * extra[level]

        higher = block = block_of(0)
        for level in range(levels_n):
            lower = block_of(level + 1) if level + 1 < levels_n else block
            eastern, western = pltpu.roll(block, cols_n - 1, 1), pltpu.roll(block, 1, 1)
            beyond = pltpu.roll(turn[at], (2 * cols_n - 2 - 4 * level) % cols_n, 1)
            sides = here * jnp.where(last, beyond, eastern) + back * jnp.where(first, beyond, western)
            if ceiling:
                north = shifted(block, -1, 0, above[level])
            else:
                north = from_ref[level, top + 1 : top + SUB + 1, :]
            if bottom:
                south = shifted(block, 1, 0, below[level])
            else:
                south = from_ref[level, top - 1 : top + SUB - 1, :]
            source = source_ref[level, at, :]
            if extra is not None:
                source = source + extra[level]
            vertical = (higher - block) + (lower - block)
            found = (
                (source - own * block)
                + sides
                + (onto * north + south_at * south)
                + mixing * vertical
            )
            store(level, top, found)
            higher, block = block, lower


def lane(shape):
    return lax.broadcasted_iota(jnp.int32, shape, 1)


def sublane(shape):
    return lax.broadcasted_iota(jnp.int32, shape, 0)


def shifted(block, steps, axis, edge):
    size = block.shape[axis]
    at = lax.broadcasted_iota(jnp.int32, block.shape, axis)
    moved = pltpu.roll(block, steps % size, axis)
    return jnp.where(at == (0 if steps > 0 else size - 1), edge, moved)


def reversed_lanes(block):
    at = block.shape[1] - 1 - lane(block.shape)
    return jnp.take_along_axis(block, at, axis=1, mode="promise_in_bounds")


def by_flag(flag_ref, place, chosen, other):
    flag = jnp.broadcast_to(flag_ref[place : place + 1, : chosen.shape[1]], chosen.shape)
    return jnp.where(flag == 1, chosen, other)


def lon_neighbours(flag_ref, first, second):
    return by_flag(flag_ref, 0, first, second), by_flag(flag_ref, 0, second, first)


def lon_columns(flag_ref, first, second):
    east, west = lon_neighbours(flag_ref, first, second)
    east = jnp.concatenate([pltpu.roll(east, 2, 1), east], axis=0)
    west = jnp.concatenate([west, pltpu.roll(west, LANES - 2, 1)], axis=0)
    return east, west


def lon_messages(flag_ref, columns):
    low, high = columns[: columns.shape[0] // 2], columns[columns.shape[0] // 2 :]
    left = jnp.bitwise_and(lane(low.shape), 3) < 2
    eastward = jnp.where(left, low, pltpu.roll(high, 2, 1))
    westward = jnp.where(left, pltpu.roll(low, LANES - 2, 1), high)
    return lon_neighbours(flag_ref, eastward, westward)


def lat_neighbours(flag_ref, first, second):
    return by_flag(flag_ref, 1, first, second), by_flag(flag_ref, 1, second, first)


def side_columns(flag_ref, first_ref, second_ref):
    filler = jnp.zeros((first_ref.shape[1] - first_ref.shape[0], first_ref.shape[1]), jnp.float32)
    east, west = lon_neighbours(flag_ref, first_ref[...], second_ref[...])
    return tuple(jnp.concatenate([block, filler], axis=0).T for block in (east, west))


def coefficient_columns_kernel(mask_ref, east_ref, north_ref, flow_ref, vertical_ref, out_ref):
    rows_n, cols_n = mask_ref.shape
    ocean = mask_ref[...].astype(jnp.float32)
    here = east_ref[...] + 0.5 * flow_ref[...]
    behind = east_ref[...] - 0.5 * flow_ref[...]
    north, vertical = north_ref[...], vertical_ref[...]
    last = cols_n - 1
    wanted = (
        (ocean, 0), (here, 0), (north, 0), (vertical, 0),
        (ocean, last), (here, last), (behind, last), (behind, last - 1), (north, last), (vertical, last),
    )
    found = jnp.zeros((rows_n, cols_n), jnp.float32)
    for place, (field, column) in enumerate(wanted):
        found = jnp.where(
            lane(found.shape) == place, pltpu.roll(field, (place - column) % cols_n, 1), found
        )
    out_ref[...] = found.T[: out_ref.shape[0]]


def coefficients_kernel(
    flag_ref, mask_ref, east_ref, north_ref, flow_ref, vertical_ref, lon_first_ref, lon_second_ref,
    field_ref, side_ref, row_ref,
):
    rows_n, cols_n = mask_ref.shape
    east, west = side_columns(flag_ref, lon_first_ref, lon_second_ref)
    ocean = mask_ref[...].astype(jnp.float32)
    here = east_ref[...] + 0.5 * flow_ref[...]
    behind = east_ref[...] - 0.5 * flow_ref[...]
    north, vertical = north_ref[...], vertical_ref[...]
    back = shifted(behind, 1, 1, west[:, 6:7])
    south = shifted(north, 1, 0, 0.0)
    parts = (ocean, here + back + north + south, here, back, north, south, vertical)
    for place, part in enumerate(parts):
        field_ref[place] = part

    def side(ocean, here, back, north, vertical):
        south = shifted(north, 1, 0, 0.0)
        return ocean, here + back + north + south, here, back, north, south, vertical

    def spread(columns, place):
        return jnp.broadcast_to(columns[:, place : place + 1], (columns.shape[0], cols_n))

    eastern = side(
        spread(east, 0), spread(east, 1), spread(behind, cols_n - 1), spread(east, 2), spread(east, 3)
    )
    western = side(
        spread(west, 4), spread(west, 5), spread(west, 7), spread(west, 8), spread(west, 9)
    )
    found = jnp.zeros((rows_n, cols_n), jnp.float32)
    for place, part in enumerate(eastern + western):
        found = jnp.where(lane(found.shape) == place, part, found)
    side_ref[...] = found

    top, last = slice(0, 1), slice(rows_n - 1, rows_n)
    rows = []
    for at in (top, last):
        rows += [ocean[at], here[at], back[at], north[at]]
        if at is last:
            rows.append(north[rows_n - 2 : rows_n - 1])
        rows.append(vertical[at])
    rows += [east[top], east[last], west[top], west[last]]
    for place, row in enumerate(rows):
        row_ref[place : place + 1, :] = row
    row_ref[len(rows) :, :] = jnp.zeros((row_ref.shape[0] - len(rows), cols_n), jnp.float32)


def edge_message_kernel(
    levels_n, flag_ref, edges_ref, lon_second_ref, lon_first_ref, row_ref, second_ref, first_ref
):
    places, levels, cols_n = edges_ref.shape
    begin = row_ref.shape[0] + 2
    for ref in (first_ref, second_ref):
        ref[: row_ref.shape[0], :] = row_ref[...]
        ref[begin + 2 * levels_n :, :] = jnp.zeros((ref.shape[0] - begin - 2 * levels_n, cols_n), jnp.float32)
    for place, (north, south) in enumerate(((places - 1, 0), (places - 2, 1))):
        at = slice(begin + place * levels_n, begin + (place + 1) * levels_n)
        northern, southern = edges_ref[north][:levels_n], edges_ref[south][:levels_n]
        first_ref[at, :] = by_flag(flag_ref, 1, northern, southern)
        second_ref[at, :] = by_flag(flag_ref, 1, southern, northern)
    east, west = lon_columns(flag_ref, lon_first_ref[...], lon_second_ref[...])
    northern = east[-1:], west[-1:]
    southern = east[:1], west[:1]
    for place in range(2):
        at = slice(begin - 2 + place, begin - 1 + place)
        first_ref[at, :] = by_flag(flag_ref, 1, northern[place], southern[place])
        second_ref[at, :] = by_flag(flag_ref, 1, southern[place], northern[place])


def steps_kernel(
    flag_ref, half_ref, masked_ref, turn_in_ref, field_ref, side_ref,
    edges_ref, lon_second_ref, lon_first_ref, lat_first_ref, lat_second_ref,
    out_ref,
    done_ref, turn_ref, edge_ref, sems,
):
    levels_n, rows_n, cols_n = half_ref.shape
    levels = edges_ref.shape[1]
    up, down = lat_neighbours(flag_ref, lat_first_ref[...], lat_second_ref[...])

    ends = 2 * SUB
    east_up = by_flag(flag_ref, 2, pltpu.roll(up[ends + 1 : ends + 2], 1, 1), up[ends : ends + 1])
    west_up = by_flag(flag_ref, 2, pltpu.roll(up[ends : ends + 1], cols_n - 1, 1), up[ends + 1 : ends + 2])
    east_down, west_down = down[ends : ends + 1], down[ends + 1 : ends + 2]

    up_rows, down_rows = up[:ends], down[:ends]
    turned = reversed_lanes(up_rows)
    into = field_ref[4, rows_n - 1 : rows_n, :]
    south_row = down_rows[8:9]
    north_row = by_flag(flag_ref, 2, turned[8:9], into)
    plain = (
        up_rows[0:1], up_rows[1:2] + up_rows[2:3] + up_rows[3:4] + into,
        up_rows[1:2], up_rows[2:3], into, up_rows[3:4], up_rows[4:5],
    )
    folded = (
        turned[5:6], turned[6:7] + turned[7:8] + turned[8:9] + turned[9:10],
        turned[7:8], turned[6:7], into, turned[9:10], turned[10:11],
    )
    low = (
        down_rows[5:6], down_rows[6:7] + down_rows[7:8] + down_rows[8:9] + down_rows[9:10],
        down_rows[6:7], down_rows[7:8], down_rows[8:9], down_rows[9:10], down_rows[10:11],
    )
    for place in range(len(plain)):
        edge_ref[place : place + 1, :] = by_flag(flag_ref, 2, folded[place], plain[place])
        edge_ref[SUB + place : SUB + place + 1, :] = low[place]

    east, west = lon_columns(flag_ref, lon_first_ref[0:1, :], lon_second_ref[0:1, :])
    east, west = east[:1], west[:1]
    east_low = side_ref[0:1, 0:1] * down_rows[12:13, 2:3] * (east_down - east)
    west_low = side_ref[0:1, 7:8] * down_rows[14:15, 8:9] * (west_down - west)
    at = slice(rows_n - 1, rows_n)
    east_onto = by_flag(flag_ref, 2, up_rows[14:15, 8:9], side_ref[at, 4:5])
    west_onto = by_flag(flag_ref, 2, up_rows[12:13, 2:3], side_ref[at, 11:12])
    east_high = side_ref[at, 0:1] * east_onto * east_up
    west_high = side_ref[at, 7:8] * west_onto * west_up
    turn_ref[...] = turn_in_ref[...]
    turn_ref[0:1, :] = turn_in_ref[0:1, :] + turned_columns(east_low, west_low)
    turn_ref[at, :] = turn_in_ref[at, :] + turned_columns(east_high, west_high)

    plane = (levels, cols_n)
    corner_at = 4 * sublane(plane)

    def corner(row, place):
        found = jnp.where(lane(plane) == corner_at + place, jnp.broadcast_to(row, plane), 0.0)
        return jnp.sum(found, axis=1, keepdims=True)

    def edge(block, place):
        begin = ends + 2 + place * levels_n
        filler = jnp.zeros((levels - levels_n, cols_n), jnp.float32)
        return jnp.concatenate([block[begin : begin + levels_n], filler], axis=0)

    def edge_step(block, outer, inner, eastern, western, base):
        def coefficient(place):
            return edge_ref[base + place : base + place + 1, :]

        level = sublane(plane)
        higher = jnp.where(level > 0, pltpu.roll(block, 1, 0) - block, 0.0)
        lower = jnp.where(level < levels_n - 1, pltpu.roll(block, levels - 1, 0) - block, 0.0)
        change = (
            coefficient(2) * shifted(block, -1, 1, eastern)
            + coefficient(3) * shifted(block, 1, 1, western)
            + coefficient(4) * inner
            + coefficient(5) * outer
            - coefficient(1) * block
            + coefficient(6) * (higher + lower)
        )
        return block + coefficient(0) * change

    above = by_flag(flag_ref, 2, reversed_lanes(edge(up, 0)), edge(up, 0))
    above_outer = by_flag(flag_ref, 2, reversed_lanes(edge(up, 1)), edge(up, 1))
    below, below_outer = edge(down, 0), edge(down, 1)
    above_next = edge_step(
        above, above_outer, edges_ref[3], corner(east_up, 2), corner(west_up, 1), 0
    )
    below_next = edge_step(
        below, below_outer, edges_ref[0], corner(east_down, 2), corner(west_down, 1), SUB
    )
    def rows_of(block):
        return [block[level : level + 1] for level in range(levels_n)]

    patch = (
        south_row, north_row, rows_of(south_row * (below - edges_ref[0])), rows_of(north_row * above)
    )
    copies = []

    def store(level, top, found):
        done_ref[level, top : top + SUB, :] = found
        if level == levels_n - 1 and (top + SUB) % (rows_n // sems.shape[0]) == 0:
            rows = slice(top + SUB - rows_n // sems.shape[0], top + SUB)
            copy = pltpu.make_async_copy(
                done_ref.at[:, rows, :], out_ref.at[:, rows, :], sems.at[len(copies)]
            )
            copy.start()
            copies.append(copy)

    advance(
        half_ref, masked_ref, field_ref, turn_ref, rows_of(below_next), rows_of(above_next), store, patch
    )
    for copy in copies:
        copy.wait()


def kernel_call(mebibytes, body, out_shape, scratch=(), ins=None, outs=None):
    memory = {}
    if ins is not None:
        memory["in_specs"] = [pl.BlockSpec(memory_space=space) for space in ins]
    if outs is not None:
        spec = pl.BlockSpec(memory_space=outs)
        memory["out_specs"] = (spec,) * len(out_shape) if isinstance(out_shape, tuple) else spec
    return pl.pallas_call(
        body,
        out_shape=out_shape,
        scratch_shapes=list(scratch),
        compiler_params=pltpu.CompilerParams(vmem_limit_bytes=mebibytes * MIB),
        **memory,
    )


def exchanged(value, devices):
    rows = value.reshape(devices, 1, value.size // devices)
    return lax.all_to_all(rows, BOTH, split_axis=0, concat_axis=0, tiled=True).reshape(value.shape)


def f32(*shape):
    return jax.ShapeDtypeStruct(shape, jnp.float32)


def lon_swaps(first_value, second_value):
    count = lax.axis_size("lon")
    assert count % 2 == 0
    first = [(i, i ^ 1) for i in range(count)]
    second = [(i, (i + 1 if i % 2 else i - 1) % count) for i in range(count)]
    second_found = lax.ppermute(second_value, "lon", second)
    return lax.ppermute(first_value, "lon", first), second_found


def lat_swaps(*values):
    lons, lats = lax.axis_size("lon"), lax.axis_size("lat")
    found = []
    for parity in (0, 1):
        pairs = []
        for i in range(lons):
            for j in range(lats):
                other = j + 1 if j % 2 == parity else j - 1
                if other == lats:
                    pairs.append((i * lats + j, (lons - 1 - i) * lats + j))
                elif other >= 0:
                    pairs.append((i * lats + j, i * lats + other))
        found.append(lax.ppermute(values[parity], BOTH, pairs))
    return tuple(found)


def on_device(
    state,
    adjoint_in,
    land_mask,
    east_coef,
    north_coef,
    zonal_flow,
    vertical_coef,
    slot_cell,
    slot_weight,
    arrive_obs,
    obs_value,
    obs_invvar,
):
    levels_n, rows_n, cols_n = state.shape
    devices = lax.axis_size(BOTH)
    slots = slot_cell.shape[1]
    obs_n = obs_value.shape[1]
    assert 2 * (slots // devices) == LANES and cols_n == LANES and 4 * levels_n <= LANES
    half = (levels_n + 1) // 2
    width = rows_n // GROUP * cols_n
    tile = min(slots, SLOT_TILE)
    tiles = slots // tile
    bf16 = jnp.bfloat16
    raw = (land_mask, east_coef, north_coef, zonal_flow, vertical_coef)
    lon, lat = lax.axis_index("lon"), lax.axis_index("lat")
    flags = jnp.stack([1 - lon % 2, 1 - lat % 2, lat == lax.axis_size("lat") - 1]).astype(jnp.int32)
    flags = jnp.broadcast_to(flags[:, None], (3, LANES))

    partial_vals = kernel_call(
        60,
        gather_kernel,
        f32(devices * half, LANES),
        [
            pltpu.VMEM((1, slots), jnp.int32),
            pltpu.VMEM((1, slots), jnp.float32),
            pltpu.VMEM((levels_n, rows_n, cols_n), jnp.float32),
            pltpu.VMEM((levels_n * GROUP, 3 * width), bf16),
            pltpu.SemaphoreType.DMA((2 + levels_n,)),
        ],
        [pltpu.HBM] * 3,
    )(slot_cell, slot_weight, state)
    levels = padded_levels(levels_n)
    partial_vals, raw = lax.optimization_barrier((partial_vals, raw))
    arrived = exchanged(partial_vals, devices)
    columns = kernel_call(4, coefficient_columns_kernel, f32(2 * SUB, rows_n))(*raw)
    arrived, side_coefs = lax.optimization_barrier((arrived, lon_swaps(columns, columns)))

    misfit, outgoing = kernel_call(
        8 + 4 * tiles,
        observe_kernel,
        (f32(levels_n, obs_n), f32(devices * half, LANES)),
        [
            pltpu.VMEM((obs_n, slots), bf16),
            pltpu.VMEM((levels_n, obs_n), jnp.float32),
            pltpu.VMEM((devices * half, LANES), jnp.float32),
            pltpu.SemaphoreType.DMA((5,)),
        ],
        [pltpu.VMEM] * 4, pltpu.HBM,
    )(arrived, arrive_obs, obs_value, obs_invvar)
    outgoing, raw, side_coefs, adjoint_early = lax.optimization_barrier(
        (outgoing, raw, side_coefs, adjoint_in)
    )
    returned = exchanged(outgoing, devices)
    strips = kernel_call(
        5,
        seed_strips_kernel,
        (f32(rows_n, cols_n), f32(rows_n, cols_n), f32(4, levels, cols_n)),
    )(adjoint_early, raw[0])
    fields, sides, row_coefs = kernel_call(
        5,
        coefficients_kernel,
        (f32(7, rows_n, cols_n), f32(rows_n, cols_n), f32(2 * SUB, cols_n)),
        (),
    )(flags, *raw, *side_coefs)
    returned, strips, fields, sides, row_coefs = lax.optimization_barrier(
        (returned, strips, fields, sides, row_coefs)
    )
    for_second, for_first, own_columns, own_edges = kernel_call(
        7 + 3 * tiles,
        functools.partial(strips_kernel, levels_n),
        (
            f32(rows_n // 2, cols_n),
            f32(rows_n // 2, cols_n),
            f32(rows_n, cols_n),
            f32(4, levels, cols_n),
        ),
        (),
    )(flags, returned, slot_cell, slot_weight, land_mask, *strips)
    columns_beside = lon_swaps(for_first, for_second)[::-1]
    whole = (levels_n, rows_n, cols_n)
    seed = kernel_call(
        22 + 3 * tiles,
        scatter_kernel,
        f32(levels_n, rows_n, cols_n),
        [pltpu.VMEM((2 * levels_n * GROUP, tile), bf16)],
    )(returned, slot_cell, slot_weight, adjoint_in)
    seed, columns_beside = lax.optimization_barrier((seed, columns_beside))
    message = f32((2 * levels_n + 2 * SUB + 2 + SUB - 1) // SUB * SUB, cols_n)
    message_kernel = functools.partial(edge_message_kernel, levels_n)
    messages = kernel_call(2, message_kernel, (message, message), ())(
        flags, own_edges, *columns_beside, row_coefs
    )
    rows_beside = lat_swaps(messages[1], messages[0])
    seed, messages = lax.optimization_barrier((seed, messages))
    beside = kernel_call(
        8,
        beside_kernel,
        (f32(*whole), f32(*whole), f32(rows_n, cols_n)),
        [pltpu.VMEM(whole, jnp.float32)],
    )(flags, seed, fields, sides, own_columns, *columns_beside)
    beside, rows_beside = lax.optimization_barrier((beside, rows_beside))
    adjoint_state = kernel_call(
        10,
        steps_kernel,
        f32(*whole),
        [
            pltpu.VMEM(whole, jnp.float32),
            pltpu.VMEM((rows_n, cols_n), jnp.float32),
            pltpu.VMEM((2 * SUB, cols_n), jnp.float32),
            pltpu.SemaphoreType.DMA((8,)),
        ],
        [pltpu.VMEM] * 11, pltpu.HBM,
    )(flags, *beside, fields, sides, own_edges, *columns_beside, *rows_beside)
    return (adjoint_state, misfit)


def solution(mesh):
    in_specs = (
        P(None, "lat", "lon"),
        P(None, "lat", "lon"),
        P("lat", "lon"),
        P("lat", "lon"),
        P("lat", "lon"),
        P("lat", "lon"),
        P("lat", "lon"),
        P(("lon", "lat"), None),
        P(("lon", "lat"), None),
        P(("lon", "lat"), None),
        P(None, ("lon", "lat")),
        P(None, ("lon", "lat")),
    )
    out_specs = (P(None, "lat", "lon"), P(None, ("lon", "lat")))
    return jax.shard_map(
        on_device, mesh=mesh, in_specs=in_specs, out_specs=out_specs, check_vma=False
    )
```

```python
import functools

import jax
import jax.numpy as jnp
from jax import lax
from jax.experimental import pallas as pl
from jax.experimental.pallas import tpu as pltpu
from jax.sharding import PartitionSpec as P

LANES = 128
GROUP = 32
SUB = 8
SLOT_TILE = 16 * LANES
MIB = 1024 * 1024
BOTH = ("lon", "lat")


def pieces(value):
    high = value.astype(jnp.bfloat16)
    rest = value - high.astype(jnp.float32)
    middle = rest.astype(jnp.bfloat16)
    low = (rest - middle.astype(jnp.float32)).astype(jnp.bfloat16)
    return high, middle, low


def log2(size):
    assert size & (size - 1) == 0
    return size.bit_length() - 1


def cell_parts(cell, rows_n, cols_n):
    cell = jnp.maximum(cell, 0)
    row = jnp.right_shift(cell, log2(cols_n))
    group = jnp.right_shift(row, log2(GROUP))
    place = jnp.bitwise_and(cell, cols_n - 1) + group * cols_n
    return place, jnp.bitwise_and(row, GROUP - 1)


def one_hot(index, size):
    rows = lax.broadcasted_iota(jnp.int32, (size, index.shape[1]), 0)
    return jnp.where(rows == index, 1.0, 0.0).astype(jnp.bfloat16)


def first_half(rows):
    return lane((rows, LANES)) < LANES // 2


def pack(values, out_ref, first_pair):
    half = values.shape[0] // 2
    for pair in range(values.shape[1] // LANES):
        block = values[:, pair * LANES : (pair + 1) * LANES]
        top, bottom = block[:half], block[half:]
        at = 2 * (first_pair + pair) * half
        out_ref[at : at + half, :] = jnp.where(
            first_half(half), top, pltpu.roll(bottom, LANES // 2, 1)
        )
        out_ref[at + half : at + 2 * half, :] = jnp.where(
            first_half(half), pltpu.roll(top, LANES // 2, 1), bottom
        )


def unpack(in_ref, half, first_pair, pairs, levels):
    found = []
    for pair in range(first_pair, first_pair + pairs):
        at = 2 * pair * half
        left, right = in_ref[at : at + half, :], in_ref[at + half : at + 2 * half, :]
        top = jnp.where(first_half(half), left, pltpu.roll(right, LANES // 2, 1))
        bottom = jnp.where(first_half(half), pltpu.roll(left, LANES // 2, 1), right)
        filler = jnp.zeros((levels - 2 * half, LANES), jnp.float32)
        found.append(jnp.concatenate([top, bottom, filler], axis=0))
    return jnp.concatenate(found, axis=1)


def gather_kernel(
    cell_in, weight_in, state_in, out_ref, cell_ref, weight_ref, state_ref, field_ref, sems
):
    levels_n, rows_n, cols_n = state_ref.shape
    groups = rows_n // GROUP
    width = groups * cols_n
    slots = cell_ref.shape[1]
    tile = min(slots, SLOT_TILE)
    chunk = levels_n
    copies = [
        pltpu.make_async_copy(cell_in, cell_ref, sems.at[0]),
        pltpu.make_async_copy(weight_in, weight_ref, sems.at[1]),
    ]
    for place, level in enumerate(range(0, levels_n, chunk)):
        at = slice(level, level + chunk)
        copies.append(pltpu.make_async_copy(state_in.at[at], state_ref.at[at], sems.at[2 + place]))
    for copy in copies:
        copy.start()
    copies[0].wait()
    for start in range(0, slots, tile):
        cell = cell_ref[:, start : start + tile]
        place, row = cell_parts(cell, rows_n, cols_n)
        hot = one_hot(place, width)
        hot = jnp.concatenate([hot, hot, hot], axis=0)
        mine = sublane((GROUP, tile)) == row
        values = []
        for index, level in enumerate(range(0, levels_n, chunk)):
            at = slice(level * GROUP, (level + chunk) * GROUP)
            if start == 0:
                copies[2 + index].wait()
                for group in range(groups):
                    block = state_ref[
                        level : level + chunk, group * GROUP : (group + 1) * GROUP, :
                    ].reshape(chunk * GROUP, cols_n)
                    for part, piece in enumerate(pieces(block)):
                        begin = part * width + group * cols_n
                        field_ref[at, begin : begin + cols_n] = piece
            found = jnp.dot(field_ref[at, :], hot, preferred_element_type=jnp.float32)
            found = found.reshape(chunk, GROUP, tile)
            values.append(jnp.sum(jnp.where(mine[None], found, 0.0), axis=1))
        if start == 0:
            copies[1].wait()
        weight = jnp.where(cell >= 0, weight_ref[:, start : start + tile], 0.0)
        if levels_n % 2:
            values.append(jnp.zeros((1, tile), jnp.float32))
        pack(jnp.concatenate(values, axis=0) * weight, out_ref, start // LANES)


def observe_kernel(
    arrived_ref, target_ref, value_ref, invvar_ref, misfit_out, out_ref, hot_ref, misfit_ref, part_ref, sems
):
    levels_n, obs_n = value_ref.shape
    half = (levels_n + 1) // 2
    levels = padded_levels(levels_n)
    slots = hot_ref.shape[1]
    tile = min(slots, SLOT_TILE)
    sums = None
    for start in range(0, slots, tile):
        hot = one_hot(target_ref[:, start : start + tile], obs_n)
        hot_ref[:, start : start + tile] = hot
        values = unpack(arrived_ref, half, start // LANES, tile // LANES, levels)
        found = across(jnp.concatenate(pieces(values), axis=0), hot)
        sums = found if sums is None else sums + found
    interp = sums[:levels] + sums[levels : 2 * levels] + sums[2 * levels :]
    misfit = invvar_ref[...] * (interp[:levels_n] - value_ref[...])
    misfit_ref[...] = misfit
    copies = [pltpu.make_async_copy(misfit_ref, misfit_out, sems.at[0])]
    copies[0].start()
    filler = jnp.zeros((levels - levels_n, obs_n), jnp.float32)
    back = jnp.concatenate(pieces(jnp.concatenate([misfit, filler], axis=0)), axis=0)
    part = slots // (sems.shape[0] - 1)
    rows_n = part_ref.shape[0] * part // slots
    for index in range(slots // part):
        start = index * part
        found = jnp.dot(
            back, hot_ref[:, start : start + part], preferred_element_type=jnp.float32
        )
        values = found[:levels] + found[levels : 2 * levels] + found[2 * levels :]
        pack(values[: 2 * half], part_ref, start // LANES)
        rows = slice(index * rows_n, (index + 1) * rows_n)
        copies.append(pltpu.make_async_copy(part_ref.at[rows], out_ref.at[rows], sems.at[index + 1]))
        copies[-1].start()
    for copy in copies:
        copy.wait()


def padded_levels(levels_n):
    return (levels_n + 15) // 16 * 16


def returned_values(returned_ref, cell_ref, weight_ref, levels_n, start, tile):
    at = slice(start, start + tile)
    weight = jnp.where(cell_ref[:, at] >= 0, weight_ref[:, at], 0.0)
    values = unpack(
        returned_ref, (levels_n + 1) // 2, start // LANES, tile // LANES, padded_levels(levels_n)
    )
    return pieces(values * weight)[:2]


def across(left, right):
    return lax.dot_general(
        left, right, (((1,), (1,)), ((), ())), preferred_element_type=jnp.float32
    )


def seed_columns_kernel(adjoint_ref, mask_ref, columns_ref, ocean_ref):
    levels_n, rows_n, cols_n = adjoint_ref.shape
    level_at = jnp.right_shift(lane((SUB, cols_n)), 2)
    for top in range(0, rows_n, SUB):
        at = slice(top, top + SUB)
        found = jnp.zeros((SUB, cols_n), jnp.float32)
        for level in range(levels_n):
            block = pltpu.roll(adjoint_ref[level, at, :], (4 * level + 2) % cols_n, 1)
            found = jnp.where(level_at == level, block, found)
        columns_ref[at, :] = found
        spread = jnp.where(level_at == 0, pltpu.roll(mask_ref[at, :].astype(jnp.float32), 2, 1), 0.0)
        shift = 4
        while shift < cols_n:
            spread = spread + pltpu.roll(spread, shift, 1)
            shift *= 2
        ocean_ref[at, :] = spread


def columns_kernel(
    levels_n, flag_ref, returned_ref, cell_ref, weight_ref, seed_ref, ocean_ref,
    second_ref, first_ref, columns_ref,
):
    rows_n, cols_n = seed_ref.shape
    levels = padded_levels(levels_n)
    slots = cell_ref.shape[1]
    tile = min(slots, SLOT_TILE)
    total = jnp.zeros((rows_n, LANES), jnp.float32)
    for start in range(0, slots, tile):
        cell = jnp.maximum(cell_ref[:, start : start + tile], 0)
        row, column = jnp.right_shift(cell, log2(cols_n)), jnp.bitwise_and(cell, cols_n - 1)
        hot = one_hot(row, rows_n)
        for piece in returned_values(returned_ref, cell_ref, weight_ref, levels_n, start, tile):
            chosen = [
                piece * jnp.where(column == wanted, 1.0, 0.0).astype(jnp.bfloat16)
                for wanted in (cols_n - 2, cols_n - 1, 0, 1)
            ]
            total += across(hot, jnp.concatenate(chosen, axis=0))
    source, target = sublane((LANES, LANES)), lane((LANES, LANES))
    turn = jnp.bitwise_and(target, 3) * levels + jnp.right_shift(target, 2)
    turn = jnp.where(source == turn, 1.0, 0.0).astype(jnp.bfloat16)
    total = sum(jnp.dot(piece, turn, preferred_element_type=jnp.float32) for piece in pieces(total))
    columns = (seed_ref[...] + total) * ocean_ref[...]
    columns_ref[...] = columns
    first_ref[...], second_ref[...] = lon_messages(flag_ref, columns)


def scatter_kernel(
    returned_ref, cell_ref, weight_ref, adjoint_ref, mask_ref, out_ref, edges_ref, rows_ref
):
    levels_n, rows_n, cols_n = out_ref.shape
    groups = rows_n // GROUP
    tile = rows_ref.shape[1]
    total = jnp.zeros((levels_n * GROUP, groups * cols_n), jnp.float32)
    for start in range(0, cell_ref.shape[1], tile):
        at = slice(start, start + tile)
        values = returned_values(returned_ref, cell_ref, weight_ref, levels_n, start, tile)
        place, member = cell_parts(cell_ref[:, at], rows_n, cols_n)
        hot, member = one_hot(place, groups * cols_n), one_hot(member, GROUP)
        for part, piece in enumerate(values):
            for level in range(levels_n):
                begin = (part * levels_n + level) * GROUP
                rows_ref[begin : begin + GROUP, :] = member * piece[level : level + 1, :]
        for part in range(len(values)):
            begin = part * levels_n * GROUP
            total += across(rows_ref[begin : begin + levels_n * GROUP, :], hot)
    for group in range(groups):
        at = slice(group * GROUP, (group + 1) * GROUP)
        forcing = total[:, group * cols_n : (group + 1) * cols_n].reshape(levels_n, GROUP, cols_n)
        out_ref[:, at, :] = adjoint_ref[:, at, :] + forcing
    places, levels, _ = edges_ref.shape
    for place, row in enumerate((0, 1, rows_n - 2, rows_n - 1)):
        ocean = mask_ref[row : row + 1, :].astype(jnp.float32)
        for level in range(levels_n):
            edges_ref[place, level : level + 1, :] = out_ref[level, row : row + 1, :] * ocean
        edges_ref[place, levels_n:, :] = jnp.zeros((levels - levels_n, cols_n), jnp.float32)


def beside_kernel(
    flag_ref, seed_ref, field_ref, side_ref, columns_ref, second_ref, first_ref,
    half_ref, masked_ref, turn_ref,
    from_ref,
):
    levels_n, rows_n, cols_n = seed_ref.shape
    east, west = lon_columns(flag_ref, first_ref[...], second_ref[...])
    own = columns_ref[...]
    level_at = jnp.right_shift(lane((rows_n, cols_n)), 2)

    def side_step(block, eastern, western, base):
        def coefficient(place):
            return side_ref[:, base + place : base + place + 1]

        higher = jnp.where(level_at > 0, pltpu.roll(block, 4, 1) - block, 0.0)
        lower = jnp.where(level_at < levels_n - 1, pltpu.roll(block, cols_n - 4, 1) - block, 0.0)
        change = (
            coefficient(2) * eastern
            + coefficient(3) * western
            + coefficient(4) * shifted(block, -1, 0, 0.0)
            + coefficient(5) * shifted(block, 1, 0, 0.0)
            - coefficient(1) * block
            + coefficient(6) * (higher + lower)
        )
        return block + coefficient(0) * change

    east_next = side_step(east, pltpu.roll(east, cols_n - 1, 1), pltpu.roll(own, 1, 1), 0)
    west_next = side_step(west, pltpu.roll(own, cols_n - 1, 1), pltpu.roll(west, 1, 1), 7)
    turn_ref[...] = turned_columns(east_next, west_next)
    for top in range(0, rows_n, SUB):
        at = slice(top, top + SUB)
        for level in range(levels_n):
            from_ref[level, at, :] = field_ref[0, at, :] * seed_ref[level, at, :]
    none = [jnp.zeros((1, cols_n), jnp.float32)] * levels_n

    def store(level, top, found):
        at = slice(top, top + SUB)
        half_ref[level, at, :] = found
        masked_ref[level, at, :] = field_ref[0, at, :] * found

    advance(seed_ref, from_ref, field_ref, turned_columns(east, west), none, none, store)


def turned_columns(eastern, western):
    slot = jnp.bitwise_and(lane(eastern.shape), 3)
    cols_n = eastern.shape[1]
    return jnp.where(slot == 1, pltpu.roll(eastern, cols_n - 1, 1), pltpu.roll(western, 1, 1))


def advance(source_ref, from_ref, field_ref, turn, below, above, store, patch=None):
    levels_n, rows_n, cols_n = source_ref.shape
    place = sublane((SUB, cols_n))
    first = lane((SUB, cols_n)) == 0
    last = lane((SUB, cols_n)) == cols_n - 1
    for top in range(0, rows_n, SUB):
        at = slice(top, top + SUB)
        bottom, ceiling = top == 0, top == rows_n - SUB
        ocean, own, here, back, onto, south_at, mixing = (
            field_ref[part, at, :] for part in range(7)
        )
        extra = None
        if patch is not None and (bottom or ceiling):
            south_row, north_row, added_below, added_above = patch
            if bottom:
                south_at = jnp.where(place == 0, south_row, south_at)
                own = jnp.where(place == 0, own + south_row, own)
                extra = [jnp.where(place == 0, row, 0.0) for row in added_below]
            else:
                onto = jnp.where(place == SUB - 1, north_row, onto)
                extra = [jnp.where(place == SUB - 1, row, 0.0) for row in added_above]

        def block_of(level):
            block = from_ref[level, at, :]
            return block if extra is None else block + ocean * extra[level]

        higher = block = block_of(0)
        for level in range(levels_n):
            lower = block_of(level + 1) if level + 1 < levels_n else block
            eastern, western = pltpu.roll(block, cols_n - 1, 1), pltpu.roll(block, 1, 1)
            beyond = pltpu.roll(turn[at], (2 * cols_n - 2 - 4 * level) % cols_n, 1)
            sides = here * jnp.where(last, beyond, eastern) + back * jnp.where(first, beyond, western)
            if ceiling:
                north = shifted(block, -1, 0, above[level])
            else:
                north = from_ref[level, top + 1 : top + SUB + 1, :]
            if bottom:
                south = shifted(block, 1, 0, below[level])
            else:
                south = from_ref[level, top - 1 : top + SUB - 1, :]
            source = source_ref[level, at, :]
            if extra is not None:
                source = source + extra[level]
            vertical = (higher - block) + (lower - block)
            found = (
                (source - own * block)
                + sides
                + (onto * north + south_at * south)
                + mixing * vertical
            )
            store(level, top, found)
            higher, block = block, lower


def lane(shape):
    return lax.broadcasted_iota(jnp.int32, shape, 1)


def sublane(shape):
    return lax.broadcasted_iota(jnp.int32, shape, 0)


def shifted(block, steps, axis, edge):
    size = block.shape[axis]
    at = lax.broadcasted_iota(jnp.int32, block.shape, axis)
    moved = pltpu.roll(block, steps % size, axis)
    return jnp.where(at == (0 if steps > 0 else size - 1), edge, moved)


def reversed_lanes(block):
    at = block.shape[1] - 1 - lane(block.shape)
    return jnp.take_along_axis(block, at, axis=1, mode="promise_in_bounds")


def by_flag(flag_ref, place, chosen, other):
    flag = jnp.broadcast_to(flag_ref[place : place + 1, : chosen.shape[1]], chosen.shape)
    return jnp.where(flag == 1, chosen, other)


def lon_neighbours(flag_ref, first, second):
    return by_flag(flag_ref, 0, first, second), by_flag(flag_ref, 0, second, first)


def lon_columns(flag_ref, first, second):
    east, west = lon_neighbours(flag_ref, first, second)
    east = jnp.concatenate([pltpu.roll(east, 2, 1), east], axis=0)
    west = jnp.concatenate([west, pltpu.roll(west, LANES - 2, 1)], axis=0)
    return east, west


def lon_messages(flag_ref, columns):
    low, high = columns[: columns.shape[0] // 2], columns[columns.shape[0] // 2 :]
    left = jnp.bitwise_and(lane(low.shape), 3) < 2
    eastward = jnp.where(left, low, pltpu.roll(high, 2, 1))
    westward = jnp.where(left, pltpu.roll(low, LANES - 2, 1), high)
    return lon_neighbours(flag_ref, eastward, westward)


def lat_neighbours(flag_ref, first, second):
    return by_flag(flag_ref, 1, first, second), by_flag(flag_ref, 1, second, first)


def side_columns(flag_ref, first_ref, second_ref):
    filler = jnp.zeros((first_ref.shape[1] - first_ref.shape[0], first_ref.shape[1]), jnp.float32)
    east, west = lon_neighbours(flag_ref, first_ref[...], second_ref[...])
    return tuple(jnp.concatenate([block, filler], axis=0).T for block in (east, west))


def coefficient_columns_kernel(mask_ref, east_ref, north_ref, flow_ref, vertical_ref, out_ref):
    rows_n, cols_n = mask_ref.shape
    ocean = mask_ref[...].astype(jnp.float32)
    here = east_ref[...] + 0.5 * flow_ref[...]
    behind = east_ref[...] - 0.5 * flow_ref[...]
    north, vertical = north_ref[...], vertical_ref[...]
    last = cols_n - 1
    wanted = (
        (ocean, 0), (here, 0), (north, 0), (vertical, 0),
        (ocean, last), (here, last), (behind, last), (behind, last - 1), (north, last), (vertical, last),
    )
    found = jnp.zeros((rows_n, cols_n), jnp.float32)
    for place, (field, column) in enumerate(wanted):
        found = jnp.where(
            lane(found.shape) == place, pltpu.roll(field, (place - column) % cols_n, 1), found
        )
    out_ref[...] = found.T[: out_ref.shape[0]]


def coefficients_kernel(
    flag_ref, mask_ref, east_ref, north_ref, flow_ref, vertical_ref, lon_first_ref, lon_second_ref,
    field_ref, side_ref, row_ref,
):
    rows_n, cols_n = mask_ref.shape
    east, west = side_columns(flag_ref, lon_first_ref, lon_second_ref)
    ocean = mask_ref[...].astype(jnp.float32)
    here = east_ref[...] + 0.5 * flow_ref[...]
    behind = east_ref[...] - 0.5 * flow_ref[...]
    north, vertical = north_ref[...], vertical_ref[...]
    back = shifted(behind, 1, 1, west[:, 6:7])
    south = shifted(north, 1, 0, 0.0)
    parts = (ocean, here + back + north + south, here, back, north, south, vertical)
    for place, part in enumerate(parts):
        field_ref[place] = part

    def side(ocean, here, back, north, vertical):
        south = shifted(north, 1, 0, 0.0)
        return ocean, here + back + north + south, here, back, north, south, vertical

    def spread(columns, place):
        return jnp.broadcast_to(columns[:, place : place + 1], (columns.shape[0], cols_n))

    eastern = side(
        spread(east, 0), spread(east, 1), spread(behind, cols_n - 1), spread(east, 2), spread(east, 3)
    )
    western = side(
        spread(west, 4), spread(west, 5), spread(west, 7), spread(west, 8), spread(west, 9)
    )
    found = jnp.zeros((rows_n, cols_n), jnp.float32)
    for place, part in enumerate(eastern + western):
        found = jnp.where(lane(found.shape) == place, part, found)
    side_ref[...] = found

    top, last = slice(0, 1), slice(rows_n - 1, rows_n)
    rows = []
    for at in (top, last):
        rows += [ocean[at], here[at], back[at], north[at]]
        if at is last:
            rows.append(north[rows_n - 2 : rows_n - 1])
        rows.append(vertical[at])
    rows += [east[top], east[last], west[top], west[last]]
    for place, row in enumerate(rows):
        row_ref[place : place + 1, :] = row
    row_ref[len(rows) :, :] = jnp.zeros((row_ref.shape[0] - len(rows), cols_n), jnp.float32)


def edge_message_kernel(
    levels_n, flag_ref, edges_ref, lon_second_ref, lon_first_ref, row_ref, second_ref, first_ref
):
    places, levels, cols_n = edges_ref.shape
    begin = row_ref.shape[0] + 2
    for ref in (first_ref, second_ref):
        ref[: row_ref.shape[0], :] = row_ref[...]
        ref[begin + 2 * levels_n :, :] = jnp.zeros((ref.shape[0] - begin - 2 * levels_n, cols_n), jnp.float32)
    for place, (north, south) in enumerate(((places - 1, 0), (places - 2, 1))):
        at = slice(begin + place * levels_n, begin + (place + 1) * levels_n)
        northern, southern = edges_ref[north][:levels_n], edges_ref[south][:levels_n]
        first_ref[at, :] = by_flag(flag_ref, 1, northern, southern)
        second_ref[at, :] = by_flag(flag_ref, 1, southern, northern)
    east, west = lon_columns(flag_ref, lon_first_ref[...], lon_second_ref[...])
    northern = east[-1:], west[-1:]
    southern = east[:1], west[:1]
    for place in range(2):
        at = slice(begin - 2 + place, begin - 1 + place)
        first_ref[at, :] = by_flag(flag_ref, 1, northern[place], southern[place])
        second_ref[at, :] = by_flag(flag_ref, 1, southern[place], northern[place])


def steps_kernel(
    flag_ref, half_ref, masked_ref, turn_in_ref, field_ref, side_ref,
    edges_ref, lon_second_ref, lon_first_ref, lat_first_ref, lat_second_ref,
    out_ref,
    done_ref, turn_ref, edge_ref, sems,
):
    levels_n, rows_n, cols_n = half_ref.shape
    levels = edges_ref.shape[1]
    up, down = lat_neighbours(flag_ref, lat_first_ref[...], lat_second_ref[...])

    ends = 2 * SUB
    east_up = by_flag(flag_ref, 2, pltpu.roll(up[ends + 1 : ends + 2], 1, 1), up[ends : ends + 1])
    west_up = by_flag(flag_ref, 2, pltpu.roll(up[ends : ends + 1], cols_n - 1, 1), up[ends + 1 : ends + 2])
    east_down, west_down = down[ends : ends + 1], down[ends + 1 : ends + 2]

    up_rows, down_rows = up[:ends], down[:ends]
    turned = reversed_lanes(up_rows)
    into = field_ref[4, rows_n - 1 : rows_n, :]
    south_row = down_rows[8:9]
    north_row = by_flag(flag_ref, 2, turned[8:9], into)
    plain = (
        up_rows[0:1], up_rows[1:2] + up_rows[2:3] + up_rows[3:4] + into,
        up_rows[1:2], up_rows[2:3], into, up_rows[3:4], up_rows[4:5],
    )
    folded = (
        turned[5:6], turned[6:7] + turned[7:8] + turned[8:9] + turned[9:10],
        turned[7:8], turned[6:7], into, turned[9:10], turned[10:11],
    )
    low = (
        down_rows[5:6], down_rows[6:7] + down_rows[7:8] + down_rows[8:9] + down_rows[9:10],
        down_rows[6:7], down_rows[7:8], down_rows[8:9], down_rows[9:10], down_rows[10:11],
    )
    for place in range(len(plain)):
        edge_ref[place : place + 1, :] = by_flag(flag_ref, 2, folded[place], plain[place])
        edge_ref[SUB + place : SUB + place + 1, :] = low[place]

    east, west = lon_columns(flag_ref, lon_first_ref[0:1, :], lon_second_ref[0:1, :])
    east, west = east[:1], west[:1]
    east_low = side_ref[0:1, 0:1] * down_rows[12:13, 2:3] * (east_down - east)
    west_low = side_ref[0:1, 7:8] * down_rows[14:15, 8:9] * (west_down - west)
    at = slice(rows_n - 1, rows_n)
    east_onto = by_flag(flag_ref, 2, up_rows[14:15, 8:9], side_ref[at, 4:5])
    west_onto = by_flag(flag_ref, 2, up_rows[12:13, 2:3], side_ref[at, 11:12])
    east_high = side_ref[at, 0:1] * east_onto * east_up
    west_high = side_ref[at, 7:8] * west_onto * west_up
    turn_ref[...] = turn_in_ref[...]
    turn_ref[0:1, :] = turn_in_ref[0:1, :] + turned_columns(east_low, west_low)
    turn_ref[at, :] = turn_in_ref[at, :] + turned_columns(east_high, west_high)

    plane = (levels, cols_n)
    corner_at = 4 * sublane(plane)

    def corner(row, place):
        found = jnp.where(lane(plane) == corner_at + place, jnp.broadcast_to(row, plane), 0.0)
        return jnp.sum(found, axis=1, keepdims=True)

    def edge(block, place):
        begin = ends + 2 + place * levels_n
        filler = jnp.zeros((levels - levels_n, cols_n), jnp.float32)
        return jnp.concatenate([block[begin : begin + levels_n], filler], axis=0)

    def edge_step(block, outer, inner, eastern, western, base):
        def coefficient(place):
            return edge_ref[base + place : base + place + 1, :]

        level = sublane(plane)
        higher = jnp.where(level > 0, pltpu.roll(block, 1, 0) - block, 0.0)
        lower = jnp.where(level < levels_n - 1, pltpu.roll(block, levels - 1, 0) - block, 0.0)
        change = (
            coefficient(2) * shifted(block, -1, 1, eastern)
            + coefficient(3) * shifted(block, 1, 1, western)
            + coefficient(4) * inner
            + coefficient(5) * outer
            - coefficient(1) * block
            + coefficient(6) * (higher + lower)
        )
        return block + coefficient(0) * change

    above = by_flag(flag_ref, 2, reversed_lanes(edge(up, 0)), edge(up, 0))
    above_outer = by_flag(flag_ref, 2, reversed_lanes(edge(up, 1)), edge(up, 1))
    below, below_outer = edge(down, 0), edge(down, 1)
    above_next = edge_step(
        above, above_outer, edges_ref[3], corner(east_up, 2), corner(west_up, 1), 0
    )
    below_next = edge_step(
        below, below_outer, edges_ref[0], corner(east_down, 2), corner(west_down, 1), SUB
    )
    def rows_of(block):
        return [block[level : level + 1] for level in range(levels_n)]

    patch = (
        south_row, north_row, rows_of(south_row * (below - edges_ref[0])), rows_of(north_row * above)
    )
    copies = []

    def store(level, top, found):
        done_ref[level, top : top + SUB, :] = found
        if level == levels_n - 1 and (top + SUB) % (rows_n // sems.shape[0]) == 0:
            rows = slice(top + SUB - rows_n // sems.shape[0], top + SUB)
            copy = pltpu.make_async_copy(
                done_ref.at[:, rows, :], out_ref.at[:, rows, :], sems.at[len(copies)]
            )
            copy.start()
            copies.append(copy)

    advance(
        half_ref, masked_ref, field_ref, turn_ref, rows_of(below_next), rows_of(above_next), store, patch
    )
    for copy in copies:
        copy.wait()


def kernel_call(mebibytes, body, out_shape, scratch=(), ins=None, outs=None):
    memory = {}
    if ins is not None:
        memory["in_specs"] = [pl.BlockSpec(memory_space=space) for space in ins]
    if outs is not None:
        spec = pl.BlockSpec(memory_space=outs)
        memory["out_specs"] = (spec,) * len(out_shape) if isinstance(out_shape, tuple) else spec
    return pl.pallas_call(
        body,
        out_shape=out_shape,
        scratch_shapes=list(scratch),
        compiler_params=pltpu.CompilerParams(vmem_limit_bytes=mebibytes * MIB),
        **memory,
    )


def exchanged(value, devices):
    rows = value.reshape(devices, 1, value.size // devices)
    return lax.all_to_all(rows, BOTH, split_axis=0, concat_axis=0, tiled=True).reshape(value.shape)


def f32(*shape):
    return jax.ShapeDtypeStruct(shape, jnp.float32)


def lon_swaps(first_value, second_value):
    count = lax.axis_size("lon")
    assert count % 2 == 0
    first = [(i, i ^ 1) for i in range(count)]
    second = [(i, (i + 1 if i % 2 else i - 1) % count) for i in range(count)]
    second_found = lax.ppermute(second_value, "lon", second)
    return lax.ppermute(first_value, "lon", first), second_found


def lat_swaps(*values):
    lons, lats = lax.axis_size("lon"), lax.axis_size("lat")
    found = []
    for parity in (0, 1):
        pairs = []
        for i in range(lons):
            for j in range(lats):
                other = j + 1 if j % 2 == parity else j - 1
                if other == lats:
                    pairs.append((i * lats + j, (lons - 1 - i) * lats + j))
                elif other >= 0:
                    pairs.append((i * lats + j, i * lats + other))
        found.append(lax.ppermute(values[parity], BOTH, pairs))
    return tuple(found)


def on_device(
    state,
    adjoint_in,
    land_mask,
    east_coef,
    north_coef,
    zonal_flow,
    vertical_coef,
    slot_cell,
    slot_weight,
    arrive_obs,
    obs_value,
    obs_invvar,
):
    levels_n, rows_n, cols_n = state.shape
    devices = lax.axis_size(BOTH)
    slots = slot_cell.shape[1]
    obs_n = obs_value.shape[1]
    assert 2 * (slots // devices) == LANES and cols_n == LANES and 4 * levels_n <= LANES
    half = (levels_n + 1) // 2
    width = rows_n // GROUP * cols_n
    tile = min(slots, SLOT_TILE)
    tiles = slots // tile
    bf16 = jnp.bfloat16
    raw = (land_mask, east_coef, north_coef, zonal_flow, vertical_coef)
    lon, lat = lax.axis_index("lon"), lax.axis_index("lat")
    flags = jnp.stack([1 - lon % 2, 1 - lat % 2, lat == lax.axis_size("lat") - 1]).astype(jnp.int32)
    flags = jnp.broadcast_to(flags[:, None], (3, LANES))

    partial_vals = kernel_call(
        60,
        gather_kernel,
        f32(devices * half, LANES),
        [
            pltpu.VMEM((1, slots), jnp.int32),
            pltpu.VMEM((1, slots), jnp.float32),
            pltpu.VMEM((levels_n, rows_n, cols_n), jnp.float32),
            pltpu.VMEM((levels_n * GROUP, 3 * width), bf16),
            pltpu.SemaphoreType.DMA((2 + levels_n,)),
        ],
        [pltpu.HBM] * 3,
    )(slot_cell, slot_weight, state)
    levels = padded_levels(levels_n)
    partial_vals, raw = lax.optimization_barrier((partial_vals, raw))
    arrived = exchanged(partial_vals, devices)
    columns = kernel_call(4, coefficient_columns_kernel, f32(2 * SUB, rows_n))(*raw)
    arrived, side_coefs = lax.optimization_barrier((arrived, lon_swaps(columns, columns)))

    misfit, outgoing = kernel_call(
        8 + 4 * tiles,
        observe_kernel,
        (f32(levels_n, obs_n), f32(devices * half, LANES)),
        [
            pltpu.VMEM((obs_n, slots), bf16),
            pltpu.VMEM((levels_n, obs_n), jnp.float32),
            pltpu.VMEM((devices * half, LANES), jnp.float32),
            pltpu.SemaphoreType.DMA((5,)),
        ],
        [pltpu.VMEM] * 4, pltpu.HBM,
    )(arrived, arrive_obs, obs_value, obs_invvar)
    outgoing, raw, side_coefs, adjoint_early = lax.optimization_barrier(
        (outgoing, raw, side_coefs, adjoint_in)
    )
    returned = exchanged(outgoing, devices)
    strips = kernel_call(
        5,
        seed_columns_kernel,
        (f32(rows_n, cols_n), f32(rows_n, cols_n)),
    )(adjoint_early, raw[0])
    fields, sides, row_coefs = kernel_call(
        5,
        coefficients_kernel,
        (f32(7, rows_n, cols_n), f32(rows_n, cols_n), f32(2 * SUB, cols_n)),
        (),
    )(flags, *raw, *side_coefs)
    returned, strips, fields, sides, row_coefs = lax.optimization_barrier(
        (returned, strips, fields, sides, row_coefs)
    )
    for_second, for_first, own_columns = kernel_call(
        6 + 3 * tiles,
        functools.partial(columns_kernel, levels_n),
        (f32(rows_n // 2, cols_n), f32(rows_n // 2, cols_n), f32(rows_n, cols_n)),
    )(flags, returned, slot_cell, slot_weight, *strips)
    columns_beside = lon_swaps(for_first, for_second)[::-1]
    whole = (levels_n, rows_n, cols_n)
    seed, own_edges = kernel_call(
        22 + 3 * tiles,
        scatter_kernel,
        (f32(*whole), f32(4, levels, cols_n)),
        [pltpu.VMEM((2 * levels_n * GROUP, tile), bf16)],
    )(returned, slot_cell, slot_weight, adjoint_in, land_mask)
    seed, columns_beside = lax.optimization_barrier((seed, columns_beside))
    message = f32((2 * levels_n + 2 * SUB + 2 + SUB - 1) // SUB * SUB, cols_n)
    message_kernel = functools.partial(edge_message_kernel, levels_n)
    messages = kernel_call(2, message_kernel, (message, message), ())(
        flags, own_edges, *columns_beside, row_coefs
    )
    rows_beside = lat_swaps(messages[1], messages[0])
    seed, messages = lax.optimization_barrier((seed, messages))
    beside = kernel_call(
        8,
        beside_kernel,
        (f32(*whole), f32(*whole), f32(rows_n, cols_n)),
        [pltpu.VMEM(whole, jnp.float32)],
    )(flags, seed, fields, sides, own_columns, *columns_beside)
    beside, rows_beside = lax.optimization_barrier((beside, rows_beside))
    adjoint_state = kernel_call(
        10,
        steps_kernel,
        f32(*whole),
        [
            pltpu.VMEM(whole, jnp.float32),
            pltpu.VMEM((rows_n, cols_n), jnp.float32),
            pltpu.VMEM((2 * SUB, cols_n), jnp.float32),
            pltpu.SemaphoreType.DMA((8,)),
        ],
        [pltpu.VMEM] * 11, pltpu.HBM,
    )(flags, *beside, fields, sides, own_edges, *columns_beside, *rows_beside)
    return (adjoint_state, misfit)


def solution(mesh):
    in_specs = (
        P(None, "lat", "lon"),
        P(None, "lat", "lon"),
        P("lat", "lon"),
        P("lat", "lon"),
        P("lat", "lon"),
        P("lat", "lon"),
        P("lat", "lon"),
        P(("lon", "lat"), None),
        P(("lon", "lat"), None),
        P(("lon", "lat"), None),
        P(None, ("lon", "lat")),
        P(None, ("lon", "lat")),
    )
    out_specs = (P(None, "lat", "lon"), P(None, ("lon", "lat")))
    return jax.shard_map(
        on_device, mesh=mesh, in_specs=in_specs, out_specs=out_specs, check_vma=False
    )
```

```python
import functools

import jax
import jax.numpy as jnp
from jax import lax
from jax.experimental import pallas as pl
from jax.experimental.pallas import tpu as pltpu
from jax.sharding import PartitionSpec as P

LANES = 128
GROUP = 32
SUB = 8
SLOT_TILE = 16 * LANES
MIB = 1024 * 1024
BOTH = ("lon", "lat")


def pieces(value):
    high = value.astype(jnp.bfloat16)
    rest = value - high.astype(jnp.float32)
    middle = rest.astype(jnp.bfloat16)
    low = (rest - middle.astype(jnp.float32)).astype(jnp.bfloat16)
    return high, middle, low


def log2(size):
    assert size & (size - 1) == 0
    return size.bit_length() - 1


def cell_parts(cell, rows_n, cols_n):
    cell = jnp.maximum(cell, 0)
    row = jnp.right_shift(cell, log2(cols_n))
    group = jnp.right_shift(row, log2(GROUP))
    place = jnp.bitwise_and(cell, cols_n - 1) + group * cols_n
    return place, jnp.bitwise_and(row, GROUP - 1)


def one_hot(index, size):
    rows = lax.broadcasted_iota(jnp.int32, (size, index.shape[1]), 0)
    return jnp.where(rows == index, 1.0, 0.0).astype(jnp.bfloat16)


def first_half(rows):
    return lane((rows, LANES)) < LANES // 2


def pack(values, out_ref, first_pair):
    half = values.shape[0] // 2
    for pair in range(values.shape[1] // LANES):
        block = values[:, pair * LANES : (pair + 1) * LANES]
        top, bottom = block[:half], block[half:]
        at = 2 * (first_pair + pair) * half
        out_ref[at : at + half, :] = jnp.where(
            first_half(half), top, pltpu.roll(bottom, LANES // 2, 1)
        )
        out_ref[at + half : at + 2 * half, :] = jnp.where(
            first_half(half), pltpu.roll(top, LANES // 2, 1), bottom
        )


def unpack(in_ref, half, first_pair, pairs, levels):
    found = []
    for pair in range(first_pair, first_pair + pairs):
        at = 2 * pair * half
        left, right = in_ref[at : at + half, :], in_ref[at + half : at + 2 * half, :]
        top = jnp.where(first_half(half), left, pltpu.roll(right, LANES // 2, 1))
        bottom = jnp.where(first_half(half), pltpu.roll(left, LANES // 2, 1), right)
        filler = jnp.zeros((levels - 2 * half, LANES), jnp.float32)
        found.append(jnp.concatenate([top, bottom, filler], axis=0))
    return jnp.concatenate(found, axis=1)


def gather_kernel(
    cell_in, weight_in, state_in, out_ref, cell_ref, weight_ref, state_ref, field_ref, sems
):
    levels_n, rows_n, cols_n = state_ref.shape
    groups = rows_n // GROUP
    width = groups * cols_n
    slots = cell_ref.shape[1]
    tile = min(slots, SLOT_TILE)
    chunk = levels_n
    copies = [
        pltpu.make_async_copy(cell_in, cell_ref, sems.at[0]),
        pltpu.make_async_copy(weight_in, weight_ref, sems.at[1]),
    ]
    for place, level in enumerate(range(0, levels_n, chunk)):
        at = slice(level, level + chunk)
        copies.append(pltpu.make_async_copy(state_in.at[at], state_ref.at[at], sems.at[2 + place]))
    for copy in copies:
        copy.start()
    copies[0].wait()
    for start in range(0, slots, tile):
        cell = cell_ref[:, start : start + tile]
        place, row = cell_parts(cell, rows_n, cols_n)
        hot = one_hot(place, width)
        hot = jnp.concatenate([hot, hot, hot], axis=0)
        mine = sublane((GROUP, tile)) == row
        values = []
        for index, level in enumerate(range(0, levels_n, chunk)):
            at = slice(level * GROUP, (level + chunk) * GROUP)
            if start == 0:
                copies[2 + index].wait()
                for group in range(groups):
                    block = state_ref[
                        level : level + chunk, group * GROUP : (group + 1) * GROUP, :
                    ].reshape(chunk * GROUP, cols_n)
                    for part, piece in enumerate(pieces(block)):
                        begin = part * width + group * cols_n
                        field_ref[at, begin : begin + cols_n] = piece
            found = jnp.dot(field_ref[at, :], hot, preferred_element_type=jnp.float32)
            found = found.reshape(chunk, GROUP, tile)
            values.append(jnp.sum(jnp.where(mine[None], found, 0.0), axis=1))
        if start == 0:
            copies[1].wait()
        weight = jnp.where(cell >= 0, weight_ref[:, start : start + tile], 0.0)
        if levels_n % 2:
            values.append(jnp.zeros((1, tile), jnp.float32))
        pack(jnp.concatenate(values, axis=0) * weight, out_ref, start // LANES)


def observe_kernel(
    arrived_ref, target_ref, value_ref, invvar_ref, misfit_out, out_ref, hot_ref, misfit_ref, part_ref, sems
):
    levels_n, obs_n = value_ref.shape
    half = (levels_n + 1) // 2
    levels = padded_levels(levels_n)
    slots = hot_ref.shape[1]
    tile = min(slots, SLOT_TILE)
    sums = None
    for start in range(0, slots, tile):
        hot = one_hot(target_ref[:, start : start + tile], obs_n)
        hot_ref[:, start : start + tile] = hot
        values = unpack(arrived_ref, half, start // LANES, tile // LANES, levels)
        found = across(jnp.concatenate(pieces(values), axis=0), hot)
        sums = found if sums is None else sums + found
    interp = sums[:levels] + sums[levels : 2 * levels] + sums[2 * levels :]
    misfit = invvar_ref[...] * (interp[:levels_n] - value_ref[...])
    misfit_ref[...] = misfit
    copies = [pltpu.make_async_copy(misfit_ref, misfit_out, sems.at[0])]
    copies[0].start()
    filler = jnp.zeros((levels - levels_n, obs_n), jnp.float32)
    back = jnp.concatenate(pieces(jnp.concatenate([misfit, filler], axis=0)), axis=0)
    part = slots // (sems.shape[0] - 1)
    rows_n = part_ref.shape[0] * part // slots
    for index in range(slots // part):
        start = index * part
        found = jnp.dot(
            back, hot_ref[:, start : start + part], preferred_element_type=jnp.float32
        )
        values = found[:levels] + found[levels : 2 * levels] + found[2 * levels :]
        pack(values[: 2 * half], part_ref, start // LANES)
        rows = slice(index * rows_n, (index + 1) * rows_n)
        copies.append(pltpu.make_async_copy(part_ref.at[rows], out_ref.at[rows], sems.at[index + 1]))
        copies[-1].start()
    for copy in copies:
        copy.wait()


def padded_levels(levels_n):
    return (levels_n + 15) // 16 * 16


def returned_values(returned_ref, cell_ref, weight_ref, levels_n, start, tile):
    at = slice(start, start + tile)
    weight = jnp.where(cell_ref[:, at] >= 0, weight_ref[:, at], 0.0)
    values = unpack(
        returned_ref, (levels_n + 1) // 2, start // LANES, tile // LANES, padded_levels(levels_n)
    )
    return pieces(values * weight)[:2]


def across(left, right):
    return lax.dot_general(
        left, right, (((1,), (1,)), ((), ())), preferred_element_type=jnp.float32
    )


def seed_columns_kernel(adjoint_ref, mask_ref, columns_ref, ocean_ref):
    levels_n, rows_n, cols_n = adjoint_ref.shape
    level_at = jnp.right_shift(lane((SUB, cols_n)), 2)
    for top in range(0, rows_n, SUB):
        at = slice(top, top + SUB)
        found = jnp.zeros((SUB, cols_n), jnp.float32)
        for level in range(levels_n):
            block = pltpu.roll(adjoint_ref[level, at, :], (4 * level + 2) % cols_n, 1)
            found = jnp.where(level_at == level, block, found)
        columns_ref[at, :] = found
        spread = jnp.where(level_at == 0, pltpu.roll(mask_ref[at, :].astype(jnp.float32), 2, 1), 0.0)
        shift = 4
        while shift < cols_n:
            spread = spread + pltpu.roll(spread, shift, 1)
            shift *= 2
        ocean_ref[at, :] = spread


def columns_kernel(
    levels_n, flag_ref, returned_ref, cell_ref, weight_ref, seed_ref, ocean_ref,
    second_ref, first_ref, columns_ref,
):
    rows_n, cols_n = seed_ref.shape
    levels = padded_levels(levels_n)
    slots = cell_ref.shape[1]
    tile = min(slots, SLOT_TILE)
    total = jnp.zeros((rows_n, LANES), jnp.float32)
    for start in range(0, slots, tile):
        cell = jnp.maximum(cell_ref[:, start : start + tile], 0)
        row, column = jnp.right_shift(cell, log2(cols_n)), jnp.bitwise_and(cell, cols_n - 1)
        hot = one_hot(row, rows_n)
        for piece in returned_values(returned_ref, cell_ref, weight_ref, levels_n, start, tile):
            chosen = [
                piece * jnp.where(column == wanted, 1.0, 0.0).astype(jnp.bfloat16)
                for wanted in (cols_n - 2, cols_n - 1, 0, 1)
            ]
            total += across(hot, jnp.concatenate(chosen, axis=0))
    source, target = sublane((LANES, LANES)), lane((LANES, LANES))
    turn = jnp.bitwise_and(target, 3) * levels + jnp.right_shift(target, 2)
    turn = jnp.where(source == turn, 1.0, 0.0).astype(jnp.bfloat16)
    total = sum(jnp.dot(piece, turn, preferred_element_type=jnp.float32) for piece in pieces(total))
    columns = (seed_ref[...] + total) * ocean_ref[...]
    columns_ref[...] = columns
    first_ref[...], second_ref[...] = lon_messages(flag_ref, columns)


def scatter_kernel(
    returned_ref, cell_ref, weight_ref, adjoint_ref, mask_ref, out_ref, edges_ref, rows_ref
):
    levels_n, rows_n, cols_n = out_ref.shape
    groups = rows_n // GROUP
    tile = rows_ref.shape[1]
    total = jnp.zeros((levels_n * GROUP, groups * cols_n), jnp.float32)
    for start in range(0, cell_ref.shape[1], tile):
        at = slice(start, start + tile)
        values = returned_values(returned_ref, cell_ref, weight_ref, levels_n, start, tile)
        place, member = cell_parts(cell_ref[:, at], rows_n, cols_n)
        hot, member = one_hot(place, groups * cols_n), one_hot(member, GROUP)
        for part, piece in enumerate(values):
            for level in range(levels_n):
                begin = (part * levels_n + level) * GROUP
                rows_ref[begin : begin + GROUP, :] = member * piece[level : level + 1, :]
        for part in range(len(values)):
            begin = part * levels_n * GROUP
            total += across(rows_ref[begin : begin + levels_n * GROUP, :], hot)
    for group in range(groups):
        at = slice(group * GROUP, (group + 1) * GROUP)
        forcing = total[:, group * cols_n : (group + 1) * cols_n].reshape(levels_n, GROUP, cols_n)
        out_ref[:, at, :] = adjoint_ref[:, at, :] + forcing
    places, levels, _ = edges_ref.shape
    for place, row in enumerate((0, 1, rows_n - 2, rows_n - 1)):
        ocean = mask_ref[row : row + 1, :].astype(jnp.float32)
        for level in range(levels_n):
            edges_ref[place, level : level + 1, :] = out_ref[level, row : row + 1, :] * ocean
        edges_ref[place, levels_n:, :] = jnp.zeros((levels - levels_n, cols_n), jnp.float32)


def beside_kernel(
    flag_ref, seed_ref, field_ref, side_ref, columns_ref, second_ref, first_ref,
    half_ref, masked_ref, turn_ref,
    from_ref,
):
    levels_n, rows_n, cols_n = seed_ref.shape
    east, west = lon_columns(flag_ref, first_ref[...], second_ref[...])
    own = columns_ref[...]
    level_at = jnp.right_shift(lane((rows_n, cols_n)), 2)

    slot = jnp.bitwise_and(lane((rows_n, cols_n)), 3)
    block = jnp.where(slot < 2, west, east)
    eastern = pltpu.roll(jnp.where(slot == 3, east, own), cols_n - 1, 1)
    western = pltpu.roll(jnp.where(slot == 0, west, own), 1, 1)
    higher = jnp.where(level_at > 0, pltpu.roll(block, 4, 1) - block, 0.0)
    lower = jnp.where(level_at < levels_n - 1, pltpu.roll(block, cols_n - 4, 1) - block, 0.0)
    change = (
        side_ref[2] * eastern
        + side_ref[3] * western
        + side_ref[4] * shifted(block, -1, 0, 0.0)
        + side_ref[5] * shifted(block, 1, 0, 0.0)
        - side_ref[1] * block
        + side_ref[6] * (higher + lower)
    )
    changed = block + side_ref[0] * change
    turn_ref[...] = turned_columns(changed, changed)
    for top in range(0, rows_n, SUB):
        at = slice(top, top + SUB)
        for level in range(levels_n):
            from_ref[level, at, :] = field_ref[0, at, :] * seed_ref[level, at, :]
    none = [jnp.zeros((1, cols_n), jnp.float32)] * levels_n

    def store(level, top, found):
        at = slice(top, top + SUB)
        half_ref[level, at, :] = found
        masked_ref[level, at, :] = field_ref[0, at, :] * found

    advance(seed_ref, from_ref, field_ref, turned_columns(east, west), none, none, store)


def turned_columns(eastern, western):
    slot = jnp.bitwise_and(lane(eastern.shape), 3)
    cols_n = eastern.shape[1]
    return jnp.where(slot == 1, pltpu.roll(eastern, cols_n - 1, 1), pltpu.roll(western, 1, 1))


def advance(source_ref, from_ref, field_ref, turn, below, above, store, patch=None):
    levels_n, rows_n, cols_n = source_ref.shape
    place = sublane((SUB, cols_n))
    first = lane((SUB, cols_n)) == 0
    last = lane((SUB, cols_n)) == cols_n - 1
    for top in range(0, rows_n, SUB):
        at = slice(top, top + SUB)
        bottom, ceiling = top == 0, top == rows_n - SUB
        ocean, own, here, back, onto, south_at, mixing = (
            field_ref[part, at, :] for part in range(7)
        )
        extra = None
        if patch is not None and (bottom or ceiling):
            south_row, north_row, added_below, added_above = patch
            if bottom:
                south_at = jnp.where(place == 0, south_row, south_at)
                own = jnp.where(place == 0, own + south_row, own)
                extra = [jnp.where(place == 0, row, 0.0) for row in added_below]
            else:
                onto = jnp.where(place == SUB - 1, north_row, onto)
                extra = [jnp.where(place == SUB - 1, row, 0.0) for row in added_above]

        def block_of(level):
            block = from_ref[level, at, :]
            return block if extra is None else block + ocean * extra[level]

        higher = block = block_of(0)
        for level in range(levels_n):
            lower = block_of(level + 1) if level + 1 < levels_n else block
            eastern, western = pltpu.roll(block, cols_n - 1, 1), pltpu.roll(block, 1, 1)
            beyond = pltpu.roll(turn[at], (2 * cols_n - 2 - 4 * level) % cols_n, 1)
            sides = here * jnp.where(last, beyond, eastern) + back * jnp.where(first, beyond, western)
            if ceiling:
                north = shifted(block, -1, 0, above[level])
            else:
                north = from_ref[level, top + 1 : top + SUB + 1, :]
            if bottom:
                south = shifted(block, 1, 0, below[level])
            else:
                south = from_ref[level, top - 1 : top + SUB - 1, :]
            source = source_ref[level, at, :]
            if extra is not None:
                source = source + extra[level]
            vertical = (higher - block) + (lower - block)
            found = (
                (source - own * block)
                + sides
                + (onto * north + south_at * south)
                + mixing * vertical
            )
            store(level, top, found)
            higher, block = block, lower


def lane(shape):
    return lax.broadcasted_iota(jnp.int32, shape, 1)


def sublane(shape):
    return lax.broadcasted_iota(jnp.int32, shape, 0)


def shifted(block, steps, axis, edge):
    size = block.shape[axis]
    at = lax.broadcasted_iota(jnp.int32, block.shape, axis)
    moved = pltpu.roll(block, steps % size, axis)
    return jnp.where(at == (0 if steps > 0 else size - 1), edge, moved)


def reversed_lanes(block):
    at = block.shape[1] - 1 - lane(block.shape)
    return jnp.take_along_axis(block, at, axis=1, mode="promise_in_bounds")


def by_flag(flag_ref, place, chosen, other):
    flag = jnp.broadcast_to(flag_ref[place : place + 1, : chosen.shape[1]], chosen.shape)
    return jnp.where(flag == 1, chosen, other)


def lon_neighbours(flag_ref, first, second):
    return by_flag(flag_ref, 0, first, second), by_flag(flag_ref, 0, second, first)


def lon_columns(flag_ref, first, second):
    east, west = lon_neighbours(flag_ref, first, second)
    east = jnp.concatenate([pltpu.roll(east, 2, 1), east], axis=0)
    west = jnp.concatenate([west, pltpu.roll(west, LANES - 2, 1)], axis=0)
    return east, west


def lon_messages(flag_ref, columns):
    low, high = columns[: columns.shape[0] // 2], columns[columns.shape[0] // 2 :]
    left = jnp.bitwise_and(lane(low.shape), 3) < 2
    eastward = jnp.where(left, low, pltpu.roll(high, 2, 1))
    westward = jnp.where(left, pltpu.roll(low, LANES - 2, 1), high)
    return lon_neighbours(flag_ref, eastward, westward)


def lat_neighbours(flag_ref, first, second):
    return by_flag(flag_ref, 1, first, second), by_flag(flag_ref, 1, second, first)


def side_columns(flag_ref, first_ref, second_ref):
    filler = jnp.zeros((first_ref.shape[1] - first_ref.shape[0], first_ref.shape[1]), jnp.float32)
    east, west = lon_neighbours(flag_ref, first_ref[...], second_ref[...])
    return tuple(jnp.concatenate([block, filler], axis=0).T for block in (east, west))


def coefficient_columns_kernel(mask_ref, east_ref, north_ref, flow_ref, vertical_ref, out_ref):
    rows_n, cols_n = mask_ref.shape
    ocean = mask_ref[...].astype(jnp.float32)
    here = east_ref[...] + 0.5 * flow_ref[...]
    behind = east_ref[...] - 0.5 * flow_ref[...]
    north, vertical = north_ref[...], vertical_ref[...]
    last = cols_n - 1
    wanted = (
        (ocean, 0), (here, 0), (north, 0), (vertical, 0),
        (ocean, last), (here, last), (behind, last), (behind, last - 1), (north, last), (vertical, last),
    )
    found = jnp.zeros((rows_n, cols_n), jnp.float32)
    for place, (field, column) in enumerate(wanted):
        found = jnp.where(
            lane(found.shape) == place, pltpu.roll(field, (place - column) % cols_n, 1), found
        )
    out_ref[...] = found.T[: out_ref.shape[0]]


def coefficients_kernel(
    flag_ref, mask_ref, east_ref, north_ref, flow_ref, vertical_ref, lon_first_ref, lon_second_ref,
    field_ref, side_ref, row_ref,
):
    rows_n, cols_n = mask_ref.shape
    east, west = side_columns(flag_ref, lon_first_ref, lon_second_ref)
    ocean = mask_ref[...].astype(jnp.float32)
    here = east_ref[...] + 0.5 * flow_ref[...]
    behind = east_ref[...] - 0.5 * flow_ref[...]
    north, vertical = north_ref[...], vertical_ref[...]
    back = shifted(behind, 1, 1, west[:, 6:7])
    south = shifted(north, 1, 0, 0.0)
    parts = (ocean, here + back + north + south, here, back, north, south, vertical)
    for place, part in enumerate(parts):
        field_ref[place] = part

    def side(ocean, here, back, north, vertical):
        south = shifted(north, 1, 0, 0.0)
        return ocean, here + back + north + south, here, back, north, south, vertical

    def spread(columns, place):
        return jnp.broadcast_to(columns[:, place : place + 1], (columns.shape[0], cols_n))

    eastern = side(
        spread(east, 0), spread(east, 1), spread(behind, cols_n - 1), spread(east, 2), spread(east, 3)
    )
    western = side(
        spread(west, 4), spread(west, 5), spread(west, 7), spread(west, 8), spread(west, 9)
    )
    slot = jnp.bitwise_and(lane((rows_n, cols_n)), 3)
    for place in range(len(eastern)):
        side_ref[place] = jnp.where(slot < 2, western[place], eastern[place])

    top, last = slice(0, 1), slice(rows_n - 1, rows_n)
    rows = []
    for at in (top, last):
        rows += [ocean[at], here[at], back[at], north[at]]
        if at is last:
            rows.append(north[rows_n - 2 : rows_n - 1])
        rows.append(vertical[at])
    rows += [east[top], east[last], west[top], west[last]]
    for place, row in enumerate(rows):
        row_ref[place : place + 1, :] = row
    row_ref[len(rows) :, :] = jnp.zeros((row_ref.shape[0] - len(rows), cols_n), jnp.float32)


def edge_message_kernel(
    levels_n, flag_ref, edges_ref, lon_second_ref, lon_first_ref, row_ref, second_ref, first_ref
):
    places, levels, cols_n = edges_ref.shape
    begin = row_ref.shape[0] + 2
    for ref in (first_ref, second_ref):
        ref[: row_ref.shape[0], :] = row_ref[...]
        ref[begin + 2 * levels_n :, :] = jnp.zeros((ref.shape[0] - begin - 2 * levels_n, cols_n), jnp.float32)
    for place, (north, south) in enumerate(((places - 1, 0), (places - 2, 1))):
        at = slice(begin + place * levels_n, begin + (place + 1) * levels_n)
        northern, southern = edges_ref[north][:levels_n], edges_ref[south][:levels_n]
        first_ref[at, :] = by_flag(flag_ref, 1, northern, southern)
        second_ref[at, :] = by_flag(flag_ref, 1, southern, northern)
    east, west = lon_columns(flag_ref, lon_first_ref[...], lon_second_ref[...])
    northern = east[-1:], west[-1:]
    southern = east[:1], west[:1]
    for place in range(2):
        at = slice(begin - 2 + place, begin - 1 + place)
        first_ref[at, :] = by_flag(flag_ref, 1, northern[place], southern[place])
        second_ref[at, :] = by_flag(flag_ref, 1, southern[place], northern[place])


def steps_kernel(
    flag_ref, half_ref, masked_ref, turn_in_ref, field_ref, side_ref,
    edges_ref, lon_second_ref, lon_first_ref, lat_first_ref, lat_second_ref,
    out_ref,
    done_ref, turn_ref, edge_ref, sems,
):
    levels_n, rows_n, cols_n = half_ref.shape
    levels = edges_ref.shape[1]
    up, down = lat_neighbours(flag_ref, lat_first_ref[...], lat_second_ref[...])

    ends = 2 * SUB
    east_up = by_flag(flag_ref, 2, pltpu.roll(up[ends + 1 : ends + 2], 1, 1), up[ends : ends + 1])
    west_up = by_flag(flag_ref, 2, pltpu.roll(up[ends : ends + 1], cols_n - 1, 1), up[ends + 1 : ends + 2])
    east_down, west_down = down[ends : ends + 1], down[ends + 1 : ends + 2]

    up_rows, down_rows = up[:ends], down[:ends]
    turned = reversed_lanes(up_rows)
    into = field_ref[4, rows_n - 1 : rows_n, :]
    south_row = down_rows[8:9]
    north_row = by_flag(flag_ref, 2, turned[8:9], into)
    plain = (
        up_rows[0:1], up_rows[1:2] + up_rows[2:3] + up_rows[3:4] + into,
        up_rows[1:2], up_rows[2:3], into, up_rows[3:4], up_rows[4:5],
    )
    folded = (
        turned[5:6], turned[6:7] + turned[7:8] + turned[8:9] + turned[9:10],
        turned[7:8], turned[6:7], into, turned[9:10], turned[10:11],
    )
    low = (
        down_rows[5:6], down_rows[6:7] + down_rows[7:8] + down_rows[8:9] + down_rows[9:10],
        down_rows[6:7], down_rows[7:8], down_rows[8:9], down_rows[9:10], down_rows[10:11],
    )
    for place in range(len(plain)):
        edge_ref[place : place + 1, :] = by_flag(flag_ref, 2, folded[place], plain[place])
        edge_ref[SUB + place : SUB + place + 1, :] = low[place]

    east, west = lon_columns(flag_ref, lon_first_ref[0:1, :], lon_second_ref[0:1, :])
    east, west = east[:1], west[:1]
    east_low = side_ref[0, 0:1, 2:3] * down_rows[12:13, 2:3] * (east_down - east)
    west_low = side_ref[0, 0:1, 1:2] * down_rows[14:15, 8:9] * (west_down - west)
    at = slice(rows_n - 1, rows_n)
    east_onto = by_flag(flag_ref, 2, up_rows[14:15, 8:9], side_ref[4, at, 2:3])
    west_onto = by_flag(flag_ref, 2, up_rows[12:13, 2:3], side_ref[4, at, 1:2])
    east_high = side_ref[0, at, 2:3] * east_onto * east_up
    west_high = side_ref[0, at, 1:2] * west_onto * west_up
    turn_ref[...] = turn_in_ref[...]
    turn_ref[0:1, :] = turn_in_ref[0:1, :] + turned_columns(east_low, west_low)
    turn_ref[at, :] = turn_in_ref[at, :] + turned_columns(east_high, west_high)

    plane = (levels, cols_n)
    corner_at = 4 * sublane(plane)

    def corner(row, place):
        found = jnp.where(lane(plane) == corner_at + place, jnp.broadcast_to(row, plane), 0.0)
        return jnp.sum(found, axis=1, keepdims=True)

    def edge(block, place):
        begin = ends + 2 + place * levels_n
        filler = jnp.zeros((levels - levels_n, cols_n), jnp.float32)
        return jnp.concatenate([block[begin : begin + levels_n], filler], axis=0)

    def edge_step(block, outer, inner, eastern, western, base):
        def coefficient(place):
            return edge_ref[base + place : base + place + 1, :]

        level = sublane(plane)
        higher = jnp.where(level > 0, pltpu.roll(block, 1, 0) - block, 0.0)
        lower = jnp.where(level < levels_n - 1, pltpu.roll(block, levels - 1, 0) - block, 0.0)
        change = (
            coefficient(2) * shifted(block, -1, 1, eastern)
            + coefficient(3) * shifted(block, 1, 1, western)
            + coefficient(4) * inner
            + coefficient(5) * outer
            - coefficient(1) * block
            + coefficient(6) * (higher + lower)
        )
        return block + coefficient(0) * change

    above = by_flag(flag_ref, 2, reversed_lanes(edge(up, 0)), edge(up, 0))
    above_outer = by_flag(flag_ref, 2, reversed_lanes(edge(up, 1)), edge(up, 1))
    below, below_outer = edge(down, 0), edge(down, 1)
    above_next = edge_step(
        above, above_outer, edges_ref[3], corner(east_up, 2), corner(west_up, 1), 0
    )
    below_next = edge_step(
        below, below_outer, edges_ref[0], corner(east_down, 2), corner(west_down, 1), SUB
    )
    def rows_of(block):
        return [block[level : level + 1] for level in range(levels_n)]

    patch = (
        south_row, north_row, rows_of(south_row * (below - edges_ref[0])), rows_of(north_row * above)
    )
    copies = []

    def store(level, top, found):
        done_ref[level, top : top + SUB, :] = found
        if level == levels_n - 1 and (top + SUB) % (rows_n // sems.shape[0]) == 0:
            rows = slice(top + SUB - rows_n // sems.shape[0], top + SUB)
            copy = pltpu.make_async_copy(
                done_ref.at[:, rows, :], out_ref.at[:, rows, :], sems.at[len(copies)]
            )
            copy.start()
            copies.append(copy)

    advance(
        half_ref, masked_ref, field_ref, turn_ref, rows_of(below_next), rows_of(above_next), store, patch
    )
    for copy in copies:
        copy.wait()


def kernel_call(mebibytes, body, out_shape, scratch=(), ins=None, outs=None):
    memory = {}
    if ins is not None:
        memory["in_specs"] = [pl.BlockSpec(memory_space=space) for space in ins]
    if outs is not None:
        spec = pl.BlockSpec(memory_space=outs)
        memory["out_specs"] = (spec,) * len(out_shape) if isinstance(out_shape, tuple) else spec
    return pl.pallas_call(
        body,
        out_shape=out_shape,
        scratch_shapes=list(scratch),
        compiler_params=pltpu.CompilerParams(vmem_limit_bytes=mebibytes * MIB),
        **memory,
    )


def exchanged(value, devices):
    rows = value.reshape(devices, 1, value.size // devices)
    return lax.all_to_all(rows, BOTH, split_axis=0, concat_axis=0, tiled=True).reshape(value.shape)


def f32(*shape):
    return jax.ShapeDtypeStruct(shape, jnp.float32)


def lon_swaps(first_value, second_value):
    count = lax.axis_size("lon")
    assert count % 2 == 0
    first = [(i, i ^ 1) for i in range(count)]
    second = [(i, (i + 1 if i % 2 else i - 1) % count) for i in range(count)]
    second_found = lax.ppermute(second_value, "lon", second)
    return lax.ppermute(first_value, "lon", first), second_found


def lat_swaps(*values):
    lons, lats = lax.axis_size("lon"), lax.axis_size("lat")
    found = []
    for parity in (0, 1):
        pairs = []
        for i in range(lons):
            for j in range(lats):
                other = j + 1 if j % 2 == parity else j - 1
                if other == lats:
                    pairs.append((i * lats + j, (lons - 1 - i) * lats + j))
                elif other >= 0:
                    pairs.append((i * lats + j, i * lats + other))
        found.append(lax.ppermute(values[parity], BOTH, pairs))
    return tuple(found)


def on_device(
    state,
    adjoint_in,
    land_mask,
    east_coef,
    north_coef,
    zonal_flow,
    vertical_coef,
    slot_cell,
    slot_weight,
    arrive_obs,
    obs_value,
    obs_invvar,
):
    levels_n, rows_n, cols_n = state.shape
    devices = lax.axis_size(BOTH)
    slots = slot_cell.shape[1]
    obs_n = obs_value.shape[1]
    assert 2 * (slots // devices) == LANES and cols_n == LANES and 4 * levels_n <= LANES
    half = (levels_n + 1) // 2
    width = rows_n // GROUP * cols_n
    tile = min(slots, SLOT_TILE)
    tiles = slots // tile
    bf16 = jnp.bfloat16
    raw = (land_mask, east_coef, north_coef, zonal_flow, vertical_coef)
    lon, lat = lax.axis_index("lon"), lax.axis_index("lat")
    flags = jnp.stack([1 - lon % 2, 1 - lat % 2, lat == lax.axis_size("lat") - 1]).astype(jnp.int32)
    flags = jnp.broadcast_to(flags[:, None], (3, LANES))

    partial_vals = kernel_call(
        60,
        gather_kernel,
        f32(devices * half, LANES),
        [
            pltpu.VMEM((1, slots), jnp.int32),
            pltpu.VMEM((1, slots), jnp.float32),
            pltpu.VMEM((levels_n, rows_n, cols_n), jnp.float32),
            pltpu.VMEM((levels_n * GROUP, 3 * width), bf16),
            pltpu.SemaphoreType.DMA((2 + levels_n,)),
        ],
        [pltpu.HBM] * 3,
    )(slot_cell, slot_weight, state)
    levels = padded_levels(levels_n)
    partial_vals, raw = lax.optimization_barrier((partial_vals, raw))
    arrived = exchanged(partial_vals, devices)
    columns = kernel_call(4, coefficient_columns_kernel, f32(2 * SUB, rows_n))(*raw)
    arrived, side_coefs = lax.optimization_barrier((arrived, lon_swaps(columns, columns)))

    misfit, outgoing = kernel_call(
        8 + 4 * tiles,
        observe_kernel,
        (f32(levels_n, obs_n), f32(devices * half, LANES)),
        [
            pltpu.VMEM((obs_n, slots), bf16),
            pltpu.VMEM((levels_n, obs_n), jnp.float32),
            pltpu.VMEM((devices * half, LANES), jnp.float32),
            pltpu.SemaphoreType.DMA((5,)),
        ],
        [pltpu.VMEM] * 4, pltpu.HBM,
    )(arrived, arrive_obs, obs_value, obs_invvar)
    outgoing, raw, side_coefs, adjoint_early = lax.optimization_barrier(
        (outgoing, raw, side_coefs, adjoint_in)
    )
    returned = exchanged(outgoing, devices)
    strips = kernel_call(
        5,
        seed_columns_kernel,
        (f32(rows_n, cols_n), f32(rows_n, cols_n)),
    )(adjoint_early, raw[0])
    fields, sides, row_coefs = kernel_call(
        5,
        coefficients_kernel,
        (f32(7, rows_n, cols_n), f32(7, rows_n, cols_n), f32(2 * SUB, cols_n)),
        (),
    )(flags, *raw, *side_coefs)
    returned, strips, fields, sides, row_coefs = lax.optimization_barrier(
        (returned, strips, fields, sides, row_coefs)
    )
    for_second, for_first, own_columns = kernel_call(
        6 + 3 * tiles,
        functools.partial(columns_kernel, levels_n),
        (f32(rows_n // 2, cols_n), f32(rows_n // 2, cols_n), f32(rows_n, cols_n)),
    )(flags, returned, slot_cell, slot_weight, *strips)
    columns_beside = lon_swaps(for_first, for_second)[::-1]
    whole = (levels_n, rows_n, cols_n)
    seed, own_edges = kernel_call(
        22 + 3 * tiles,
        scatter_kernel,
        (f32(*whole), f32(4, levels, cols_n)),
        [pltpu.VMEM((2 * levels_n * GROUP, tile), bf16)],
    )(returned, slot_cell, slot_weight, adjoint_in, land_mask)
    seed, columns_beside = lax.optimization_barrier((seed, columns_beside))
    message = f32((2 * levels_n + 2 * SUB + 2 + SUB - 1) // SUB * SUB, cols_n)
    message_kernel = functools.partial(edge_message_kernel, levels_n)
    messages = kernel_call(2, message_kernel, (message, message), ())(
        flags, own_edges, *columns_beside, row_coefs
    )
    rows_beside = lat_swaps(messages[1], messages[0])
    seed, messages = lax.optimization_barrier((seed, messages))
    beside = kernel_call(
        8,
        beside_kernel,
        (f32(*whole), f32(*whole), f32(rows_n, cols_n)),
        [pltpu.VMEM(whole, jnp.float32)],
    )(flags, seed, fields, sides, own_columns, *columns_beside)
    beside, rows_beside = lax.optimization_barrier((beside, rows_beside))
    adjoint_state = kernel_call(
        10,
        steps_kernel,
        f32(*whole),
        [
            pltpu.VMEM(whole, jnp.float32),
            pltpu.VMEM((rows_n, cols_n), jnp.float32),
            pltpu.VMEM((2 * SUB, cols_n), jnp.float32),
            pltpu.SemaphoreType.DMA((8,)),
        ],
        [pltpu.VMEM] * 11, pltpu.HBM,
    )(flags, *beside, fields, sides, own_edges, *columns_beside, *rows_beside)
    return (adjoint_state, misfit)


def solution(mesh):
    in_specs = (
        P(None, "lat", "lon"),
        P(None, "lat", "lon"),
        P("lat", "lon"),
        P("lat", "lon"),
        P("lat", "lon"),
        P("lat", "lon"),
        P("lat", "lon"),
        P(("lon", "lat"), None),
        P(("lon", "lat"), None),
        P(("lon", "lat"), None),
        P(None, ("lon", "lat")),
        P(None, ("lon", "lat")),
    )
    out_specs = (P(None, "lat", "lon"), P(None, ("lon", "lat")))
    return jax.shard_map(
        on_device, mesh=mesh, in_specs=in_specs, out_specs=out_specs, check_vma=False
    )
```

```python
import functools

import jax
import jax.numpy as jnp
from jax import lax
from jax.experimental import pallas as pl
from jax.experimental.pallas import tpu as pltpu
from jax.sharding import PartitionSpec as P

LANES = 128
GROUP = 32
SUB = 8
SLOT_TILE = 16 * LANES
MIB = 1024 * 1024
BOTH = ("lon", "lat")


def pieces(value):
    high = value.astype(jnp.bfloat16)
    rest = value - high.astype(jnp.float32)
    middle = rest.astype(jnp.bfloat16)
    low = (rest - middle.astype(jnp.float32)).astype(jnp.bfloat16)
    return high, middle, low


def log2(size):
    assert size & (size - 1) == 0
    return size.bit_length() - 1


def cell_parts(cell, rows_n, cols_n):
    cell = jnp.maximum(cell, 0)
    row = jnp.right_shift(cell, log2(cols_n))
    group = jnp.right_shift(row, log2(GROUP))
    place = jnp.bitwise_and(cell, cols_n - 1) + group * cols_n
    return place, jnp.bitwise_and(row, GROUP - 1)


def one_hot(index, size):
    rows = lax.broadcasted_iota(jnp.int32, (size, index.shape[1]), 0)
    return jnp.where(rows == index, 1.0, 0.0).astype(jnp.bfloat16)


def first_half(rows):
    return lane((rows, LANES)) < LANES // 2


def pack(values, out_ref, first_pair):
    half = values.shape[0] // 2
    for pair in range(values.shape[1] // LANES):
        block = values[:, pair * LANES : (pair + 1) * LANES]
        top, bottom = block[:half], block[half:]
        at = 2 * (first_pair + pair) * half
        out_ref[at : at + half, :] = jnp.where(
            first_half(half), top, pltpu.roll(bottom, LANES // 2, 1)
        )
        out_ref[at + half : at + 2 * half, :] = jnp.where(
            first_half(half), pltpu.roll(top, LANES // 2, 1), bottom
        )


def unpack(in_ref, half, first_pair, pairs, levels):
    found = []
    for pair in range(first_pair, first_pair + pairs):
        at = 2 * pair * half
        left, right = in_ref[at : at + half, :], in_ref[at + half : at + 2 * half, :]
        top = jnp.where(first_half(half), left, pltpu.roll(right, LANES // 2, 1))
        bottom = jnp.where(first_half(half), pltpu.roll(left, LANES // 2, 1), right)
        filler = jnp.zeros((levels - 2 * half, LANES), jnp.float32)
        found.append(jnp.concatenate([top, bottom, filler], axis=0))
    return jnp.concatenate(found, axis=1)


def gather_kernel(
    cell_in, weight_in, state_in, out_ref, cell_ref, weight_ref, state_ref, field_ref, sems
):
    levels_n, rows_n, cols_n = state_ref.shape
    groups = rows_n // GROUP
    width = groups * cols_n
    slots = cell_ref.shape[1]
    tile = min(slots, SLOT_TILE)
    chunk = levels_n
    copies = [
        pltpu.make_async_copy(cell_in, cell_ref, sems.at[0]),
        pltpu.make_async_copy(weight_in, weight_ref, sems.at[1]),
    ]
    for place, level in enumerate(range(0, levels_n, chunk)):
        at = slice(level, level + chunk)
        copies.append(pltpu.make_async_copy(state_in.at[at], state_ref.at[at], sems.at[2 + place]))
    for copy in copies:
        copy.start()
    copies[0].wait()
    for start in range(0, slots, tile):
        cell = cell_ref[:, start : start + tile]
        place, row = cell_parts(cell, rows_n, cols_n)
        hot = one_hot(place, width)
        hot = jnp.concatenate([hot, hot, hot], axis=0)
        mine = sublane((GROUP, tile)) == row
        values = []
        for index, level in enumerate(range(0, levels_n, chunk)):
            at = slice(level * GROUP, (level + chunk) * GROUP)
            if start == 0:
                copies[2 + index].wait()
                for group in range(groups):
                    block = state_ref[
                        level : level + chunk, group * GROUP : (group + 1) * GROUP, :
                    ].reshape(chunk * GROUP, cols_n)
                    for part, piece in enumerate(pieces(block)):
                        begin = part * width + group * cols_n
                        field_ref[at, begin : begin + cols_n] = piece
            found = jnp.dot(field_ref[at, :], hot, preferred_element_type=jnp.float32)
            found = found.reshape(chunk, GROUP, tile)
            values.append(jnp.sum(jnp.where(mine[None], found, 0.0), axis=1))
        if start == 0:
            copies[1].wait()
        weight = jnp.where(cell >= 0, weight_ref[:, start : start + tile], 0.0)
        if levels_n % 2:
            values.append(jnp.zeros((1, tile), jnp.float32))
        pack(jnp.concatenate(values, axis=0) * weight, out_ref, start // LANES)


def observe_kernel(
    arrived_ref, target_ref, value_ref, invvar_ref, misfit_out, out_ref, hot_ref, misfit_ref, part_ref, sems
):
    levels_n, obs_n = value_ref.shape
    half = (levels_n + 1) // 2
    levels = padded_levels(levels_n)
    slots = hot_ref.shape[1]
    tile = min(slots, SLOT_TILE)
    sums = None
    for start in range(0, slots, tile):
        hot = one_hot(target_ref[:, start : start + tile], obs_n)
        hot_ref[:, start : start + tile] = hot
        values = unpack(arrived_ref, half, start // LANES, tile // LANES, levels)
        found = across(jnp.concatenate(pieces(values), axis=0), hot)
        sums = found if sums is None else sums + found
    interp = sums[:levels] + sums[levels : 2 * levels] + sums[2 * levels :]
    misfit = invvar_ref[...] * (interp[:levels_n] - value_ref[...])
    misfit_ref[...] = misfit
    copies = [pltpu.make_async_copy(misfit_ref, misfit_out, sems.at[0])]
    copies[0].start()
    filler = jnp.zeros((levels - levels_n, obs_n), jnp.float32)
    back = jnp.concatenate(pieces(jnp.concatenate([misfit, filler], axis=0)), axis=0)
    part = slots // (sems.shape[0] - 1)
    rows_n = part_ref.shape[0] * part // slots
    for index in range(slots // part):
        start = index * part
        found = jnp.dot(
            back, hot_ref[:, start : start + part], preferred_element_type=jnp.float32
        )
        values = found[:levels] + found[levels : 2 * levels] + found[2 * levels :]
        pack(values[: 2 * half], part_ref, start // LANES)
        rows = slice(index * rows_n, (index + 1) * rows_n)
        copies.append(pltpu.make_async_copy(part_ref.at[rows], out_ref.at[rows], sems.at[index + 1]))
        copies[-1].start()
    for copy in copies:
        copy.wait()


def padded_levels(levels_n):
    return (levels_n + 15) // 16 * 16


def returned_values(returned_ref, cell_ref, weight_ref, levels_n, start, tile):
    at = slice(start, start + tile)
    weight = jnp.where(cell_ref[:, at] >= 0, weight_ref[:, at], 0.0)
    values = unpack(
        returned_ref, (levels_n + 1) // 2, start // LANES, tile // LANES, padded_levels(levels_n)
    )
    return pieces(values * weight)[:2]


def across(left, right):
    return lax.dot_general(
        left, right, (((1,), (1,)), ((), ())), preferred_element_type=jnp.float32
    )


def seed_columns_kernel(adjoint_ref, mask_ref, columns_ref, ocean_ref):
    levels_n, rows_n, cols_n = adjoint_ref.shape
    level_at = jnp.right_shift(lane((SUB, cols_n)), 2)
    for top in range(0, rows_n, SUB):
        at = slice(top, top + SUB)
        found = jnp.zeros((SUB, cols_n), jnp.float32)
        for level in range(levels_n):
            block = pltpu.roll(adjoint_ref[level, at, :], (4 * level + 2) % cols_n, 1)
            found = jnp.where(level_at == level, block, found)
        columns_ref[at, :] = found
        spread = jnp.where(level_at == 0, pltpu.roll(mask_ref[at, :].astype(jnp.float32), 2, 1), 0.0)
        shift = 4
        while shift < cols_n:
            spread = spread + pltpu.roll(spread, shift, 1)
            shift *= 2
        ocean_ref[at, :] = spread


def columns_kernel(
    levels_n, flag_ref, returned_ref, cell_ref, weight_ref, seed_ref, ocean_ref,
    second_ref, first_ref, columns_ref,
):
    rows_n, cols_n = seed_ref.shape
    levels = padded_levels(levels_n)
    slots = cell_ref.shape[1]
    tile = min(slots, SLOT_TILE)
    total = jnp.zeros((rows_n, LANES), jnp.float32)
    for start in range(0, slots, tile):
        cell = jnp.maximum(cell_ref[:, start : start + tile], 0)
        row, column = jnp.right_shift(cell, log2(cols_n)), jnp.bitwise_and(cell, cols_n - 1)
        hot = one_hot(row, rows_n)
        values = returned_values(returned_ref, cell_ref, weight_ref, levels_n, start, tile)
        values = jnp.concatenate(values, axis=1)
        column = jnp.concatenate([column, column], axis=1)
        chosen = [
            values * jnp.where(column == wanted, 1.0, 0.0).astype(jnp.bfloat16)
            for wanted in (cols_n - 2, cols_n - 1, 0, 1)
        ]
        hot = jnp.concatenate([hot, hot], axis=1)
        total += across(hot, jnp.concatenate(chosen, axis=0))
    source, target = sublane((LANES, LANES)), lane((LANES, LANES))
    turn = jnp.bitwise_and(target, 3) * levels + jnp.right_shift(target, 2)
    turn = jnp.where(source == turn, 1.0, 0.0).astype(jnp.bfloat16)
    total = jnp.dot(
        jnp.concatenate(pieces(total), axis=1),
        jnp.concatenate([turn, turn, turn], axis=0),
        preferred_element_type=jnp.float32,
    )
    columns = (seed_ref[...] + total) * ocean_ref[...]
    columns_ref[...] = columns
    first_ref[...], second_ref[...] = lon_messages(flag_ref, columns)


def scatter_kernel(
    returned_ref, cell_ref, weight_ref, adjoint_ref, mask_ref, out_ref, edges_ref, rows_ref
):
    levels_n, rows_n, cols_n = out_ref.shape
    groups = rows_n // GROUP
    tile = rows_ref.shape[1]
    total = jnp.zeros((levels_n * GROUP, groups * cols_n), jnp.float32)
    for start in range(0, cell_ref.shape[1], tile):
        at = slice(start, start + tile)
        values = returned_values(returned_ref, cell_ref, weight_ref, levels_n, start, tile)
        place, member = cell_parts(cell_ref[:, at], rows_n, cols_n)
        hot, member = one_hot(place, groups * cols_n), one_hot(member, GROUP)
        for part, piece in enumerate(values):
            for level in range(levels_n):
                begin = (part * levels_n + level) * GROUP
                rows_ref[begin : begin + GROUP, :] = member * piece[level : level + 1, :]
        for part in range(len(values)):
            begin = part * levels_n * GROUP
            total += across(rows_ref[begin : begin + levels_n * GROUP, :], hot)
    for group in range(groups):
        at = slice(group * GROUP, (group + 1) * GROUP)
        forcing = total[:, group * cols_n : (group + 1) * cols_n].reshape(levels_n, GROUP, cols_n)
        out_ref[:, at, :] = adjoint_ref[:, at, :] + forcing
    places, levels, _ = edges_ref.shape
    for place, row in enumerate((0, 1, rows_n - 2, rows_n - 1)):
        ocean = mask_ref[row : row + 1, :].astype(jnp.float32)
        for level in range(levels_n):
            edges_ref[place, level : level + 1, :] = out_ref[level, row : row + 1, :] * ocean
        edges_ref[place, levels_n:, :] = jnp.zeros((levels - levels_n, cols_n), jnp.float32)


def beside_kernel(
    flag_ref, seed_ref, field_ref, side_ref, columns_ref, second_ref, first_ref,
    half_ref, masked_ref, turn_ref,
    from_ref,
):
    levels_n, rows_n, cols_n = seed_ref.shape
    east, west = lon_columns(flag_ref, first_ref[...], second_ref[...])
    own = columns_ref[...]
    level_at = jnp.right_shift(lane((rows_n, cols_n)), 2)

    slot = jnp.bitwise_and(lane((rows_n, cols_n)), 3)
    block = jnp.where(slot < 2, west, east)
    eastern = pltpu.roll(jnp.where(slot == 3, east, own), cols_n - 1, 1)
    western = pltpu.roll(jnp.where(slot == 0, west, own), 1, 1)
    higher = jnp.where(level_at > 0, pltpu.roll(block, 4, 1) - block, 0.0)
    lower = jnp.where(level_at < levels_n - 1, pltpu.roll(block, cols_n - 4, 1) - block, 0.0)
    change = (
        side_ref[2] * eastern
        + side_ref[3] * western
        + side_ref[4] * shifted(block, -1, 0, 0.0)
        + side_ref[5] * shifted(block, 1, 0, 0.0)
        - side_ref[1] * block
        + side_ref[6] * (higher + lower)
    )
    changed = block + side_ref[0] * change
    turn_ref[...] = turned_columns(changed, changed)
    for top in range(0, rows_n, SUB):
        at = slice(top, top + SUB)
        for level in range(levels_n):
            from_ref[level, at, :] = field_ref[0, at, :] * seed_ref[level, at, :]
    none = [jnp.zeros((1, cols_n), jnp.float32)] * levels_n

    def store(level, top, found):
        at = slice(top, top + SUB)
        half_ref[level, at, :] = found
        masked_ref[level, at, :] = field_ref[0, at, :] * found

    advance(seed_ref, from_ref, field_ref, turned_columns(east, west), none, none, store)


def turned_columns(eastern, western):
    slot = jnp.bitwise_and(lane(eastern.shape), 3)
    cols_n = eastern.shape[1]
    return jnp.where(slot == 1, pltpu.roll(eastern, cols_n - 1, 1), pltpu.roll(western, 1, 1))


def advance(source_ref, from_ref, field_ref, turn, below, above, store, patch=None):
    levels_n, rows_n, cols_n = source_ref.shape
    place = sublane((SUB, cols_n))
    first = lane((SUB, cols_n)) == 0
    last = lane((SUB, cols_n)) == cols_n - 1
    for top in range(0, rows_n, SUB):
        at = slice(top, top + SUB)
        bottom, ceiling = top == 0, top == rows_n - SUB
        ocean, own, here, back, onto, south_at, mixing = (
            field_ref[part, at, :] for part in range(7)
        )
        extra = None
        if patch is not None and (bottom or ceiling):
            south_row, north_row, added_below, added_above = patch
            if bottom:
                south_at = jnp.where(place == 0, south_row, south_at)
                own = jnp.where(place == 0, own + south_row, own)
                extra = [jnp.where(place == 0, row, 0.0) for row in added_below]
            else:
                onto = jnp.where(place == SUB - 1, north_row, onto)
                extra = [jnp.where(place == SUB - 1, row, 0.0) for row in added_above]

        def block_of(level):
            block = from_ref[level, at, :]
            return block if extra is None else block + ocean * extra[level]

        higher = block = block_of(0)
        for level in range(levels_n):
            lower = block_of(level + 1) if level + 1 < levels_n else block
            eastern, western = pltpu.roll(block, cols_n - 1, 1), pltpu.roll(block, 1, 1)
            beyond = pltpu.roll(turn[at], (2 * cols_n - 2 - 4 * level) % cols_n, 1)
            sides = here * jnp.where(last, beyond, eastern) + back * jnp.where(first, beyond, western)
            if ceiling:
                north = shifted(block, -1, 0, above[level])
            else:
                north = from_ref[level, top + 1 : top + SUB + 1, :]
            if bottom:
                south = shifted(block, 1, 0, below[level])
            else:
                south = from_ref[level, top - 1 : top + SUB - 1, :]
            source = source_ref[level, at, :]
            if extra is not None:
                source = source + extra[level]
            vertical = (higher - block) + (lower - block)
            found = (
                (source - own * block)
                + sides
                + (onto * north + south_at * south)
                + mixing * vertical
            )
            store(level, top, found)
            higher, block = block, lower


def lane(shape):
    return lax.broadcasted_iota(jnp.int32, shape, 1)


def sublane(shape):
    return lax.broadcasted_iota(jnp.int32, shape, 0)


def shifted(block, steps, axis, edge):
    size = block.shape[axis]
    at = lax.broadcasted_iota(jnp.int32, block.shape, axis)
    moved = pltpu.roll(block, steps % size, axis)
    return jnp.where(at == (0 if steps > 0 else size - 1), edge, moved)


def reversed_lanes(block):
    at = block.shape[1] - 1 - lane(block.shape)
    return jnp.take_along_axis(block, at, axis=1, mode="promise_in_bounds")


def by_flag(flag_ref, place, chosen, other):
    flag = jnp.broadcast_to(flag_ref[place : place + 1, : chosen.shape[1]], chosen.shape)
    return jnp.where(flag == 1, chosen, other)


def lon_neighbours(flag_ref, first, second):
    return by_flag(flag_ref, 0, first, second), by_flag(flag_ref, 0, second, first)


def lon_columns(flag_ref, first, second):
    east, west = lon_neighbours(flag_ref, first, second)
    east = jnp.concatenate([pltpu.roll(east, 2, 1), east], axis=0)
    west = jnp.concatenate([west, pltpu.roll(west, LANES - 2, 1)], axis=0)
    return east, west


def lon_messages(flag_ref, columns):
    low, high = columns[: columns.shape[0] // 2], columns[columns.shape[0] // 2 :]
    left = jnp.bitwise_and(lane(low.shape), 3) < 2
    eastward = jnp.where(left, low, pltpu.roll(high, 2, 1))
    westward = jnp.where(left, pltpu.roll(low, LANES - 2, 1), high)
    return lon_neighbours(flag_ref, eastward, westward)


def lat_neighbours(flag_ref, first, second):
    return by_flag(flag_ref, 1, first, second), by_flag(flag_ref, 1, second, first)


def side_columns(flag_ref, first_ref, second_ref):
    filler = jnp.zeros((first_ref.shape[1] - first_ref.shape[0], first_ref.shape[1]), jnp.float32)
    east, west = lon_neighbours(flag_ref, first_ref[...], second_ref[...])
    return tuple(jnp.concatenate([block, filler], axis=0).T for block in (east, west))


def coefficient_columns_kernel(mask_ref, east_ref, north_ref, flow_ref, vertical_ref, out_ref):
    rows_n, cols_n = mask_ref.shape
    ocean = mask_ref[...].astype(jnp.float32)
    here = east_ref[...] + 0.5 * flow_ref[...]
    behind = east_ref[...] - 0.5 * flow_ref[...]
    north, vertical = north_ref[...], vertical_ref[...]
    last = cols_n - 1
    wanted = (
        (ocean, 0), (here, 0), (north, 0), (vertical, 0),
        (ocean, last), (here, last), (behind, last), (behind, last - 1), (north, last), (vertical, last),
    )
    found = jnp.zeros((rows_n, cols_n), jnp.float32)
    for place, (field, column) in enumerate(wanted):
        found = jnp.where(
            lane(found.shape) == place, pltpu.roll(field, (place - column) % cols_n, 1), found
        )
    out_ref[...] = found.T[: out_ref.shape[0]]


def coefficients_kernel(
    flag_ref, mask_ref, east_ref, north_ref, flow_ref, vertical_ref, lon_first_ref, lon_second_ref,
    field_ref, side_ref, row_ref,
):
    rows_n, cols_n = mask_ref.shape
    east, west = side_columns(flag_ref, lon_first_ref, lon_second_ref)
    ocean = mask_ref[...].astype(jnp.float32)
    here = east_ref[...] + 0.5 * flow_ref[...]
    behind = east_ref[...] - 0.5 * flow_ref[...]
    north, vertical = north_ref[...], vertical_ref[...]
    back = shifted(behind, 1, 1, west[:, 6:7])
    south = shifted(north, 1, 0, 0.0)
    parts = (ocean, here + back + north + south, here, back, north, south, vertical)
    for place, part in enumerate(parts):
        field_ref[place] = part

    def side(ocean, here, back, north, vertical):
        south = shifted(north, 1, 0, 0.0)
        return ocean, here + back + north + south, here, back, north, south, vertical

    def spread(columns, place):
        return jnp.broadcast_to(columns[:, place : place + 1], (columns.shape[0], cols_n))

    eastern = side(
        spread(east, 0), spread(east, 1), spread(behind, cols_n - 1), spread(east, 2), spread(east, 3)
    )
    western = side(
        spread(west, 4), spread(west, 5), spread(west, 7), spread(west, 8), spread(west, 9)
    )
    slot = jnp.bitwise_and(lane((rows_n, cols_n)), 3)
    for place in range(len(eastern)):
        side_ref[place] = jnp.where(slot < 2, western[place], eastern[place])

    top, last = slice(0, 1), slice(rows_n - 1, rows_n)
    rows = []
    for at in (top, last):
        rows += [ocean[at], here[at], back[at], north[at]]
        if at is last:
            rows.append(north[rows_n - 2 : rows_n - 1])
        rows.append(vertical[at])
    rows += [east[top], east[last], west[top], west[last]]
    for place, row in enumerate(rows):
        row_ref[place : place + 1, :] = row
    row_ref[len(rows) :, :] = jnp.zeros((row_ref.shape[0] - len(rows), cols_n), jnp.float32)


def edge_message_kernel(
    levels_n, flag_ref, edges_ref, lon_second_ref, lon_first_ref, row_ref, second_ref, first_ref
):
    places, levels, cols_n = edges_ref.shape
    begin = row_ref.shape[0] + 2
    for ref in (first_ref, second_ref):
        ref[: row_ref.shape[0], :] = row_ref[...]
        ref[begin + 2 * levels_n :, :] = jnp.zeros((ref.shape[0] - begin - 2 * levels_n, cols_n), jnp.float32)
    for place, (north, south) in enumerate(((places - 1, 0), (places - 2, 1))):
        at = slice(begin + place * levels_n, begin + (place + 1) * levels_n)
        northern, southern = edges_ref[north][:levels_n], edges_ref[south][:levels_n]
        first_ref[at, :] = by_flag(flag_ref, 1, northern, southern)
        second_ref[at, :] = by_flag(flag_ref, 1, southern, northern)
    east, west = lon_columns(flag_ref, lon_first_ref[...], lon_second_ref[...])
    northern = east[-1:], west[-1:]
    southern = east[:1], west[:1]
    for place in range(2):
        at = slice(begin - 2 + place, begin - 1 + place)
        first_ref[at, :] = by_flag(flag_ref, 1, northern[place], southern[place])
        second_ref[at, :] = by_flag(flag_ref, 1, southern[place], northern[place])


def steps_kernel(
    flag_ref, half_ref, masked_ref, turn_in_ref, field_ref, side_ref,
    edges_ref, lon_second_ref, lon_first_ref, lat_first_ref, lat_second_ref,
    out_ref,
    done_ref, turn_ref, edge_ref, sems,
):
    levels_n, rows_n, cols_n = half_ref.shape
    levels = edges_ref.shape[1]
    up, down = lat_neighbours(flag_ref, lat_first_ref[...], lat_second_ref[...])

    ends = 2 * SUB
    east_up = by_flag(flag_ref, 2, pltpu.roll(up[ends + 1 : ends + 2], 1, 1), up[ends : ends + 1])
    west_up = by_flag(flag_ref, 2, pltpu.roll(up[ends : ends + 1], cols_n - 1, 1), up[ends + 1 : ends + 2])
    east_down, west_down = down[ends : ends + 1], down[ends + 1 : ends + 2]

    up_rows, down_rows = up[:ends], down[:ends]
    turned = reversed_lanes(up_rows)
    into = field_ref[4, rows_n - 1 : rows_n, :]
    south_row = down_rows[8:9]
    north_row = by_flag(flag_ref, 2, turned[8:9], into)
    plain = (
        up_rows[0:1], up_rows[1:2] + up_rows[2:3] + up_rows[3:4] + into,
        up_rows[1:2], up_rows[2:3], into, up_rows[3:4], up_rows[4:5],
    )
    folded = (
        turned[5:6], turned[6:7] + turned[7:8] + turned[8:9] + turned[9:10],
        turned[7:8], turned[6:7], into, turned[9:10], turned[10:11],
    )
    low = (
        down_rows[5:6], down_rows[6:7] + down_rows[7:8] + down_rows[8:9] + down_rows[9:10],
        down_rows[6:7], down_rows[7:8], down_rows[8:9], down_rows[9:10], down_rows[10:11],
    )
    for place in range(len(plain)):
        edge_ref[place : place + 1, :] = by_flag(flag_ref, 2, folded[place], plain[place])
        edge_ref[SUB + place : SUB + place + 1, :] = low[place]

    east, west = lon_columns(flag_ref, lon_first_ref[0:1, :], lon_second_ref[0:1, :])
    east, west = east[:1], west[:1]
    east_low = side_ref[0, 0:1, 2:3] * down_rows[12:13, 2:3] * (east_down - east)
    west_low = side_ref[0, 0:1, 1:2] * down_rows[14:15, 8:9] * (west_down - west)
    at = slice(rows_n - 1, rows_n)
    east_onto = by_flag(flag_ref, 2, up_rows[14:15, 8:9], side_ref[4, at, 2:3])
    west_onto = by_flag(flag_ref, 2, up_rows[12:13, 2:3], side_ref[4, at, 1:2])
    east_high = side_ref[0, at, 2:3] * east_onto * east_up
    west_high = side_ref[0, at, 1:2] * west_onto * west_up
    turn_ref[...] = turn_in_ref[...]
    turn_ref[0:1, :] = turn_in_ref[0:1, :] + turned_columns(east_low, west_low)
    turn_ref[at, :] = turn_in_ref[at, :] + turned_columns(east_high, west_high)

    plane = (levels, cols_n)
    corner_at = 4 * sublane(plane)

    def corner(row, place):
        found = jnp.where(lane(plane) == corner_at + place, jnp.broadcast_to(row, plane), 0.0)
        return jnp.sum(found, axis=1, keepdims=True)

    def edge(block, place):
        begin = ends + 2 + place * levels_n
        filler = jnp.zeros((levels - levels_n, cols_n), jnp.float32)
        return jnp.concatenate([block[begin : begin + levels_n], filler], axis=0)

    def edge_step(block, outer, inner, eastern, western, base):
        def coefficient(place):
            return edge_ref[base + place : base + place + 1, :]

        level = sublane(plane)
        higher = jnp.where(level > 0, pltpu.roll(block, 1, 0) - block, 0.0)
        lower = jnp.where(level < levels_n - 1, pltpu.roll(block, levels - 1, 0) - block, 0.0)
        change = (
            coefficient(2) * shifted(block, -1, 1, eastern)
            + coefficient(3) * shifted(block, 1, 1, western)
            + coefficient(4) * inner
            + coefficient(5) * outer
            - coefficient(1) * block
            + coefficient(6) * (higher + lower)
        )
        return block + coefficient(0) * change

    above = by_flag(flag_ref, 2, reversed_lanes(edge(up, 0)), edge(up, 0))
    above_outer = by_flag(flag_ref, 2, reversed_lanes(edge(up, 1)), edge(up, 1))
    below, below_outer = edge(down, 0), edge(down, 1)
    above_next = edge_step(
        above, above_outer, edges_ref[3], corner(east_up, 2), corner(west_up, 1), 0
    )
    below_next = edge_step(
        below, below_outer, edges_ref[0], corner(east_down, 2), corner(west_down, 1), SUB
    )
    def rows_of(block):
        return [block[level : level + 1] for level in range(levels_n)]

    patch = (
        south_row, north_row, rows_of(south_row * (below - edges_ref[0])), rows_of(north_row * above)
    )
    copies = []

    def store(level, top, found):
        done_ref[level, top : top + SUB, :] = found
        if level == levels_n - 1 and (top + SUB) % (rows_n // sems.shape[0]) == 0:
            rows = slice(top + SUB - rows_n // sems.shape[0], top + SUB)
            copy = pltpu.make_async_copy(
                done_ref.at[:, rows, :], out_ref.at[:, rows, :], sems.at[len(copies)]
            )
            copy.start()
            copies.append(copy)

    advance(
        half_ref, masked_ref, field_ref, turn_ref, rows_of(below_next), rows_of(above_next), store, patch
    )
    for copy in copies:
        copy.wait()


def kernel_call(mebibytes, body, out_shape, scratch=(), ins=None, outs=None):
    memory = {}
    if ins is not None:
        memory["in_specs"] = [pl.BlockSpec(memory_space=space) for space in ins]
    if outs is not None:
        spec = pl.BlockSpec(memory_space=outs)
        memory["out_specs"] = (spec,) * len(out_shape) if isinstance(out_shape, tuple) else spec
    return pl.pallas_call(
        body,
        out_shape=out_shape,
        scratch_shapes=list(scratch),
        compiler_params=pltpu.CompilerParams(vmem_limit_bytes=mebibytes * MIB),
        **memory,
    )


def exchanged(value, devices):
    rows = value.reshape(devices, 1, value.size // devices)
    return lax.all_to_all(rows, BOTH, split_axis=0, concat_axis=0, tiled=True).reshape(value.shape)


def f32(*shape):
    return jax.ShapeDtypeStruct(shape, jnp.float32)


def lon_swaps(first_value, second_value):
    count = lax.axis_size("lon")
    assert count % 2 == 0
    first = [(i, i ^ 1) for i in range(count)]
    second = [(i, (i + 1 if i % 2 else i - 1) % count) for i in range(count)]
    second_found = lax.ppermute(second_value, "lon", second)
    return lax.ppermute(first_value, "lon", first), second_found


def lat_swaps(*values):
    lons, lats = lax.axis_size("lon"), lax.axis_size("lat")
    found = []
    for parity in (0, 1):
        pairs = []
        for i in range(lons):
            for j in range(lats):
                other = j + 1 if j % 2 == parity else j - 1
                if other == lats:
                    pairs.append((i * lats + j, (lons - 1 - i) * lats + j))
                elif other >= 0:
                    pairs.append((i * lats + j, i * lats + other))
        found.append(lax.ppermute(values[parity], BOTH, pairs))
    return tuple(found)


def on_device(
    state,
    adjoint_in,
    land_mask,
    east_coef,
    north_coef,
    zonal_flow,
    vertical_coef,
    slot_cell,
    slot_weight,
    arrive_obs,
    obs_value,
    obs_invvar,
):
    levels_n, rows_n, cols_n = state.shape
    devices = lax.axis_size(BOTH)
    slots = slot_cell.shape[1]
    obs_n = obs_value.shape[1]
    assert 2 * (slots // devices) == LANES and cols_n == LANES and 4 * levels_n <= LANES
    half = (levels_n + 1) // 2
    width = rows_n // GROUP * cols_n
    tile = min(slots, SLOT_TILE)
    tiles = slots // tile
    bf16 = jnp.bfloat16
    raw = (land_mask, east_coef, north_coef, zonal_flow, vertical_coef)
    lon, lat = lax.axis_index("lon"), lax.axis_index("lat")
    flags = jnp.stack([1 - lon % 2, 1 - lat % 2, lat == lax.axis_size("lat") - 1]).astype(jnp.int32)
    flags = jnp.broadcast_to(flags[:, None], (3, LANES))

    partial_vals = kernel_call(
        60,
        gather_kernel,
        f32(devices * half, LANES),
        [
            pltpu.VMEM((1, slots), jnp.int32),
            pltpu.VMEM((1, slots), jnp.float32),
            pltpu.VMEM((levels_n, rows_n, cols_n), jnp.float32),
            pltpu.VMEM((levels_n * GROUP, 3 * width), bf16),
            pltpu.SemaphoreType.DMA((2 + levels_n,)),
        ],
        [pltpu.HBM] * 3,
    )(slot_cell, slot_weight, state)
    levels = padded_levels(levels_n)
    partial_vals, raw = lax.optimization_barrier((partial_vals, raw))
    arrived = exchanged(partial_vals, devices)
    columns = kernel_call(4, coefficient_columns_kernel, f32(2 * SUB, rows_n))(*raw)
    arrived, side_coefs = lax.optimization_barrier((arrived, lon_swaps(columns, columns)))

    misfit, outgoing = kernel_call(
        8 + 4 * tiles,
        observe_kernel,
        (f32(levels_n, obs_n), f32(devices * half, LANES)),
        [
            pltpu.VMEM((obs_n, slots), bf16),
            pltpu.VMEM((levels_n, obs_n), jnp.float32),
            pltpu.VMEM((devices * half, LANES), jnp.float32),
            pltpu.SemaphoreType.DMA((5,)),
        ],
        [pltpu.VMEM] * 4, pltpu.HBM,
    )(arrived, arrive_obs, obs_value, obs_invvar)
    outgoing, raw, side_coefs, adjoint_early = lax.optimization_barrier(
        (outgoing, raw, side_coefs, adjoint_in)
    )
    returned = exchanged(outgoing, devices)
    strips = kernel_call(
        5,
        seed_columns_kernel,
        (f32(rows_n, cols_n), f32(rows_n, cols_n)),
    )(adjoint_early, raw[0])
    fields, sides, row_coefs = kernel_call(
        5,
        coefficients_kernel,
        (f32(7, rows_n, cols_n), f32(7, rows_n, cols_n), f32(2 * SUB, cols_n)),
        (),
    )(flags, *raw, *side_coefs)
    returned, strips, fields, sides, row_coefs = lax.optimization_barrier(
        (returned, strips, fields, sides, row_coefs)
    )
    for_second, for_first, own_columns = kernel_call(
        6 + 3 * tiles,
        functools.partial(columns_kernel, levels_n),
        (f32(rows_n // 2, cols_n), f32(rows_n // 2, cols_n), f32(rows_n, cols_n)),
    )(flags, returned, slot_cell, slot_weight, *strips)
    columns_beside = lon_swaps(for_first, for_second)[::-1]
    whole = (levels_n, rows_n, cols_n)
    seed, own_edges = kernel_call(
        22 + 3 * tiles,
        scatter_kernel,
        (f32(*whole), f32(4, levels, cols_n)),
        [pltpu.VMEM((2 * levels_n * GROUP, tile), bf16)],
    )(returned, slot_cell, slot_weight, adjoint_in, land_mask)
    seed, columns_beside = lax.optimization_barrier((seed, columns_beside))
    message = f32((2 * levels_n + 2 * SUB + 2 + SUB - 1) // SUB * SUB, cols_n)
    message_kernel = functools.partial(edge_message_kernel, levels_n)
    messages = kernel_call(2, message_kernel, (message, message), ())(
        flags, own_edges, *columns_beside, row_coefs
    )
    rows_beside = lat_swaps(messages[1], messages[0])
    seed, messages = lax.optimization_barrier((seed, messages))
    beside = kernel_call(
        8,
        beside_kernel,
        (f32(*whole), f32(*whole), f32(rows_n, cols_n)),
        [pltpu.VMEM(whole, jnp.float32)],
    )(flags, seed, fields, sides, own_columns, *columns_beside)
    beside, rows_beside = lax.optimization_barrier((beside, rows_beside))
    adjoint_state = kernel_call(
        10,
        steps_kernel,
        f32(*whole),
        [
            pltpu.VMEM(whole, jnp.float32),
            pltpu.VMEM((rows_n, cols_n), jnp.float32),
            pltpu.VMEM((2 * SUB, cols_n), jnp.float32),
            pltpu.SemaphoreType.DMA((8,)),
        ],
        [pltpu.VMEM] * 11, pltpu.HBM,
    )(flags, *beside, fields, sides, own_edges, *columns_beside, *rows_beside)
    return (adjoint_state, misfit)


def solution(mesh):
    in_specs = (
        P(None, "lat", "lon"),
        P(None, "lat", "lon"),
        P("lat", "lon"),
        P("lat", "lon"),
        P("lat", "lon"),
        P("lat", "lon"),
        P("lat", "lon"),
        P(("lon", "lat"), None),
        P(("lon", "lat"), None),
        P(("lon", "lat"), None),
        P(None, ("lon", "lat")),
        P(None, ("lon", "lat")),
    )
    out_specs = (P(None, "lat", "lon"), P(None, ("lon", "lat")))
    return jax.shard_map(
        on_device, mesh=mesh, in_specs=in_specs, out_specs=out_specs, check_vma=False
    )
```

```python
import functools

import jax
import jax.numpy as jnp
from jax import lax
from jax.experimental import pallas as pl
from jax.experimental.pallas import tpu as pltpu
from jax.sharding import PartitionSpec as P

LANES = 128
GROUP = 32
SUB = 8
SLOT_TILE = 16 * LANES
MIB = 1024 * 1024
BOTH = ("lon", "lat")


def pieces(value):
    high = value.astype(jnp.bfloat16)
    rest = value - high.astype(jnp.float32)
    middle = rest.astype(jnp.bfloat16)
    low = (rest - middle.astype(jnp.float32)).astype(jnp.bfloat16)
    return high, middle, low


def log2(size):
    assert size & (size - 1) == 0
    return size.bit_length() - 1


def cell_parts(cell, rows_n, cols_n):
    cell = jnp.maximum(cell, 0)
    row = jnp.right_shift(cell, log2(cols_n))
    group = jnp.right_shift(row, log2(GROUP))
    place = jnp.bitwise_and(cell, cols_n - 1) + group * cols_n
    return place, jnp.bitwise_and(row, GROUP - 1)


def one_hot(index, size):
    rows = lax.broadcasted_iota(jnp.int32, (size, index.shape[1]), 0)
    return jnp.where(rows == index, 1.0, 0.0).astype(jnp.bfloat16)


def first_half(rows):
    return lane((rows, LANES)) < LANES // 2


def pack(values, out_ref, first_pair):
    half = values.shape[0] // 2
    for pair in range(values.shape[1] // LANES):
        block = values[:, pair * LANES : (pair + 1) * LANES]
        top, bottom = block[:half], block[half:]
        at = 2 * (first_pair + pair) * half
        out_ref[at : at + half, :] = jnp.where(
            first_half(half), top, pltpu.roll(bottom, LANES // 2, 1)
        )
        out_ref[at + half : at + 2 * half, :] = jnp.where(
            first_half(half), pltpu.roll(top, LANES // 2, 1), bottom
        )


def unpack(in_ref, half, first_pair, pairs, levels):
    found = []
    for pair in range(first_pair, first_pair + pairs):
        at = 2 * pair * half
        left, right = in_ref[at : at + half, :], in_ref[at + half : at + 2 * half, :]
        top = jnp.where(first_half(half), left, pltpu.roll(right, LANES // 2, 1))
        bottom = jnp.where(first_half(half), pltpu.roll(left, LANES // 2, 1), right)
        filler = jnp.zeros((levels - 2 * half, LANES), jnp.float32)
        found.append(jnp.concatenate([top, bottom, filler], axis=0))
    return jnp.concatenate(found, axis=1)


def gather_kernel(
    cell_in, weight_in, state_in, out_ref, cell_ref, weight_ref, state_ref, field_ref, sems
):
    levels_n, rows_n, cols_n = state_ref.shape
    groups = rows_n // GROUP
    width = groups * cols_n
    slots = cell_ref.shape[1]
    tile = min(slots, SLOT_TILE)
    chunk = levels_n
    copies = [
        pltpu.make_async_copy(cell_in, cell_ref, sems.at[0]),
        pltpu.make_async_copy(weight_in, weight_ref, sems.at[1]),
    ]
    step = max(n for n in range(1, 9) if levels_n % n == 0)
    for place, level in enumerate(range(0, levels_n, step)):
        at = slice(level, level + step)
        copies.append(pltpu.make_async_copy(state_in.at[at], state_ref.at[at], sems.at[2 + place]))
    for copy in copies:
        copy.start()
    copies[0].wait()
    for start in range(0, slots, tile):
        cell = cell_ref[:, start : start + tile]
        place, row = cell_parts(cell, rows_n, cols_n)
        hot = one_hot(place, width)
        hot = jnp.concatenate([hot, hot, hot], axis=0)
        mine = sublane((GROUP, tile)) == row
        values = []
        for level in range(0, levels_n, chunk):
            at = slice(level * GROUP, (level + chunk) * GROUP)
            if start == 0:
                for copy in copies[2:]:
                    copy.wait()
                for group in range(groups):
                    block = state_ref[
                        level : level + chunk, group * GROUP : (group + 1) * GROUP, :
                    ].reshape(chunk * GROUP, cols_n)
                    for part, piece in enumerate(pieces(block)):
                        begin = part * width + group * cols_n
                        field_ref[at, begin : begin + cols_n] = piece
            found = jnp.dot(field_ref[at, :], hot, preferred_element_type=jnp.float32)
            found = found.reshape(chunk, GROUP, tile)
            values.append(jnp.sum(jnp.where(mine[None], found, 0.0), axis=1))
        if start == 0:
            copies[1].wait()
        weight = jnp.where(cell >= 0, weight_ref[:, start : start + tile], 0.0)
        if levels_n % 2:
            values.append(jnp.zeros((1, tile), jnp.float32))
        pack(jnp.concatenate(values, axis=0) * weight, out_ref, start // LANES)


def observe_kernel(
    arrived_ref, target_ref, value_ref, invvar_ref, misfit_out, out_ref, hot_ref, misfit_ref, part_ref, sems
):
    levels_n, obs_n = value_ref.shape
    half = (levels_n + 1) // 2
    levels = padded_levels(levels_n)
    slots = hot_ref.shape[1]
    tile = min(slots, SLOT_TILE)
    sums = None
    for start in range(0, slots, tile):
        hot = one_hot(target_ref[:, start : start + tile], obs_n)
        hot_ref[:, start : start + tile] = hot
        values = unpack(arrived_ref, half, start // LANES, tile // LANES, levels)
        found = across(jnp.concatenate(pieces(values), axis=0), hot)
        sums = found if sums is None else sums + found
    interp = sums[:levels] + sums[levels : 2 * levels] + sums[2 * levels :]
    misfit = invvar_ref[...] * (interp[:levels_n] - value_ref[...])
    misfit_ref[...] = misfit
    copies = [pltpu.make_async_copy(misfit_ref, misfit_out, sems.at[0])]
    copies[0].start()
    filler = jnp.zeros((levels - levels_n, obs_n), jnp.float32)
    back = jnp.concatenate(pieces(jnp.concatenate([misfit, filler], axis=0)), axis=0)
    part = slots // (sems.shape[0] - 1)
    rows_n = part_ref.shape[0] * part // slots
    for index in range(slots // part):
        start = index * part
        found = jnp.dot(
            back, hot_ref[:, start : start + part], preferred_element_type=jnp.float32
        )
        values = found[:levels] + found[levels : 2 * levels] + found[2 * levels :]
        pack(values[: 2 * half], part_ref, start // LANES)
        rows = slice(index * rows_n, (index + 1) * rows_n)
        copies.append(pltpu.make_async_copy(part_ref.at[rows], out_ref.at[rows], sems.at[index + 1]))
        copies[-1].start()
    for copy in copies:
        copy.wait()


def padded_levels(levels_n):
    return (levels_n + 15) // 16 * 16


def returned_values(returned_ref, cell_ref, weight_ref, levels_n, start, tile):
    at = slice(start, start + tile)
    weight = jnp.where(cell_ref[:, at] >= 0, weight_ref[:, at], 0.0)
    values = unpack(
        returned_ref, (levels_n + 1) // 2, start // LANES, tile // LANES, padded_levels(levels_n)
    )
    return pieces(values * weight)[:2]


def across(left, right):
    return lax.dot_general(
        left, right, (((1,), (1,)), ((), ())), preferred_element_type=jnp.float32
    )


def seed_columns_kernel(adjoint_ref, mask_ref, columns_ref, ocean_ref):
    levels_n, rows_n, cols_n = adjoint_ref.shape
    level_at = jnp.right_shift(lane((SUB, cols_n)), 2)
    for top in range(0, rows_n, SUB):
        at = slice(top, top + SUB)
        found = jnp.zeros((SUB, cols_n), jnp.float32)
        for level in range(levels_n):
            block = pltpu.roll(adjoint_ref[level, at, :], (4 * level + 2) % cols_n, 1)
            found = jnp.where(level_at == level, block, found)
        columns_ref[at, :] = found
        spread = jnp.where(level_at == 0, pltpu.roll(mask_ref[at, :].astype(jnp.float32), 2, 1), 0.0)
        shift = 4
        while shift < cols_n:
            spread = spread + pltpu.roll(spread, shift, 1)
            shift *= 2
        ocean_ref[at, :] = spread


def columns_kernel(
    levels_n, flag_ref, returned_ref, cell_ref, weight_ref, seed_ref, ocean_ref,
    second_ref, first_ref, columns_ref,
):
    rows_n, cols_n = seed_ref.shape
    levels = padded_levels(levels_n)
    slots = cell_ref.shape[1]
    tile = min(slots, SLOT_TILE)
    total = jnp.zeros((rows_n, LANES), jnp.float32)
    for start in range(0, slots, tile):
        cell = jnp.maximum(cell_ref[:, start : start + tile], 0)
        row, column = jnp.right_shift(cell, log2(cols_n)), jnp.bitwise_and(cell, cols_n - 1)
        hot = one_hot(row, rows_n)
        for piece in returned_values(returned_ref, cell_ref, weight_ref, levels_n, start, tile):
            chosen = [
                piece * jnp.where(column == wanted, 1.0, 0.0).astype(jnp.bfloat16)
                for wanted in (cols_n - 2, cols_n - 1, 0, 1)
            ]
            total += across(hot, jnp.concatenate(chosen, axis=0))
    source, target = sublane((LANES, LANES)), lane((LANES, LANES))
    turn = jnp.bitwise_and(target, 3) * levels + jnp.right_shift(target, 2)
    turn = jnp.where(source == turn, 1.0, 0.0).astype(jnp.bfloat16)
    total = sum(jnp.dot(piece, turn, preferred_element_type=jnp.float32) for piece in pieces(total))
    columns = (seed_ref[...] + total) * ocean_ref[...]
    columns_ref[...] = columns
    first_ref[...], second_ref[...] = lon_messages(flag_ref, columns)


def scatter_kernel(
    returned_ref, cell_ref, weight_ref, adjoint_ref, mask_ref, out_ref, edges_ref, rows_ref
):
    levels_n, rows_n, cols_n = out_ref.shape
    groups = rows_n // GROUP
    tile = rows_ref.shape[1]
    total = jnp.zeros((levels_n * GROUP, groups * cols_n), jnp.float32)
    for start in range(0, cell_ref.shape[1], tile):
        at = slice(start, start + tile)
        values = returned_values(returned_ref, cell_ref, weight_ref, levels_n, start, tile)
        place, member = cell_parts(cell_ref[:, at], rows_n, cols_n)
        hot, member = one_hot(place, groups * cols_n), one_hot(member, GROUP)
        for part, piece in enumerate(values):
            for level in range(levels_n):
                begin = (part * levels_n + level) * GROUP
                rows_ref[begin : begin + GROUP, :] = member * piece[level : level + 1, :]
        for part in range(len(values)):
            begin = part * levels_n * GROUP
            total += across(rows_ref[begin : begin + levels_n * GROUP, :], hot)
    for group in range(groups):
        at = slice(group * GROUP, (group + 1) * GROUP)
        forcing = total[:, group * cols_n : (group + 1) * cols_n].reshape(levels_n, GROUP, cols_n)
        out_ref[:, at, :] = adjoint_ref[:, at, :] + forcing
    places, levels, _ = edges_ref.shape
    for place, row in enumerate((0, 1, rows_n - 2, rows_n - 1)):
        ocean = mask_ref[row : row + 1, :].astype(jnp.float32)
        for level in range(levels_n):
            edges_ref[place, level : level + 1, :] = out_ref[level, row : row + 1, :] * ocean
        edges_ref[place, levels_n:, :] = jnp.zeros((levels - levels_n, cols_n), jnp.float32)


def beside_kernel(
    flag_ref, seed_ref, field_ref, side_ref, columns_ref, second_ref, first_ref,
    half_ref, masked_ref, turn_ref,
    from_ref,
):
    levels_n, rows_n, cols_n = seed_ref.shape
    east, west = lon_columns(flag_ref, first_ref[...], second_ref[...])
    own = columns_ref[...]
    level_at = jnp.right_shift(lane((rows_n, cols_n)), 2)

    slot = jnp.bitwise_and(lane((rows_n, cols_n)), 3)
    block = jnp.where(slot < 2, west, east)
    eastern = pltpu.roll(jnp.where(slot == 3, east, own), cols_n - 1, 1)
    western = pltpu.roll(jnp.where(slot == 0, west, own), 1, 1)
    higher = jnp.where(level_at > 0, pltpu.roll(block, 4, 1) - block, 0.0)
    lower = jnp.where(level_at < levels_n - 1, pltpu.roll(block, cols_n - 4, 1) - block, 0.0)
    change = (
        side_ref[2] * eastern
        + side_ref[3] * western
        + side_ref[4] * shifted(block, -1, 0, 0.0)
        + side_ref[5] * shifted(block, 1, 0, 0.0)
        - side_ref[1] * block
        + side_ref[6] * (higher + lower)
    )
    changed = block + side_ref[0] * change
    turn_ref[...] = turned_columns(changed, changed)
    for top in range(0, rows_n, SUB):
        at = slice(top, top + SUB)
        for level in range(levels_n):
            from_ref[level, at, :] = field_ref[0, at, :] * seed_ref[level, at, :]
    none = [jnp.zeros((1, cols_n), jnp.float32)] * levels_n

    def store(level, top, found):
        at = slice(top, top + SUB)
        half_ref[level, at, :] = found
        masked_ref[level, at, :] = field_ref[0, at, :] * found

    advance(seed_ref, from_ref, field_ref, turned_columns(east, west), none, none, store)


def turned_columns(eastern, western):
    slot = jnp.bitwise_and(lane(eastern.shape), 3)
    cols_n = eastern.shape[1]
    return jnp.where(slot == 1, pltpu.roll(eastern, cols_n - 1, 1), pltpu.roll(western, 1, 1))


def advance(source_ref, from_ref, field_ref, turn, below, above, store, patch=None):
    levels_n, rows_n, cols_n = source_ref.shape
    place = sublane((SUB, cols_n))
    first = lane((SUB, cols_n)) == 0
    last = lane((SUB, cols_n)) == cols_n - 1
    for top in range(0, rows_n, SUB):
        at = slice(top, top + SUB)
        bottom, ceiling = top == 0, top == rows_n - SUB
        ocean, own, here, back, onto, south_at, mixing = (
            field_ref[part, at, :] for part in range(7)
        )
        extra = None
        if patch is not None and (bottom or ceiling):
            south_row, north_row, added_below, added_above = patch
            if bottom:
                south_at = jnp.where(place == 0, south_row, south_at)
                own = jnp.where(place == 0, own + south_row, own)
                extra = [jnp.where(place == 0, row, 0.0) for row in added_below]
            else:
                onto = jnp.where(place == SUB - 1, north_row, onto)
                extra = [jnp.where(place == SUB - 1, row, 0.0) for row in added_above]

        def block_of(level):
            block = from_ref[level, at, :]
            return block if extra is None else block + ocean * extra[level]

        higher = block = block_of(0)
        for level in range(levels_n):
            lower = block_of(level + 1) if level + 1 < levels_n else block
            eastern, western = pltpu.roll(block, cols_n - 1, 1), pltpu.roll(block, 1, 1)
            beyond = pltpu.roll(turn[at], (2 * cols_n - 2 - 4 * level) % cols_n, 1)
            sides = here * jnp.where(last, beyond, eastern) + back * jnp.where(first, beyond, western)
            if ceiling:
                north = shifted(block, -1, 0, above[level])
            else:
                north = from_ref[level, top + 1 : top + SUB + 1, :]
            if bottom:
                south = shifted(block, 1, 0, below[level])
            else:
                south = from_ref[level, top - 1 : top + SUB - 1, :]
            source = source_ref[level, at, :]
            if extra is not None:
                source = source + extra[level]
            vertical = (higher - block) + (lower - block)
            found = (
                (source - own * block)
                + sides
                + (onto * north + south_at * south)
                + mixing * vertical
            )
            store(level, top, found)
            higher, block = block, lower


def lane(shape):
    return lax.broadcasted_iota(jnp.int32, shape, 1)


def sublane(shape):
    return lax.broadcasted_iota(jnp.int32, shape, 0)


def shifted(block, steps, axis, edge):
    size = block.shape[axis]
    at = lax.broadcasted_iota(jnp.int32, block.shape, axis)
    moved = pltpu.roll(block, steps % size, axis)
    return jnp.where(at == (0 if steps > 0 else size - 1), edge, moved)


def reversed_lanes(block):
    at = block.shape[1] - 1 - lane(block.shape)
    return jnp.take_along_axis(block, at, axis=1, mode="promise_in_bounds")


def by_flag(flag_ref, place, chosen, other):
    flag = jnp.broadcast_to(flag_ref[place : place + 1, : chosen.shape[1]], chosen.shape)
    return jnp.where(flag == 1, chosen, other)


def lon_neighbours(flag_ref, first, second):
    return by_flag(flag_ref, 0, first, second), by_flag(flag_ref, 0, second, first)


def lon_columns(flag_ref, first, second):
    east, west = lon_neighbours(flag_ref, first, second)
    east = jnp.concatenate([pltpu.roll(east, 2, 1), east], axis=0)
    west = jnp.concatenate([west, pltpu.roll(west, LANES - 2, 1)], axis=0)
    return east, west


def lon_messages(flag_ref, columns):
    low, high = columns[: columns.shape[0] // 2], columns[columns.shape[0] // 2 :]
    left = jnp.bitwise_and(lane(low.shape), 3) < 2
    eastward = jnp.where(left, low, pltpu.roll(high, 2, 1))
    westward = jnp.where(left, pltpu.roll(low, LANES - 2, 1), high)
    return lon_neighbours(flag_ref, eastward, westward)


def lat_neighbours(flag_ref, first, second):
    return by_flag(flag_ref, 1, first, second), by_flag(flag_ref, 1, second, first)


def side_columns(flag_ref, first_ref, second_ref):
    filler = jnp.zeros((first_ref.shape[1] - first_ref.shape[0], first_ref.shape[1]), jnp.float32)
    east, west = lon_neighbours(flag_ref, first_ref[...], second_ref[...])
    return tuple(jnp.concatenate([block, filler], axis=0).T for block in (east, west))


def coefficient_columns_kernel(mask_ref, east_ref, north_ref, flow_ref, vertical_ref, out_ref):
    rows_n, cols_n = mask_ref.shape
    ocean = mask_ref[...].astype(jnp.float32)
    here = east_ref[...] + 0.5 * flow_ref[...]
    behind = east_ref[...] - 0.5 * flow_ref[...]
    north, vertical = north_ref[...], vertical_ref[...]
    last = cols_n - 1
    wanted = (
        (ocean, 0), (here, 0), (north, 0), (vertical, 0),
        (ocean, last), (here, last), (behind, last), (behind, last - 1), (north, last), (vertical, last),
    )
    found = jnp.zeros((rows_n, cols_n), jnp.float32)
    for place, (field, column) in enumerate(wanted):
        found = jnp.where(
            lane(found.shape) == place, pltpu.roll(field, (place - column) % cols_n, 1), found
        )
    out_ref[...] = found.T[: out_ref.shape[0]]


def coefficients_kernel(
    flag_ref, mask_ref, east_ref, north_ref, flow_ref, vertical_ref, lon_first_ref, lon_second_ref,
    field_ref, side_ref, row_ref,
):
    rows_n, cols_n = mask_ref.shape
    east, west = side_columns(flag_ref, lon_first_ref, lon_second_ref)
    ocean = mask_ref[...].astype(jnp.float32)
    here = east_ref[...] + 0.5 * flow_ref[...]
    behind = east_ref[...] - 0.5 * flow_ref[...]
    north, vertical = north_ref[...], vertical_ref[...]
    back = shifted(behind, 1, 1, west[:, 6:7])
    south = shifted(north, 1, 0, 0.0)
    parts = (ocean, here + back + north + south, here, back, north, south, vertical)
    for place, part in enumerate(parts):
        field_ref[place] = part

    def side(ocean, here, back, north, vertical):
        south = shifted(north, 1, 0, 0.0)
        return ocean, here + back + north + south, here, back, north, south, vertical

    def spread(columns, place):
        return jnp.broadcast_to(columns[:, place : place + 1], (columns.shape[0], cols_n))

    eastern = side(
        spread(east, 0), spread(east, 1), spread(behind, cols_n - 1), spread(east, 2), spread(east, 3)
    )
    western = side(
        spread(west, 4), spread(west, 5), spread(west, 7), spread(west, 8), spread(west, 9)
    )
    slot = jnp.bitwise_and(lane((rows_n, cols_n)), 3)
    for place in range(len(eastern)):
        side_ref[place] = jnp.where(slot < 2, western[place], eastern[place])

    top, last = slice(0, 1), slice(rows_n - 1, rows_n)
    rows = []
    for at in (top, last):
        rows += [ocean[at], here[at], back[at], north[at]]
        if at is last:
            rows.append(north[rows_n - 2 : rows_n - 1])
        rows.append(vertical[at])
    rows += [east[top], east[last], west[top], west[last]]
    for place, row in enumerate(rows):
        row_ref[place : place + 1, :] = row
    row_ref[len(rows) :, :] = jnp.zeros((row_ref.shape[0] - len(rows), cols_n), jnp.float32)


def edge_message_kernel(
    levels_n, flag_ref, edges_ref, lon_second_ref, lon_first_ref, row_ref, second_ref, first_ref
):
    places, levels, cols_n = edges_ref.shape
    begin = row_ref.shape[0] + 2
    for ref in (first_ref, second_ref):
        ref[: row_ref.shape[0], :] = row_ref[...]
        ref[begin + 2 * levels_n :, :] = jnp.zeros((ref.shape[0] - begin - 2 * levels_n, cols_n), jnp.float32)
    for place, (north, south) in enumerate(((places - 1, 0), (places - 2, 1))):
        at = slice(begin + place * levels_n, begin + (place + 1) * levels_n)
        northern, southern = edges_ref[north][:levels_n], edges_ref[south][:levels_n]
        first_ref[at, :] = by_flag(flag_ref, 1, northern, southern)
        second_ref[at, :] = by_flag(flag_ref, 1, southern, northern)
    east, west = lon_columns(flag_ref, lon_first_ref[...], lon_second_ref[...])
    northern = east[-1:], west[-1:]
    southern = east[:1], west[:1]
    for place in range(2):
        at = slice(begin - 2 + place, begin - 1 + place)
        first_ref[at, :] = by_flag(flag_ref, 1, northern[place], southern[place])
        second_ref[at, :] = by_flag(flag_ref, 1, southern[place], northern[place])


def steps_kernel(
    flag_ref, half_ref, masked_ref, turn_in_ref, field_ref, side_ref,
    edges_ref, lon_second_ref, lon_first_ref, lat_first_ref, lat_second_ref,
    out_ref,
    done_ref, turn_ref, edge_ref, sems,
):
    levels_n, rows_n, cols_n = half_ref.shape
    levels = edges_ref.shape[1]
    up, down = lat_neighbours(flag_ref, lat_first_ref[...], lat_second_ref[...])

    ends = 2 * SUB
    east_up = by_flag(flag_ref, 2, pltpu.roll(up[ends + 1 : ends + 2], 1, 1), up[ends : ends + 1])
    west_up = by_flag(flag_ref, 2, pltpu.roll(up[ends : ends + 1], cols_n - 1, 1), up[ends + 1 : ends + 2])
    east_down, west_down = down[ends : ends + 1], down[ends + 1 : ends + 2]

    up_rows, down_rows = up[:ends], down[:ends]
    turned = reversed_lanes(up_rows)
    into = field_ref[4, rows_n - 1 : rows_n, :]
    south_row = down_rows[8:9]
    north_row = by_flag(flag_ref, 2, turned[8:9], into)
    plain = (
        up_rows[0:1], up_rows[1:2] + up_rows[2:3] + up_rows[3:4] + into,
        up_rows[1:2], up_rows[2:3], into, up_rows[3:4], up_rows[4:5],
    )
    folded = (
        turned[5:6], turned[6:7] + turned[7:8] + turned[8:9] + turned[9:10],
        turned[7:8], turned[6:7], into, turned[9:10], turned[10:11],
    )
    low = (
        down_rows[5:6], down_rows[6:7] + down_rows[7:8] + down_rows[8:9] + down_rows[9:10],
        down_rows[6:7], down_rows[7:8], down_rows[8:9], down_rows[9:10], down_rows[10:11],
    )
    for place in range(len(plain)):
        edge_ref[place : place + 1, :] = by_flag(flag_ref, 2, folded[place], plain[place])
        edge_ref[SUB + place : SUB + place + 1, :] = low[place]

    east, west = lon_columns(flag_ref, lon_first_ref[0:1, :], lon_second_ref[0:1, :])
    east, west = east[:1], west[:1]
    east_low = side_ref[0, 0:1, 2:3] * down_rows[12:13, 2:3] * (east_down - east)
    west_low = side_ref[0, 0:1, 1:2] * down_rows[14:15, 8:9] * (west_down - west)
    at = slice(rows_n - 1, rows_n)
    east_onto = by_flag(flag_ref, 2, up_rows[14:15, 8:9], side_ref[4, at, 2:3])
    west_onto = by_flag(flag_ref, 2, up_rows[12:13, 2:3], side_ref[4, at, 1:2])
    east_high = side_ref[0, at, 2:3] * east_onto * east_up
    west_high = side_ref[0, at, 1:2] * west_onto * west_up
    turn_ref[...] = turn_in_ref[...]
    turn_ref[0:1, :] = turn_in_ref[0:1, :] + turned_columns(east_low, west_low)
    turn_ref[at, :] = turn_in_ref[at, :] + turned_columns(east_high, west_high)

    plane = (levels, cols_n)
    corner_at = 4 * sublane(plane)

    def corner(row, place):
        found = jnp.where(lane(plane) == corner_at + place, jnp.broadcast_to(row, plane), 0.0)
        return jnp.sum(found, axis=1, keepdims=True)

    def edge(block, place):
        begin = ends + 2 + place * levels_n
        filler = jnp.zeros((levels - levels_n, cols_n), jnp.float32)
        return jnp.concatenate([block[begin : begin + levels_n], filler], axis=0)

    def edge_step(block, outer, inner, eastern, western, base):
        def coefficient(place):
            return edge_ref[base + place : base + place + 1, :]

        level = sublane(plane)
        higher = jnp.where(level > 0, pltpu.roll(block, 1, 0) - block, 0.0)
        lower = jnp.where(level < levels_n - 1, pltpu.roll(block, levels - 1, 0) - block, 0.0)
        change = (
            coefficient(2) * shifted(block, -1, 1, eastern)
            + coefficient(3) * shifted(block, 1, 1, western)
            + coefficient(4) * inner
            + coefficient(5) * outer
            - coefficient(1) * block
            + coefficient(6) * (higher + lower)
        )
        return block + coefficient(0) * change

    above = by_flag(flag_ref, 2, reversed_lanes(edge(up, 0)), edge(up, 0))
    above_outer = by_flag(flag_ref, 2, reversed_lanes(edge(up, 1)), edge(up, 1))
    below, below_outer = edge(down, 0), edge(down, 1)
    above_next = edge_step(
        above, above_outer, edges_ref[3], corner(east_up, 2), corner(west_up, 1), 0
    )
    below_next = edge_step(
        below, below_outer, edges_ref[0], corner(east_down, 2), corner(west_down, 1), SUB
    )
    def rows_of(block):
        return [block[level : level + 1] for level in range(levels_n)]

    patch = (
        south_row, north_row, rows_of(south_row * (below - edges_ref[0])), rows_of(north_row * above)
    )
    copies = []

    def store(level, top, found):
        done_ref[level, top : top + SUB, :] = found
        if level == levels_n - 1 and (top + SUB) % (rows_n // sems.shape[0]) == 0:
            rows = slice(top + SUB - rows_n // sems.shape[0], top + SUB)
            copy = pltpu.make_async_copy(
                done_ref.at[:, rows, :], out_ref.at[:, rows, :], sems.at[len(copies)]
            )
            copy.start()
            copies.append(copy)

    advance(
        half_ref, masked_ref, field_ref, turn_ref, rows_of(below_next), rows_of(above_next), store, patch
    )
    for copy in copies:
        copy.wait()


def kernel_call(mebibytes, body, out_shape, scratch=(), ins=None, outs=None):
    memory = {}
    if ins is not None:
        memory["in_specs"] = [pl.BlockSpec(memory_space=space) for space in ins]
    if outs is not None:
        spec = pl.BlockSpec(memory_space=outs)
        memory["out_specs"] = (spec,) * len(out_shape) if isinstance(out_shape, tuple) else spec
    return pl.pallas_call(
        body,
        out_shape=out_shape,
        scratch_shapes=list(scratch),
        compiler_params=pltpu.CompilerParams(vmem_limit_bytes=mebibytes * MIB),
        **memory,
    )


def exchanged(value, devices):
    rows = value.reshape(devices, 1, value.size // devices)
    return lax.all_to_all(rows, BOTH, split_axis=0, concat_axis=0, tiled=True).reshape(value.shape)


def f32(*shape):
    return jax.ShapeDtypeStruct(shape, jnp.float32)


def lon_swaps(first_value, second_value):
    count = lax.axis_size("lon")
    assert count % 2 == 0
    first = [(i, i ^ 1) for i in range(count)]
    second = [(i, (i + 1 if i % 2 else i - 1) % count) for i in range(count)]
    second_found = lax.ppermute(second_value, "lon", second)
    return lax.ppermute(first_value, "lon", first), second_found


def lat_swaps(*values):
    lons, lats = lax.axis_size("lon"), lax.axis_size("lat")
    found = []
    for parity in (0, 1):
        pairs = []
        for i in range(lons):
            for j in range(lats):
                other = j + 1 if j % 2 == parity else j - 1
                if other == lats:
                    pairs.append((i * lats + j, (lons - 1 - i) * lats + j))
                elif other >= 0:
                    pairs.append((i * lats + j, i * lats + other))
        found.append(lax.ppermute(values[parity], BOTH, pairs))
    return tuple(found)


def on_device(
    state,
    adjoint_in,
    land_mask,
    east_coef,
    north_coef,
    zonal_flow,
    vertical_coef,
    slot_cell,
    slot_weight,
    arrive_obs,
    obs_value,
    obs_invvar,
):
    levels_n, rows_n, cols_n = state.shape
    devices = lax.axis_size(BOTH)
    slots = slot_cell.shape[1]
    obs_n = obs_value.shape[1]
    assert 2 * (slots // devices) == LANES and cols_n == LANES and 4 * levels_n <= LANES
    half = (levels_n + 1) // 2
    width = rows_n // GROUP * cols_n
    tile = min(slots, SLOT_TILE)
    tiles = slots // tile
    bf16 = jnp.bfloat16
    raw = (land_mask, east_coef, north_coef, zonal_flow, vertical_coef)
    lon, lat = lax.axis_index("lon"), lax.axis_index("lat")
    flags = jnp.stack([1 - lon % 2, 1 - lat % 2, lat == lax.axis_size("lat") - 1]).astype(jnp.int32)
    flags = jnp.broadcast_to(flags[:, None], (3, LANES))

    partial_vals = kernel_call(
        60,
        gather_kernel,
        f32(devices * half, LANES),
        [
            pltpu.VMEM((1, slots), jnp.int32),
            pltpu.VMEM((1, slots), jnp.float32),
            pltpu.VMEM((levels_n, rows_n, cols_n), jnp.float32),
            pltpu.VMEM((levels_n * GROUP, 3 * width), bf16),
            pltpu.SemaphoreType.DMA((2 + levels_n,)),
        ],
        [pltpu.HBM] * 3,
    )(slot_cell, slot_weight, state)
    levels = padded_levels(levels_n)
    partial_vals, raw = lax.optimization_barrier((partial_vals, raw))
    arrived = exchanged(partial_vals, devices)
    columns = kernel_call(4, coefficient_columns_kernel, f32(2 * SUB, rows_n))(*raw)
    arrived, side_coefs = lax.optimization_barrier((arrived, lon_swaps(columns, columns)))

    misfit, outgoing = kernel_call(
        8 + 4 * tiles,
        observe_kernel,
        (f32(levels_n, obs_n), f32(devices * half, LANES)),
        [
            pltpu.VMEM((obs_n, slots), bf16),
            pltpu.VMEM((levels_n, obs_n), jnp.float32),
            pltpu.VMEM((devices * half, LANES), jnp.float32),
            pltpu.SemaphoreType.DMA((5,)),
        ],
        [pltpu.VMEM] * 4, pltpu.HBM,
    )(arrived, arrive_obs, obs_value, obs_invvar)
    outgoing, raw, side_coefs, adjoint_early = lax.optimization_barrier(
        (outgoing, raw, side_coefs, adjoint_in)
    )
    returned = exchanged(outgoing, devices)
    strips = kernel_call(
        5,
        seed_columns_kernel,
        (f32(rows_n, cols_n), f32(rows_n, cols_n)),
    )(adjoint_early, raw[0])
    fields, sides, row_coefs = kernel_call(
        5,
        coefficients_kernel,
        (f32(7, rows_n, cols_n), f32(7, rows_n, cols_n), f32(2 * SUB, cols_n)),
        (),
    )(flags, *raw, *side_coefs)
    returned, strips, fields, sides, row_coefs = lax.optimization_barrier(
        (returned, strips, fields, sides, row_coefs)
    )
    for_second, for_first, own_columns = kernel_call(
        6 + 3 * tiles,
        functools.partial(columns_kernel, levels_n),
        (f32(rows_n // 2, cols_n), f32(rows_n // 2, cols_n), f32(rows_n, cols_n)),
    )(flags, returned, slot_cell, slot_weight, *strips)
    columns_beside = lon_swaps(for_first, for_second)[::-1]
    whole = (levels_n, rows_n, cols_n)
    seed, own_edges = kernel_call(
        22 + 3 * tiles,
        scatter_kernel,
        (f32(*whole), f32(4, levels, cols_n)),
        [pltpu.VMEM((2 * levels_n * GROUP, tile), bf16)],
    )(returned, slot_cell, slot_weight, adjoint_in, land_mask)
    seed, columns_beside = lax.optimization_barrier((seed, columns_beside))
    message = f32((2 * levels_n + 2 * SUB + 2 + SUB - 1) // SUB * SUB, cols_n)
    message_kernel = functools.partial(edge_message_kernel, levels_n)
    messages = kernel_call(2, message_kernel, (message, message), ())(
        flags, own_edges, *columns_beside, row_coefs
    )
    rows_beside = lat_swaps(messages[1], messages[0])
    seed, messages = lax.optimization_barrier((seed, messages))
    beside = kernel_call(
        8,
        beside_kernel,
        (f32(*whole), f32(*whole), f32(rows_n, cols_n)),
        [pltpu.VMEM(whole, jnp.float32)],
    )(flags, seed, fields, sides, own_columns, *columns_beside)
    beside, rows_beside = lax.optimization_barrier((beside, rows_beside))
    adjoint_state = kernel_call(
        10,
        steps_kernel,
        f32(*whole),
        [
            pltpu.VMEM(whole, jnp.float32),
            pltpu.VMEM((rows_n, cols_n), jnp.float32),
            pltpu.VMEM((2 * SUB, cols_n), jnp.float32),
            pltpu.SemaphoreType.DMA((8,)),
        ],
        [pltpu.VMEM] * 11, pltpu.HBM,
    )(flags, *beside, fields, sides, own_edges, *columns_beside, *rows_beside)
    return (adjoint_state, misfit)


def solution(mesh):
    in_specs = (
        P(None, "lat", "lon"),
        P(None, "lat", "lon"),
        P("lat", "lon"),
        P("lat", "lon"),
        P("lat", "lon"),
        P("lat", "lon"),
        P("lat", "lon"),
        P(("lon", "lat"), None),
        P(("lon", "lat"), None),
        P(("lon", "lat"), None),
        P(None, ("lon", "lat")),
        P(None, ("lon", "lat")),
    )
    out_specs = (P(None, "lat", "lon"), P(None, ("lon", "lat")))
    return jax.shard_map(
        on_device, mesh=mesh, in_specs=in_specs, out_specs=out_specs, check_vma=False
    )
```
